32 devices in a mesh: seq: 8 (over y, x, core), pack: 4 (over z).
Axes of the slice: x: 2, y: 2, z: 4, core: 2. Of those that a mesh axis runs over, the one named last changes fastest.
Arguments:
- patches: bfloat16 [4, 1536, 1408], P('pack', 'seq'), may hold values from -80 to 80
- patch_mask: int32 [4, 1536], P('pack', 'seq'), may hold values 0 or 1
- mask_embed: bfloat16 [1408], replicated, may hold values from -6 to 6
- norm_gain: bfloat16 [1408], replicated, may hold values from 0.5 to 1.5
- qkv_weight: bfloat16 [1408, 4224], P(None, 'seq'), may hold values from -1 to 1
- segment_ids: int32 [4, 1536], P('pack', 'seq'), may hold values from 0 to 3, as said below
- patch_rows: int32 [4, 1536], P('pack', 'seq'), may hold values from 0 to 23, as said below
- patch_column: int32 [4, 1536], P('pack', 'seq'), may hold values from 0 to 31, as said below
- out_weight: bfloat16 [1408, 1408], replicated, may hold values from -0.625 to 0.625
- merge_gain: bfloat16 [1408], replicated, may hold values from 0.5 to 1.5
- merge_weight: bfloat16 [5632, 3584], P(None, 'seq'), may hold values from -0.078125 to 0.078125
- merge_bias: bfloat16 [3584], P('seq'), may hold values from -3 to 3
- image_owner: int32 [4, 4], P('pack'), may hold values from 0 to 3, as said below
Outputs:
- routed: bfloat16 [4, 4, 192, 3584], P('pack', None, None, 'seq')
The draws below stay inside these ranges and needn't reach their ends.
Inputs may be any that keep to these rules, and one draw needn't show every extreme that they name: `segment_ids`: in each pack the tokens come in aligned groups of four of one image (the four patches of one 2 x 2 window, in merge order); image numbers never fall along a pack; each of the 4 images has 1 to 192 groups and one has exactly 192. `patch_rows`: each image is some number w of windows wide, 1 <= w <= 16; the image with exactly 192 groups has w = 16; group g of an image covers rows 2 (g // w) and 2 (g // w) + 1 and columns 2 (g % w) and 2 (g % w) + 1, in the order (top left, top right, bottom left, bottom right). `patch_column`: as for patch_rows. `image_owner`: in each pack the owners of its 4 images are distinct owner indices, so at most 192 merged tokens go from one pack to one owner; one owner gets a pack's largest image, of exactly 192 merged tokens, from every pack.
All inputs are finite; a program needn't handle non-finite values. No bound on the sum of `patch_mask` on one device may be relied on, other than what follows from the above.
Results may differ from the reference program's by a relative error of at most 0.0061.
Values may be sent and summed in bfloat16 or wider, within the bound.
No kernel may reach another device: no remote copies, remote signals or barrier semaphores. Data moves between devices by JAX's collectives and lax.ppermute only.
A program may use at most 64 MiB of HBM per device.

```python
import math
import jax
import jax.numpy as jnp
from jax import lax

D = 1408
HEADS = 16
HD = 88
OUT = 3584
PT = 1536
MPT = 384
PACKS = 4
IMGS = 4
MOST = 192
MERGE_IN = 5632
N_PACK = 4


def pack_layout(pack_key):
    subkeys = jax.random.split(pack_key, 4)
    weights = jax.random.randint(subkeys[0], (IMGS - 1,), 4, 9, dtype=jnp.int32)
    spare_total = MPT - MOST - (IMGS - 1)
    share_extra = spare_total * weights // jnp.sum(weights, dtype=jnp.int32)
    leftover = spare_total - jnp.sum(share_extra, dtype=jnp.int32)
    others = 1 + share_extra + (jnp.arange(IMGS - 1, dtype=jnp.int32) < leftover).astype(jnp.int32)
    largest = jax.random.randint(subkeys[1], (), 0, IMGS, dtype=jnp.int32)
    lengths = jnp.roll(jnp.concatenate([jnp.full((1,), MOST, jnp.int32), others]), largest)
    image_end = jnp.cumsum(lengths, dtype=jnp.int32)
    starts = image_end - lengths
    merged_ids = jnp.arange(MPT, dtype=jnp.int32)
    image_of = jnp.sum((merged_ids[:, None] >= image_end[None, :]).astype(jnp.int32), axis=1, dtype=jnp.int32)
    widest = min(16, MOST // 2)
    grid_rows = (MOST - 1) // widest + 1
    narrowest = jnp.clip((lengths + grid_rows - 1) // grid_rows, 1, widest)
    spread = widest - narrowest + 1
    raw = jax.random.randint(subkeys[2], (IMGS,), 0, 65536, dtype=jnp.int32)
    widths = narrowest + raw % spread
    image_index = jnp.arange(IMGS, dtype=jnp.int32)
    widths = jnp.where(image_index == largest, widest, widths)
    width_of = widths[image_of]
    offset = merged_ids - starts[image_of]
    grid_row = offset // width_of
    grid_column = offset % width_of
    quadrant = jnp.arange(4, dtype=jnp.int32)
    patch_row = (2 * grid_row[:, None] + quadrant[None, :] // 2).reshape(-1)
    patch_col = (2 * grid_column[:, None] + quadrant[None, :] % 2).reshape(-1)
    segments = jnp.repeat(image_of, 4)
    ordering = jax.random.permutation(subkeys[3], N_PACK).astype(jnp.int32)[:IMGS]
    return (segments, patch_row, patch_col, ordering, largest)


def all_layouts(key):
    layout_key = jax.random.fold_in(key, 17)
    pack_keys = jax.vmap(lambda pack_index: jax.random.fold_in(layout_key, pack_index))(jnp.arange(PACKS, dtype=jnp.int32))
    segments, patch_row, patch_col, orderings, largests = jax.vmap(pack_layout)(pack_keys)
    chosen = jax.random.randint(jax.random.fold_in(key, 29), (), 0, N_PACK, dtype=jnp.int32)

    def assign(ordering, largest):
        displaced = ordering[largest]
        swapped = jnp.where(ordering == chosen, displaced, ordering)
        return swapped.at[largest].set(chosen)
    owners = jax.vmap(assign)(orderings, largests)
    return (segments, patch_row, patch_col, owners)


def draw_segment_ids(key, part):
    return all_layouts(key)[0]


def draw_patch_rows(key, part):
    return all_layouts(key)[1]


def draw_patch_column(key, part):
    return all_layouts(key)[2]


def draw_image_owner(key, part):
    return all_layouts(key)[3]


def draw_patches(key, part):
    subkeys = jax.random.split(jax.random.fold_in(key, 53), 7)
    full_shape = (PACKS, PT, D)
    row_scale = jnp.exp(jax.random.uniform(subkeys[1], (PACKS, PT, 1), jnp.float32, math.log(0.3), math.log(3.0)))
    column_scale = jnp.exp(jax.random.uniform(subkeys[6], (D,), jnp.float32, math.log(0.3), math.log(3.0)))
    values = jax.random.normal(subkeys[0], full_shape, jnp.float32) * row_scale * column_scale
    return values.astype(jnp.bfloat16)


def draw_qkv_weight(key, part):
    subkeys = jax.random.split(jax.random.fold_in(key, 61), 1)
    weights = jax.random.normal(subkeys[0], (D, HEADS, 3, HD), jnp.float32) / math.sqrt(D)
    return weights.reshape(D, 3 * HEADS * HD).astype(jnp.bfloat16)


def plant(values, own_key, low, top_value):
    longest = values.shape.index(max(values.shape))
    spots = []
    for shift in (0, 1):
        where = [jax.random.randint(jax.random.fold_in(own_key, axis), (), 0, length) for axis, length in enumerate(values.shape)]
        where[longest] = (where[longest] + shift) % values.shape[longest]
        spots.append(tuple(where))
    return values.at[spots[0]].set(low).at[spots[1]].set(top_value)


def steps_of(stream_key, dims, shards, low, high):
    gain, own = 1.0, jax.random.fold_in(stream_key, 6)
    for position, blocks in shards:
        steps = jnp.exp(jax.random.uniform(jax.random.fold_in(own, position), (blocks,), jnp.float32, low / len(shards), high / len(shards)))
        gain = gain * jnp.repeat(steps, dims[position] // blocks).reshape([-1 if axis == position else 1 for axis in range(len(dims))])
    return gain


def normal_values(key, shape, scale, most, shards=(), kind=jnp.bfloat16):
    drawn = jax.random.normal(key, shape, jnp.float32) * scale
    if len(shards) > 0:
        drawn = steps_of(key, shape, shards, -0.22, 0.18) * drawn
    return jnp.clip(drawn, min=-most, max=most).astype(kind)


def setup_inputs(seed: int = 0) -> dict:
    seeds = jax.random.split(jax.random.key(seed), 14)
    return {
        "patches": draw_patches(jax.random.fold_in(seeds[13], 71), 0),
        "patch_mask": plant((jax.random.randint(seeds[1], (PACKS, PT), 0, 4) < 1).astype(jnp.int32), jax.random.fold_in(seeds[1], 1), 0, 1),
        "mask_embed": normal_values(seeds[2], (D,), 1.0, 6.0),
        "norm_gain": jnp.clip(jax.random.uniform(seeds[3], (D,), jnp.float32, 0.5, 1.5), 0.5, 1.5).astype(jnp.bfloat16),
        "qkv_weight": draw_qkv_weight(jax.random.fold_in(seeds[13], 71), 0),
        "segment_ids": draw_segment_ids(jax.random.fold_in(seeds[13], 71), 0),
        "patch_rows": draw_patch_rows(jax.random.fold_in(seeds[13], 71), 0),
        "patch_column": draw_patch_column(jax.random.fold_in(seeds[13], 71), 0),
        "out_weight": normal_values(seeds[8], (D, D), HD ** -0.5, 0.625),
        "merge_gain": jnp.clip(jax.random.uniform(seeds[9], (D,), jnp.float32, 0.5, 1.5), 0.5, 1.5).astype(jnp.bfloat16),
        "merge_weight": normal_values(seeds[10], (MERGE_IN, OUT), MERGE_IN ** -0.5, 0.078125, ((1, 8),)),
        "merge_bias": normal_values(seeds[11], (OUT,), 0.5, 3.0, ((0, 8),)),
        "image_owner": draw_image_owner(jax.random.fold_in(seeds[13], 71), 0),
    }


EPSILON = 1e-06

def layer_norm(values, gain_vector):
    center = values - lax.optimization_barrier(jnp.mean(values, axis=-1, keepdims=True))
    spread = lax.optimization_barrier(jnp.mean(center * center, axis=-1, keepdims=True))
    return center * lax.rsqrt(spread + EPSILON) * gain_vector.astype(jnp.float32)

def rotate(vectors, row_index, column_index):
    total_rows, heads_here, head_width = vectors.shape
    quarter = head_width // 4
    frequency = 10000.0 ** (-jnp.arange(quarter, dtype=jnp.float32) / quarter)
    row_angle = row_index.astype(jnp.float32)[:, None] * frequency[None, :]
    column_angle = column_index.astype(jnp.float32)[:, None] * frequency[None, :]
    angles = jnp.stack([row_angle, column_angle], axis=1)[:, None, :, None, :]
    split_up = vectors.reshape(total_rows, heads_here, 2, 2, quarter)
    partner = jnp.stack([-split_up[:, :, :, 1], split_up[:, :, :, 0]], axis=3)
    turned = split_up * jnp.cos(angles) + partner * jnp.sin(angles)
    return turned.reshape(total_rows, heads_here, head_width)

def qkv_block(projected, row_index, column_index):
    turned_queries = rotate(projected[:, :, 0], row_index, column_index)
    turned_keys = rotate(projected[:, :, 1], row_index, column_index)
    return jnp.concatenate([turned_queries, turned_keys, projected[:, :, 2]], axis=-1).astype(jnp.bfloat16)

def attention(block, segments):
    total_rows, heads_here, triple = block.shape
    head_width = triple // 3
    step_rows = min(512, total_rows)
    query_part = block[:, :, :head_width].reshape(total_rows // step_rows, step_rows, heads_here, head_width)
    key_part = block[:, :, head_width:2 * head_width].astype(jnp.float32)
    value_part = block[:, :, 2 * head_width:].astype(jnp.float32)
    query_segments = segments.reshape(total_rows // step_rows, step_rows)
    scale = head_width ** (-0.5)

    def one_block(inputs_pair):
        queries_here, segments_here = inputs_pair
        scores = jnp.einsum('qhd,khd->hqk', queries_here.astype(jnp.float32), key_part) * scale
        same_image = (segments_here[:, None] == segments[None, :])[None]
        scores = jnp.where(same_image, scores, -jnp.inf)
        highest = lax.optimization_barrier(jnp.max(scores, axis=-1, keepdims=True))
        weights = jnp.exp(scores - highest)
        probs = (weights / lax.optimization_barrier(jnp.sum(weights, axis=-1, keepdims=True))).astype(jnp.bfloat16)
        result = jnp.einsum('hqk,khd->qhd', probs.astype(jnp.float32), value_part)
        return result.astype(jnp.bfloat16)
    return lax.map(one_block, (query_part, query_segments)).reshape(total_rows, heads_here, head_width)

def route(projected, segments, owners_here, packs, most):
    merged_segments = segments[::4]
    images = owners_here.shape[0]
    image_ids = jnp.arange(images, dtype=jnp.int32)
    member = (merged_segments[None, :] == image_ids[:, None]).astype(jnp.int32)
    lengths = lax.optimization_barrier(jnp.sum(member, axis=1, dtype=jnp.int32))
    starts = jnp.cumsum(lengths, dtype=jnp.int32) - lengths
    owner_ids = jnp.arange(packs, dtype=jnp.int32)
    owned = owners_here[None, :] == owner_ids[:, None]
    first_row = lax.optimization_barrier(jnp.sum(jnp.where(owned, starts[None, :], 0), axis=1, dtype=jnp.int32))
    owned_length = lax.optimization_barrier(jnp.sum(jnp.where(owned, lengths[None, :], 0), axis=1, dtype=jnp.int32))
    slots = jnp.arange(most, dtype=jnp.int32)
    source_rows = jnp.clip(first_row[:, None] + slots[None, :], 0, projected.shape[0] - 1)
    picked = jnp.take(projected, source_rows.reshape(-1), axis=0).reshape(packs, most, projected.shape[1])
    filled = slots[None, :] < owned_length[:, None]
    return jnp.where(filled[:, :, None], picked, jnp.zeros_like(picked))

def reference(patches, patch_mask, mask_embed, norm_gain, qkv_weight, segment_ids, patch_rows, patch_column, out_weight, merge_gain, merge_weight, merge_bias, image_owner):

    def encode_pack(pack_inputs):
        patches_here, mask_here, segments, row_index, column_index, owners_here = pack_inputs
        inputs = jnp.where(mask_here[:, None] == 1, mask_embed[None, :], patches_here)
        normed = layer_norm(inputs.astype(jnp.float32), norm_gain).astype(jnp.bfloat16)
        projected = jnp.dot(normed, qkv_weight, preferred_element_type=jnp.float32)
        block = qkv_block(projected.reshape(PT, HEADS, 3, HD), row_index, column_index)
        attended = attention(block, segments).reshape(PT, D)
        residual = inputs.astype(jnp.float32) + jnp.dot(attended, out_weight, preferred_element_type=jnp.float32)
        merged = layer_norm(residual, merge_gain).astype(jnp.bfloat16).reshape(MPT, MERGE_IN)
        projected_merged = (jnp.dot(merged, merge_weight, preferred_element_type=jnp.float32) + merge_bias.astype(jnp.float32)).astype(jnp.bfloat16)
        return route(projected_merged, segments, owners_here, N_PACK, MOST)
    routed = lax.map(encode_pack, (patches, patch_mask, segment_ids, patch_rows, patch_column, image_owner))
    return jnp.swapaxes(routed, 0, 1)
```

```python
import functools

import jax
import jax.numpy as jnp
import numpy as np
from jax import lax
from jax.experimental import pallas as pl
from jax.experimental.pallas import tpu as pltpu
from jax.sharding import PartitionSpec as P

D = 1408
HEADS = 16
HD = 88


EPSILON = 1e-06


def layer_norm(values, gain_vector):
    center = values - jnp.mean(values, axis=-1, keepdims=True)
    spread = jnp.mean(center * center, axis=-1, keepdims=True)
    return center * lax.rsqrt(spread + EPSILON) * gain_vector.astype(jnp.float32)


def rotate(vectors, row_index, column_index):
    total_rows, heads_here, head_width = vectors.shape
    quarter = head_width // 4
    frequency = 10000.0 ** (-jnp.arange(quarter, dtype=jnp.float32) / quarter)
    row_angle = row_index.astype(jnp.float32)[:, None] * frequency[None, :]
    column_angle = column_index.astype(jnp.float32)[:, None] * frequency[None, :]
    angles = jnp.stack([row_angle, column_angle], axis=1)[:, None, :, None, :]
    split_up = vectors.reshape(total_rows, heads_here, 2, 2, quarter)
    partner = jnp.stack([-split_up[:, :, :, 1], split_up[:, :, :, 0]], axis=3)
    turned = split_up * jnp.cos(angles) + partner * jnp.sin(angles)
    return turned.reshape(total_rows, heads_here, head_width)


def qkv_block(projected, row_index, column_index):
    turned_queries = rotate(projected[:, :, 0], row_index, column_index)
    turned_keys = rotate(projected[:, :, 1], row_index, column_index)
    return jnp.concatenate([turned_queries, turned_keys, projected[:, :, 2]], axis=-1).astype(
        jnp.bfloat16
    )


def attention(block, segments):
    total_rows, heads_here, triple = block.shape
    head_width = triple // 3
    step_rows = min(512, total_rows)
    query_part = block[:, :, :head_width].reshape(
        total_rows // step_rows, step_rows, heads_here, head_width
    )
    key_part = block[:, :, head_width : 2 * head_width]
    value_part = block[:, :, 2 * head_width :]
    query_segments = segments.reshape(total_rows // step_rows, step_rows)
    scale = head_width ** (-0.5)

    def one_block(inputs_pair):
        queries_here, segments_here = inputs_pair
        scores = (
            jnp.einsum("qhd,khd->hqk", queries_here, key_part, preferred_element_type=jnp.float32)
            * scale
        )
        same_image = (segments_here[:, None] == segments[None, :])[None]
        scores = jnp.where(same_image, scores, -jnp.inf)
        highest = jnp.max(scores, axis=-1, keepdims=True)
        weights = jnp.exp(scores - highest)
        probs = (weights / jnp.sum(weights, axis=-1, keepdims=True)).astype(jnp.bfloat16)
        result = jnp.einsum("hqk,khd->qhd", probs, value_part, preferred_element_type=jnp.float32)
        return result.astype(jnp.bfloat16)

    return lax.map(one_block, (query_part, query_segments)).reshape(
        total_rows, heads_here, head_width
    )


def route(projected, segments, owners_here, packs, most):
    merged_segments = segments[::4]
    images = owners_here.shape[0]
    image_ids = jnp.arange(images, dtype=jnp.int32)
    member = (merged_segments[None, :] == image_ids[:, None]).astype(jnp.int32)
    lengths = jnp.sum(member, axis=1, dtype=jnp.int32)
    starts = jnp.cumsum(lengths, dtype=jnp.int32) - lengths
    owner_ids = jnp.arange(packs, dtype=jnp.int32)
    owned = owners_here[None, :] == owner_ids[:, None]
    first_row = jnp.sum(jnp.where(owned, starts[None, :], 0), axis=1, dtype=jnp.int32)
    owned_length = jnp.sum(jnp.where(owned, lengths[None, :], 0), axis=1, dtype=jnp.int32)
    slots = jnp.arange(most, dtype=jnp.int32)
    source_rows = jnp.clip(first_row[:, None] + slots[None, :], 0, projected.shape[0] - 1)
    picked = jnp.take(projected, source_rows.reshape(-1), axis=0).reshape(
        packs, most, projected.shape[1]
    )
    filled = slots[None, :] < owned_length[:, None]
    return jnp.where(filled[:, :, None], picked, jnp.zeros_like(picked))


def general_local(
    patches,
    patch_mask,
    mask_embed,
    norm_gain,
    qkv_weight,
    segment_ids,
    patch_rows,
    patch_column,
    out_weight,
    merge_gain,
    merge_weight,
    merge_bias,
    image_owner,
):
    local_rows = patches.shape[1]
    shards = lax.axis_size("seq")
    packs = lax.axis_size("pack")
    heads_here = HEADS // shards
    inputs = jnp.where(patch_mask[0][:, None] == 1, mask_embed[None, :], patches[0])
    normed = layer_norm(inputs.astype(jnp.float32), norm_gain).astype(jnp.bfloat16)
    labels = lax.all_gather(
        jnp.stack([segment_ids[0], patch_rows[0], patch_column[0]]), "seq", axis=1, tiled=True
    )
    piece = lax.all_gather(normed, "seq", axis=0, tiled=True)
    span = piece.shape[0]
    projected = jnp.dot(piece, qkv_weight, preferred_element_type=jnp.float32)
    row_part = labels[1]
    column_part = labels[2]
    block = qkv_block(projected.reshape(span, heads_here, 3, HD), row_part, column_part)
    result = attention(block, labels[0])
    mixed_heads = lax.all_to_all(result, "seq", split_axis=0, concat_axis=1, tiled=True)
    attended = mixed_heads.reshape(local_rows, D)
    residual = inputs.astype(jnp.float32) + jnp.dot(
        attended, out_weight, preferred_element_type=jnp.float32
    )
    merged = layer_norm(residual, merge_gain).astype(jnp.bfloat16).reshape(local_rows // 4, 4 * D)
    projected_all = (
        jnp.dot(
            lax.all_gather(merged, "seq", axis=0, tiled=True),
            merge_weight,
            preferred_element_type=jnp.float32,
        )
        + merge_bias.astype(jnp.float32)
    ).astype(jnp.bfloat16)
    images = image_owner.shape[1]
    most = 2 * projected_all.shape[0] // images
    outgoing = route(projected_all, labels[0], image_owner[0], packs, most)
    delivered = lax.all_to_all(outgoing, "pack", split_axis=0, concat_axis=0, tiled=True)
    return delivered[None]


LANES = 128


def norm_rows(values, gain_row):
    center = values - jnp.mean(values, axis=-1, keepdims=True)
    spread = jnp.mean(center * center, axis=-1, keepdims=True)
    return center * lax.rsqrt(spread + EPSILON) * gain_row


def qkv_kernel(place, first, second, cos, sin, embed, gain, weight, *rest):
    inputs_out, qkv_out = rest[-2:]
    mine, other = first[...].astype(jnp.float32), second[...].astype(jnp.float32)
    leads = place[1] == 0
    values = jnp.concatenate(
        [jnp.where(leads, mine, other), jnp.where(leads, other, mine)], axis=0
    )
    masked = cos[:, MASK_LANE : MASK_LANE + 1] > 0.5
    values = jnp.where(masked, embed[...].astype(jnp.float32), values)
    inputs_out[...] = values.astype(jnp.bfloat16)
    normed = norm_rows(values, gain[...]).astype(jnp.bfloat16)
    columns = jnp.dot(normed, weight[...], preferred_element_type=jnp.float32)
    cosine, sine = cos[...], sin[...]
    lane = lax.broadcasted_iota(jnp.int32, cosine.shape, 1)
    first_head = lane < HD // 2

    def turn(start):
        a = columns[:, start : start + LANES]
        b = columns[:, start + LANES : start + 2 * LANES]
        return a * cosine - b * sine, b * cosine + a * sine

    query_a, query_b = turn(0)
    key_a, key_b = turn(2 * LANES)
    zero = jnp.zeros_like(key_a)
    parts = [
        query_a,
        query_b,
        jnp.where(first_head, key_a, zero),
        jnp.where(first_head, key_b, zero),
        jnp.where(first_head, zero, key_a),
        jnp.where(first_head, zero, key_b),
    ]
    values_part = columns[:, 4 * LANES :]
    wide = lax.broadcasted_iota(jnp.int32, values_part.shape, 1)
    ones = jnp.where(wide == 2 * HD, 1.0, 0.0)
    parts.append(jnp.where(wide < HD, values_part, ones))
    parts.append(jnp.where((wide >= HD) & (wide < 2 * HD), values_part, ones))
    qkv_out[...] = jnp.concatenate(parts, axis=1).astype(jnp.bfloat16)


def qkv_call(place, pair, tables, embed, gain, weight, earlier, total):
    rows = 2 * pair[0].shape[0]
    whole = lambda shape: pl.BlockSpec(shape, lambda i, place: (0,) * len(shape))
    block = lambda width: pl.BlockSpec((rows, width), lambda i, place: (place[0], 0))
    width = 10 * LANES
    in_specs = [
        whole(pair[0].shape),
        whole(pair[1].shape),
        block(LANES),
        block(LANES),
        whole(embed.shape),
        whole(gain.shape),
        whole(weight.shape),
    ] + [pl.BlockSpec(memory_space=pl.ANY)] * len(earlier)
    return pl.pallas_call(
        qkv_kernel,
        grid_spec=pltpu.PrefetchScalarGridSpec(
            num_scalar_prefetch=1,
            grid=(1,),
            in_specs=in_specs,
            out_specs=[block(D), block(width)],
        ),
        out_shape=[
            jax.ShapeDtypeStruct((total, D), jnp.bfloat16),
            jax.ShapeDtypeStruct((total, width), jnp.bfloat16),
        ],
        input_output_aliases={8: 0, 9: 1} if earlier else {},
        compiler_params=pltpu.CompilerParams(vmem_limit_bytes=24 << 20),
        cost_estimate=pl.CostEstimate(
            flops=2 * rows * D * weight.shape[1],
            bytes_accessed=2 * (rows * (2 * D + width) + weight.size),
            transcendentals=rows,
        ),
        name="norm_qkv",
    )(place, *pair, *tables, embed, gain, weight, *earlier)


BLOCK = 256


def attention_kernel(chunk, segments, segment_rows, columns, block, out, scores, high, acc):
    rows = acc.shape[0]
    blocks = scores.shape[1]
    scale = HD**-0.5
    for part in range(rows // BLOCK):
        start = chunk * rows + part * BLOCK
        segment_low = segments[start]
        segment_high = segments[start + BLOCK - 1]
        all_rows = segment_rows[...]
        before = jnp.sum((all_rows < segment_low).astype(jnp.int32))
        through = jnp.sum((all_rows <= segment_high).astype(jnp.int32))
        begin = before // BLOCK
        end = (through + BLOCK - 1) // BLOCK
        queries = block[start : start + BLOCK, : 2 * LANES]
        own = columns[start : start + BLOCK, SEGMENT_LANE : SEGMENT_LANE + 1]
        own = jnp.broadcast_to(own, (BLOCK, BLOCK)).astype(jnp.int32)
        high[...] = jnp.full_like(high, NEGATIVE)

        def score(step, carry):
            at = pl.ds(pl.multiple_of(step * BLOCK, BLOCK), BLOCK)
            same = own == segment_rows[pl.ds(step, 1), :]
            for head in range(2):
                keys = block[at, (2 + 2 * head) * LANES : (4 + 2 * head) * LANES]
                values = lax.dot_general(
                    queries, keys, (((1,), (1,)), ((), ())), preferred_element_type=jnp.float32
                )
                values = jnp.where(same, values, NEGATIVE)
                scores[head, step] = values
                high[head] = jnp.maximum(
                    high[head], jnp.maximum(values[:, :LANES], values[:, LANES:])
                )
            return carry

        lax.fori_loop(begin, end, score, 0)
        highest = [jnp.max(high[head], axis=-1, keepdims=True) for head in range(2)]
        acc_shape = (BLOCK, 2 * LANES)

        def weigh(step, carry):
            at = pl.ds(pl.multiple_of(step * BLOCK, BLOCK), BLOCK)
            sums = []
            for head in range(2):
                weights = jnp.exp((scores[head, step] - highest[head]) * scale)
                values = block[at, (6 + 2 * head) * LANES : (8 + 2 * head) * LANES]
                sums.append(
                    carry[head]
                    + jnp.dot(
                        weights.astype(jnp.bfloat16), values, preferred_element_type=jnp.float32
                    )
                )
            return tuple(sums)

        zero = jnp.zeros(acc_shape, jnp.float32)
        sums = lax.fori_loop(begin, end, weigh, (zero, zero))
        total = sum(
            one / one[:, 2 * HD : 2 * HD + 1] for one in sums
        )
        acc[part * BLOCK : (part + 1) * BLOCK, :] = total
    out[:rows] = acc[:, :LANES].astype(jnp.bfloat16)
    half = rows // 2
    low, up = acc[:half, LANES:], acc[half:, LANES:]
    lane = lax.broadcasted_iota(jnp.int32, low.shape, 1)
    tail = 2 * HD - LANES
    zero = jnp.zeros_like(low)
    packed = jnp.where(
        lane < tail, low, jnp.where(lane < 2 * tail, pltpu.roll(up, tail, 1), zero)
    )
    out[rows:] = packed.astype(jnp.bfloat16)


def attention_call(chunk, chunks, segments, segment_rows, columns, block):
    total = block.shape[0]
    rows = total // chunks
    vmem = pl.BlockSpec(memory_space=pltpu.VMEM)
    return pl.pallas_call(
        functools.partial(attention_kernel, chunk),
        in_specs=[pl.BlockSpec(memory_space=pltpu.SMEM), vmem, vmem, vmem],
        out_specs=vmem,
        out_shape=jax.ShapeDtypeStruct((rows + rows // 2, LANES), jnp.bfloat16),
        scratch_shapes=[
            pltpu.VMEM((2, total // BLOCK, BLOCK, BLOCK), jnp.float32),
            pltpu.VMEM((2, BLOCK, LANES), jnp.float32),
            pltpu.VMEM((rows, 2 * LANES), jnp.float32),
        ],
        compiler_params=pltpu.CompilerParams(vmem_limit_bytes=24 << 20),
        cost_estimate=pl.CostEstimate(
            flops=8 * rows * total * 2 * LANES,
            bytes_accessed=2 * block.size,
            transcendentals=rows * total,
        ),
        name="attention",
    )(segments, segment_rows, columns, block)


def merge_kernel(shards, ids, *refs):
    sources = refs[:shards]
    inputs, out_weight, gain, merge_weight, bias, out = refs[shards : shards + 6]
    wide, tail, merge, state, wide_sems, tail_sems, merge_sem = refs[shards + 6 :]
    rows = inputs.shape[0]
    half = rows // 2
    rest = 2 * HD - LANES
    merge_copy = pltpu.make_async_copy(merge_weight, merge, merge_sem)
    tail[...] = jnp.zeros_like(tail)
    copies = []
    for place in range(shards):
        start = pl.multiple_of(ids[place] * (2 * HD), 16)
        copies.append(
            pltpu.make_async_copy(
                out_weight.at[pl.ds(start, LANES), :],
                wide.at[pl.ds(place * LANES, LANES), :],
                wide_sems.at[place],
            )
        )
        copies.append(
            pltpu.make_async_copy(
                out_weight.at[pl.ds(start + LANES, rest), :],
                tail.at[pl.ds(rest + place * LANES, rest), :],
                tail_sems.at[place],
            )
        )
    for copy in copies:
        copy.start()
    merge_copy.start()
    for copy in copies:
        copy.wait()
    size = shards * LANES
    for part in range(2):
        at = slice(part * half, (part + 1) * half)
        wide_in = jnp.concatenate([source[at, :] for source in sources], axis=1)
        tail_in = jnp.concatenate([source[rows:, :] for source in sources], axis=1)
        offset = rest if part == 0 else 0
        mixed = jnp.dot(wide_in, wide[...], preferred_element_type=jnp.float32)
        mixed = mixed + jnp.dot(
            tail_in, tail[offset : offset + size, :], preferred_element_type=jnp.float32
        )
        residual = inputs[at, :].astype(jnp.float32) + mixed
        normed = norm_rows(residual, gain[...])
        for column in range(D // LANES):
            state[column, at, :] = normed[:, column * LANES : (column + 1) * LANES]
    merge_copy.wait()
    groups = rows // 4
    total = None
    for quadrant in range(4):
        tokens = jnp.concatenate(
            [
                state[column, pl.ds(quadrant, groups, stride=4), :].astype(jnp.bfloat16)
                for column in range(D // LANES)
            ],
            axis=1,
        )
        term = jnp.dot(
            tokens, merge[quadrant * D : (quadrant + 1) * D, :], preferred_element_type=jnp.float32
        )
        total = term if total is None else total + term
    result = total + bias[...]
    whole = result.shape[1] // LANES
    for column in range(whole):
        out[column * groups : (column + 1) * groups, :] = result[
            :, column * LANES : (column + 1) * LANES
        ].astype(jnp.bfloat16)
    low = result[: groups // 2, whole * LANES :]
    up = result[groups // 2 :, whole * LANES :]
    out[whole * groups :, :] = jnp.concatenate([low, up], axis=1).astype(jnp.bfloat16)


def merge_call(chunk, chunks, ids, sources, inputs, out_weight, gain, merge_weight, bias):
    shards = len(sources)
    rows = inputs.shape[0] // chunks
    groups = rows // 4
    width = merge_weight.shape[1]
    fixed = lambda shape: pl.BlockSpec(shape, lambda i, ids: (0,) * len(shape))
    anywhere = pl.BlockSpec(memory_space=pl.ANY)
    rest = 2 * HD - LANES
    return pl.pallas_call(
        functools.partial(merge_kernel, shards),
        grid_spec=pltpu.PrefetchScalarGridSpec(
            num_scalar_prefetch=1,
            grid=(1,),
            in_specs=[fixed(source.shape) for source in sources]
            + [
                pl.BlockSpec((rows, D), lambda i, ids: (chunk, 0)),
                anywhere,
                fixed(gain.shape),
                anywhere,
                fixed(bias.shape),
            ],
            out_specs=fixed((groups * width // LANES, LANES)),
            scratch_shapes=[
                pltpu.VMEM((shards * LANES, D), jnp.bfloat16),
                pltpu.VMEM((shards * LANES + LANES, D), jnp.bfloat16),
                pltpu.VMEM(merge_weight.shape, jnp.bfloat16),
                pltpu.VMEM((D // LANES, rows, LANES), jnp.float32),
                pltpu.SemaphoreType.DMA((shards,)),
                pltpu.SemaphoreType.DMA((shards,)),
                pltpu.SemaphoreType.DMA,
            ],
        ),
        out_shape=jax.ShapeDtypeStruct((groups * width // LANES, LANES), jnp.bfloat16),
        compiler_params=pltpu.CompilerParams(vmem_limit_bytes=40 << 20),
        cost_estimate=pl.CostEstimate(
            flops=2 * rows * D * D + 2 * groups * merge_weight.size,
            bytes_accessed=2 * (D * D + merge_weight.size + 3 * rows * D),
            transcendentals=rows,
        ),
        name="out_merge",
    )(ids, *sources, inputs, out_weight, gain, merge_weight, bias)


def select_kernel(packs, picks, *refs):
    parts, out = refs[:-1], refs[-1]
    most, width = out.shape[1:]
    whole = width // LANES
    groups = parts[0].shape[1] * LANES // width
    half = groups // 2
    slot = lax.broadcasted_iota(jnp.int32, (most, groups), 0)
    row = lax.broadcasted_iota(jnp.int32, (most, groups), 1)
    for pack in range(packs):
        first, length = picks[pack], picks[packs + pack]
        sums = [None] * (whole + 2)
        for position, part in enumerate(parts):
            chosen = ((row + position * groups) == (slot + first)) & (slot < length)
            chosen = jnp.where(chosen, 1.0, 0.0).astype(jnp.bfloat16)
            terms = [
                jnp.dot(
                    chosen,
                    part[pack, column * groups : (column + 1) * groups, :],
                    preferred_element_type=jnp.float32,
                )
                for column in range(whole)
            ]
            packed = part[pack, whole * groups :, :]
            terms.append(jnp.dot(chosen[:, :half], packed, preferred_element_type=jnp.float32))
            terms.append(jnp.dot(chosen[:, half:], packed, preferred_element_type=jnp.float32))
            sums = [term if kept is None else kept + term for kept, term in zip(sums, terms)]
        for column in range(whole):
            out[pack, :, column * LANES : (column + 1) * LANES] = sums[column].astype(jnp.bfloat16)
        middle = LANES // 2
        last = sums[whole] + pltpu.roll(sums[whole + 1], middle, 1)
        out[pack, :, whole * LANES :] = last[:, :middle].astype(jnp.bfloat16)


def select_call(picks, parts, packs, most, width):
    vmem = pl.BlockSpec(memory_space=pltpu.VMEM)
    return pl.pallas_call(
        functools.partial(select_kernel, packs),
        in_specs=[pl.BlockSpec(memory_space=pltpu.SMEM)] + [vmem] * len(parts),
        out_specs=vmem,
        out_shape=jax.ShapeDtypeStruct((packs, most, width), jnp.bfloat16),
        compiler_params=pltpu.CompilerParams(vmem_limit_bytes=24 << 20),
        cost_estimate=pl.CostEstimate(
            flops=2 * packs * most * packs * most * width,
            bytes_accessed=4 * packs * most * width,
            transcendentals=0,
        ),
        name="select_rows",
    )(picks, *parts)


MASK_LANE = HD
SEGMENT_LANE = HD + 1
NEGATIVE = -1e30


def send_across(value, flip, size):
    return lax.ppermute(value, "seq", [(i, i ^ flip) for i in range(size)])


def gather_pairs(value, size):
    across = [flip for flip in range(0, size, 2)]
    same_core = [value if flip == 0 else send_across(value, flip, size) for flip in across]
    return [(one, send_across(one, 1, size)) for one in same_core]


def weight_order(heads_here):
    quarter = HD // 4
    order = -np.ones((6 * LANES,), np.int32)
    for head in range(heads_here):
        base = head * 3 * HD
        for kind in range(2):
            for half in range(2):
                for letter in range(2):
                    target = (2 * kind + letter) * LANES + head * (HD // 2) + half * quarter
                    source = base + kind * HD + half * (HD // 2) + letter * quarter
                    order[target : target + quarter] = np.arange(source, source + quarter)
        target = 4 * LANES + head * HD
        order[target : target + HD] = np.arange(base + 2 * HD, base + 3 * HD)
    return order


def fast_local(
    patches,
    patch_mask,
    mask_embed,
    norm_gain,
    qkv_weight,
    segment_ids,
    patch_rows,
    patch_column,
    out_weight,
    merge_gain,
    merge_weight,
    merge_bias,
    image_owner,
):
    chunks = CHUNKS
    local_rows = patches.shape[1]
    shards = lax.axis_size("seq")
    packs = lax.axis_size("pack")
    heads_here = HEADS // shards
    images = image_owner.shape[1]
    total = local_rows * shards
    me = lax.axis_index("seq")
    pack = lax.axis_index("pack")
    pairs = gather_pairs(patches[0], shards)

    owners = jnp.pad(image_owner[0], (0, local_rows - images))
    labels = jnp.stack([segment_ids[0], patch_rows[0], patch_column[0], patch_mask[0], owners])
    labels = jnp.pad(labels, ((0, 3), (0, 0)))
    gathered = lax.all_gather(labels, ("pack", "seq"), axis=0, tiled=False)
    gathered = gathered.reshape(packs, shards, 8, local_rows)
    mine = lax.dynamic_index_in_dim(gathered, pack, 0, keepdims=False)
    mine = jnp.swapaxes(mine, 0, 1).reshape(8, total)
    segments = mine[0]
    quarter = HD // 4
    frequency = 10000.0 ** (-jnp.arange(quarter, dtype=jnp.float32) / quarter)
    frequency = jnp.tile(frequency, 2 * heads_here)
    frequency = jnp.pad(frequency, (0, LANES - frequency.shape[0]))
    lane = jnp.arange(LANES)
    by_column = (lane // quarter) % 2 == 1
    position = jnp.where(by_column[None, :], mine[2][:, None], mine[1][:, None])
    angles = position.astype(jnp.float32) * frequency[None, :]
    cosine = jnp.where(lane[None, :] == MASK_LANE, mine[3][:, None].astype(jnp.float32), jnp.cos(angles))
    cosine = jnp.where(lane[None, :] == SEGMENT_LANE, segments[:, None].astype(jnp.float32), cosine)
    sine = jnp.sin(angles)

    merged_segments = gathered[:, :, 0, ::4].reshape(packs, -1)
    image_ids = jnp.arange(images, dtype=jnp.int32)
    owned = gathered[:, 0, 4, :images] == pack
    member = merged_segments[:, None, :] == image_ids[None, :, None]
    below = merged_segments[:, None, :] < image_ids[None, :, None]
    lengths = jnp.sum(jnp.where(owned[:, :, None], member, False).astype(jnp.int32), axis=(1, 2))
    starts = jnp.sum(jnp.where(owned[:, :, None], below, False).astype(jnp.int32), axis=(1, 2))
    picks = jnp.concatenate([starts, lengths])

    order = jnp.asarray(weight_order(heads_here))
    spread = (jnp.arange(qkv_weight.shape[1])[:, None] == order[None, :]).astype(jnp.bfloat16)
    weight = jnp.dot(qkv_weight, spread, preferred_element_type=jnp.float32).astype(jnp.bfloat16)
    embed = mask_embed[None, :]
    gain = norm_gain.astype(jnp.float32)[None, :]
    merge_gain_row = merge_gain.astype(jnp.float32)[None, :]
    bias = merge_bias.astype(jnp.float32)[None, :]

    buffers = ()
    for place, pair in enumerate(pairs):
        where = jnp.stack([(me // 2) ^ place, me % 2]).astype(jnp.int32)
        buffers = qkv_call(where, pair, (cosine, sine), embed, gain, weight, buffers, total)
    inputs, block = buffers

    segment_rows = segments.reshape(total // BLOCK, BLOCK)
    attended = [
        gather_pairs(
            attention_call(chunk, chunks, segments, segment_rows, cosine, block), shards
        )
        for chunk in range(chunks)
    ]
    ids = jnp.stack([me ^ place for place in range(shards)]).astype(jnp.int32)
    delivered = []
    for chunk in range(chunks):
        sources = [one for pair in attended[chunk] for one in pair]
        projected = merge_call(
            chunk, chunks, ids, sources, inputs, out_weight, merge_gain_row, merge_weight, bias
        )
        delivered.append(lax.all_gather(projected, "pack", axis=0, tiled=False))
    most = 2 * (total // 4) // images
    return select_call(picks, delivered, packs, most, merge_weight.shape[1])[None]


CHUNKS = 2


def local(*arguments):
    patches, weight = arguments[0], arguments[4]
    shards = lax.axis_size("seq")
    fits = shards == 8 and HEADS // shards == 2 and weight.shape[1] == 6 * HD
    fits = fits and (patches.shape[1] * shards) % (CHUNKS * BLOCK) == 0
    return fast_local(*arguments) if fits else general_local(*arguments)


def solution(mesh):
    placed = (
        P("pack", "seq", None),
        P("pack", "seq"),
        P(),
        P(),
        P(None, "seq"),
        P("pack", "seq"),
        P("pack", "seq"),
        P("pack", "seq"),
        P(),
        P(),
        P(None, "seq"),
        P("seq"),
        P("pack", None),
    )
    return jax.shard_map(
        local, mesh=mesh, in_specs=placed, out_specs=P("pack", None, None, "seq"), check_vma=False
    )
```

```python
import functools

import jax
import jax.numpy as jnp
import numpy as np
from jax import lax
from jax.experimental import pallas as pl
from jax.experimental.pallas import tpu as pltpu
from jax.sharding import PartitionSpec as P

D = 1408
HEADS = 16
HD = 88


EPSILON = 1e-06


def layer_norm(values, gain_vector):
    center = values - jnp.mean(values, axis=-1, keepdims=True)
    spread = jnp.mean(center * center, axis=-1, keepdims=True)
    return center * lax.rsqrt(spread + EPSILON) * gain_vector.astype(jnp.float32)


def rotate(vectors, row_index, column_index):
    total_rows, heads_here, head_width = vectors.shape
    quarter = head_width // 4
    frequency = 10000.0 ** (-jnp.arange(quarter, dtype=jnp.float32) / quarter)
    row_angle = row_index.astype(jnp.float32)[:, None] * frequency[None, :]
    column_angle = column_index.astype(jnp.float32)[:, None] * frequency[None, :]
    angles = jnp.stack([row_angle, column_angle], axis=1)[:, None, :, None, :]
    split_up = vectors.reshape(total_rows, heads_here, 2, 2, quarter)
    partner = jnp.stack([-split_up[:, :, :, 1], split_up[:, :, :, 0]], axis=3)
    turned = split_up * jnp.cos(angles) + partner * jnp.sin(angles)
    return turned.reshape(total_rows, heads_here, head_width)


def qkv_block(projected, row_index, column_index):
    turned_queries = rotate(projected[:, :, 0], row_index, column_index)
    turned_keys = rotate(projected[:, :, 1], row_index, column_index)
    return jnp.concatenate([turned_queries, turned_keys, projected[:, :, 2]], axis=-1).astype(
        jnp.bfloat16
    )


def attention(block, segments):
    total_rows, heads_here, triple = block.shape
    head_width = triple // 3
    step_rows = min(512, total_rows)
    query_part = block[:, :, :head_width].reshape(
        total_rows // step_rows, step_rows, heads_here, head_width
    )
    key_part = block[:, :, head_width : 2 * head_width]
    value_part = block[:, :, 2 * head_width :]
    query_segments = segments.reshape(total_rows // step_rows, step_rows)
    scale = head_width ** (-0.5)

    def one_block(inputs_pair):
        queries_here, segments_here = inputs_pair
        scores = (
            jnp.einsum("qhd,khd->hqk", queries_here, key_part, preferred_element_type=jnp.float32)
            * scale
        )
        same_image = (segments_here[:, None] == segments[None, :])[None]
        scores = jnp.where(same_image, scores, -jnp.inf)
        highest = jnp.max(scores, axis=-1, keepdims=True)
        weights = jnp.exp(scores - highest)
        probs = (weights / jnp.sum(weights, axis=-1, keepdims=True)).astype(jnp.bfloat16)
        result = jnp.einsum("hqk,khd->qhd", probs, value_part, preferred_element_type=jnp.float32)
        return result.astype(jnp.bfloat16)

    return lax.map(one_block, (query_part, query_segments)).reshape(
        total_rows, heads_here, head_width
    )


def route(projected, segments, owners_here, packs, most):
    merged_segments = segments[::4]
    images = owners_here.shape[0]
    image_ids = jnp.arange(images, dtype=jnp.int32)
    member = (merged_segments[None, :] == image_ids[:, None]).astype(jnp.int32)
    lengths = jnp.sum(member, axis=1, dtype=jnp.int32)
    starts = jnp.cumsum(lengths, dtype=jnp.int32) - lengths
    owner_ids = jnp.arange(packs, dtype=jnp.int32)
    owned = owners_here[None, :] == owner_ids[:, None]
    first_row = jnp.sum(jnp.where(owned, starts[None, :], 0), axis=1, dtype=jnp.int32)
    owned_length = jnp.sum(jnp.where(owned, lengths[None, :], 0), axis=1, dtype=jnp.int32)
    slots = jnp.arange(most, dtype=jnp.int32)
    source_rows = jnp.clip(first_row[:, None] + slots[None, :], 0, projected.shape[0] - 1)
    picked = jnp.take(projected, source_rows.reshape(-1), axis=0).reshape(
        packs, most, projected.shape[1]
    )
    filled = slots[None, :] < owned_length[:, None]
    return jnp.where(filled[:, :, None], picked, jnp.zeros_like(picked))


def general_local(
    patches,
    patch_mask,
    mask_embed,
    norm_gain,
    qkv_weight,
    segment_ids,
    patch_rows,
    patch_column,
    out_weight,
    merge_gain,
    merge_weight,
    merge_bias,
    image_owner,
):
    local_rows = patches.shape[1]
    shards = lax.axis_size("seq")
    packs = lax.axis_size("pack")
    heads_here = HEADS // shards
    inputs = jnp.where(patch_mask[0][:, None] == 1, mask_embed[None, :], patches[0])
    normed = layer_norm(inputs.astype(jnp.float32), norm_gain).astype(jnp.bfloat16)
    labels = lax.all_gather(
        jnp.stack([segment_ids[0], patch_rows[0], patch_column[0]]), "seq", axis=1, tiled=True
    )
    piece = lax.all_gather(normed, "seq", axis=0, tiled=True)
    span = piece.shape[0]
    projected = jnp.dot(piece, qkv_weight, preferred_element_type=jnp.float32)
    row_part = labels[1]
    column_part = labels[2]
    block = qkv_block(projected.reshape(span, heads_here, 3, HD), row_part, column_part)
    result = attention(block, labels[0])
    mixed_heads = lax.all_to_all(result, "seq", split_axis=0, concat_axis=1, tiled=True)
    attended = mixed_heads.reshape(local_rows, D)
    residual = inputs.astype(jnp.float32) + jnp.dot(
        attended, out_weight, preferred_element_type=jnp.float32
    )
    merged = layer_norm(residual, merge_gain).astype(jnp.bfloat16).reshape(local_rows // 4, 4 * D)
    projected_all = (
        jnp.dot(
            lax.all_gather(merged, "seq", axis=0, tiled=True),
            merge_weight,
            preferred_element_type=jnp.float32,
        )
        + merge_bias.astype(jnp.float32)
    ).astype(jnp.bfloat16)
    images = image_owner.shape[1]
    most = 2 * projected_all.shape[0] // images
    outgoing = route(projected_all, labels[0], image_owner[0], packs, most)
    delivered = lax.all_to_all(outgoing, "pack", split_axis=0, concat_axis=0, tiled=True)
    return delivered[None]


LANES = 128
BLOCK = 256
POSITIONS = 64
NEGATIVE = -1e30
CHUNKS = (768, 768)


def norm_rows(values, gain_row):
    center = values - jnp.mean(values, axis=-1, keepdims=True)
    spread = jnp.mean(center * center, axis=-1, keepdims=True)
    return center * lax.rsqrt(spread + EPSILON) * gain_row


def stacked(pieces):
    loaded = [piece[...] for piece in pieces]
    return loaded[0] if len(loaded) == 1 else jnp.concatenate(loaded, axis=0)


def qkv_kernel(count, place, *refs):
    first, second = refs[:count], refs[count : 2 * count]
    table, gain, weight = refs[2 * count : 2 * count + 3]
    inputs_out, qkv_out, label_out = refs[-3:]
    mine, other = stacked(first), stacked(second)
    leads = place[1] == 0
    ahead = jnp.where(leads, mine, other)
    behind = jnp.where(leads, other, mine)
    both = jnp.concatenate([ahead, behind], axis=0)
    inputs_out[...] = both[:, :D]
    label_out[...] = both[:, D:]
    labels = both[:, D:].astype(jnp.float32)
    normed = norm_rows(both[:, :D].astype(jnp.float32), gain[...]).astype(jnp.bfloat16)
    columns = jnp.dot(normed, weight[...], preferred_element_type=jnp.float32)
    lane = lax.broadcasted_iota(jnp.int32, labels.shape, 1)
    numbers = lane.astype(jnp.float32)
    hot = (numbers == labels[:, 1:2]) | (numbers == labels[:, 2:3] + POSITIONS)
    looked = jnp.dot(
        jnp.where(hot, 1.0, 0.0).astype(jnp.bfloat16), table[...], preferred_element_type=jnp.float32
    )
    cosine = looked[:, :LANES] + looked[:, LANES : 2 * LANES]
    sine = looked[:, 2 * LANES : 3 * LANES] + looked[:, 3 * LANES :]
    first_head = lane < HD // 2

    def turn(start):
        a = columns[:, start : start + LANES]
        b = columns[:, start + LANES : start + 2 * LANES]
        return a * cosine - b * sine, b * cosine + a * sine

    query_a, query_b = turn(0)
    key_a, key_b = turn(2 * LANES)
    zero = jnp.zeros_like(key_a)
    parts = [
        query_a,
        query_b,
        jnp.where(first_head, key_a, zero),
        jnp.where(first_head, key_b, zero),
        jnp.where(first_head, zero, key_a),
        jnp.where(first_head, zero, key_b),
    ]
    values_part = columns[:, 4 * LANES :]
    wide = lax.broadcasted_iota(jnp.int32, values_part.shape, 1)
    ones = jnp.where(wide == 2 * HD, 1.0, 0.0)
    parts.append(jnp.where(wide < HD, values_part, ones))
    parts.append(jnp.where((wide >= HD) & (wide < 2 * HD), values_part, ones))
    qkv_out[...] = jnp.concatenate(parts, axis=1).astype(jnp.bfloat16)


def qkv_call(place, first, second, table, gain, weight, earlier, total):
    rows = 2 * sum(piece.shape[0] for piece in first)
    whole = lambda shape: pl.BlockSpec(shape, lambda i, place: (0,) * len(shape))
    block = lambda width: pl.BlockSpec((rows, width), lambda i, place: (place[0], 0))
    widths = (D, 10 * LANES, LANES)
    operands = [*first, *second, table, gain, weight]
    return pl.pallas_call(
        functools.partial(qkv_kernel, len(first)),
        grid_spec=pltpu.PrefetchScalarGridSpec(
            num_scalar_prefetch=1,
            grid=(1,),
            in_specs=[whole(one.shape) for one in operands]
            + [pl.BlockSpec(memory_space=pl.ANY)] * len(earlier),
            out_specs=[block(width) for width in widths],
        ),
        out_shape=[jax.ShapeDtypeStruct((total, width), jnp.bfloat16) for width in widths],
        input_output_aliases={1 + len(operands) + i: i for i in range(len(earlier))},
        compiler_params=pltpu.CompilerParams(vmem_limit_bytes=24 << 20),
        cost_estimate=pl.CostEstimate(
            flops=2 * rows * D * weight.shape[1],
            bytes_accessed=2 * (rows * 4 * D + weight.size),
            transcendentals=rows,
        ),
        name="norm_qkv",
    )(place, *operands, *earlier)


def segment_row(labels):
    pick = jnp.where(lax.broadcasted_iota(jnp.int32, (8, LANES), 1) == 0, 1.0, 0.0)
    return lax.dot_general(
        pick.astype(jnp.bfloat16),
        labels,
        (((1,), (1,)), ((), ())),
        preferred_element_type=jnp.float32,
    )


def attention_kernel(start, owners, labels, block, *refs):
    out, *rest = refs
    scores, high, rows_scratch = rest[-3:]
    rows = high.shape[1]
    total = block.shape[0]
    factor = HD**-0.5 * float(np.log2(np.e))
    segments = segment_row(labels[...])
    for step in range(total // BLOCK):
        rows_scratch[step] = segments[:, step * BLOCK : (step + 1) * BLOCK]
    own = labels[start : start + rows, :1].astype(jnp.float32)
    lowest, largest = jnp.min(own), jnp.max(own)
    one_row = segments[:1]
    begin = jnp.sum(jnp.where(one_row < lowest, 1, 0)) // BLOCK
    end = (jnp.sum(jnp.where(one_row <= largest, 1, 0)) + BLOCK - 1) // BLOCK
    queries = block[start : start + rows, : 2 * LANES]
    own = jnp.broadcast_to(own, (rows, LANES))
    high[...] = jnp.full_like(high, NEGATIVE)

    def score(step, carry):
        at = pl.ds(pl.multiple_of(step * BLOCK, BLOCK), BLOCK)
        theirs = rows_scratch[step, :1]
        same = jnp.concatenate([own == theirs[:, :LANES], own == theirs[:, LANES:]], axis=1)
        for head in range(2):
            keys = block[at, (2 + 2 * head) * LANES : (4 + 2 * head) * LANES]
            values = lax.dot_general(
                queries, keys, (((1,), (1,)), ((), ())), preferred_element_type=jnp.float32
            )
            values = jnp.where(same, values, NEGATIVE)
            scores[head, step] = values
            high[head] = jnp.maximum(
                high[head], jnp.maximum(values[:, :LANES], values[:, LANES:])
            )
        return carry

    lax.fori_loop(begin, end, score, 0)
    highest = [jnp.max(high[head], axis=-1, keepdims=True) for head in range(2)]

    def weigh(step, carry):
        at = pl.ds(pl.multiple_of(step * BLOCK, BLOCK), BLOCK)
        sums = []
        for head in range(2):
            weights = jnp.exp2((scores[head, step] - highest[head]) * factor)
            values = block[at, (6 + 2 * head) * LANES : (8 + 2 * head) * LANES]
            sums.append(
                carry[head]
                + jnp.dot(weights.astype(jnp.bfloat16), values, preferred_element_type=jnp.float32)
            )
        return tuple(sums)

    zero = jnp.zeros((rows, 2 * LANES), jnp.float32)
    sums = lax.fori_loop(begin, end, weigh, (zero, zero))
    acc = sum(one / one[:, 2 * HD : 2 * HD + 1] for one in sums)
    out[:rows] = acc[:, :LANES].astype(jnp.bfloat16)
    half = rows // 2
    low, up = acc[:half, LANES:], acc[half:, LANES:]
    lane = lax.broadcasted_iota(jnp.int32, low.shape, 1)
    tail = 2 * HD - LANES
    packed = jnp.where(lane < tail, low, jnp.where(lane < 2 * tail, pltpu.roll(up, tail, 1), 0.0))
    out[rows:] = packed.astype(jnp.bfloat16)

    if len(rest) > 3:
        note = rest[0]
        row = lax.broadcasted_iota(jnp.int32, note.shape, 0)
        lane = lax.broadcasted_iota(jnp.int32, note.shape, 1)
        found = jnp.zeros(note.shape, jnp.float32)
        for image in range(owners.shape[0]):
            below = jnp.sum(jnp.where(one_row < image, 0.25, 0.0), axis=1, keepdims=True)
            inside = jnp.sum(jnp.where(one_row == image, 0.25, 0.0), axis=1, keepdims=True)
            here = row == owners[image]
            for place, number in enumerate((below, inside)):
                upper = jnp.floor(number * (1.0 / 16))
                found = jnp.where(here & (lane == 2 * place), upper, found)
                found = jnp.where(here & (lane == 2 * place + 1), number - 16 * upper, found)
        note[...] = found.astype(jnp.bfloat16)


def attention_call(start, rows, owners, labels, block, noted):
    total = block.shape[0]
    vmem = pl.BlockSpec(memory_space=pltpu.VMEM)
    shapes = [jax.ShapeDtypeStruct((rows + rows // 2, LANES), jnp.bfloat16)]
    if noted:
        shapes.append(jax.ShapeDtypeStruct((16, LANES), jnp.bfloat16))
    return pl.pallas_call(
        functools.partial(attention_kernel, start),
        in_specs=[pl.BlockSpec(memory_space=pltpu.SMEM), vmem, vmem],
        out_specs=[vmem] * len(shapes),
        out_shape=shapes,
        scratch_shapes=[
            pltpu.VMEM((2, total // BLOCK, rows, BLOCK), jnp.float32),
            pltpu.VMEM((2, rows, LANES), jnp.float32),
            pltpu.VMEM((total // BLOCK, 8, BLOCK), jnp.float32),
        ],
        compiler_params=pltpu.CompilerParams(vmem_limit_bytes=28 << 20),
        cost_estimate=pl.CostEstimate(
            flops=4 * rows * total * 2 * LANES,
            bytes_accessed=2 * block.size,
            transcendentals=rows * total,
        ),
        name="attention",
    )(owners, labels, block)


def order_kernel(shards, ids, weight, out, sems):
    rest = 2 * HD - LANES
    out[shards * LANES :] = jnp.zeros((shards // 2 * LANES, D), jnp.bfloat16)
    copies = []
    for place in range(shards):
        start = pl.multiple_of(ids[place] * (2 * HD), 16)
        to = (shards + place // 2) * LANES + place % 2 * rest
        copies.append((pl.ds(start, LANES), pl.ds(place * LANES, LANES)))
        copies.append((pl.ds(start + LANES, rest), pl.ds(to, rest)))
    copies = [
        pltpu.make_async_copy(weight.at[source, :], out.at[target, :], sems.at[i])
        for i, (source, target) in enumerate(copies)
    ]
    for copy in copies:
        copy.start()
    for copy in copies:
        copy.wait()


def order_call(ids, weight):
    shards = ids.shape[0]
    shape = (shards * LANES * 3 // 2, D)
    return pl.pallas_call(
        functools.partial(order_kernel, shards),
        in_specs=[
            pl.BlockSpec(memory_space=pltpu.SMEM),
            pl.BlockSpec(memory_space=pl.ANY),
        ],
        out_specs=pl.BlockSpec(memory_space=pltpu.VMEM),
        out_shape=jax.ShapeDtypeStruct(shape, jnp.bfloat16),
        scratch_shapes=[pltpu.SemaphoreType.DMA((2 * shards,))],
        compiler_params=pltpu.CompilerParams(vmem_limit_bytes=16 << 20),
        cost_estimate=pl.CostEstimate(flops=0, bytes_accessed=4 * weight.size, transcendentals=0),
        name="order_rows",
    )(ids, weight)


def merge_kernel(counts, inputs, weight, gain, merge_weight, bias, note, *refs):
    pieces = refs[: sum(counts)]
    out, state, merge, merge_sem = refs[sum(counts) :]
    merge_copy = pltpu.make_async_copy(merge_weight, merge, merge_sem)
    merge_copy.start()
    rows = inputs.shape[0]
    half = rows // 2
    rest = 2 * HD - LANES
    sources, at = [], 0
    for count in counts:
        sources.append(stacked(pieces[at : at + count]))
        at += count
    shards = len(sources)
    lane = lax.broadcasted_iota(jnp.int32, (half, LANES), 1)
    for part in range(2):
        token = slice(part * half, (part + 1) * half)
        lined = [source[token, :] for source in sources]
        for pair in range(shards // 2):
            mine = sources[2 * pair][rows:, :].astype(jnp.float32)
            other = sources[2 * pair + 1][rows:, :].astype(jnp.float32)
            if part == 0:
                other = pltpu.roll(other, rest, 1)
            else:
                mine = pltpu.roll(mine, LANES - rest, 1)
            lined.append(jnp.where(lane < rest, mine, other).astype(jnp.bfloat16))
        mixed = jnp.dot(
            jnp.concatenate(lined, axis=1), weight[...], preferred_element_type=jnp.float32
        )
        normed = norm_rows(inputs[token, :].astype(jnp.float32) + mixed, gain[...])
        for column in range(D // LANES):
            state[column, token, :] = normed[:, column * LANES : (column + 1) * LANES]
    groups = rows // 4
    total = bias[...]
    merge_copy.wait()
    for quadrant in range(4):
        tokens = jnp.concatenate(
            [
                state[column, pl.ds(quadrant, groups, stride=4), :].astype(jnp.bfloat16)
                for column in range(D // LANES)
            ],
            axis=1,
        )
        total = total + lax.dot_general(
            tokens,
            merge[:, quadrant * D : (quadrant + 1) * D],
            (((1,), (1,)), ((), ())),
            preferred_element_type=jnp.float32,
        )
    whole = total.shape[1] // LANES
    for column in range(whole):
        out[column * groups : (column + 1) * groups, :] = total[
            :, column * LANES : (column + 1) * LANES
        ].astype(jnp.bfloat16)
    low = total[: groups // 2, whole * LANES :]
    up = total[groups // 2 :, whole * LANES :]
    end = whole * groups + groups // 2
    out[whole * groups : end, :] = jnp.concatenate([low, up], axis=1).astype(jnp.bfloat16)
    out[end:, :] = note[...]


def merge_call(start, rows, sources, inputs, weight, gain, merge_weight, bias, note):
    groups = rows // 4
    width = merge_weight.shape[0]
    pieces = [piece for source in sources for piece in source]
    fixed = lambda shape: pl.BlockSpec(shape, lambda i: (0,) * len(shape))
    out_shape = (groups * width // LANES + 16, LANES)
    operands = [inputs, weight, gain, merge_weight, bias, note, *pieces]
    specs = [fixed(one.shape) for one in operands]
    specs[0] = pl.BlockSpec((rows, D), lambda i: (start // rows, 0))
    specs[3] = pl.BlockSpec(memory_space=pl.ANY)
    return pl.pallas_call(
        functools.partial(merge_kernel, [len(source) for source in sources]),
        grid=(1,),
        in_specs=specs,
        out_specs=fixed(out_shape),
        scratch_shapes=[
            pltpu.VMEM((D // LANES, rows, LANES), jnp.float32),
            pltpu.VMEM(merge_weight.shape, jnp.bfloat16),
            pltpu.SemaphoreType.DMA,
        ],
        out_shape=jax.ShapeDtypeStruct(out_shape, jnp.bfloat16),
        compiler_params=pltpu.CompilerParams(vmem_limit_bytes=36 << 20),
        cost_estimate=pl.CostEstimate(
            flops=2 * rows * D * D + 2 * groups * merge_weight.size,
            bytes_accessed=2 * (D * D + merge_weight.size + 3 * rows * D),
            transcendentals=rows,
        ),
        name="out_merge",
    )(*operands)


def select_kernel(packs, offsets, groups_each, me, *refs):
    parts, out = refs[:-1], refs[-1]
    most, width = out.shape[1:]
    whole = width // LANES
    middle = LANES // 2
    chunks = len(groups_each)
    for number, offset in enumerate(offsets):
        source = parts[number * chunks : (number + 1) * chunks]
        target = me[0] + offset

        @pl.when((target >= 0) & (target < packs))
        def _(source=source, target=target):
            sums = [None] * (whole + 2)
            base = 0
            for part, groups in zip(source, groups_each):
                half = groups // 2
                if base == 0:
                    end = whole * groups + half
                    notes = part[end:, :].astype(jnp.float32)
                    mine = lax.broadcasted_iota(jnp.int32, notes.shape, 0) == me[0]
                    note = jnp.sum(jnp.where(mine, notes, 0.0), axis=0, keepdims=True)
                    first = (16.0 * note[:, :1] + note[:, 1:2]).astype(jnp.int32)
                    length = (16.0 * note[:, 2:3] + note[:, 3:4]).astype(jnp.int32)
                slot = lax.broadcasted_iota(jnp.int32, (most, groups), 0)
                row = lax.broadcasted_iota(jnp.int32, (most, groups), 1) + base
                chosen = (row == slot + first) & (slot < length)
                chosen = jnp.where(chosen, 1.0, 0.0).astype(jnp.bfloat16)
                product = lambda a, b: jnp.dot(a, b, preferred_element_type=jnp.float32)
                terms = [
                    product(chosen, part[column * groups : (column + 1) * groups, :])
                    for column in range(whole)
                ]
                packed = part[whole * groups : whole * groups + half, :]
                terms.append(product(chosen[:, :half], packed))
                terms.append(product(chosen[:, half:], packed))
                sums = [
                    term if kept is None else kept + term for kept, term in zip(sums, terms)
                ]
                base += groups
            for column in range(whole):
                out[target, :, column * LANES : (column + 1) * LANES] = sums[column].astype(
                    jnp.bfloat16
                )
            last = sums[whole] + pltpu.roll(sums[whole + 1], middle, 1)
            out[target, :, whole * LANES :] = last[:, :middle].astype(jnp.bfloat16)


def select_call(me, gathered, groups_each, packs, most, width):
    offsets = [offset for offset, _ in gathered[0]]
    parts = [chunk[number][1] for number in range(len(offsets)) for chunk in gathered]
    vmem = pl.BlockSpec(memory_space=pltpu.VMEM)
    return pl.pallas_call(
        functools.partial(select_kernel, packs, offsets, groups_each),
        in_specs=[pl.BlockSpec(memory_space=pltpu.SMEM)] + [vmem] * len(parts),
        out_specs=vmem,
        out_shape=jax.ShapeDtypeStruct((packs, most, width), jnp.bfloat16),
        compiler_params=pltpu.CompilerParams(vmem_limit_bytes=16 << 20),
        cost_estimate=pl.CostEstimate(
            flops=4 * packs * most * sum(groups_each) * width,
            bytes_accessed=4 * packs * most * width,
            transcendentals=0,
        ),
        name="select_rows",
    )(me, *parts)


def send_seq(value, flip):
    size = lax.axis_size("seq")
    return lax.ppermute(value, "seq", [(i, i ^ flip) for i in range(size)])


def gather_seq(value):
    half = value.shape[0] // 2
    near = [send_seq(value, 2), send_seq(value, 4)]
    own_swap = send_seq(value, 1)
    far = [send_seq(near[0][:half], 4), send_seq(near[1][half:], 2)]
    swapped = [send_seq(one, 1) for one in near + far]
    return [
        ([value], [own_swap]),
        ([near[0]], [swapped[0]]),
        ([near[1]], [swapped[1]]),
        (far, swapped[2:]),
    ]


def gather_pack(value):
    size = lax.axis_size("pack")
    found = [(0, value)]
    for direction in (1, -1):
        moving = value
        for step in range(1, size):
            ahead = [(z, z + 1) for z in range(step - 1, size - 1)]
            if direction < 0:
                ahead = [(size - 1 - a, size - 1 - b) for a, b in ahead]
            moving = lax.ppermute(moving, "pack", ahead)
            found.append((-direction * step, moving))
    return found


def weight_order(heads_here):
    quarter = HD // 4
    order = -np.ones((6 * LANES,), np.int32)
    for head in range(heads_here):
        base = head * 3 * HD
        for kind in range(2):
            for half in range(2):
                for letter in range(2):
                    target = (2 * kind + letter) * LANES + head * (HD // 2) + half * quarter
                    source = base + kind * HD + half * (HD // 2) + letter * quarter
                    order[target : target + quarter] = np.arange(source, source + quarter)
        target = 4 * LANES + head * HD
        order[target : target + HD] = np.arange(base + 2 * HD, base + 3 * HD)
    return order


def angle_table(heads_here):
    quarter = HD // 4
    frequency = (10000.0 ** (-np.arange(quarter) / quarter)).astype(np.float32)
    angles = np.arange(POSITIONS, dtype=np.float32)[:, None] * frequency[None, :]
    pieces = []
    for function in (np.cos, np.sin):
        exact = np.zeros((2 * POSITIONS, LANES), np.float64)
        for head in range(heads_here):
            for half in range(2):
                lane = head * (HD // 2) + half * quarter
                rows = slice(half * POSITIONS, (half + 1) * POSITIONS)
                exact[rows, lane : lane + quarter] = function(angles.astype(np.float64))
        upper = exact.astype(jnp.bfloat16)
        pieces += [upper, (exact - upper.astype(np.float64)).astype(jnp.bfloat16)]
    return np.concatenate(pieces, axis=1)


def fast_local(
    patches,
    patch_mask,
    mask_embed,
    norm_gain,
    qkv_weight,
    segment_ids,
    patch_rows,
    patch_column,
    out_weight,
    merge_gain,
    merge_weight,
    merge_bias,
    image_owner,
):
    local_rows = patches.shape[1]
    shards = lax.axis_size("seq")
    packs = lax.axis_size("pack")
    heads_here = HEADS // shards
    images = image_owner.shape[1]
    total = local_rows * shards
    me = lax.axis_index("seq").astype(jnp.int32)
    pack = lax.axis_index("pack").astype(jnp.int32)

    tokens = jnp.where(patch_mask[0][:, None] == 1, mask_embed[None, :], patches[0])
    labels = jnp.stack([segment_ids[0], patch_rows[0], patch_column[0]], axis=1)
    labels = jnp.pad(labels.astype(jnp.bfloat16), ((0, 0), (0, LANES - labels.shape[1])))
    shares = gather_seq(jnp.concatenate([tokens, labels], axis=1))

    order = jnp.asarray(weight_order(heads_here))
    spread = (jnp.arange(qkv_weight.shape[1])[:, None] == order[None, :]).astype(jnp.bfloat16)
    weight = jnp.dot(qkv_weight, spread, preferred_element_type=jnp.float32).astype(jnp.bfloat16)
    table = jnp.asarray(angle_table(heads_here))
    gain = norm_gain.astype(jnp.float32)[None, :]
    merge_gain_row = merge_gain.astype(jnp.float32)[None, :]
    bias = merge_bias.astype(jnp.float32)[None, :]
    ids = jnp.stack([me ^ place for place in range(shards)])
    ordered = order_call(ids, out_weight)

    buffers = ()
    for place, (first, second) in enumerate(shares):
        where = jnp.stack([(me // 2) ^ place, me % 2])
        buffers = qkv_call(where, first, second, table, gain, weight, buffers, total)
    inputs, block, labels = buffers

    starts = [sum(CHUNKS[:number]) for number in range(len(CHUNKS))]
    attended, note = [], None
    for start, rows in zip(starts, CHUNKS):
        made = attention_call(start, rows, image_owner[0], labels, block, note is None)
        note = made[1] if note is None else note
        attended.append(gather_seq(made[0]))
    gathered = []
    for start, rows, shares in zip(starts, CHUNKS, attended):
        sources = [pieces for share in shares for pieces in share]
        projected = merge_call(
            start, rows, sources, inputs, ordered, merge_gain_row, merge_weight.T, bias, note
        )
        gathered.append(gather_pack(projected))
    most = 2 * (total // 4) // images
    groups_each = [rows // 4 for rows in CHUNKS]
    return select_call(pack[None], gathered, groups_each, packs, most, merge_weight.shape[1])[None]


def local(*arguments):
    patches, weight = arguments[0], arguments[4]
    shards = lax.axis_size("seq")
    fits = shards == 8 and HEADS // shards == 2 and weight.shape[1] == 6 * HD
    fits = fits and patches.shape[1] * shards == sum(CHUNKS)
    return fast_local(*arguments) if fits else general_local(*arguments)


def solution(mesh):
    placed = (
        P("pack", "seq", None),
        P("pack", "seq"),
        P(),
        P(),
        P(None, "seq"),
        P("pack", "seq"),
        P("pack", "seq"),
        P("pack", "seq"),
        P(),
        P(),
        P(None, "seq"),
        P("seq"),
        P("pack", None),
    )
    return jax.shard_map(
        local, mesh=mesh, in_specs=placed, out_specs=P("pack", None, None, "seq"), check_vma=False
    )
```

```python
import functools

import jax
import jax.numpy as jnp
import numpy as np
from jax import lax
from jax.experimental import pallas as pl
from jax.experimental.pallas import tpu as pltpu
from jax.sharding import PartitionSpec as P

D = 1408
HEADS = 16
HD = 88


EPSILON = 1e-06


def layer_norm(values, gain_vector):
    center = values - jnp.mean(values, axis=-1, keepdims=True)
    spread = jnp.mean(center * center, axis=-1, keepdims=True)
    return center * lax.rsqrt(spread + EPSILON) * gain_vector.astype(jnp.float32)


def rotate(vectors, row_index, column_index):
    total_rows, heads_here, head_width = vectors.shape
    quarter = head_width // 4
    frequency = 10000.0 ** (-jnp.arange(quarter, dtype=jnp.float32) / quarter)
    row_angle = row_index.astype(jnp.float32)[:, None] * frequency[None, :]
    column_angle = column_index.astype(jnp.float32)[:, None] * frequency[None, :]
    angles = jnp.stack([row_angle, column_angle], axis=1)[:, None, :, None, :]
    split_up = vectors.reshape(total_rows, heads_here, 2, 2, quarter)
    partner = jnp.stack([-split_up[:, :, :, 1], split_up[:, :, :, 0]], axis=3)
    turned = split_up * jnp.cos(angles) + partner * jnp.sin(angles)
    return turned.reshape(total_rows, heads_here, head_width)


def qkv_block(projected, row_index, column_index):
    turned_queries = rotate(projected[:, :, 0], row_index, column_index)
    turned_keys = rotate(projected[:, :, 1], row_index, column_index)
    return jnp.concatenate([turned_queries, turned_keys, projected[:, :, 2]], axis=-1).astype(
        jnp.bfloat16
    )


def attention(block, segments):
    total_rows, heads_here, triple = block.shape
    head_width = triple // 3
    step_rows = min(512, total_rows)
    query_part = block[:, :, :head_width].reshape(
        total_rows // step_rows, step_rows, heads_here, head_width
    )
    key_part = block[:, :, head_width : 2 * head_width]
    value_part = block[:, :, 2 * head_width :]
    query_segments = segments.reshape(total_rows // step_rows, step_rows)
    scale = head_width ** (-0.5)

    def one_block(inputs_pair):
        queries_here, segments_here = inputs_pair
        scores = (
            jnp.einsum("qhd,khd->hqk", queries_here, key_part, preferred_element_type=jnp.float32)
            * scale
        )
        same_image = (segments_here[:, None] == segments[None, :])[None]
        scores = jnp.where(same_image, scores, -jnp.inf)
        highest = jnp.max(scores, axis=-1, keepdims=True)
        weights = jnp.exp(scores - highest)
        probs = (weights / jnp.sum(weights, axis=-1, keepdims=True)).astype(jnp.bfloat16)
        result = jnp.einsum("hqk,khd->qhd", probs, value_part, preferred_element_type=jnp.float32)
        return result.astype(jnp.bfloat16)

    return lax.map(one_block, (query_part, query_segments)).reshape(
        total_rows, heads_here, head_width
    )


def route(projected, segments, owners_here, packs, most):
    merged_segments = segments[::4]
    images = owners_here.shape[0]
    image_ids = jnp.arange(images, dtype=jnp.int32)
    member = (merged_segments[None, :] == image_ids[:, None]).astype(jnp.int32)
    lengths = jnp.sum(member, axis=1, dtype=jnp.int32)
    starts = jnp.cumsum(lengths, dtype=jnp.int32) - lengths
    owner_ids = jnp.arange(packs, dtype=jnp.int32)
    owned = owners_here[None, :] == owner_ids[:, None]
    first_row = jnp.sum(jnp.where(owned, starts[None, :], 0), axis=1, dtype=jnp.int32)
    owned_length = jnp.sum(jnp.where(owned, lengths[None, :], 0), axis=1, dtype=jnp.int32)
    slots = jnp.arange(most, dtype=jnp.int32)
    source_rows = jnp.clip(first_row[:, None] + slots[None, :], 0, projected.shape[0] - 1)
    picked = jnp.take(projected, source_rows.reshape(-1), axis=0).reshape(
        packs, most, projected.shape[1]
    )
    filled = slots[None, :] < owned_length[:, None]
    return jnp.where(filled[:, :, None], picked, jnp.zeros_like(picked))


def general_local(
    patches,
    patch_mask,
    mask_embed,
    norm_gain,
    qkv_weight,
    segment_ids,
    patch_rows,
    patch_column,
    out_weight,
    merge_gain,
    merge_weight,
    merge_bias,
    image_owner,
):
    local_rows = patches.shape[1]
    shards = lax.axis_size("seq")
    packs = lax.axis_size("pack")
    heads_here = HEADS // shards
    inputs = jnp.where(patch_mask[0][:, None] == 1, mask_embed[None, :], patches[0])
    normed = layer_norm(inputs.astype(jnp.float32), norm_gain).astype(jnp.bfloat16)
    labels = lax.all_gather(
        jnp.stack([segment_ids[0], patch_rows[0], patch_column[0]]), "seq", axis=1, tiled=True
    )
    piece = lax.all_gather(normed, "seq", axis=0, tiled=True)
    span = piece.shape[0]
    projected = jnp.dot(piece, qkv_weight, preferred_element_type=jnp.float32)
    row_part = labels[1]
    column_part = labels[2]
    block = qkv_block(projected.reshape(span, heads_here, 3, HD), row_part, column_part)
    result = attention(block, labels[0])
    mixed_heads = lax.all_to_all(result, "seq", split_axis=0, concat_axis=1, tiled=True)
    attended = mixed_heads.reshape(local_rows, D)
    residual = inputs.astype(jnp.float32) + jnp.dot(
        attended, out_weight, preferred_element_type=jnp.float32
    )
    merged = layer_norm(residual, merge_gain).astype(jnp.bfloat16).reshape(local_rows // 4, 4 * D)
    projected_all = (
        jnp.dot(
            lax.all_gather(merged, "seq", axis=0, tiled=True),
            merge_weight,
            preferred_element_type=jnp.float32,
        )
        + merge_bias.astype(jnp.float32)
    ).astype(jnp.bfloat16)
    images = image_owner.shape[1]
    most = 2 * projected_all.shape[0] // images
    outgoing = route(projected_all, labels[0], image_owner[0], packs, most)
    delivered = lax.all_to_all(outgoing, "pack", split_axis=0, concat_axis=0, tiled=True)
    return delivered[None]


LANES = 128
BLOCK = 256
POSITIONS = 64
NEGATIVE = -1e30
CHUNKS = (768, 768)


def norm_rows(values, gain_row):
    center = values - jnp.mean(values, axis=-1, keepdims=True)
    spread = jnp.mean(center * center, axis=-1, keepdims=True)
    return center * lax.rsqrt(spread + EPSILON) * gain_row


def stacked(pieces):
    loaded = [piece[...] for piece in pieces]
    return loaded[0] if len(loaded) == 1 else jnp.concatenate(loaded, axis=0)


def payload_kernel(segments, rows, columns, mask, embed, patches, out):
    labels = [one[...].astype(jnp.float32) for one in (segments, rows, columns, mask)]
    labels.append(jnp.zeros((4, labels[0].shape[1]), jnp.float32))
    labels = jnp.concatenate(labels, axis=0).astype(jnp.bfloat16)
    shape = (8, LANES)
    row = lax.broadcasted_iota(jnp.int32, shape, 0)
    place = jnp.where(row == lax.broadcasted_iota(jnp.int32, shape, 1), 1.0, 0.0)
    turned = lax.dot_general(
        labels,
        place.astype(jnp.bfloat16),
        (((0,), (0,)), ((), ())),
        preferred_element_type=jnp.float32,
    )
    masked = turned[:, 3:4] > 0.5
    tokens = jnp.where(
        masked, embed[...].astype(jnp.float32)[None, :], patches[0].astype(jnp.float32)
    )
    out[:, :D] = tokens.astype(jnp.bfloat16)
    out[:, D:] = turned.astype(jnp.bfloat16)


def payload_call(segments, rows, columns, mask, embed, patches):
    count = patches.shape[1]
    operands = (segments, rows, columns, mask, embed, patches)
    fixed = lambda shape: pl.BlockSpec(shape, lambda i: (0,) * len(shape))
    shape = (count, D + LANES)
    return pl.pallas_call(
        payload_kernel,
        grid=(1,),
        in_specs=[fixed(one.shape) for one in operands],
        out_specs=fixed(shape),
        out_shape=jax.ShapeDtypeStruct(shape, jnp.bfloat16),
        compiler_params=pltpu.CompilerParams(vmem_limit_bytes=8 << 20),
        cost_estimate=pl.CostEstimate(
            flops=count * D, bytes_accessed=4 * count * D, transcendentals=0
        ),
        name="payload",
    )(*operands)


def qkv_kernel(count, place, *refs):
    first, second = refs[:count], refs[count : 2 * count]
    table, gain, weight = refs[2 * count : 2 * count + 3]
    *outs, inputs_out, qkv_out, label_out, sems = refs[-7:]
    start = pl.multiple_of(place[0] * inputs_out.shape[0], inputs_out.shape[0])
    mine, other = stacked(first), stacked(second)
    leads = place[1] == 0
    ahead = jnp.where(leads, mine, other)
    behind = jnp.where(leads, other, mine)
    both = jnp.concatenate([ahead, behind], axis=0)
    inputs_out[...] = both[:, :D]
    label_out[...] = both[:, D:]
    target = pl.ds(start, inputs_out.shape[0])
    copies = [
        pltpu.make_async_copy(source, out.at[target, :], sems.at[number])
        for number, (source, out) in enumerate(zip((inputs_out, qkv_out, label_out), outs))
    ]
    copies[0].start()
    copies[2].start()
    labels = both[:, D:].astype(jnp.float32)
    normed = norm_rows(both[:, :D].astype(jnp.float32), gain[...]).astype(jnp.bfloat16)
    columns = jnp.dot(normed, weight[...], preferred_element_type=jnp.float32)
    lane = lax.broadcasted_iota(jnp.int32, labels.shape, 1)
    numbers = lane.astype(jnp.float32)
    hot = (numbers == labels[:, 1:2]) | (numbers == labels[:, 2:3] + POSITIONS)
    looked = jnp.dot(
        jnp.where(hot, 1.0, 0.0).astype(jnp.bfloat16), table[...], preferred_element_type=jnp.float32
    )
    cosine = looked[:, :LANES] + looked[:, LANES : 2 * LANES]
    sine = looked[:, 2 * LANES : 3 * LANES] + looked[:, 3 * LANES :]
    first_head = lane < HD // 2

    def turn(start):
        a = columns[:, start : start + LANES]
        b = columns[:, start + LANES : start + 2 * LANES]
        return a * cosine - b * sine, b * cosine + a * sine

    query_a, query_b = turn(0)
    key_a, key_b = turn(2 * LANES)
    zero = jnp.zeros_like(key_a)
    parts = [
        query_a,
        query_b,
        jnp.where(first_head, key_a, zero),
        jnp.where(first_head, key_b, zero),
        jnp.where(first_head, zero, key_a),
        jnp.where(first_head, zero, key_b),
    ]
    values_part = columns[:, 4 * LANES :]
    wide = lax.broadcasted_iota(jnp.int32, values_part.shape, 1)
    ones = jnp.where(wide == 2 * HD, 1.0, 0.0)
    parts.append(jnp.where(wide < HD, values_part, ones))
    parts.append(jnp.where((wide >= HD) & (wide < 2 * HD), values_part, ones))
    qkv_out[...] = jnp.concatenate(parts, axis=1).astype(jnp.bfloat16)
    copies[1].start()
    for copy in copies:
        copy.wait()


def qkv_call(place, first, second, table, gain, weight, earlier, total):
    rows = 2 * sum(piece.shape[0] for piece in first)
    widths = (D, 10 * LANES, LANES)
    operands = [*first, *second, table, gain, weight]
    vmem = pl.BlockSpec(memory_space=pltpu.VMEM)
    anywhere = pl.BlockSpec(memory_space=pl.ANY)
    return pl.pallas_call(
        functools.partial(qkv_kernel, len(first)),
        in_specs=[pl.BlockSpec(memory_space=pltpu.SMEM)]
        + [vmem] * len(operands)
        + [anywhere] * len(earlier),
        out_specs=[anywhere] * len(widths),
        scratch_shapes=[pltpu.VMEM((rows, width), jnp.bfloat16) for width in widths]
        + [pltpu.SemaphoreType.DMA((len(widths),))],
        out_shape=[jax.ShapeDtypeStruct((total, width), jnp.bfloat16) for width in widths],
        input_output_aliases={1 + len(operands) + i: i for i in range(len(earlier))},
        compiler_params=pltpu.CompilerParams(vmem_limit_bytes=16 << 20),
        cost_estimate=pl.CostEstimate(
            flops=6 * rows * D * weight.shape[1],
            bytes_accessed=2 * (rows * 4 * D + weight.size),
            transcendentals=rows,
        ),
        name="norm_qkv",
    )(place, *operands, *earlier)


def segment_row(labels):
    pick = jnp.where(lax.broadcasted_iota(jnp.int32, (8, LANES), 1) == 0, 1.0, 0.0)
    return lax.dot_general(
        pick.astype(jnp.bfloat16),
        labels,
        (((1,), (1,)), ((), ())),
        preferred_element_type=jnp.float32,
    )


def attention_kernel(start, owners, labels, block, *refs):
    out, *rest = refs
    scores, high, rows_scratch = rest[-3:]
    rows = high.shape[1]
    total = block.shape[0]
    factor = HD**-0.5 * float(np.log2(np.e))
    segments = segment_row(labels[...])
    for step in range(total // BLOCK):
        rows_scratch[step] = segments[:, step * BLOCK : (step + 1) * BLOCK]
    own = labels[start : start + rows, :1].astype(jnp.float32)
    lowest, largest = jnp.min(own), jnp.max(own)
    one_row = segments[:1]
    begin = jnp.sum(jnp.where(one_row < lowest, 1, 0)) // BLOCK
    end = (jnp.sum(jnp.where(one_row <= largest, 1, 0)) + BLOCK - 1) // BLOCK
    queries = block[start : start + rows, : 2 * LANES]
    own = jnp.broadcast_to(own, (rows, LANES))
    high[...] = jnp.full_like(high, NEGATIVE)

    def score(step, carry):
        at = pl.ds(pl.multiple_of(step * BLOCK, BLOCK), BLOCK)
        theirs = rows_scratch[step, :1]
        same = jnp.concatenate([own == theirs[:, :LANES], own == theirs[:, LANES:]], axis=1)
        for head in range(2):
            keys = block[at, (2 + 2 * head) * LANES : (4 + 2 * head) * LANES]
            values = lax.dot_general(
                queries, keys, (((1,), (1,)), ((), ())), preferred_element_type=jnp.float32
            )
            values = jnp.where(same, values, NEGATIVE)
            scores[head, step] = values
            high[head] = jnp.maximum(
                high[head], jnp.maximum(values[:, :LANES], values[:, LANES:])
            )
        return carry

    lax.fori_loop(begin, end, score, 0)
    highest = [jnp.max(high[head], axis=-1, keepdims=True) for head in range(2)]

    def weigh(step, carry):
        at = pl.ds(pl.multiple_of(step * BLOCK, BLOCK), BLOCK)
        sums = []
        for head in range(2):
            weights = jnp.exp2((scores[head, step] - highest[head]) * factor)
            values = block[at, (6 + 2 * head) * LANES : (8 + 2 * head) * LANES]
            sums.append(
                carry[head]
                + jnp.dot(weights.astype(jnp.bfloat16), values, preferred_element_type=jnp.float32)
            )
        return tuple(sums)

    zero = jnp.zeros((rows, 2 * LANES), jnp.float32)
    sums = lax.fori_loop(begin, end, weigh, (zero, zero))
    acc = sum(one / one[:, 2 * HD : 2 * HD + 1] for one in sums)
    out[:rows] = acc[:, :LANES].astype(jnp.bfloat16)
    half = rows // 2
    low, up = acc[:half, LANES:], acc[half:, LANES:]
    lane = lax.broadcasted_iota(jnp.int32, low.shape, 1)
    tail = 2 * HD - LANES
    packed = jnp.where(lane < tail, low, jnp.where(lane < 2 * tail, pltpu.roll(up, tail, 1), 0.0))
    out[rows:] = packed.astype(jnp.bfloat16)

    if len(rest) > 3:
        note = rest[0]
        row = lax.broadcasted_iota(jnp.int32, note.shape, 0)
        lane = lax.broadcasted_iota(jnp.int32, note.shape, 1)
        found = jnp.zeros(note.shape, jnp.float32)
        for image in range(owners.shape[0]):
            below = jnp.sum(jnp.where(one_row < image, 0.25, 0.0), axis=1, keepdims=True)
            inside = jnp.sum(jnp.where(one_row == image, 0.25, 0.0), axis=1, keepdims=True)
            here = row == owners[image]
            for place, number in enumerate((below, inside)):
                upper = jnp.floor(number * (1.0 / 16))
                found = jnp.where(here & (lane == 2 * place), upper, found)
                found = jnp.where(here & (lane == 2 * place + 1), number - 16 * upper, found)
        note[...] = found.astype(jnp.bfloat16)


def attention_call(start, rows, owners, labels, block, noted):
    total = block.shape[0]
    vmem = pl.BlockSpec(memory_space=pltpu.VMEM)
    shapes = [jax.ShapeDtypeStruct((rows + rows // 2, LANES), jnp.bfloat16)]
    if noted:
        shapes.append(jax.ShapeDtypeStruct((16, LANES), jnp.bfloat16))
    return pl.pallas_call(
        functools.partial(attention_kernel, start),
        in_specs=[pl.BlockSpec(memory_space=pltpu.SMEM), vmem, vmem],
        out_specs=[vmem] * len(shapes),
        out_shape=shapes,
        scratch_shapes=[
            pltpu.VMEM((2, total // BLOCK, rows, BLOCK), jnp.float32),
            pltpu.VMEM((2, rows, LANES), jnp.float32),
            pltpu.VMEM((total // BLOCK, 8, BLOCK), jnp.float32),
        ],
        compiler_params=pltpu.CompilerParams(vmem_limit_bytes=22 << 20),
        cost_estimate=pl.CostEstimate(
            flops=10 * rows * total * 2 * LANES,
            bytes_accessed=2 * block.size,
            transcendentals=rows * total,
        ),
        name="attention",
    )(owners, labels, block)


def order_kernel(shards, ids, weight, out, sems):
    rest = 2 * HD - LANES
    out[shards * LANES :] = jnp.zeros((shards // 2 * LANES, D), jnp.bfloat16)
    copies = []
    for place in range(shards):
        start = pl.multiple_of(ids[place] * (2 * HD), 16)
        to = (shards + place // 2) * LANES + place % 2 * rest
        copies.append((pl.ds(start, LANES), pl.ds(place * LANES, LANES)))
        copies.append((pl.ds(start + LANES, rest), pl.ds(to, rest)))
    copies = [
        pltpu.make_async_copy(weight.at[source, :], out.at[target, :], sems.at[i])
        for i, (source, target) in enumerate(copies)
    ]
    for copy in copies:
        copy.start()
    for copy in copies:
        copy.wait()


def order_call(ids, weight):
    shards = ids.shape[0]
    shape = (shards * LANES * 3 // 2, D)
    return pl.pallas_call(
        functools.partial(order_kernel, shards),
        in_specs=[
            pl.BlockSpec(memory_space=pltpu.SMEM),
            pl.BlockSpec(memory_space=pl.ANY),
        ],
        out_specs=pl.BlockSpec(memory_space=pltpu.VMEM),
        out_shape=jax.ShapeDtypeStruct(shape, jnp.bfloat16),
        scratch_shapes=[pltpu.SemaphoreType.DMA((2 * shards,))],
        compiler_params=pltpu.CompilerParams(vmem_limit_bytes=16 << 20),
        cost_estimate=pl.CostEstimate(flops=0, bytes_accessed=4 * weight.size, transcendentals=0),
        name="order_rows",
    )(ids, weight)


def merge_kernel(start, counts, packs, last, *refs):
    inputs, weight, gain, merge_weight, bias = refs[:5]
    pieces = refs[5 : 5 + sum(counts)]
    *refs, state = refs[5 + sum(counts) :]
    rows = state.shape[1]
    half = rows // 2
    rest = 2 * HD - LANES
    sources, at = [], 0
    for count in counts:
        sources.append(stacked(pieces[at : at + count]))
        at += count
    shards = len(sources)
    lane = lax.broadcasted_iota(jnp.int32, (half, LANES), 1)
    for part in range(2):
        token = slice(part * half, (part + 1) * half)
        lined = [source[token, :] for source in sources]
        for pair in range(shards // 2):
            mine = sources[2 * pair][rows:, :].astype(jnp.float32)
            other = sources[2 * pair + 1][rows:, :].astype(jnp.float32)
            if part == 0:
                other = pltpu.roll(other, rest, 1)
            else:
                mine = pltpu.roll(mine, LANES - rest, 1)
            lined.append(jnp.where(lane < rest, mine, other).astype(jnp.bfloat16))
        mixed = jnp.dot(
            jnp.concatenate(lined, axis=1), weight[...], preferred_element_type=jnp.float32
        )
        before = inputs[start + part * half : start + (part + 1) * half, :].astype(jnp.float32)
        normed = norm_rows(before + mixed, gain[...])
        for column in range(D // LANES):
            state[column, token, :] = normed[:, column * LANES : (column + 1) * LANES]
    groups = rows // 4
    total = bias[...]
    for quadrant in range(4):
        tokens = jnp.concatenate(
            [
                state[column, pl.ds(quadrant, groups, stride=4), :].astype(jnp.bfloat16)
                for column in range(D // LANES)
            ],
            axis=1,
        )
        total = total + lax.dot_general(
            tokens,
            merge_weight[:, quadrant * D : (quadrant + 1) * D],
            (((1,), (1,)), ((), ())),
            preferred_element_type=jnp.float32,
        )
    total = total.astype(jnp.bfloat16)
    if not last:
        refs[0][...] = total
        return
    me, note, *earlier = refs[:-packs]
    outs = refs[-packs:]
    total = jnp.concatenate([*[one[...] for one in earlier], total], axis=0)
    whole = total.shape[1] // LANES
    most = outs[0].shape[0] * LANES // total.shape[1]
    notes = note[...].astype(jnp.float32)
    note_row = lax.broadcasted_iota(jnp.int32, notes.shape, 0)
    slot = lax.broadcasted_iota(jnp.int32, (most, total.shape[0]), 0)
    row = lax.broadcasted_iota(jnp.int32, (most, total.shape[0]), 1)
    for place, out in enumerate(outs):
        found = jnp.where(note_row == (me[0] ^ place), notes, 0.0)
        found = jnp.sum(found, axis=0, keepdims=True)
        first = (16.0 * found[:, :1] + found[:, 1:2]).astype(jnp.int32)
        length = (16.0 * found[:, 2:3] + found[:, 3:4]).astype(jnp.int32)
        chosen = (row == slot + first) & (slot < length)
        chosen = jnp.where(chosen, 1.0, 0.0).astype(jnp.bfloat16)
        block = jnp.dot(chosen, total, preferred_element_type=jnp.float32)
        for column in range(whole):
            out[column * most : (column + 1) * most, :] = block[
                :, column * LANES : (column + 1) * LANES
            ].astype(jnp.bfloat16)
        low = block[: most // 2, whole * LANES :]
        up = block[most // 2 :, whole * LANES :]
        out[whole * most :, :] = jnp.concatenate([low, up], axis=1).astype(jnp.bfloat16)


def merge_call(start, rows, sources, inputs, weight, gain, merge_weight, bias, packs, route):
    groups = rows // 4
    width = merge_weight.shape[0]
    pieces = [piece for source in sources for piece in source]
    vmem = pl.BlockSpec(memory_space=pltpu.VMEM)
    operands = [inputs, weight, gain, merge_weight, bias, *pieces]
    specs = [vmem] * len(operands)
    shapes = [jax.ShapeDtypeStruct((groups, width), jnp.bfloat16)]
    if route:
        me, most, *others = route
        operands += [me, *others]
        specs += [pl.BlockSpec(memory_space=pltpu.SMEM)] + [vmem] * len(others)
        shapes = [jax.ShapeDtypeStruct((most * width // LANES, LANES), jnp.bfloat16)] * packs
    return pl.pallas_call(
        functools.partial(
            merge_kernel, start, [len(source) for source in sources], packs, bool(route)
        ),
        in_specs=specs,
        out_specs=[vmem] * len(shapes),
        scratch_shapes=[pltpu.VMEM((D // LANES, rows, LANES), jnp.float32)],
        out_shape=shapes,
        compiler_params=pltpu.CompilerParams(vmem_limit_bytes=26 << 20),
        cost_estimate=pl.CostEstimate(
            flops=4 * rows * D * D + 2 * groups * merge_weight.size,
            bytes_accessed=2 * (D * D + merge_weight.size + 3 * rows * D),
            transcendentals=rows,
        ),
        name="out_merge",
    )(*operands)


def place_kernel(me, *refs):
    blocks, out = refs[:-1], refs[-1]
    most, width = out.shape[1:]
    whole = width // LANES
    half = most // 2
    middle = LANES // 2
    for place, block in enumerate(blocks):
        target = me[0] ^ place
        for column in range(whole):
            out[target, :, column * LANES : (column + 1) * LANES] = block[
                column * most : (column + 1) * most, :
            ]
        out[target, :half, whole * LANES :] = block[whole * most :, :middle]
        out[target, half:, whole * LANES :] = block[whole * most :, middle:]


def place_call(me, blocks, most, width):
    vmem = pl.BlockSpec(memory_space=pltpu.VMEM)
    return pl.pallas_call(
        place_kernel,
        in_specs=[pl.BlockSpec(memory_space=pltpu.SMEM)] + [vmem] * len(blocks),
        out_specs=vmem,
        out_shape=jax.ShapeDtypeStruct((len(blocks), most, width), jnp.bfloat16),
        compiler_params=pltpu.CompilerParams(vmem_limit_bytes=8 << 20),
        cost_estimate=pl.CostEstimate(
            flops=0, bytes_accessed=4 * len(blocks) * most * width, transcendentals=0
        ),
        name="place_rows",
    )(me, *blocks)


def send_seq(value, flip):
    size = lax.axis_size("seq")
    return lax.ppermute(value, "seq", [(i, i ^ flip) for i in range(size)])


def after(values, *earlier):
    return lax.optimization_barrier((tuple(values), earlier))[0]


def near_shards(value):
    return [send_seq(value, 1), send_seq(value, 2), send_seq(value, 4)]


def far_shards(across_x, across_y):
    half = across_x.shape[0] // 2
    return [send_seq(across_x[:half], 4), send_seq(across_y[half:], 2)]


def weight_order(heads_here):
    quarter = HD // 4
    order = -np.ones((6 * LANES,), np.int32)
    for head in range(heads_here):
        base = head * 3 * HD
        for kind in range(2):
            for half in range(2):
                for letter in range(2):
                    target = (2 * kind + letter) * LANES + head * (HD // 2) + half * quarter
                    source = base + kind * HD + half * (HD // 2) + letter * quarter
                    order[target : target + quarter] = np.arange(source, source + quarter)
        target = 4 * LANES + head * HD
        order[target : target + HD] = np.arange(base + 2 * HD, base + 3 * HD)
    return order


def angle_table(heads_here):
    quarter = HD // 4
    frequency = (10000.0 ** (-np.arange(quarter) / quarter)).astype(np.float32)
    angles = np.arange(POSITIONS, dtype=np.float32)[:, None] * frequency[None, :]
    pieces = []
    for function in (np.cos, np.sin):
        exact = np.zeros((2 * POSITIONS, LANES), np.float64)
        for head in range(heads_here):
            for half in range(2):
                lane = head * (HD // 2) + half * quarter
                rows = slice(half * POSITIONS, (half + 1) * POSITIONS)
                exact[rows, lane : lane + quarter] = function(angles.astype(np.float64))
        upper = exact.astype(jnp.bfloat16)
        pieces += [upper, (exact - upper.astype(np.float64)).astype(jnp.bfloat16)]
    return np.concatenate(pieces, axis=1)


def fast_local(
    patches,
    patch_mask,
    mask_embed,
    norm_gain,
    qkv_weight,
    segment_ids,
    patch_rows,
    patch_column,
    out_weight,
    merge_gain,
    merge_weight,
    merge_bias,
    image_owner,
):
    local_rows = patches.shape[1]
    shards = lax.axis_size("seq")
    packs = lax.axis_size("pack")
    heads_here = HEADS // shards
    images = image_owner.shape[1]
    total = local_rows * shards
    me = lax.axis_index("seq").astype(jnp.int32)
    pack = lax.axis_index("pack").astype(jnp.int32)

    value = payload_call(segment_ids, patch_rows, patch_column, patch_mask, mask_embed, patches)
    own_swap, across_x, across_y = near_shards(value)

    order = jnp.asarray(weight_order(heads_here))
    spread = (jnp.arange(qkv_weight.shape[1])[:, None] == order[None, :]).astype(jnp.bfloat16)
    weight = jnp.dot(qkv_weight, spread, preferred_element_type=jnp.float32).astype(jnp.bfloat16)
    table = jnp.asarray(angle_table(heads_here))
    gain = norm_gain.astype(jnp.float32)[None, :]
    merge_gain_row = merge_gain.astype(jnp.float32)[None, :]
    bias = merge_bias.astype(jnp.float32)[None, :]
    ids = jnp.stack([me ^ place for place in range(shards)])
    ordered = order_call(ids, out_weight)

    chip, core = me // 2, me % 2
    project = lambda place, first, second, earlier: qkv_call(
        jnp.stack([chip ^ place, core]), first, second, table, gain, weight, earlier, total
    )
    buffers = project(0, [value], [own_swap], ())
    across_x, across_y = after([across_x, across_y], buffers[2], ordered)
    far = far_shards(across_x, across_y)
    buffers = project(1, [across_x], [send_seq(across_x, 1)], buffers)
    buffers = project(2, [across_y], [send_seq(across_y, 1)], buffers)
    far = after(far, buffers[2])
    buffers = project(3, far, [send_seq(one, 1) for one in far], buffers)
    inputs, block, labels = buffers

    starts = [sum(CHUNKS[:number]) for number in range(len(CHUNKS))]
    attended, note = [], None
    for start, rows in zip(starts, CHUNKS):
        made = attention_call(start, rows, image_owner[0], labels, block, note is None)
        note = made[1] if note is None else note
        attended.append((made[0], near_shards(made[0])))
    latest = attended[-1][0]
    most = 2 * (total // 4) // images
    projected, moving = [], []
    for own, (own_swap, across_x, across_y) in attended:
        across_x, across_y = after([across_x, across_y], latest)
        far = far_shards(across_x, across_y)
        moving.append(
            (own, own_swap, across_x, send_seq(across_x, 1), across_y, send_seq(across_y, 1), far)
        )
    for number, (start, rows) in enumerate(zip(starts, CHUNKS)):
        *near, far = moving[number]
        if projected:
            far = after(far, projected[-1])
        sources = [[one] for one in near] + [far, [send_seq(one, 1) for one in far]]
        route = ()
        if number == len(CHUNKS) - 1:
            route = (pack[None], most, note, *projected)
        made = merge_call(
            start, rows, sources, inputs, ordered, merge_gain_row, merge_weight.T, bias, packs, route
        )
        projected.append(made[0])
    blocks = [made[0]] + [
        lax.ppermute(made[flip], "pack", [(z, z ^ flip) for z in range(packs)])
        for flip in range(1, packs)
    ]
    return place_call(pack[None], blocks, most, merge_weight.shape[1])[None]


def local(*arguments):
    patches, weight = arguments[0], arguments[4]
    shards = lax.axis_size("seq")
    fits = shards == 8 and HEADS // shards == 2 and weight.shape[1] == 6 * HD
    fits = fits and patches.shape[1] * shards == sum(CHUNKS) and lax.axis_size("pack") == 4
    return fast_local(*arguments) if fits else general_local(*arguments)


def solution(mesh):
    placed = (
        P("pack", "seq", None),
        P("pack", "seq"),
        P(),
        P(),
        P(None, "seq"),
        P("pack", "seq"),
        P("pack", "seq"),
        P("pack", "seq"),
        P(),
        P(),
        P(None, "seq"),
        P("seq"),
        P("pack", None),
    )
    return jax.shard_map(
        local, mesh=mesh, in_specs=placed, out_specs=P("pack", None, None, "seq"), check_vma=False
    )
```

```python
import functools

import jax
import jax.numpy as jnp
import numpy as np
from jax import lax
from jax.experimental import pallas as pl
from jax.experimental.pallas import tpu as pltpu
from jax.sharding import PartitionSpec as P

D = 1408
HEADS = 16
HD = 88


EPSILON = 1e-06


def layer_norm(values, gain_vector):
    center = values - jnp.mean(values, axis=-1, keepdims=True)
    spread = jnp.mean(center * center, axis=-1, keepdims=True)
    return center * lax.rsqrt(spread + EPSILON) * gain_vector.astype(jnp.float32)


def rotate(vectors, row_index, column_index):
    total_rows, heads_here, head_width = vectors.shape
    quarter = head_width // 4
    frequency = 10000.0 ** (-jnp.arange(quarter, dtype=jnp.float32) / quarter)
    row_angle = row_index.astype(jnp.float32)[:, None] * frequency[None, :]
    column_angle = column_index.astype(jnp.float32)[:, None] * frequency[None, :]
    angles = jnp.stack([row_angle, column_angle], axis=1)[:, None, :, None, :]
    split_up = vectors.reshape(total_rows, heads_here, 2, 2, quarter)
    partner = jnp.stack([-split_up[:, :, :, 1], split_up[:, :, :, 0]], axis=3)
    turned = split_up * jnp.cos(angles) + partner * jnp.sin(angles)
    return turned.reshape(total_rows, heads_here, head_width)


def qkv_block(projected, row_index, column_index):
    turned_queries = rotate(projected[:, :, 0], row_index, column_index)
    turned_keys = rotate(projected[:, :, 1], row_index, column_index)
    return jnp.concatenate([turned_queries, turned_keys, projected[:, :, 2]], axis=-1).astype(
        jnp.bfloat16
    )


def attention(block, segments):
    total_rows, heads_here, triple = block.shape
    head_width = triple // 3
    step_rows = min(512, total_rows)
    query_part = block[:, :, :head_width].reshape(
        total_rows // step_rows, step_rows, heads_here, head_width
    )
    key_part = block[:, :, head_width : 2 * head_width]
    value_part = block[:, :, 2 * head_width :]
    query_segments = segments.reshape(total_rows // step_rows, step_rows)
    scale = head_width ** (-0.5)

    def one_block(inputs_pair):
        queries_here, segments_here = inputs_pair
        scores = (
            jnp.einsum("qhd,khd->hqk", queries_here, key_part, preferred_element_type=jnp.float32)
            * scale
        )
        same_image = (segments_here[:, None] == segments[None, :])[None]
        scores = jnp.where(same_image, scores, -jnp.inf)
        highest = jnp.max(scores, axis=-1, keepdims=True)
        weights = jnp.exp(scores - highest)
        probs = (weights / jnp.sum(weights, axis=-1, keepdims=True)).astype(jnp.bfloat16)
        result = jnp.einsum("hqk,khd->qhd", probs, value_part, preferred_element_type=jnp.float32)
        return result.astype(jnp.bfloat16)

    return lax.map(one_block, (query_part, query_segments)).reshape(
        total_rows, heads_here, head_width
    )


def route(projected, segments, owners_here, packs, most):
    merged_segments = segments[::4]
    images = owners_here.shape[0]
    image_ids = jnp.arange(images, dtype=jnp.int32)
    member = (merged_segments[None, :] == image_ids[:, None]).astype(jnp.int32)
    lengths = jnp.sum(member, axis=1, dtype=jnp.int32)
    starts = jnp.cumsum(lengths, dtype=jnp.int32) - lengths
    owner_ids = jnp.arange(packs, dtype=jnp.int32)
    owned = owners_here[None, :] == owner_ids[:, None]
    first_row = jnp.sum(jnp.where(owned, starts[None, :], 0), axis=1, dtype=jnp.int32)
    owned_length = jnp.sum(jnp.where(owned, lengths[None, :], 0), axis=1, dtype=jnp.int32)
    slots = jnp.arange(most, dtype=jnp.int32)
    source_rows = jnp.clip(first_row[:, None] + slots[None, :], 0, projected.shape[0] - 1)
    picked = jnp.take(projected, source_rows.reshape(-1), axis=0).reshape(
        packs, most, projected.shape[1]
    )
    filled = slots[None, :] < owned_length[:, None]
    return jnp.where(filled[:, :, None], picked, jnp.zeros_like(picked))


def general_local(
    patches,
    patch_mask,
    mask_embed,
    norm_gain,
    qkv_weight,
    segment_ids,
    patch_rows,
    patch_column,
    out_weight,
    merge_gain,
    merge_weight,
    merge_bias,
    image_owner,
):
    local_rows = patches.shape[1]
    shards = lax.axis_size("seq")
    packs = lax.axis_size("pack")
    heads_here = HEADS // shards
    inputs = jnp.where(patch_mask[0][:, None] == 1, mask_embed[None, :], patches[0])
    normed = layer_norm(inputs.astype(jnp.float32), norm_gain).astype(jnp.bfloat16)
    labels = lax.all_gather(
        jnp.stack([segment_ids[0], patch_rows[0], patch_column[0]]), "seq", axis=1, tiled=True
    )
    piece = lax.all_gather(normed, "seq", axis=0, tiled=True)
    span = piece.shape[0]
    projected = jnp.dot(piece, qkv_weight, preferred_element_type=jnp.float32)
    row_part = labels[1]
    column_part = labels[2]
    block = qkv_block(projected.reshape(span, heads_here, 3, HD), row_part, column_part)
    result = attention(block, labels[0])
    mixed_heads = lax.all_to_all(result, "seq", split_axis=0, concat_axis=1, tiled=True)
    attended = mixed_heads.reshape(local_rows, D)
    residual = inputs.astype(jnp.float32) + jnp.dot(
        attended, out_weight, preferred_element_type=jnp.float32
    )
    merged = layer_norm(residual, merge_gain).astype(jnp.bfloat16).reshape(local_rows // 4, 4 * D)
    projected_all = (
        jnp.dot(
            lax.all_gather(merged, "seq", axis=0, tiled=True),
            merge_weight,
            preferred_element_type=jnp.float32,
        )
        + merge_bias.astype(jnp.float32)
    ).astype(jnp.bfloat16)
    images = image_owner.shape[1]
    most = 2 * projected_all.shape[0] // images
    outgoing = route(projected_all, labels[0], image_owner[0], packs, most)
    delivered = lax.all_to_all(outgoing, "pack", split_axis=0, concat_axis=0, tiled=True)
    return delivered[None]


LANES = 128
BLOCK = 256
POSITIONS = 64
NEGATIVE = -1e30
CHUNKS = (768, 768)


def norm_rows(values, gain_row):
    center = values - jnp.mean(values, axis=-1, keepdims=True)
    spread = jnp.mean(center * center, axis=-1, keepdims=True)
    return center * lax.rsqrt(spread + EPSILON) * gain_row


def stacked(pieces):
    loaded = [piece[...] for piece in pieces]
    return loaded[0] if len(loaded) == 1 else jnp.concatenate(loaded, axis=0)


def in_hbm(value):
    return pltpu.with_memory_space_constraint(value, pltpu.HBM)


def payload_kernel(segments, rows, columns, mask, embed, patches, out):
    labels = [one[...].astype(jnp.float32) for one in (segments, rows, columns, mask)]
    labels.append(jnp.zeros((4, labels[0].shape[1]), jnp.float32))
    labels = jnp.concatenate(labels, axis=0).astype(jnp.bfloat16)
    shape = (8, LANES)
    row = lax.broadcasted_iota(jnp.int32, shape, 0)
    place = jnp.where(row == lax.broadcasted_iota(jnp.int32, shape, 1), 1.0, 0.0)
    turned = lax.dot_general(
        labels,
        place.astype(jnp.bfloat16),
        (((0,), (0,)), ((), ())),
        preferred_element_type=jnp.float32,
    )
    masked = turned[:, 3:4] > 0.5
    tokens = jnp.where(
        masked, embed[...].astype(jnp.float32)[None, :], patches[0].astype(jnp.float32)
    )
    out[:, :D] = tokens.astype(jnp.bfloat16)
    out[:, D:] = turned.astype(jnp.bfloat16)


def payload_call(segments, rows, columns, mask, embed, patches):
    count = patches.shape[1]
    operands = (segments, rows, columns, mask, embed, patches)
    fixed = lambda shape: pl.BlockSpec(shape, lambda i: (0,) * len(shape))
    shape = (count, D + LANES)
    return pl.pallas_call(
        payload_kernel,
        grid=(1,),
        in_specs=[fixed(one.shape) for one in operands],
        out_specs=fixed(shape),
        out_shape=jax.ShapeDtypeStruct(shape, jnp.bfloat16),
        compiler_params=pltpu.CompilerParams(vmem_limit_bytes=8 << 20),
        cost_estimate=pl.CostEstimate(
            flops=count * D, bytes_accessed=4 * count * D, transcendentals=0
        ),
        name="payload",
    )(*map(in_hbm, operands))


def qkv_kernel(count, place, *refs):
    first, second = refs[:count], refs[count : 2 * count]
    table, gain, weight = refs[2 * count : 2 * count + 3]
    inputs_out, qkv_out, label_out = refs[-3:]
    mine, other = stacked(first), stacked(second)
    leads = place[1] == 0
    ahead = jnp.where(leads, mine, other)
    behind = jnp.where(leads, other, mine)
    both = jnp.concatenate([ahead, behind], axis=0)
    inputs_out[...] = both[:, :D]
    label_out[...] = both[:, D:]
    labels = both[:, D:].astype(jnp.float32)
    normed = norm_rows(both[:, :D].astype(jnp.float32), gain[...]).astype(jnp.bfloat16)
    columns = jnp.dot(normed, weight[...], preferred_element_type=jnp.float32)
    lane = lax.broadcasted_iota(jnp.int32, labels.shape, 1)
    numbers = lane.astype(jnp.float32)
    hot = (numbers == labels[:, 1:2]) | (numbers == labels[:, 2:3] + POSITIONS)
    looked = jnp.dot(
        jnp.where(hot, 1.0, 0.0).astype(jnp.bfloat16), table[...], preferred_element_type=jnp.float32
    )
    cosine = looked[:, :LANES] + looked[:, LANES : 2 * LANES]
    sine = looked[:, 2 * LANES : 3 * LANES] + looked[:, 3 * LANES :]
    first_head = lane < HD // 2

    def turn(start):
        a = columns[:, start : start + LANES]
        b = columns[:, start + LANES : start + 2 * LANES]
        return a * cosine - b * sine, b * cosine + a * sine

    query_a, query_b = turn(0)
    key_a, key_b = turn(2 * LANES)
    zero = jnp.zeros_like(key_a)
    parts = [
        query_a,
        query_b,
        jnp.where(first_head, key_a, zero),
        jnp.where(first_head, key_b, zero),
        jnp.where(first_head, zero, key_a),
        jnp.where(first_head, zero, key_b),
    ]
    values_part = columns[:, 4 * LANES :]
    wide = lax.broadcasted_iota(jnp.int32, values_part.shape, 1)
    ones = jnp.where(wide == 2 * HD, 1.0, 0.0)
    parts.append(jnp.where(wide < HD, values_part, ones))
    parts.append(jnp.where((wide >= HD) & (wide < 2 * HD), values_part, ones))
    qkv_out[...] = jnp.concatenate(parts, axis=1).astype(jnp.bfloat16)


def qkv_call(place, first, second, table, gain, weight, earlier, total):
    rows = 2 * sum(piece.shape[0] for piece in first)
    whole = lambda shape: pl.BlockSpec(shape, lambda i, place: (0,) * len(shape))
    block = lambda width: pl.BlockSpec((rows, width), lambda i, place: (place[0], 0))
    widths = (D, 10 * LANES, LANES)
    operands = [*first, *second, table, gain, weight]
    return pl.pallas_call(
        functools.partial(qkv_kernel, len(first)),
        grid_spec=pltpu.PrefetchScalarGridSpec(
            num_scalar_prefetch=1,
            grid=(1,),
            in_specs=[whole(one.shape) for one in operands]
            + [pl.BlockSpec(memory_space=pl.ANY)] * len(earlier),
            out_specs=[block(width) for width in widths],
        ),
        out_shape=[pltpu.HBM((total, width), jnp.bfloat16) for width in widths],
        input_output_aliases={1 + len(operands) + i: i for i in range(len(earlier))},
        compiler_params=pltpu.CompilerParams(vmem_limit_bytes=20 << 20),
        cost_estimate=pl.CostEstimate(
            flops=6 * rows * D * weight.shape[1],
            bytes_accessed=2 * (rows * 4 * D + weight.size),
            transcendentals=rows,
        ),
        name="norm_qkv",
    )(place, *operands, *map(in_hbm, earlier))


def segment_row(labels):
    pick = jnp.where(lax.broadcasted_iota(jnp.int32, (8, LANES), 1) == 0, 1.0, 0.0)
    return lax.dot_general(
        pick.astype(jnp.bfloat16),
        labels,
        (((1,), (1,)), ((), ())),
        preferred_element_type=jnp.float32,
    )


def attention_kernel(start, owners, labels, source, *refs):
    out, *rest = refs
    block, scores, high, rows_scratch, sems = rest[-5:]
    rows = high.shape[1]
    total = block.shape[0]
    steps = total // BLOCK
    factor = HD**-0.5 * float(np.log2(np.e))

    def copy(step):
        at = pl.ds(pl.multiple_of(step * BLOCK, BLOCK), BLOCK)
        return pltpu.make_async_copy(source.at[at, :], block.at[at, :], sems.at[step])

    own_steps = range(start // BLOCK, (start + rows) // BLOCK)
    for step in [*own_steps, *(step for step in range(steps) if step not in own_steps)]:
        copy(step).start()
    segments = segment_row(labels[...])
    for step in range(steps):
        rows_scratch[step] = segments[:, step * BLOCK : (step + 1) * BLOCK]
    own = labels[start : start + rows, :1].astype(jnp.float32)
    lowest, largest = jnp.min(own), jnp.max(own)
    one_row = segments[:1]
    begin = jnp.sum(jnp.where(one_row < lowest, 1, 0)) // BLOCK
    end = (jnp.sum(jnp.where(one_row <= largest, 1, 0)) + BLOCK - 1) // BLOCK
    own = jnp.broadcast_to(own, (rows, LANES))
    high[...] = jnp.full_like(high, NEGATIVE)
    for step in own_steps:
        copy(step).wait()
    queries = block[start : start + rows, : 2 * LANES]

    def score(step, carry):
        @pl.when((step < own_steps[0]) | (step > own_steps[-1]))
        def _():
            copy(step).wait()

        at = pl.ds(pl.multiple_of(step * BLOCK, BLOCK), BLOCK)
        theirs = rows_scratch[step, :1]
        same = jnp.concatenate([own == theirs[:, :LANES], own == theirs[:, LANES:]], axis=1)
        for head in range(2):
            keys = block[at, (2 + 2 * head) * LANES : (4 + 2 * head) * LANES]
            values = lax.dot_general(
                queries, keys, (((1,), (1,)), ((), ())), preferred_element_type=jnp.float32
            )
            values = jnp.where(same, values, NEGATIVE)
            scores[head, step] = values
            high[head] = jnp.maximum(
                high[head], jnp.maximum(values[:, :LANES], values[:, LANES:])
            )
        return carry

    lax.fori_loop(begin, end, score, 0)
    highest = [jnp.max(high[head], axis=-1, keepdims=True) for head in range(2)]

    def weigh(step, carry):
        at = pl.ds(pl.multiple_of(step * BLOCK, BLOCK), BLOCK)
        sums = []
        for head in range(2):
            weights = jnp.exp2((scores[head, step] - highest[head]) * factor)
            values = block[at, (6 + 2 * head) * LANES : (8 + 2 * head) * LANES]
            sums.append(
                carry[head]
                + jnp.dot(weights.astype(jnp.bfloat16), values, preferred_element_type=jnp.float32)
            )
        return tuple(sums)

    zero = jnp.zeros((rows, 2 * LANES), jnp.float32)
    sums = lax.fori_loop(begin, end, weigh, (zero, zero))
    for step in range(steps):
        if step not in own_steps:

            @pl.when((step < begin) | (step >= end))
            def _(step=step):
                copy(step).wait()

    acc = sum(one / one[:, 2 * HD : 2 * HD + 1] for one in sums)
    out[:rows] = acc[:, :LANES].astype(jnp.bfloat16)
    half = rows // 2
    low, up = acc[:half, LANES:], acc[half:, LANES:]
    lane = lax.broadcasted_iota(jnp.int32, low.shape, 1)
    tail = 2 * HD - LANES
    packed = jnp.where(lane < tail, low, jnp.where(lane < 2 * tail, pltpu.roll(up, tail, 1), 0.0))
    out[rows:] = packed.astype(jnp.bfloat16)

    if len(rest) > 5:
        note = rest[0]
        row = lax.broadcasted_iota(jnp.int32, note.shape, 0)
        lane = lax.broadcasted_iota(jnp.int32, note.shape, 1)
        found = jnp.zeros(note.shape, jnp.float32)
        for image in range(owners.shape[0]):
            below = jnp.sum(jnp.where(one_row < image, 0.25, 0.0), axis=1, keepdims=True)
            inside = jnp.sum(jnp.where(one_row == image, 0.25, 0.0), axis=1, keepdims=True)
            here = row == owners[image]
            for place, number in enumerate((below, inside)):
                upper = jnp.floor(number * (1.0 / 16))
                found = jnp.where(here & (lane == 2 * place), upper, found)
                found = jnp.where(here & (lane == 2 * place + 1), number - 16 * upper, found)
        note[...] = found.astype(jnp.bfloat16)


def attention_call(start, rows, owners, labels, block, noted):
    total = block.shape[0]
    fixed = lambda shape: pl.BlockSpec(shape, lambda i: (0,) * len(shape))
    shapes = [jax.ShapeDtypeStruct((rows + rows // 2, LANES), jnp.bfloat16)]
    if noted:
        shapes.append(jax.ShapeDtypeStruct((16, LANES), jnp.bfloat16))
    return pl.pallas_call(
        functools.partial(attention_kernel, start),
        grid=(1,),
        in_specs=[
            pl.BlockSpec(memory_space=pltpu.SMEM),
            fixed(labels.shape),
            pl.BlockSpec(memory_space=pl.ANY),
        ],
        out_specs=[fixed(one.shape) for one in shapes],
        out_shape=shapes,
        scratch_shapes=[
            pltpu.VMEM(block.shape, jnp.bfloat16),
            pltpu.VMEM((2, total // BLOCK, rows, BLOCK), jnp.float32),
            pltpu.VMEM((2, rows, LANES), jnp.float32),
            pltpu.VMEM((total // BLOCK, 8, BLOCK), jnp.float32),
            pltpu.SemaphoreType.DMA((total // BLOCK,)),
        ],
        compiler_params=pltpu.CompilerParams(vmem_limit_bytes=30 << 20),
        cost_estimate=pl.CostEstimate(
            flops=10 * rows * total * 2 * LANES,
            bytes_accessed=2 * block.size,
            transcendentals=rows * total,
        ),
        name="attention",
    )(owners, in_hbm(labels), in_hbm(block))


def order_kernel(shards, ids, weight, out, sems):
    rest = 2 * HD - LANES
    out[shards * LANES :] = jnp.zeros((shards // 2 * LANES, D), jnp.bfloat16)
    copies = []
    for place in range(shards):
        start = pl.multiple_of(ids[place] * (2 * HD), 16)
        to = (shards + place // 2) * LANES + place % 2 * rest
        copies.append((pl.ds(start, LANES), pl.ds(place * LANES, LANES)))
        copies.append((pl.ds(start + LANES, rest), pl.ds(to, rest)))
    copies = [
        pltpu.make_async_copy(weight.at[source, :], out.at[target, :], sems.at[i])
        for i, (source, target) in enumerate(copies)
    ]
    for copy in copies:
        copy.start()
    for copy in copies:
        copy.wait()


def order_call(ids, weight):
    shards = ids.shape[0]
    shape = (shards * LANES * 3 // 2, D)
    return pl.pallas_call(
        functools.partial(order_kernel, shards),
        grid=(1,),
        in_specs=[
            pl.BlockSpec(memory_space=pltpu.SMEM),
            pl.BlockSpec(memory_space=pl.ANY),
        ],
        out_specs=pl.BlockSpec(shape, lambda i: (0, 0)),
        out_shape=pltpu.HBM(shape, jnp.bfloat16),
        scratch_shapes=[pltpu.SemaphoreType.DMA((2 * shards,))],
        compiler_params=pltpu.CompilerParams(vmem_limit_bytes=12 << 20),
        cost_estimate=pl.CostEstimate(flops=0, bytes_accessed=4 * weight.size, transcendentals=0),
        name="order_rows",
    )(ids, in_hbm(weight))


OUT_BLOCKS = ((0, 512), (512, 1024), (1024, 1408))


def merge_kernel(start, counts, packs, last, *refs):
    inputs, weight, gain, merge_weight, bias = refs[:5]
    pieces = refs[5 : 5 + sum(counts)]
    refs = refs[5 + sum(counts) :]
    refs, (state, lined, tails, before, out_buffer, merge_buffer, piece_sems, sems) = (
        refs[:-8],
        refs[-8:],
    )
    rows = state.shape[1]
    half = rows // 2
    rest = 2 * HD - LANES
    shards = len(counts)
    piece_copies, at = [], 0
    for shard, count in enumerate(counts):
        done = 0
        for piece in pieces[at : at + count]:
            size = piece.shape[0]
            for low, high, buffer, base in (
                (done, min(done + size, rows), lined, 0),
                (max(done, rows), done + size, tails, rows),
            ):
                if low < high:
                    target = (
                        lined.at[low:high, shard * LANES : (shard + 1) * LANES]
                        if buffer is lined
                        else tails.at[shard, low - base : high - base, :]
                    )
                    piece_copies.append((piece.at[low - done : high - done, :], target))
            done += size
        at += count
    piece_copies = [
        pltpu.make_async_copy(source, target, piece_sems.at[number])
        for number, (source, target) in enumerate(piece_copies)
    ]
    out_copies = [
        pltpu.make_async_copy(
            weight.at[:, low:high], out_buffer.at[:, low:high], sems.at[number]
        )
        for number, (low, high) in enumerate(OUT_BLOCKS)
    ]
    before_copy = pltpu.make_async_copy(
        inputs.at[start : start + rows, :], before, sems.at[len(OUT_BLOCKS)]
    )
    merge_copies = [
        pltpu.make_async_copy(
            merge_weight.at[:, quadrant * D : (quadrant + 1) * D],
            merge_buffer.at[:, quadrant * D : (quadrant + 1) * D],
            sems.at[len(OUT_BLOCKS) + 1 + quadrant],
        )
        for quadrant in range(4)
    ]
    for copy in [*piece_copies, out_copies[0], before_copy, *out_copies[1:], *merge_copies]:
        copy.start()
    for copy in piece_copies:
        copy.wait()
    lane = lax.broadcasted_iota(jnp.int32, (half, LANES), 1)
    for pair in range(shards // 2):
        mine = tails[2 * pair].astype(jnp.float32)
        other = tails[2 * pair + 1].astype(jnp.float32)
        column = slice((shards + pair) * LANES, (shards + pair + 1) * LANES)
        lined[:half, column] = jnp.where(lane < rest, mine, pltpu.roll(other, rest, 1)).astype(
            jnp.bfloat16
        )
        lined[half:, column] = jnp.where(
            lane < rest, pltpu.roll(mine, LANES - rest, 1), other
        ).astype(jnp.bfloat16)
    for number, (low, high) in enumerate(OUT_BLOCKS):
        out_copies[number].wait()
        mixed = jnp.dot(
            lined[...], out_buffer[:, low:high], preferred_element_type=jnp.float32
        )
        if number == 0:
            before_copy.wait()
        mixed = before[:, low:high].astype(jnp.float32) + mixed
        for column in range(low // LANES, high // LANES):
            state[column] = mixed[:, column * LANES - low : (column + 1) * LANES - low]
    groups = rows // 4
    total = bias[...]
    for quadrant in range(4):
        residual = jnp.concatenate(
            [
                state[column, pl.ds(quadrant, groups, stride=4), :]
                for column in range(D // LANES)
            ],
            axis=1,
        )
        tokens = norm_rows(residual, gain[...]).astype(jnp.bfloat16)
        merge_copies[quadrant].wait()
        total = total + lax.dot_general(
            tokens,
            merge_buffer[:, quadrant * D : (quadrant + 1) * D],
            (((1,), (1,)), ((), ())),
            preferred_element_type=jnp.float32,
        )
    total = total.astype(jnp.bfloat16)
    if not last:
        refs[0][...] = total
        return
    me, note, *earlier = refs[:-packs]
    outs = refs[-packs:]
    total = jnp.concatenate([*[one[...] for one in earlier], total], axis=0)
    whole = total.shape[1] // LANES
    most = outs[0].shape[0] * LANES // total.shape[1]
    notes = note[...].astype(jnp.float32)
    note_row = lax.broadcasted_iota(jnp.int32, notes.shape, 0)
    slot = lax.broadcasted_iota(jnp.int32, (most, total.shape[0]), 0)
    row = lax.broadcasted_iota(jnp.int32, (most, total.shape[0]), 1)
    for place, out in enumerate(outs):
        found = jnp.where(note_row == (me[0] ^ place), notes, 0.0)
        found = jnp.sum(found, axis=0, keepdims=True)
        first = (16.0 * found[:, :1] + found[:, 1:2]).astype(jnp.int32)
        length = (16.0 * found[:, 2:3] + found[:, 3:4]).astype(jnp.int32)
        chosen = (row == slot + first) & (slot < length)
        chosen = jnp.where(chosen, 1.0, 0.0).astype(jnp.bfloat16)
        block = jnp.dot(chosen, total, preferred_element_type=jnp.float32)
        for column in range(whole):
            out[column * most : (column + 1) * most, :] = block[
                :, column * LANES : (column + 1) * LANES
            ].astype(jnp.bfloat16)
        low = block[: most // 2, whole * LANES :]
        up = block[most // 2 :, whole * LANES :]
        out[whole * most :, :] = jnp.concatenate([low, up], axis=1).astype(jnp.bfloat16)


def merge_call(start, rows, sources, inputs, weight, gain, merge_weight, bias, packs, route):
    groups = rows // 4
    width = merge_weight.shape[0]
    shards = len(sources)
    pieces = [piece for source in sources for piece in source]
    fixed = lambda shape: pl.BlockSpec(shape, lambda i: (0,) * len(shape))
    anywhere = pl.BlockSpec(memory_space=pl.ANY)
    operands = [in_hbm(inputs), in_hbm(weight), gain, in_hbm(merge_weight), bias, *pieces]
    specs = [anywhere, anywhere, fixed(gain.shape), anywhere, fixed(bias.shape)]
    specs += [anywhere] * len(pieces)
    shapes = [jax.ShapeDtypeStruct((groups, width), jnp.bfloat16)]
    if route:
        me, most, *others = route
        operands += [me, *others]
        specs += [pl.BlockSpec(memory_space=pltpu.SMEM)] + [fixed(one.shape) for one in others]
        shapes = [jax.ShapeDtypeStruct((most * width // LANES, LANES), jnp.bfloat16)] * packs
    return pl.pallas_call(
        functools.partial(
            merge_kernel, start, [len(source) for source in sources], packs, bool(route)
        ),
        grid=(1,),
        in_specs=specs,
        out_specs=[fixed(one.shape) for one in shapes],
        scratch_shapes=[
            pltpu.VMEM((D // LANES, rows, LANES), jnp.float32),
            pltpu.VMEM((rows, weight.shape[0]), jnp.bfloat16),
            pltpu.VMEM((shards, rows // 2, LANES), jnp.bfloat16),
            pltpu.VMEM((rows, D), jnp.bfloat16),
            pltpu.VMEM(weight.shape, jnp.bfloat16),
            pltpu.VMEM(merge_weight.shape, jnp.bfloat16),
            pltpu.SemaphoreType.DMA((3 * shards,)),
            pltpu.SemaphoreType.DMA((len(OUT_BLOCKS) + 5,)),
        ],
        out_shape=shapes,
        compiler_params=pltpu.CompilerParams(vmem_limit_bytes=30 << 20),
        cost_estimate=pl.CostEstimate(
            flops=4 * rows * D * D + 2 * groups * merge_weight.size,
            bytes_accessed=2 * (D * D + merge_weight.size + 3 * rows * D),
            transcendentals=rows,
        ),
        name="out_merge",
    )(*operands)


def place_kernel(me, *refs):
    blocks, out = refs[:-1], refs[-1]
    most, width = out.shape[1:]
    whole = width // LANES
    half = most // 2
    middle = LANES // 2
    for place, block in enumerate(blocks):
        target = me[0] ^ place
        for column in range(whole):
            out[target, :, column * LANES : (column + 1) * LANES] = block[
                column * most : (column + 1) * most, :
            ]
        out[target, :half, whole * LANES :] = block[whole * most :, :middle]
        out[target, half:, whole * LANES :] = block[whole * most :, middle:]


def place_call(me, blocks, most, width):
    fixed = lambda shape: pl.BlockSpec(shape, lambda i: (0,) * len(shape))
    shape = (len(blocks), most, width)
    return pl.pallas_call(
        place_kernel,
        grid=(1,),
        in_specs=[pl.BlockSpec(memory_space=pltpu.SMEM)] + [fixed(one.shape) for one in blocks],
        out_specs=fixed(shape),
        out_shape=jax.ShapeDtypeStruct(shape, jnp.bfloat16),
        compiler_params=pltpu.CompilerParams(vmem_limit_bytes=8 << 20),
        cost_estimate=pl.CostEstimate(
            flops=0, bytes_accessed=4 * len(blocks) * most * width, transcendentals=0
        ),
        name="place_rows",
    )(me, *blocks)


def send_seq(value, flip):
    size = lax.axis_size("seq")
    return lax.ppermute(value, "seq", [(i, i ^ flip) for i in range(size)])


def after(values, *earlier):
    return lax.optimization_barrier((tuple(values), earlier))[0]


def near_shards(value):
    return [send_seq(value, 1), send_seq(value, 2), send_seq(value, 4)]


def far_shards(across_x, across_y):
    half = across_x.shape[0] // 2
    return [send_seq(across_x[:half], 4), send_seq(across_y[half:], 2)]


def weight_order(heads_here):
    quarter = HD // 4
    order = -np.ones((6 * LANES,), np.int32)
    for head in range(heads_here):
        base = head * 3 * HD
        for kind in range(2):
            for half in range(2):
                for letter in range(2):
                    target = (2 * kind + letter) * LANES + head * (HD // 2) + half * quarter
                    source = base + kind * HD + half * (HD // 2) + letter * quarter
                    order[target : target + quarter] = np.arange(source, source + quarter)
        target = 4 * LANES + head * HD
        order[target : target + HD] = np.arange(base + 2 * HD, base + 3 * HD)
    return order


def angle_table(heads_here):
    quarter = HD // 4
    frequency = (10000.0 ** (-np.arange(quarter) / quarter)).astype(np.float32)
    angles = np.arange(POSITIONS, dtype=np.float32)[:, None] * frequency[None, :]
    pieces = []
    for function in (np.cos, np.sin):
        exact = np.zeros((2 * POSITIONS, LANES), np.float64)
        for head in range(heads_here):
            for half in range(2):
                lane = head * (HD // 2) + half * quarter
                rows = slice(half * POSITIONS, (half + 1) * POSITIONS)
                exact[rows, lane : lane + quarter] = function(angles.astype(np.float64))
        upper = exact.astype(jnp.bfloat16)
        pieces += [upper, (exact - upper.astype(np.float64)).astype(jnp.bfloat16)]
    return np.concatenate(pieces, axis=1)


def fast_local(
    patches,
    patch_mask,
    mask_embed,
    norm_gain,
    qkv_weight,
    segment_ids,
    patch_rows,
    patch_column,
    out_weight,
    merge_gain,
    merge_weight,
    merge_bias,
    image_owner,
):
    local_rows = patches.shape[1]
    shards = lax.axis_size("seq")
    packs = lax.axis_size("pack")
    heads_here = HEADS // shards
    images = image_owner.shape[1]
    total = local_rows * shards
    me = lax.axis_index("seq").astype(jnp.int32)
    pack = lax.axis_index("pack").astype(jnp.int32)

    value = payload_call(segment_ids, patch_rows, patch_column, patch_mask, mask_embed, patches)
    own_swap, across_x, across_y = near_shards(value)

    order = jnp.asarray(weight_order(heads_here))
    spread = (jnp.arange(qkv_weight.shape[1])[:, None] == order[None, :]).astype(jnp.bfloat16)
    weight = jnp.dot(qkv_weight, spread, preferred_element_type=jnp.float32).astype(jnp.bfloat16)
    table = jnp.asarray(angle_table(heads_here))
    gain = norm_gain.astype(jnp.float32)[None, :]
    merge_gain_row = merge_gain.astype(jnp.float32)[None, :]
    bias = merge_bias.astype(jnp.float32)[None, :]
    ids = jnp.stack([me ^ place for place in range(shards)])
    ordered = order_call(ids, out_weight)

    chip, core = me // 2, me % 2
    project = lambda place, first, second, earlier: qkv_call(
        jnp.stack([chip ^ place, core]), first, second, table, gain, weight, earlier, total
    )
    buffers = project(0, [value], [own_swap], ())
    across_x, across_y = after([across_x, across_y], buffers[2], ordered)
    far = far_shards(across_x, across_y)
    buffers = project(1, [across_x], [send_seq(across_x, 1)], buffers)
    buffers = project(2, [across_y], [send_seq(across_y, 1)], buffers)
    far = after(far, buffers[2])
    buffers = project(3, far, [send_seq(one, 1) for one in far], buffers)
    inputs, block, labels = buffers

    starts = [sum(CHUNKS[:number]) for number in range(len(CHUNKS))]
    attended, note = [], None
    for start, rows in zip(starts, CHUNKS):
        made = attention_call(start, rows, image_owner[0], labels, block, note is None)
        note = made[1] if note is None else note
        attended.append((made[0], near_shards(made[0])))
    latest = attended[-1][0]
    most = 2 * (total // 4) // images
    projected, moving = [], []
    for own, (own_swap, across_x, across_y) in attended:
        across_x, across_y = after([across_x, across_y], latest)
        far = far_shards(across_x, across_y)
        moving.append(
            (own, own_swap, across_x, send_seq(across_x, 1), across_y, send_seq(across_y, 1), far)
        )
    for number, (start, rows) in enumerate(zip(starts, CHUNKS)):
        *near, far = moving[number]
        if projected:
            far = after(far, projected[-1])
        sources = [[one] for one in near] + [far, [send_seq(one, 1) for one in far]]
        route = ()
        if number == len(CHUNKS) - 1:
            route = (pack[None], most, note, *projected)
        made = merge_call(
            start, rows, sources, inputs, ordered, merge_gain_row, merge_weight.T, bias, packs, route
        )
        projected.append(made[0])
    blocks = [made[0]] + [
        lax.ppermute(made[flip], "pack", [(z, z ^ flip) for z in range(packs)])
        for flip in range(1, packs)
    ]
    return place_call(pack[None], blocks, most, merge_weight.shape[1])[None]


def local(*arguments):
    patches, weight = arguments[0], arguments[4]
    shards = lax.axis_size("seq")
    fits = shards == 8 and HEADS // shards == 2 and weight.shape[1] == 6 * HD
    fits = fits and patches.shape[1] * shards == sum(CHUNKS) and lax.axis_size("pack") == 4
    return fast_local(*arguments) if fits else general_local(*arguments)


def solution(mesh):
    placed = (
        P("pack", "seq", None),
        P("pack", "seq"),
        P(),
        P(),
        P(None, "seq"),
        P("pack", "seq"),
        P("pack", "seq"),
        P("pack", "seq"),
        P(),
        P(),
        P(None, "seq"),
        P("seq"),
        P("pack", None),
    )
    return jax.shard_map(
        local, mesh=mesh, in_specs=placed, out_specs=P("pack", None, None, "seq"), check_vma=False
    )
```

```python
import functools

import jax
import jax.numpy as jnp
import numpy as np
from jax import lax
from jax.experimental import pallas as pl
from jax.experimental.pallas import tpu as pltpu
from jax.sharding import PartitionSpec as P

D = 1408
HEADS = 16
HD = 88


EPSILON = 1e-06


def layer_norm(values, gain_vector):
    center = values - jnp.mean(values, axis=-1, keepdims=True)
    spread = jnp.mean(center * center, axis=-1, keepdims=True)
    return center * lax.rsqrt(spread + EPSILON) * gain_vector.astype(jnp.float32)


def rotate(vectors, row_index, column_index):
    total_rows, heads_here, head_width = vectors.shape
    quarter = head_width // 4
    frequency = 10000.0 ** (-jnp.arange(quarter, dtype=jnp.float32) / quarter)
    row_angle = row_index.astype(jnp.float32)[:, None] * frequency[None, :]
    column_angle = column_index.astype(jnp.float32)[:, None] * frequency[None, :]
    angles = jnp.stack([row_angle, column_angle], axis=1)[:, None, :, None, :]
    split_up = vectors.reshape(total_rows, heads_here, 2, 2, quarter)
    partner = jnp.stack([-split_up[:, :, :, 1], split_up[:, :, :, 0]], axis=3)
    turned = split_up * jnp.cos(angles) + partner * jnp.sin(angles)
    return turned.reshape(total_rows, heads_here, head_width)


def qkv_block(projected, row_index, column_index):
    turned_queries = rotate(projected[:, :, 0], row_index, column_index)
    turned_keys = rotate(projected[:, :, 1], row_index, column_index)
    return jnp.concatenate([turned_queries, turned_keys, projected[:, :, 2]], axis=-1).astype(
        jnp.bfloat16
    )


def attention(block, segments):
    total_rows, heads_here, triple = block.shape
    head_width = triple // 3
    step_rows = min(512, total_rows)
    query_part = block[:, :, :head_width].reshape(
        total_rows // step_rows, step_rows, heads_here, head_width
    )
    key_part = block[:, :, head_width : 2 * head_width]
    value_part = block[:, :, 2 * head_width :]
    query_segments = segments.reshape(total_rows // step_rows, step_rows)
    scale = head_width ** (-0.5)

    def one_block(inputs_pair):
        queries_here, segments_here = inputs_pair
        scores = (
            jnp.einsum("qhd,khd->hqk", queries_here, key_part, preferred_element_type=jnp.float32)
            * scale
        )
        same_image = (segments_here[:, None] == segments[None, :])[None]
        scores = jnp.where(same_image, scores, -jnp.inf)
        highest = jnp.max(scores, axis=-1, keepdims=True)
        weights = jnp.exp(scores - highest)
        probs = (weights / jnp.sum(weights, axis=-1, keepdims=True)).astype(jnp.bfloat16)
        result = jnp.einsum("hqk,khd->qhd", probs, value_part, preferred_element_type=jnp.float32)
        return result.astype(jnp.bfloat16)

    return lax.map(one_block, (query_part, query_segments)).reshape(
        total_rows, heads_here, head_width
    )


def route(projected, segments, owners_here, packs, most):
    merged_segments = segments[::4]
    images = owners_here.shape[0]
    image_ids = jnp.arange(images, dtype=jnp.int32)
    member = (merged_segments[None, :] == image_ids[:, None]).astype(jnp.int32)
    lengths = jnp.sum(member, axis=1, dtype=jnp.int32)
    starts = jnp.cumsum(lengths, dtype=jnp.int32) - lengths
    owner_ids = jnp.arange(packs, dtype=jnp.int32)
    owned = owners_here[None, :] == owner_ids[:, None]
    first_row = jnp.sum(jnp.where(owned, starts[None, :], 0), axis=1, dtype=jnp.int32)
    owned_length = jnp.sum(jnp.where(owned, lengths[None, :], 0), axis=1, dtype=jnp.int32)
    slots = jnp.arange(most, dtype=jnp.int32)
    source_rows = jnp.clip(first_row[:, None] + slots[None, :], 0, projected.shape[0] - 1)
    picked = jnp.take(projected, source_rows.reshape(-1), axis=0).reshape(
        packs, most, projected.shape[1]
    )
    filled = slots[None, :] < owned_length[:, None]
    return jnp.where(filled[:, :, None], picked, jnp.zeros_like(picked))


def general_local(
    patches,
    patch_mask,
    mask_embed,
    norm_gain,
    qkv_weight,
    segment_ids,
    patch_rows,
    patch_column,
    out_weight,
    merge_gain,
    merge_weight,
    merge_bias,
    image_owner,
):
    local_rows = patches.shape[1]
    shards = lax.axis_size("seq")
    packs = lax.axis_size("pack")
    heads_here = HEADS // shards
    inputs = jnp.where(patch_mask[0][:, None] == 1, mask_embed[None, :], patches[0])
    normed = layer_norm(inputs.astype(jnp.float32), norm_gain).astype(jnp.bfloat16)
    labels = lax.all_gather(
        jnp.stack([segment_ids[0], patch_rows[0], patch_column[0]]), "seq", axis=1, tiled=True
    )
    piece = lax.all_gather(normed, "seq", axis=0, tiled=True)
    span = piece.shape[0]
    projected = jnp.dot(piece, qkv_weight, preferred_element_type=jnp.float32)
    row_part = labels[1]
    column_part = labels[2]
    block = qkv_block(projected.reshape(span, heads_here, 3, HD), row_part, column_part)
    result = attention(block, labels[0])
    mixed_heads = lax.all_to_all(result, "seq", split_axis=0, concat_axis=1, tiled=True)
    attended = mixed_heads.reshape(local_rows, D)
    residual = inputs.astype(jnp.float32) + jnp.dot(
        attended, out_weight, preferred_element_type=jnp.float32
    )
    merged = layer_norm(residual, merge_gain).astype(jnp.bfloat16).reshape(local_rows // 4, 4 * D)
    projected_all = (
        jnp.dot(
            lax.all_gather(merged, "seq", axis=0, tiled=True),
            merge_weight,
            preferred_element_type=jnp.float32,
        )
        + merge_bias.astype(jnp.float32)
    ).astype(jnp.bfloat16)
    images = image_owner.shape[1]
    most = 2 * projected_all.shape[0] // images
    outgoing = route(projected_all, labels[0], image_owner[0], packs, most)
    delivered = lax.all_to_all(outgoing, "pack", split_axis=0, concat_axis=0, tiled=True)
    return delivered[None]


LANES = 128
BLOCK = 256
POSITIONS = 64
NEGATIVE = -1e30
CHUNKS = (768, 768)


def norm_rows(values, gain_row):
    center = values - jnp.mean(values, axis=-1, keepdims=True)
    spread = jnp.mean(center * center, axis=-1, keepdims=True)
    return center * lax.rsqrt(spread + EPSILON) * gain_row


def stacked(pieces):
    loaded = [piece[...] for piece in pieces]
    return loaded[0] if len(loaded) == 1 else jnp.concatenate(loaded, axis=0)


def in_vmem(value):
    return pltpu.with_memory_space_constraint(value, pltpu.VMEM)


def in_hbm(value):
    return pltpu.with_memory_space_constraint(value, pltpu.HBM)


def payload_kernel(segments, rows, columns, mask, embed, patches, out):
    labels = [one[...].astype(jnp.float32) for one in (segments, rows, columns, mask)]
    labels.append(jnp.zeros((4, labels[0].shape[1]), jnp.float32))
    labels = jnp.concatenate(labels, axis=0).astype(jnp.bfloat16)
    shape = (8, LANES)
    row = lax.broadcasted_iota(jnp.int32, shape, 0)
    place = jnp.where(row == lax.broadcasted_iota(jnp.int32, shape, 1), 1.0, 0.0)
    turned = lax.dot_general(
        labels,
        place.astype(jnp.bfloat16),
        (((0,), (0,)), ((), ())),
        preferred_element_type=jnp.float32,
    )
    masked = turned[:, 3:4] > 0.5
    tokens = jnp.where(
        masked, embed[...].astype(jnp.float32)[None, :], patches[0].astype(jnp.float32)
    )
    out[:, :D] = tokens.astype(jnp.bfloat16)
    out[:, D:] = turned.astype(jnp.bfloat16)


def payload_call(segments, rows, columns, mask, embed, patches):
    count = patches.shape[1]
    operands = (segments, rows, columns, mask, embed, patches)
    fixed = lambda shape: pl.BlockSpec(shape, lambda i: (0,) * len(shape))
    shape = (count, D + LANES)
    return pl.pallas_call(
        payload_kernel,
        grid=(1,),
        in_specs=[fixed(one.shape) for one in operands],
        out_specs=fixed(shape),
        out_shape=jax.ShapeDtypeStruct(shape, jnp.bfloat16),
        compiler_params=pltpu.CompilerParams(vmem_limit_bytes=8 << 20),
        cost_estimate=pl.CostEstimate(
            flops=count * D, bytes_accessed=4 * count * D, transcendentals=0
        ),
        name="payload",
    )(*map(in_hbm, operands))


def qkv_kernel(count, place, *refs):
    first, second = refs[:count], refs[count : 2 * count]
    table, gain, weight = refs[2 * count : 2 * count + 3]
    inputs_out, qkv_out, label_out = refs[-3:]
    mine, other = stacked(first), stacked(second)
    leads = place[1] == 0
    ahead = jnp.where(leads, mine, other)
    behind = jnp.where(leads, other, mine)
    both = jnp.concatenate([ahead, behind], axis=0)
    rows = both.shape[0]
    at = pl.ds(pl.multiple_of(place[0] * rows, rows), rows)
    inputs_out[at, :] = both[:, :D]
    label_out[at, :] = both[:, D:]
    labels = both[:, D:].astype(jnp.float32)
    normed = norm_rows(both[:, :D].astype(jnp.float32), gain[...]).astype(jnp.bfloat16)
    columns = lax.dot_general(
        normed, weight[...], (((1,), (1,)), ((), ())), preferred_element_type=jnp.float32
    )
    lane = lax.broadcasted_iota(jnp.int32, labels.shape, 1)
    numbers = lane.astype(jnp.float32)
    hot = (numbers == labels[:, 1:2]) | (numbers == labels[:, 2:3] + POSITIONS)
    looked = jnp.dot(
        jnp.where(hot, 1.0, 0.0).astype(jnp.bfloat16), table[...], preferred_element_type=jnp.float32
    )
    cosine = looked[:, :LANES] + looked[:, LANES : 2 * LANES]
    sine = looked[:, 2 * LANES : 3 * LANES] + looked[:, 3 * LANES :]
    first_head = lane < HD // 2

    def turn(start):
        a = columns[:, start : start + LANES]
        b = columns[:, start + LANES : start + 2 * LANES]
        return a * cosine - b * sine, b * cosine + a * sine

    query_a, query_b = turn(0)
    key_a, key_b = turn(2 * LANES)
    zero = jnp.zeros_like(key_a)
    parts = [
        query_a,
        query_b,
        jnp.where(first_head, key_a, zero),
        jnp.where(first_head, key_b, zero),
        jnp.where(first_head, zero, key_a),
        jnp.where(first_head, zero, key_b),
    ]
    values_part = columns[:, 4 * LANES :]
    wide = lax.broadcasted_iota(jnp.int32, values_part.shape, 1)
    ones = jnp.where(wide == 2 * HD, 1.0, 0.0)
    parts.append(jnp.where(wide < HD, values_part, ones))
    parts.append(jnp.where((wide >= HD) & (wide < 2 * HD), values_part, ones))
    for number, part in enumerate(parts[:6]):
        qkv_out[at, number * LANES : (number + 1) * LANES] = part.astype(jnp.bfloat16)
    for number, part in enumerate(parts[6:]):
        low = (6 + 2 * number) * LANES
        qkv_out[at, low : low + 2 * LANES] = part.astype(jnp.bfloat16)


def qkv_call(place, first, second, table, gain, weight, earlier, total):
    rows = 2 * sum(piece.shape[0] for piece in first)
    widths = (D, 10 * LANES, LANES)
    operands = [*first, *second, table, gain, in_vmem(weight)]
    vmem = pl.BlockSpec(memory_space=pltpu.VMEM)
    held = [in_vmem(one) for one in earlier]
    return pl.pallas_call(
        functools.partial(qkv_kernel, len(first)),
        in_specs=[pl.BlockSpec(memory_space=pltpu.SMEM)]
        + [vmem] * (len(operands) + len(earlier)),
        out_specs=[vmem] * len(widths),
        out_shape=[pltpu.VMEM((total, width), jnp.bfloat16) for width in widths],
        input_output_aliases={1 + len(operands) + i: i for i in range(len(earlier))},
        compiler_params=pltpu.CompilerParams(vmem_limit_bytes=14 << 20),
        cost_estimate=pl.CostEstimate(
            flops=6 * rows * D * weight.shape[0],
            bytes_accessed=2 * (rows * 4 * D + weight.size),
            transcendentals=rows,
        ),
        name="norm_qkv",
    )(place, *operands, *held)


def segment_row(labels):
    pick = jnp.where(lax.broadcasted_iota(jnp.int32, (8, LANES), 1) == 0, 1.0, 0.0)
    return lax.dot_general(
        pick.astype(jnp.bfloat16),
        labels,
        (((1,), (1,)), ((), ())),
        preferred_element_type=jnp.float32,
    )


def attention_kernel(start, owners, labels, block, *refs):
    out, *rest = refs
    scores, high, rows_scratch = rest[-3:]
    rows = high.shape[1]
    total = block.shape[0]
    factor = HD**-0.5 * float(np.log2(np.e))
    segments = segment_row(labels[...])
    for step in range(total // BLOCK):
        rows_scratch[step] = segments[:, step * BLOCK : (step + 1) * BLOCK]
    own = labels[start : start + rows, :1].astype(jnp.float32)
    lowest, largest = jnp.min(own), jnp.max(own)
    one_row = segments[:1]
    begin = jnp.sum(jnp.where(one_row < lowest, 1, 0)) // BLOCK
    end = (jnp.sum(jnp.where(one_row <= largest, 1, 0)) + BLOCK - 1) // BLOCK
    queries = block[start : start + rows, : 2 * LANES]
    own = jnp.broadcast_to(own, (rows, LANES))
    high[...] = jnp.full_like(high, NEGATIVE)

    def score(step, carry):
        at = pl.ds(pl.multiple_of(step * BLOCK, BLOCK), BLOCK)
        theirs = rows_scratch[step, :1]
        same = jnp.concatenate([own == theirs[:, :LANES], own == theirs[:, LANES:]], axis=1)
        for head in range(2):
            keys = block[at, (2 + 2 * head) * LANES : (4 + 2 * head) * LANES]
            values = lax.dot_general(
                queries, keys, (((1,), (1,)), ((), ())), preferred_element_type=jnp.float32
            )
            values = jnp.where(same, values, NEGATIVE)
            scores[head, step] = values
            high[head] = jnp.maximum(
                high[head], jnp.maximum(values[:, :LANES], values[:, LANES:])
            )
        return carry

    lax.fori_loop(begin, end, score, 0)
    highest = [jnp.max(high[head], axis=-1, keepdims=True) for head in range(2)]

    def weigh(step, carry):
        at = pl.ds(pl.multiple_of(step * BLOCK, BLOCK), BLOCK)
        sums = []
        for head in range(2):
            weights = jnp.exp2((scores[head, step] - highest[head]) * factor)
            values = block[at, (6 + 2 * head) * LANES : (8 + 2 * head) * LANES]
            sums.append(
                carry[head]
                + jnp.dot(weights.astype(jnp.bfloat16), values, preferred_element_type=jnp.float32)
            )
        return tuple(sums)

    zero = jnp.zeros((rows, 2 * LANES), jnp.float32)
    sums = lax.fori_loop(begin, end, weigh, (zero, zero))
    acc = sum(one / one[:, 2 * HD : 2 * HD + 1] for one in sums)
    out[:rows] = acc[:, :LANES].astype(jnp.bfloat16)
    half = rows // 2
    low, up = acc[:half, LANES:], acc[half:, LANES:]
    lane = lax.broadcasted_iota(jnp.int32, low.shape, 1)
    tail = 2 * HD - LANES
    packed = jnp.where(lane < tail, low, jnp.where(lane < 2 * tail, pltpu.roll(up, tail, 1), 0.0))
    out[rows:] = packed.astype(jnp.bfloat16)

    if len(rest) > 3:
        note = rest[0]
        row = lax.broadcasted_iota(jnp.int32, note.shape, 0)
        lane = lax.broadcasted_iota(jnp.int32, note.shape, 1)
        found = jnp.zeros(note.shape, jnp.float32)
        for image in range(owners.shape[0]):
            below = jnp.sum(jnp.where(one_row < image, 0.25, 0.0), axis=1, keepdims=True)
            inside = jnp.sum(jnp.where(one_row == image, 0.25, 0.0), axis=1, keepdims=True)
            here = row == owners[image]
            for place, number in enumerate((below, inside)):
                upper = jnp.floor(number * (1.0 / 16))
                found = jnp.where(here & (lane == 2 * place), upper, found)
                found = jnp.where(here & (lane == 2 * place + 1), number - 16 * upper, found)
        note[...] = found.astype(jnp.bfloat16)


def attention_call(start, rows, owners, labels, block, noted):
    total = block.shape[0]
    vmem = pl.BlockSpec(memory_space=pltpu.VMEM)
    shapes = [jax.ShapeDtypeStruct((rows + rows // 2, LANES), jnp.bfloat16)]
    if noted:
        shapes.append(jax.ShapeDtypeStruct((16, LANES), jnp.bfloat16))
    return pl.pallas_call(
        functools.partial(attention_kernel, start),
        in_specs=[pl.BlockSpec(memory_space=pltpu.SMEM), vmem, vmem],
        out_specs=[vmem] * len(shapes),
        out_shape=shapes,
        scratch_shapes=[
            pltpu.VMEM((2, total // BLOCK, rows, BLOCK), jnp.float32),
            pltpu.VMEM((2, rows, LANES), jnp.float32),
            pltpu.VMEM((total // BLOCK, 8, BLOCK), jnp.float32),
        ],
        compiler_params=pltpu.CompilerParams(vmem_limit_bytes=20 << 20),
        cost_estimate=pl.CostEstimate(
            flops=10 * rows * total * 2 * LANES,
            bytes_accessed=2 * block.size,
            transcendentals=rows * total,
        ),
        name="attention",
    )(owners, in_vmem(labels), in_vmem(block))


def prepare_kernel(shards, ids, out_weight, merge_weight, qkv_weight, spread, *refs):
    out, merge, qkv, qkv_buffer, spread_buffer, sems = refs
    rest = 2 * HD - LANES
    copies = [(qkv_weight, qkv_buffer), (spread, spread_buffer)]
    out[shards * LANES :] = jnp.zeros((shards // 2 * LANES, D), jnp.bfloat16)
    for place in range(shards):
        start = pl.multiple_of(ids[place] * (2 * HD), 16)
        to = (shards + place // 2) * LANES + place % 2 * rest
        copies.append(
            (out_weight.at[pl.ds(start, LANES), :], out.at[pl.ds(place * LANES, LANES), :])
        )
        copies.append((out_weight.at[pl.ds(start + LANES, rest), :], out.at[pl.ds(to, rest), :]))
    copies.append((merge_weight, merge))
    copies = [
        pltpu.make_async_copy(source, target, sems.at[i])
        for i, (source, target) in enumerate(copies)
    ]
    for copy in copies:
        copy.start()
    copies[0].wait()
    copies[1].wait()
    qkv[...] = jnp.dot(
        spread_buffer[...], qkv_buffer[...], preferred_element_type=jnp.float32
    ).astype(jnp.bfloat16)
    for copy in copies[2:]:
        copy.wait()


def prepare_call(ids, out_weight, merge_weight, qkv_weight, spread):
    shards = ids.shape[0]
    anywhere = pl.BlockSpec(memory_space=pl.ANY)
    vmem = pl.BlockSpec(memory_space=pltpu.VMEM)
    operands = (out_weight, merge_weight, qkv_weight, spread)
    shapes = [(shards * LANES * 3 // 2, D), merge_weight.shape, (spread.shape[0], D)]
    return pl.pallas_call(
        functools.partial(prepare_kernel, shards),
        in_specs=[pl.BlockSpec(memory_space=pltpu.SMEM)] + [anywhere] * len(operands),
        out_specs=[vmem] * len(shapes),
        out_shape=[pltpu.VMEM(shape, jnp.bfloat16) for shape in shapes],
        scratch_shapes=[
            pltpu.VMEM(qkv_weight.shape, jnp.bfloat16),
            pltpu.VMEM(spread.shape, jnp.bfloat16),
            pltpu.SemaphoreType.DMA((2 * shards + 3,)),
        ],
        compiler_params=pltpu.CompilerParams(vmem_limit_bytes=10 << 20),
        cost_estimate=pl.CostEstimate(
            flops=2 * spread.size * D,
            bytes_accessed=4 * (out_weight.size + merge_weight.size + qkv_weight.size),
            transcendentals=0,
        ),
        name="prepare",
    )(ids, *map(in_hbm, operands))


def merge_kernel(start, counts, packs, last, *refs):
    inputs, weight, gain, merge_weight, bias = refs[:5]
    pieces = refs[5 : 5 + sum(counts)]
    *refs, state = refs[5 + sum(counts) :]
    rows = state.shape[1]
    half = rows // 2
    rest = 2 * HD - LANES
    sources, at = [], 0
    for count in counts:
        sources.append(stacked(pieces[at : at + count]))
        at += count
    shards = len(sources)
    lane = lax.broadcasted_iota(jnp.int32, (half, LANES), 1)
    for part in range(2):
        token = slice(part * half, (part + 1) * half)
        lined = [source[token, :] for source in sources]
        for pair in range(shards // 2):
            mine = sources[2 * pair][rows:, :].astype(jnp.float32)
            other = sources[2 * pair + 1][rows:, :].astype(jnp.float32)
            if part == 0:
                other = pltpu.roll(other, rest, 1)
            else:
                mine = pltpu.roll(mine, LANES - rest, 1)
            lined.append(jnp.where(lane < rest, mine, other).astype(jnp.bfloat16))
        mixed = jnp.dot(
            jnp.concatenate(lined, axis=1), weight[...], preferred_element_type=jnp.float32
        )
        before = inputs[start + part * half : start + (part + 1) * half, :].astype(jnp.float32)
        normed = norm_rows(before + mixed, gain[...])
        for column in range(D // LANES):
            state[column, token, :] = normed[:, column * LANES : (column + 1) * LANES]
    groups = rows // 4
    total = bias[...]
    for quadrant in range(4):
        tokens = jnp.concatenate(
            [
                state[column, pl.ds(quadrant, groups, stride=4), :].astype(jnp.bfloat16)
                for column in range(D // LANES)
            ],
            axis=1,
        )
        total = total + lax.dot_general(
            tokens,
            merge_weight[:, quadrant * D : (quadrant + 1) * D],
            (((1,), (1,)), ((), ())),
            preferred_element_type=jnp.float32,
        )
    total = total.astype(jnp.bfloat16)
    if not last:
        refs[0][...] = total
        return
    me, note, *earlier = refs[:-packs]
    outs = refs[-packs:]
    total = jnp.concatenate([*[one[...] for one in earlier], total], axis=0)
    whole = total.shape[1] // LANES
    most = outs[0].shape[0] * LANES // total.shape[1]
    notes = note[...].astype(jnp.float32)
    note_row = lax.broadcasted_iota(jnp.int32, notes.shape, 0)
    slot = lax.broadcasted_iota(jnp.int32, (most, total.shape[0]), 0)
    row = lax.broadcasted_iota(jnp.int32, (most, total.shape[0]), 1)
    for place, out in enumerate(outs):
        found = jnp.where(note_row == (me[0] ^ place), notes, 0.0)
        found = jnp.sum(found, axis=0, keepdims=True)
        first = (16.0 * found[:, :1] + found[:, 1:2]).astype(jnp.int32)
        length = (16.0 * found[:, 2:3] + found[:, 3:4]).astype(jnp.int32)
        chosen = (row == slot + first) & (slot < length)
        chosen = jnp.where(chosen, 1.0, 0.0).astype(jnp.bfloat16)
        block = jnp.dot(chosen, total, preferred_element_type=jnp.float32)
        for column in range(whole):
            out[column * most : (column + 1) * most, :] = block[
                :, column * LANES : (column + 1) * LANES
            ].astype(jnp.bfloat16)
        low = block[: most // 2, whole * LANES :]
        up = block[most // 2 :, whole * LANES :]
        out[whole * most :, :] = jnp.concatenate([low, up], axis=1).astype(jnp.bfloat16)


def merge_call(start, rows, sources, inputs, weight, gain, merge_weight, bias, packs, route):
    groups = rows // 4
    width = merge_weight.shape[0]
    pieces = [piece for source in sources for piece in source]
    vmem = pl.BlockSpec(memory_space=pltpu.VMEM)
    operands = [in_vmem(inputs), in_vmem(weight), gain, in_vmem(merge_weight), bias, *pieces]
    specs = [vmem] * len(operands)
    shapes = [jax.ShapeDtypeStruct((groups, width), jnp.bfloat16)]
    if route:
        me, most, *others = route
        operands += [me, *others]
        specs += [pl.BlockSpec(memory_space=pltpu.SMEM)] + [vmem] * len(others)
        shapes = [jax.ShapeDtypeStruct((most * width // LANES, LANES), jnp.bfloat16)] * packs
    return pl.pallas_call(
        functools.partial(
            merge_kernel, start, [len(source) for source in sources], packs, bool(route)
        ),
        in_specs=specs,
        out_specs=[vmem] * len(shapes),
        scratch_shapes=[pltpu.VMEM((D // LANES, rows, LANES), jnp.float32)],
        out_shape=shapes,
        compiler_params=pltpu.CompilerParams(vmem_limit_bytes=20 << 20),
        cost_estimate=pl.CostEstimate(
            flops=4 * rows * D * D + 2 * groups * merge_weight.size,
            bytes_accessed=2 * (D * D + merge_weight.size + 3 * rows * D),
            transcendentals=rows,
        ),
        name="out_merge",
    )(*operands)


def place_kernel(me, *refs):
    blocks, out = refs[:-1], refs[-1]
    most, width = out.shape[1:]
    whole = width // LANES
    half = most // 2
    middle = LANES // 2
    for place, block in enumerate(blocks):
        target = me[0] ^ place
        for column in range(whole):
            out[target, :, column * LANES : (column + 1) * LANES] = block[
                column * most : (column + 1) * most, :
            ]
        out[target, :half, whole * LANES :] = block[whole * most :, :middle]
        out[target, half:, whole * LANES :] = block[whole * most :, middle:]


def place_call(me, blocks, most, width):
    fixed = lambda shape: pl.BlockSpec(shape, lambda i: (0,) * len(shape))
    shape = (len(blocks), most, width)
    return pl.pallas_call(
        place_kernel,
        grid=(1,),
        in_specs=[pl.BlockSpec(memory_space=pltpu.SMEM)] + [fixed(one.shape) for one in blocks],
        out_specs=fixed(shape),
        out_shape=jax.ShapeDtypeStruct(shape, jnp.bfloat16),
        compiler_params=pltpu.CompilerParams(vmem_limit_bytes=8 << 20),
        cost_estimate=pl.CostEstimate(
            flops=0, bytes_accessed=4 * len(blocks) * most * width, transcendentals=0
        ),
        name="place_rows",
    )(me, *blocks)


def send_seq(value, flip):
    size = lax.axis_size("seq")
    return lax.ppermute(value, "seq", [(i, i ^ flip) for i in range(size)])


def after(values, *earlier):
    return lax.optimization_barrier((tuple(values), earlier))[0]


def near_shards(value):
    return [send_seq(value, 1), send_seq(value, 2), send_seq(value, 4)]


def far_shards(across_x, across_y):
    half = across_x.shape[0] // 2
    return [send_seq(across_x[:half], 4), send_seq(across_y[half:], 2)]


def weight_order(heads_here):
    quarter = HD // 4
    order = -np.ones((6 * LANES,), np.int32)
    for head in range(heads_here):
        base = head * 3 * HD
        for kind in range(2):
            for half in range(2):
                for letter in range(2):
                    target = (2 * kind + letter) * LANES + head * (HD // 2) + half * quarter
                    source = base + kind * HD + half * (HD // 2) + letter * quarter
                    order[target : target + quarter] = np.arange(source, source + quarter)
        target = 4 * LANES + head * HD
        order[target : target + HD] = np.arange(base + 2 * HD, base + 3 * HD)
    return order


def angle_table(heads_here):
    quarter = HD // 4
    frequency = (10000.0 ** (-np.arange(quarter) / quarter)).astype(np.float32)
    angles = np.arange(POSITIONS, dtype=np.float32)[:, None] * frequency[None, :]
    pieces = []
    for function in (np.cos, np.sin):
        exact = np.zeros((2 * POSITIONS, LANES), np.float64)
        for head in range(heads_here):
            for half in range(2):
                lane = head * (HD // 2) + half * quarter
                rows = slice(half * POSITIONS, (half + 1) * POSITIONS)
                exact[rows, lane : lane + quarter] = function(angles.astype(np.float64))
        upper = exact.astype(jnp.bfloat16)
        pieces += [upper, (exact - upper.astype(np.float64)).astype(jnp.bfloat16)]
    return np.concatenate(pieces, axis=1)


def fast_local(
    patches,
    patch_mask,
    mask_embed,
    norm_gain,
    qkv_weight,
    segment_ids,
    patch_rows,
    patch_column,
    out_weight,
    merge_gain,
    merge_weight,
    merge_bias,
    image_owner,
):
    local_rows = patches.shape[1]
    shards = lax.axis_size("seq")
    packs = lax.axis_size("pack")
    heads_here = HEADS // shards
    images = image_owner.shape[1]
    total = local_rows * shards
    me = lax.axis_index("seq").astype(jnp.int32)
    pack = lax.axis_index("pack").astype(jnp.int32)

    value = payload_call(segment_ids, patch_rows, patch_column, patch_mask, mask_embed, patches)
    own_swap, across_x, across_y = near_shards(value)

    order = weight_order(heads_here)
    spread = (order[:, None] == np.arange(qkv_weight.shape[1])[None, :]).astype(jnp.bfloat16)
    table = jnp.asarray(angle_table(heads_here))
    gain = norm_gain.astype(jnp.float32)[None, :]
    merge_gain_row = merge_gain.astype(jnp.float32)[None, :]
    bias = merge_bias.astype(jnp.float32)[None, :]
    ids = jnp.stack([me ^ place for place in range(shards)])
    ordered, merge_rows, weight = prepare_call(
        ids, out_weight, merge_weight.T, qkv_weight.T, jnp.asarray(spread)
    )

    chip, core = me // 2, me % 2
    project = lambda place, first, second, earlier: qkv_call(
        jnp.stack([chip ^ place, core]), first, second, table, gain, weight, earlier, total
    )
    buffers = project(0, [value], [own_swap], ())
    across_x, across_y = after([across_x, across_y], buffers[2], ordered)
    far = far_shards(across_x, across_y)
    buffers = project(1, [across_x], [send_seq(across_x, 1)], buffers)
    buffers = project(2, [across_y], [send_seq(across_y, 1)], buffers)
    far = after(far, buffers[2])
    buffers = project(3, far, [send_seq(one, 1) for one in far], buffers)
    inputs, block, labels = buffers

    starts = [sum(CHUNKS[:number]) for number in range(len(CHUNKS))]
    attended, note = [], None
    for start, rows in zip(starts, CHUNKS):
        made = attention_call(start, rows, image_owner[0], labels, block, note is None)
        note = made[1] if note is None else note
        value = made[0]
        if attended:
            (value,) = after([value], *attended[-1][1])
        attended.append((value, near_shards(value)))
    latest = attended[-1][0]
    most = 2 * (total // 4) // images
    projected, moving = [], []
    for own, (own_swap, across_x, across_y) in attended:
        previous = moving[-1][-1] if moving else ()
        across_x, across_y = after([across_x, across_y], latest, *previous)
        far = far_shards(across_x, across_y)
        moving.append(
            (own, own_swap, across_x, send_seq(across_x, 1), across_y, send_seq(across_y, 1), far)
        )
    for number, (start, rows) in enumerate(zip(starts, CHUNKS)):
        *near, far = moving[number]
        if projected:
            far = after(far, projected[-1])
        sources = [[one] for one in near] + [far, [send_seq(one, 1) for one in far]]
        route = ()
        if number == len(CHUNKS) - 1:
            route = (pack[None], most, note, *projected)
        made = merge_call(
            start, rows, sources, inputs, ordered, merge_gain_row, merge_rows, bias, packs, route
        )
        projected.append(made[0])
    blocks = [made[0]] + [
        lax.ppermute(made[flip], "pack", [(z, z ^ flip) for z in range(packs)])
        for flip in range(1, packs)
    ]
    return place_call(pack[None], blocks, most, merge_weight.shape[1])[None]


def local(*arguments):
    patches, weight = arguments[0], arguments[4]
    shards = lax.axis_size("seq")
    fits = shards == 8 and HEADS // shards == 2 and weight.shape[1] == 6 * HD
    fits = fits and patches.shape[1] * shards == sum(CHUNKS) and lax.axis_size("pack") == 4
    return fast_local(*arguments) if fits else general_local(*arguments)


def solution(mesh):
    placed = (
        P("pack", "seq", None),
        P("pack", "seq"),
        P(),
        P(),
        P(None, "seq"),
        P("pack", "seq"),
        P("pack", "seq"),
        P("pack", "seq"),
        P(),
        P(),
        P(None, "seq"),
        P("seq"),
        P("pack", None),
    )
    return jax.shard_map(
        local, mesh=mesh, in_specs=placed, out_specs=P("pack", None, None, "seq"), check_vma=False
    )
```

```python
import functools

import jax
import jax.numpy as jnp
import numpy as np
from jax import lax
from jax.experimental import pallas as pl
from jax.experimental.pallas import tpu as pltpu
from jax.sharding import PartitionSpec as P

D = 1408
HEADS = 16
HD = 88


EPSILON = 1e-06


def layer_norm(values, gain_vector):
    center = values - jnp.mean(values, axis=-1, keepdims=True)
    spread = jnp.mean(center * center, axis=-1, keepdims=True)
    return center * lax.rsqrt(spread + EPSILON) * gain_vector.astype(jnp.float32)


def rotate(vectors, row_index, column_index):
    total_rows, heads_here, head_width = vectors.shape
    quarter = head_width // 4
    frequency = 10000.0 ** (-jnp.arange(quarter, dtype=jnp.float32) / quarter)
    row_angle = row_index.astype(jnp.float32)[:, None] * frequency[None, :]
    column_angle = column_index.astype(jnp.float32)[:, None] * frequency[None, :]
    angles = jnp.stack([row_angle, column_angle], axis=1)[:, None, :, None, :]
    split_up = vectors.reshape(total_rows, heads_here, 2, 2, quarter)
    partner = jnp.stack([-split_up[:, :, :, 1], split_up[:, :, :, 0]], axis=3)
    turned = split_up * jnp.cos(angles) + partner * jnp.sin(angles)
    return turned.reshape(total_rows, heads_here, head_width)


def qkv_block(projected, row_index, column_index):
    turned_queries = rotate(projected[:, :, 0], row_index, column_index)
    turned_keys = rotate(projected[:, :, 1], row_index, column_index)
    return jnp.concatenate([turned_queries, turned_keys, projected[:, :, 2]], axis=-1).astype(
        jnp.bfloat16
    )


def attention(block, segments):
    total_rows, heads_here, triple = block.shape
    head_width = triple // 3
    step_rows = min(512, total_rows)
    query_part = block[:, :, :head_width].reshape(
        total_rows // step_rows, step_rows, heads_here, head_width
    )
    key_part = block[:, :, head_width : 2 * head_width]
    value_part = block[:, :, 2 * head_width :]
    query_segments = segments.reshape(total_rows // step_rows, step_rows)
    scale = head_width ** (-0.5)

    def one_block(inputs_pair):
        queries_here, segments_here = inputs_pair
        scores = (
            jnp.einsum("qhd,khd->hqk", queries_here, key_part, preferred_element_type=jnp.float32)
            * scale
        )
        same_image = (segments_here[:, None] == segments[None, :])[None]
        scores = jnp.where(same_image, scores, -jnp.inf)
        highest = jnp.max(scores, axis=-1, keepdims=True)
        weights = jnp.exp(scores - highest)
        probs = (weights / jnp.sum(weights, axis=-1, keepdims=True)).astype(jnp.bfloat16)
        result = jnp.einsum("hqk,khd->qhd", probs, value_part, preferred_element_type=jnp.float32)
        return result.astype(jnp.bfloat16)

    return lax.map(one_block, (query_part, query_segments)).reshape(
        total_rows, heads_here, head_width
    )


def route(projected, segments, owners_here, packs, most):
    merged_segments = segments[::4]
    images = owners_here.shape[0]
    image_ids = jnp.arange(images, dtype=jnp.int32)
    member = (merged_segments[None, :] == image_ids[:, None]).astype(jnp.int32)
    lengths = jnp.sum(member, axis=1, dtype=jnp.int32)
    starts = jnp.cumsum(lengths, dtype=jnp.int32) - lengths
    owner_ids = jnp.arange(packs, dtype=jnp.int32)
    owned = owners_here[None, :] == owner_ids[:, None]
    first_row = jnp.sum(jnp.where(owned, starts[None, :], 0), axis=1, dtype=jnp.int32)
    owned_length = jnp.sum(jnp.where(owned, lengths[None, :], 0), axis=1, dtype=jnp.int32)
    slots = jnp.arange(most, dtype=jnp.int32)
    source_rows = jnp.clip(first_row[:, None] + slots[None, :], 0, projected.shape[0] - 1)
    picked = jnp.take(projected, source_rows.reshape(-1), axis=0).reshape(
        packs, most, projected.shape[1]
    )
    filled = slots[None, :] < owned_length[:, None]
    return jnp.where(filled[:, :, None], picked, jnp.zeros_like(picked))


def general_local(
    patches,
    patch_mask,
    mask_embed,
    norm_gain,
    qkv_weight,
    segment_ids,
    patch_rows,
    patch_column,
    out_weight,
    merge_gain,
    merge_weight,
    merge_bias,
    image_owner,
):
    local_rows = patches.shape[1]
    shards = lax.axis_size("seq")
    packs = lax.axis_size("pack")
    heads_here = HEADS // shards
    inputs = jnp.where(patch_mask[0][:, None] == 1, mask_embed[None, :], patches[0])
    normed = layer_norm(inputs.astype(jnp.float32), norm_gain).astype(jnp.bfloat16)
    labels = lax.all_gather(
        jnp.stack([segment_ids[0], patch_rows[0], patch_column[0]]), "seq", axis=1, tiled=True
    )
    piece = lax.all_gather(normed, "seq", axis=0, tiled=True)
    span = piece.shape[0]
    projected = jnp.dot(piece, qkv_weight, preferred_element_type=jnp.float32)
    row_part = labels[1]
    column_part = labels[2]
    block = qkv_block(projected.reshape(span, heads_here, 3, HD), row_part, column_part)
    result = attention(block, labels[0])
    mixed_heads = lax.all_to_all(result, "seq", split_axis=0, concat_axis=1, tiled=True)
    attended = mixed_heads.reshape(local_rows, D)
    residual = inputs.astype(jnp.float32) + jnp.dot(
        attended, out_weight, preferred_element_type=jnp.float32
    )
    merged = layer_norm(residual, merge_gain).astype(jnp.bfloat16).reshape(local_rows // 4, 4 * D)
    projected_all = (
        jnp.dot(
            lax.all_gather(merged, "seq", axis=0, tiled=True),
            merge_weight,
            preferred_element_type=jnp.float32,
        )
        + merge_bias.astype(jnp.float32)
    ).astype(jnp.bfloat16)
    images = image_owner.shape[1]
    most = 2 * projected_all.shape[0] // images
    outgoing = route(projected_all, labels[0], image_owner[0], packs, most)
    delivered = lax.all_to_all(outgoing, "pack", split_axis=0, concat_axis=0, tiled=True)
    return delivered[None]


LANES = 128
CHIP, CORE, PACK, IDS = 0, 1, 2, 3
BLOCK = 256
POSITIONS = 64
NEGATIVE = -1e30
CHUNKS = (768, 768)


def norm_rows(values, gain_row):
    center = values - jnp.mean(values, axis=-1, keepdims=True)
    spread = jnp.mean(center * center, axis=-1, keepdims=True)
    return center * lax.rsqrt(spread + EPSILON) * gain_row


def stacked(pieces):
    loaded = [piece[...] for piece in pieces]
    return loaded[0] if len(loaded) == 1 else jnp.concatenate(loaded, axis=0)


def in_vmem(value):
    return pltpu.with_memory_space_constraint(value, pltpu.VMEM)


def in_hbm(value):
    return pltpu.with_memory_space_constraint(value, pltpu.HBM)


def payload_kernel(segments, rows, columns, mask, embed, patches, out):
    labels = [one[...].astype(jnp.float32) for one in (segments, rows, columns, mask)]
    labels.append(jnp.zeros((4, labels[0].shape[1]), jnp.float32))
    labels = jnp.concatenate(labels, axis=0).astype(jnp.bfloat16)
    shape = (8, LANES)
    row = lax.broadcasted_iota(jnp.int32, shape, 0)
    place = jnp.where(row == lax.broadcasted_iota(jnp.int32, shape, 1), 1.0, 0.0)
    turned = lax.dot_general(
        labels,
        place.astype(jnp.bfloat16),
        (((0,), (0,)), ((), ())),
        preferred_element_type=jnp.float32,
    )
    masked = turned[:, 3:4] > 0.5
    tokens = jnp.where(
        masked, embed[...].astype(jnp.float32)[None, :], patches[0].astype(jnp.float32)
    )
    out[:, :D] = tokens.astype(jnp.bfloat16)
    out[:, D:] = turned.astype(jnp.bfloat16)


def payload_call(segments, rows, columns, mask, embed, patches):
    count = patches.shape[1]
    operands = (segments, rows, columns, mask, embed, patches)
    fixed = lambda shape: pl.BlockSpec(shape, lambda i: (0,) * len(shape))
    shape = (count, D + LANES)
    return pl.pallas_call(
        payload_kernel,
        grid=(1,),
        in_specs=[fixed(one.shape) for one in operands],
        out_specs=fixed(shape),
        out_shape=jax.ShapeDtypeStruct(shape, jnp.bfloat16),
        compiler_params=pltpu.CompilerParams(vmem_limit_bytes=8 << 20),
        cost_estimate=pl.CostEstimate(
            flops=count * D, bytes_accessed=4 * count * D, transcendentals=0
        ),
        name="payload",
    )(*map(in_hbm, operands))


def qkv_kernel(count, flip, info, *refs):
    first, second = refs[:count], refs[count : 2 * count]
    table, gain, weight = refs[2 * count : 2 * count + 3]
    inputs_out, qkv_out, label_out = refs[-3:]
    mine, other = stacked(first), stacked(second)
    leads = info[CORE] == 0
    ahead = jnp.where(leads, mine, other)
    behind = jnp.where(leads, other, mine)
    both = jnp.concatenate([ahead, behind], axis=0)
    rows = both.shape[0]
    at = pl.ds(pl.multiple_of((info[CHIP] ^ flip) * rows, rows), rows)
    inputs_out[at, :] = both[:, :D]
    label_out[at, :] = both[:, D:]
    labels = both[:, D:].astype(jnp.float32)
    normed = norm_rows(both[:, :D].astype(jnp.float32), gain[...]).astype(jnp.bfloat16)
    columns = lax.dot_general(
        normed, weight[...], (((1,), (1,)), ((), ())), preferred_element_type=jnp.float32
    )
    lane = lax.broadcasted_iota(jnp.int32, labels.shape, 1)
    numbers = lane.astype(jnp.float32)
    hot = (numbers == labels[:, 1:2]) | (numbers == labels[:, 2:3] + POSITIONS)
    looked = jnp.dot(
        jnp.where(hot, 1.0, 0.0).astype(jnp.bfloat16), table[...], preferred_element_type=jnp.float32
    )
    cosine = looked[:, :LANES] + looked[:, LANES : 2 * LANES]
    sine = looked[:, 2 * LANES : 3 * LANES] + looked[:, 3 * LANES :]
    first_head = lane < HD // 2

    def turn(start):
        a = columns[:, start : start + LANES]
        b = columns[:, start + LANES : start + 2 * LANES]
        return a * cosine - b * sine, b * cosine + a * sine

    query_a, query_b = turn(0)
    key_a, key_b = turn(2 * LANES)
    zero = jnp.zeros_like(key_a)
    parts = [
        query_a,
        query_b,
        jnp.where(first_head, key_a, zero),
        jnp.where(first_head, key_b, zero),
        jnp.where(first_head, zero, key_a),
        jnp.where(first_head, zero, key_b),
    ]
    values_part = columns[:, 4 * LANES :]
    wide = lax.broadcasted_iota(jnp.int32, values_part.shape, 1)
    ones = jnp.where(wide == 2 * HD, 1.0, 0.0)
    parts.append(jnp.where(wide < HD, values_part, ones))
    parts.append(jnp.where((wide >= HD) & (wide < 2 * HD), values_part, ones))
    for number, part in enumerate(parts[:6]):
        qkv_out[at, number * LANES : (number + 1) * LANES] = part.astype(jnp.bfloat16)
    for number, part in enumerate(parts[6:]):
        low = (6 + 2 * number) * LANES
        qkv_out[at, low : low + 2 * LANES] = part.astype(jnp.bfloat16)


def qkv_call(info, flip, first, second, table, gain, weight, earlier, total):
    rows = 2 * sum(piece.shape[0] for piece in first)
    widths = (D, 10 * LANES, LANES)
    operands = [*first, *second, table, gain, in_vmem(weight)]
    vmem = pl.BlockSpec(memory_space=pltpu.VMEM)
    held = [in_vmem(one) for one in earlier]
    return pl.pallas_call(
        functools.partial(qkv_kernel, len(first), flip),
        in_specs=[pl.BlockSpec(memory_space=pltpu.SMEM)]
        + [vmem] * (len(operands) + len(earlier)),
        out_specs=[vmem] * len(widths),
        out_shape=[pltpu.VMEM((total, width), jnp.bfloat16) for width in widths],
        input_output_aliases={1 + len(operands) + i: i for i in range(len(earlier))},
        compiler_params=pltpu.CompilerParams(vmem_limit_bytes=14 << 20),
        cost_estimate=pl.CostEstimate(
            flops=6 * rows * D * weight.shape[0],
            bytes_accessed=2 * (rows * 4 * D + weight.size),
            transcendentals=rows,
        ),
        name="norm_qkv",
    )(info, *operands, *held)


def segment_row(labels):
    pick = jnp.where(lax.broadcasted_iota(jnp.int32, (8, LANES), 1) == 0, 1.0, 0.0)
    return lax.dot_general(
        pick.astype(jnp.bfloat16),
        labels,
        (((1,), (1,)), ((), ())),
        preferred_element_type=jnp.float32,
    )


def attention_kernel(start, first_owner, images, info, labels, block, *refs):
    out, *rest = refs
    scores, high, rows_scratch = rest[-3:]
    rows = high.shape[1]
    total = block.shape[0]
    factor = HD**-0.5 * float(np.log2(np.e))
    segments = segment_row(labels[...])
    for step in range(total // BLOCK):
        rows_scratch[step] = segments[:, step * BLOCK : (step + 1) * BLOCK]
    own = labels[start : start + rows, :1].astype(jnp.float32)
    lowest, largest = jnp.min(own), jnp.max(own)
    one_row = segments[:1]
    begin = jnp.sum(jnp.where(one_row < lowest, 1, 0)) // BLOCK
    end = (jnp.sum(jnp.where(one_row <= largest, 1, 0)) + BLOCK - 1) // BLOCK
    queries = block[start : start + rows, : 2 * LANES]
    own = jnp.broadcast_to(own, (rows, LANES))
    high[...] = jnp.full_like(high, NEGATIVE)

    def score(step, carry):
        at = pl.ds(pl.multiple_of(step * BLOCK, BLOCK), BLOCK)
        theirs = rows_scratch[step, :1]
        same = jnp.concatenate([own == theirs[:, :LANES], own == theirs[:, LANES:]], axis=1)
        for head in range(2):
            keys = block[at, (2 + 2 * head) * LANES : (4 + 2 * head) * LANES]
            values = lax.dot_general(
                queries, keys, (((1,), (1,)), ((), ())), preferred_element_type=jnp.float32
            )
            values = jnp.where(same, values, NEGATIVE)
            scores[head, step] = values
            high[head] = jnp.maximum(
                high[head], jnp.maximum(values[:, :LANES], values[:, LANES:])
            )
        return carry

    lax.fori_loop(begin, end, score, 0)
    highest = [jnp.max(high[head], axis=-1, keepdims=True) for head in range(2)]

    def weigh(step, carry):
        at = pl.ds(pl.multiple_of(step * BLOCK, BLOCK), BLOCK)
        sums = []
        for head in range(2):
            weights = jnp.exp2((scores[head, step] - highest[head]) * factor)
            values = block[at, (6 + 2 * head) * LANES : (8 + 2 * head) * LANES]
            sums.append(
                carry[head]
                + jnp.dot(weights.astype(jnp.bfloat16), values, preferred_element_type=jnp.float32)
            )
        return tuple(sums)

    zero = jnp.zeros((rows, 2 * LANES), jnp.float32)
    sums = lax.fori_loop(begin, end, weigh, (zero, zero))
    acc = sum(one / one[:, 2 * HD : 2 * HD + 1] for one in sums)
    out[:rows] = acc[:, :LANES].astype(jnp.bfloat16)
    half = rows // 2
    low, up = acc[:half, LANES:], acc[half:, LANES:]
    lane = lax.broadcasted_iota(jnp.int32, low.shape, 1)
    tail = 2 * HD - LANES
    packed = jnp.where(lane < tail, low, jnp.where(lane < 2 * tail, pltpu.roll(up, tail, 1), 0.0))
    out[rows:] = packed.astype(jnp.bfloat16)

    if len(rest) > 3:
        note = rest[0]
        row = lax.broadcasted_iota(jnp.int32, note.shape, 0)
        lane = lax.broadcasted_iota(jnp.int32, note.shape, 1)
        found = jnp.zeros(note.shape, jnp.float32)
        for image in range(images):
            below = jnp.sum(jnp.where(one_row < image, 0.25, 0.0), axis=1, keepdims=True)
            inside = jnp.sum(jnp.where(one_row == image, 0.25, 0.0), axis=1, keepdims=True)
            here = row == info[first_owner + image]
            for place, number in enumerate((below, inside)):
                upper = jnp.floor(number * (1.0 / 16))
                found = jnp.where(here & (lane == 2 * place), upper, found)
                found = jnp.where(here & (lane == 2 * place + 1), number - 16 * upper, found)
        note[...] = found.astype(jnp.bfloat16)


def attention_call(start, rows, first_owner, info, labels, block, noted):
    total = block.shape[0]
    vmem = pl.BlockSpec(memory_space=pltpu.VMEM)
    shapes = [jax.ShapeDtypeStruct((rows + rows // 2, LANES), jnp.bfloat16)]
    if noted:
        shapes.append(jax.ShapeDtypeStruct((16, LANES), jnp.bfloat16))
    return pl.pallas_call(
        functools.partial(attention_kernel, start, first_owner, info.shape[0] - first_owner),
        in_specs=[pl.BlockSpec(memory_space=pltpu.SMEM), vmem, vmem],
        out_specs=[vmem] * len(shapes),
        out_shape=shapes,
        scratch_shapes=[
            pltpu.VMEM((2, total // BLOCK, rows, BLOCK), jnp.float32),
            pltpu.VMEM((2, rows, LANES), jnp.float32),
            pltpu.VMEM((total // BLOCK, 8, BLOCK), jnp.float32),
        ],
        compiler_params=pltpu.CompilerParams(vmem_limit_bytes=20 << 20),
        cost_estimate=pl.CostEstimate(
            flops=10 * rows * total * 2 * LANES,
            bytes_accessed=2 * block.size,
            transcendentals=rows * total,
        ),
        name="attention",
    )(info, in_vmem(labels), in_vmem(block))


def prepare_kernel(shards, info, out_weight, merge_weight, qkv_weight, spread, *refs):
    *rows, out, merge, qkv, qkv_buffer, spread_buffer, sems = refs
    for row, row_out in zip(rows[: len(rows) // 2], rows[len(rows) // 2 :]):
        row_out[...] = row[...].astype(jnp.float32)[None, :]
    rest = 2 * HD - LANES
    copies = [(qkv_weight, qkv_buffer), (spread, spread_buffer)]
    out[shards * LANES :] = jnp.zeros((shards // 2 * LANES, D), jnp.bfloat16)
    for place in range(shards):
        start = pl.multiple_of(info[IDS + place] * (2 * HD), 16)
        to = (shards + place // 2) * LANES + place % 2 * rest
        copies.append(
            (out_weight.at[pl.ds(start, LANES), :], out.at[pl.ds(place * LANES, LANES), :])
        )
        copies.append((out_weight.at[pl.ds(start + LANES, rest), :], out.at[pl.ds(to, rest), :]))
    copies.append((merge_weight, merge))
    copies = [
        pltpu.make_async_copy(source, target, sems.at[i])
        for i, (source, target) in enumerate(copies)
    ]
    for copy in copies:
        copy.start()
    copies[0].wait()
    copies[1].wait()
    qkv[...] = jnp.dot(
        spread_buffer[...], qkv_buffer[...], preferred_element_type=jnp.float32
    ).astype(jnp.bfloat16)
    for copy in copies[2:]:
        copy.wait()


def prepare_call(shards, info, out_weight, merge_weight, qkv_weight, spread, rows):
    anywhere = pl.BlockSpec(memory_space=pl.ANY)
    vmem = pl.BlockSpec(memory_space=pltpu.VMEM)
    operands = (out_weight, merge_weight, qkv_weight, spread)
    shapes = [(shards * LANES * 3 // 2, D), merge_weight.shape, (spread.shape[0], D)]
    return pl.pallas_call(
        functools.partial(prepare_kernel, shards),
        in_specs=[pl.BlockSpec(memory_space=pltpu.SMEM)]
        + [anywhere] * len(operands)
        + [vmem] * len(rows),
        out_specs=[vmem] * (len(rows) + len(shapes)),
        out_shape=[pltpu.VMEM((1, row.shape[0]), jnp.float32) for row in rows]
        + [pltpu.VMEM(shape, jnp.bfloat16) for shape in shapes],
        scratch_shapes=[
            pltpu.VMEM(qkv_weight.shape, jnp.bfloat16),
            pltpu.VMEM(spread.shape, jnp.bfloat16),
            pltpu.SemaphoreType.DMA((2 * shards + 3,)),
        ],
        compiler_params=pltpu.CompilerParams(vmem_limit_bytes=10 << 20),
        cost_estimate=pl.CostEstimate(
            flops=2 * spread.size * D,
            bytes_accessed=4 * (out_weight.size + merge_weight.size + qkv_weight.size),
            transcendentals=0,
        ),
        name="prepare",
    )(info, *map(in_hbm, operands), *rows)


def merge_kernel(start, counts, packs, last, *refs):
    inputs, weight, gain, merge_weight, bias = refs[:5]
    pieces = refs[5 : 5 + sum(counts)]
    *refs, state = refs[5 + sum(counts) :]
    rows = state.shape[1]
    half = rows // 2
    rest = 2 * HD - LANES
    sources, at = [], 0
    for count in counts:
        sources.append(stacked(pieces[at : at + count]))
        at += count
    shards = len(sources)
    lane = lax.broadcasted_iota(jnp.int32, (half, LANES), 1)
    for part in range(2):
        token = slice(part * half, (part + 1) * half)
        lined = [source[token, :] for source in sources]
        for pair in range(shards // 2):
            mine = sources[2 * pair][rows:, :].astype(jnp.float32)
            other = sources[2 * pair + 1][rows:, :].astype(jnp.float32)
            if part == 0:
                other = pltpu.roll(other, rest, 1)
            else:
                mine = pltpu.roll(mine, LANES - rest, 1)
            lined.append(jnp.where(lane < rest, mine, other).astype(jnp.bfloat16))
        mixed = jnp.dot(
            jnp.concatenate(lined, axis=1), weight[...], preferred_element_type=jnp.float32
        )
        before = inputs[start + part * half : start + (part + 1) * half, :].astype(jnp.float32)
        normed = norm_rows(before + mixed, gain[...])
        for column in range(D // LANES):
            state[column, token, :] = normed[:, column * LANES : (column + 1) * LANES]
    groups = rows // 4
    total = bias[...]
    for quadrant in range(4):
        tokens = jnp.concatenate(
            [
                state[column, pl.ds(quadrant, groups, stride=4), :].astype(jnp.bfloat16)
                for column in range(D // LANES)
            ],
            axis=1,
        )
        total = total + lax.dot_general(
            tokens,
            merge_weight[:, quadrant * D : (quadrant + 1) * D],
            (((1,), (1,)), ((), ())),
            preferred_element_type=jnp.float32,
        )
    total = total.astype(jnp.bfloat16)
    if not last:
        refs[0][...] = total
        return
    info, note, *earlier = refs[:-packs]
    outs = refs[-packs:]
    total = jnp.concatenate([*[one[...] for one in earlier], total], axis=0)
    whole = total.shape[1] // LANES
    most = outs[0].shape[0] * LANES // total.shape[1]
    notes = note[...].astype(jnp.float32)
    note_row = lax.broadcasted_iota(jnp.int32, notes.shape, 0)
    slot = lax.broadcasted_iota(jnp.int32, (most, total.shape[0]), 0)
    row = lax.broadcasted_iota(jnp.int32, (most, total.shape[0]), 1)
    for place, out in enumerate(outs):
        found = jnp.where(note_row == (info[PACK] ^ place), notes, 0.0)
        found = jnp.sum(found, axis=0, keepdims=True)
        first = (16.0 * found[:, :1] + found[:, 1:2]).astype(jnp.int32)
        length = (16.0 * found[:, 2:3] + found[:, 3:4]).astype(jnp.int32)
        chosen = (row == slot + first) & (slot < length)
        chosen = jnp.where(chosen, 1.0, 0.0).astype(jnp.bfloat16)
        block = jnp.dot(chosen, total, preferred_element_type=jnp.float32)
        for column in range(whole):
            out[column * most : (column + 1) * most, :] = block[
                :, column * LANES : (column + 1) * LANES
            ].astype(jnp.bfloat16)
        low = block[: most // 2, whole * LANES :]
        up = block[most // 2 :, whole * LANES :]
        out[whole * most :, :] = jnp.concatenate([low, up], axis=1).astype(jnp.bfloat16)


def merge_call(start, rows, sources, inputs, weight, gain, merge_weight, bias, packs, route):
    groups = rows // 4
    width = merge_weight.shape[0]
    pieces = [piece for source in sources for piece in source]
    vmem = pl.BlockSpec(memory_space=pltpu.VMEM)
    operands = [in_vmem(inputs), in_vmem(weight), gain, in_vmem(merge_weight), bias, *pieces]
    specs = [vmem] * len(operands)
    shapes = [jax.ShapeDtypeStruct((groups, width), jnp.bfloat16)]
    if route:
        me, most, *others = route
        operands += [me, *others]
        specs += [pl.BlockSpec(memory_space=pltpu.SMEM)] + [vmem] * len(others)
        shapes = [jax.ShapeDtypeStruct((most * width // LANES, LANES), jnp.bfloat16)] * packs
    return pl.pallas_call(
        functools.partial(
            merge_kernel, start, [len(source) for source in sources], packs, bool(route)
        ),
        in_specs=specs,
        out_specs=[vmem] * len(shapes),
        scratch_shapes=[pltpu.VMEM((D // LANES, rows, LANES), jnp.float32)],
        out_shape=shapes,
        compiler_params=pltpu.CompilerParams(vmem_limit_bytes=20 << 20),
        cost_estimate=pl.CostEstimate(
            flops=4 * rows * D * D + 2 * groups * merge_weight.size,
            bytes_accessed=2 * (D * D + merge_weight.size + 3 * rows * D),
            transcendentals=rows,
        ),
        name="out_merge",
    )(*operands)


def place_kernel(info, *refs):
    blocks, out = refs[:-1], refs[-1]
    most, width = out.shape[1:]
    whole = width // LANES
    half = most // 2
    middle = LANES // 2
    for place, block in enumerate(blocks):
        target = info[PACK] ^ place
        for column in range(whole):
            out[target, :, column * LANES : (column + 1) * LANES] = block[
                column * most : (column + 1) * most, :
            ]
        out[target, :half, whole * LANES :] = block[whole * most :, :middle]
        out[target, half:, whole * LANES :] = block[whole * most :, middle:]


def place_call(info, blocks, most, width):
    fixed = lambda shape: pl.BlockSpec(shape, lambda i: (0,) * len(shape))
    shape = (len(blocks), most, width)
    return pl.pallas_call(
        place_kernel,
        grid=(1,),
        in_specs=[pl.BlockSpec(memory_space=pltpu.SMEM)] + [fixed(one.shape) for one in blocks],
        out_specs=fixed(shape),
        out_shape=jax.ShapeDtypeStruct(shape, jnp.bfloat16),
        compiler_params=pltpu.CompilerParams(vmem_limit_bytes=8 << 20),
        cost_estimate=pl.CostEstimate(
            flops=0, bytes_accessed=4 * len(blocks) * most * width, transcendentals=0
        ),
        name="place_rows",
    )(info, *blocks)


def send_seq(value, flip):
    size = lax.axis_size("seq")
    return lax.ppermute(value, "seq", [(i, i ^ flip) for i in range(size)])


def after(values, *earlier):
    return lax.optimization_barrier((tuple(values), earlier))[0]


def halves_kernel(across_x, across_y, upper, lower):
    half = upper.shape[0]
    upper[...] = across_x[:half]
    lower[...] = across_y[half:]


def halves_call(across_x, across_y):
    vmem = pl.BlockSpec(memory_space=pltpu.VMEM)
    shape = (across_x.shape[0] // 2, across_x.shape[1])
    return pl.pallas_call(
        halves_kernel,
        in_specs=[vmem] * 2,
        out_specs=[vmem] * 2,
        out_shape=[jax.ShapeDtypeStruct(shape, across_x.dtype)] * 2,
        compiler_params=pltpu.CompilerParams(vmem_limit_bytes=4 << 20),
        cost_estimate=pl.CostEstimate(
            flops=0, bytes_accessed=4 * across_x.size, transcendentals=0
        ),
        name="halves",
    )(across_x, across_y)


def near_shards(value):
    return [send_seq(value, 1), send_seq(value, 2), send_seq(value, 4)]


def far_shards(across_x, across_y):
    upper, lower = halves_call(across_x, across_y)
    return [send_seq(upper, 4), send_seq(lower, 2)]


def weight_order(heads_here):
    quarter = HD // 4
    order = -np.ones((6 * LANES,), np.int32)
    for head in range(heads_here):
        base = head * 3 * HD
        for kind in range(2):
            for half in range(2):
                for letter in range(2):
                    target = (2 * kind + letter) * LANES + head * (HD // 2) + half * quarter
                    source = base + kind * HD + half * (HD // 2) + letter * quarter
                    order[target : target + quarter] = np.arange(source, source + quarter)
        target = 4 * LANES + head * HD
        order[target : target + HD] = np.arange(base + 2 * HD, base + 3 * HD)
    return order


def angle_table(heads_here):
    quarter = HD // 4
    frequency = (10000.0 ** (-np.arange(quarter) / quarter)).astype(np.float32)
    angles = np.arange(POSITIONS, dtype=np.float32)[:, None] * frequency[None, :]
    pieces = []
    for function in (np.cos, np.sin):
        exact = np.zeros((2 * POSITIONS, LANES), np.float64)
        for head in range(heads_here):
            for half in range(2):
                lane = head * (HD // 2) + half * quarter
                rows = slice(half * POSITIONS, (half + 1) * POSITIONS)
                exact[rows, lane : lane + quarter] = function(angles.astype(np.float64))
        upper = exact.astype(jnp.bfloat16)
        pieces += [upper, (exact - upper.astype(np.float64)).astype(jnp.bfloat16)]
    return np.concatenate(pieces, axis=1)


def fast_local(
    patches,
    patch_mask,
    mask_embed,
    norm_gain,
    qkv_weight,
    segment_ids,
    patch_rows,
    patch_column,
    out_weight,
    merge_gain,
    merge_weight,
    merge_bias,
    image_owner,
):
    local_rows = patches.shape[1]
    shards = lax.axis_size("seq")
    packs = lax.axis_size("pack")
    heads_here = HEADS // shards
    images = image_owner.shape[1]
    total = local_rows * shards
    me = lax.axis_index("seq").astype(jnp.int32)
    pack = lax.axis_index("pack").astype(jnp.int32)

    value = payload_call(segment_ids, patch_rows, patch_column, patch_mask, mask_embed, patches)
    own_swap, across_x, across_y = near_shards(value)

    order = weight_order(heads_here)
    spread = (order[:, None] == np.arange(qkv_weight.shape[1])[None, :]).astype(jnp.bfloat16)
    table = jnp.asarray(angle_table(heads_here))
    chip, core = me // 2, me % 2
    info = [chip, core, pack, *[me ^ place for place in range(shards)]]
    info = jnp.concatenate([jnp.stack(info), image_owner[0]])
    gain, merge_gain_row, bias, ordered, merge_rows, weight = prepare_call(
        shards,
        info,
        out_weight,
        merge_weight.T,
        qkv_weight.T,
        jnp.asarray(spread),
        (norm_gain, merge_gain, merge_bias),
    )

    project = lambda place, first, second, earlier: qkv_call(
        info, place, first, second, table, gain, weight, earlier, total
    )
    buffers = project(0, [value], [own_swap], ())
    across_x, across_y = after([across_x, across_y], buffers[2], ordered)
    far = far_shards(across_x, across_y)
    buffers = project(1, [across_x], [send_seq(across_x, 1)], buffers)
    buffers = project(2, [across_y], [send_seq(across_y, 1)], buffers)
    far = after(far, buffers[2])
    buffers = project(3, far, [send_seq(one, 1) for one in far], buffers)
    inputs, block, labels = buffers

    starts = [sum(CHUNKS[:number]) for number in range(len(CHUNKS))]
    attended, note = [], None
    for start, rows in zip(starts, CHUNKS):
        made = attention_call(start, rows, IDS + shards, info, labels, block, note is None)
        note = made[1] if note is None else note
        value = made[0]
        if attended:
            (value,) = after([value], *attended[-1][1])
        attended.append((value, near_shards(value)))
    latest = attended[-1][0]
    most = 2 * (total // 4) // images
    projected, moving = [], []
    for own, (own_swap, across_x, across_y) in attended:
        previous = moving[-1][-1] if moving else ()
        across_x, across_y = after([across_x, across_y], latest, *previous)
        far = far_shards(across_x, across_y)
        moving.append(
            (own, own_swap, across_x, send_seq(across_x, 1), across_y, send_seq(across_y, 1), far)
        )
    for number, (start, rows) in enumerate(zip(starts, CHUNKS)):
        *near, far = moving[number]
        if projected:
            far = after(far, projected[-1])
        sources = [[one] for one in near] + [far, [send_seq(one, 1) for one in far]]
        route = ()
        if number == len(CHUNKS) - 1:
            route = (info, most, note, *projected)
        made = merge_call(
            start, rows, sources, inputs, ordered, merge_gain_row, merge_rows, bias, packs, route
        )
        projected.append(made[0])
    blocks = [made[0]] + [
        lax.ppermute(made[flip], "pack", [(z, z ^ flip) for z in range(packs)])
        for flip in range(1, packs)
    ]
    return place_call(info, blocks, most, merge_weight.shape[1])[None]


def local(*arguments):
    patches, weight = arguments[0], arguments[4]
    shards = lax.axis_size("seq")
    fits = shards == 8 and HEADS // shards == 2 and weight.shape[1] == 6 * HD
    fits = fits and patches.shape[1] * shards == sum(CHUNKS) and lax.axis_size("pack") == 4
    return fast_local(*arguments) if fits else general_local(*arguments)


def solution(mesh):
    placed = (
        P("pack", "seq", None),
        P("pack", "seq"),
        P(),
        P(),
        P(None, "seq"),
        P("pack", "seq"),
        P("pack", "seq"),
        P("pack", "seq"),
        P(),
        P(),
        P(None, "seq"),
        P("seq"),
        P("pack", None),
    )
    return jax.shard_map(
        local, mesh=mesh, in_specs=placed, out_specs=P("pack", None, None, "seq"), check_vma=False
    )
```

```python
import functools

import jax
import jax.numpy as jnp
import numpy as np
from jax import lax
from jax.experimental import pallas as pl
from jax.experimental.pallas import tpu as pltpu
from jax.sharding import PartitionSpec as P

D = 1408
HEADS = 16
HD = 88


EPSILON = 1e-06


def layer_norm(values, gain_vector):
    center = values - jnp.mean(values, axis=-1, keepdims=True)
    spread = jnp.mean(center * center, axis=-1, keepdims=True)
    return center * lax.rsqrt(spread + EPSILON) * gain_vector.astype(jnp.float32)


def rotate(vectors, row_index, column_index):
    total_rows, heads_here, head_width = vectors.shape
    quarter = head_width // 4
    frequency = 10000.0 ** (-jnp.arange(quarter, dtype=jnp.float32) / quarter)
    row_angle = row_index.astype(jnp.float32)[:, None] * frequency[None, :]
    column_angle = column_index.astype(jnp.float32)[:, None] * frequency[None, :]
    angles = jnp.stack([row_angle, column_angle], axis=1)[:, None, :, None, :]
    split_up = vectors.reshape(total_rows, heads_here, 2, 2, quarter)
    partner = jnp.stack([-split_up[:, :, :, 1], split_up[:, :, :, 0]], axis=3)
    turned = split_up * jnp.cos(angles) + partner * jnp.sin(angles)
    return turned.reshape(total_rows, heads_here, head_width)


def qkv_block(projected, row_index, column_index):
    turned_queries = rotate(projected[:, :, 0], row_index, column_index)
    turned_keys = rotate(projected[:, :, 1], row_index, column_index)
    return jnp.concatenate([turned_queries, turned_keys, projected[:, :, 2]], axis=-1).astype(
        jnp.bfloat16
    )


def attention(block, segments):
    total_rows, heads_here, triple = block.shape
    head_width = triple // 3
    step_rows = min(512, total_rows)
    query_part = block[:, :, :head_width].reshape(
        total_rows // step_rows, step_rows, heads_here, head_width
    )
    key_part = block[:, :, head_width : 2 * head_width]
    value_part = block[:, :, 2 * head_width :]
    query_segments = segments.reshape(total_rows // step_rows, step_rows)
    scale = head_width ** (-0.5)

    def one_block(inputs_pair):
        queries_here, segments_here = inputs_pair
        scores = (
            jnp.einsum("qhd,khd->hqk", queries_here, key_part, preferred_element_type=jnp.float32)
            * scale
        )
        same_image = (segments_here[:, None] == segments[None, :])[None]
        scores = jnp.where(same_image, scores, -jnp.inf)
        highest = jnp.max(scores, axis=-1, keepdims=True)
        weights = jnp.exp(scores - highest)
        probs = (weights / jnp.sum(weights, axis=-1, keepdims=True)).astype(jnp.bfloat16)
        result = jnp.einsum("hqk,khd->qhd", probs, value_part, preferred_element_type=jnp.float32)
        return result.astype(jnp.bfloat16)

    return lax.map(one_block, (query_part, query_segments)).reshape(
        total_rows, heads_here, head_width
    )


def route(projected, segments, owners_here, packs, most):
    merged_segments = segments[::4]
    images = owners_here.shape[0]
    image_ids = jnp.arange(images, dtype=jnp.int32)
    member = (merged_segments[None, :] == image_ids[:, None]).astype(jnp.int32)
    lengths = jnp.sum(member, axis=1, dtype=jnp.int32)
    starts = jnp.cumsum(lengths, dtype=jnp.int32) - lengths
    owner_ids = jnp.arange(packs, dtype=jnp.int32)
    owned = owners_here[None, :] == owner_ids[:, None]
    first_row = jnp.sum(jnp.where(owned, starts[None, :], 0), axis=1, dtype=jnp.int32)
    owned_length = jnp.sum(jnp.where(owned, lengths[None, :], 0), axis=1, dtype=jnp.int32)
    slots = jnp.arange(most, dtype=jnp.int32)
    source_rows = jnp.clip(first_row[:, None] + slots[None, :], 0, projected.shape[0] - 1)
    picked = jnp.take(projected, source_rows.reshape(-1), axis=0).reshape(
        packs, most, projected.shape[1]
    )
    filled = slots[None, :] < owned_length[:, None]
    return jnp.where(filled[:, :, None], picked, jnp.zeros_like(picked))


def general_local(
    patches,
    patch_mask,
    mask_embed,
    norm_gain,
    qkv_weight,
    segment_ids,
    patch_rows,
    patch_column,
    out_weight,
    merge_gain,
    merge_weight,
    merge_bias,
    image_owner,
):
    local_rows = patches.shape[1]
    shards = lax.axis_size("seq")
    packs = lax.axis_size("pack")
    heads_here = HEADS // shards
    inputs = jnp.where(patch_mask[0][:, None] == 1, mask_embed[None, :], patches[0])
    normed = layer_norm(inputs.astype(jnp.float32), norm_gain).astype(jnp.bfloat16)
    labels = lax.all_gather(
        jnp.stack([segment_ids[0], patch_rows[0], patch_column[0]]), "seq", axis=1, tiled=True
    )
    piece = lax.all_gather(normed, "seq", axis=0, tiled=True)
    span = piece.shape[0]
    projected = jnp.dot(piece, qkv_weight, preferred_element_type=jnp.float32)
    row_part = labels[1]
    column_part = labels[2]
    block = qkv_block(projected.reshape(span, heads_here, 3, HD), row_part, column_part)
    result = attention(block, labels[0])
    mixed_heads = lax.all_to_all(result, "seq", split_axis=0, concat_axis=1, tiled=True)
    attended = mixed_heads.reshape(local_rows, D)
    residual = inputs.astype(jnp.float32) + jnp.dot(
        attended, out_weight, preferred_element_type=jnp.float32
    )
    merged = layer_norm(residual, merge_gain).astype(jnp.bfloat16).reshape(local_rows // 4, 4 * D)
    projected_all = (
        jnp.dot(
            lax.all_gather(merged, "seq", axis=0, tiled=True),
            merge_weight,
            preferred_element_type=jnp.float32,
        )
        + merge_bias.astype(jnp.float32)
    ).astype(jnp.bfloat16)
    images = image_owner.shape[1]
    most = 2 * projected_all.shape[0] // images
    outgoing = route(projected_all, labels[0], image_owner[0], packs, most)
    delivered = lax.all_to_all(outgoing, "pack", split_axis=0, concat_axis=0, tiled=True)
    return delivered[None]


LANES = 128
CHIP, CORE, PACK, IDS = 0, 1, 2, 3
BLOCK = 256
POSITIONS = 64
NEGATIVE = -1e30
CHUNKS = (512, 512, 512)


def norm_rows(values, gain_row):
    center = values - jnp.mean(values, axis=-1, keepdims=True)
    spread = jnp.mean(center * center, axis=-1, keepdims=True)
    return center * lax.rsqrt(spread + EPSILON) * gain_row


def stacked(pieces):
    loaded = [piece[...] for piece in pieces]
    return loaded[0] if len(loaded) == 1 else jnp.concatenate(loaded, axis=0)


def in_vmem(value):
    return pltpu.with_memory_space_constraint(value, pltpu.VMEM)


def in_hbm(value):
    return pltpu.with_memory_space_constraint(value, pltpu.HBM)


def payload_kernel(segments, rows, columns, mask, embed, patches, out):
    labels = [one[...].astype(jnp.float32) for one in (segments, rows, columns, mask)]
    labels.append(jnp.zeros((4, labels[0].shape[1]), jnp.float32))
    labels = jnp.concatenate(labels, axis=0).astype(jnp.bfloat16)
    shape = (8, LANES)
    row = lax.broadcasted_iota(jnp.int32, shape, 0)
    place = jnp.where(row == lax.broadcasted_iota(jnp.int32, shape, 1), 1.0, 0.0)
    turned = lax.dot_general(
        labels,
        place.astype(jnp.bfloat16),
        (((0,), (0,)), ((), ())),
        preferred_element_type=jnp.float32,
    )
    masked = turned[:, 3:4] > 0.5
    tokens = jnp.where(
        masked, embed[...].astype(jnp.float32)[None, :], patches[0].astype(jnp.float32)
    )
    out[:, :D] = tokens.astype(jnp.bfloat16)
    out[:, D:] = turned.astype(jnp.bfloat16)


def payload_call(segments, rows, columns, mask, embed, patches):
    count = patches.shape[1]
    operands = (segments, rows, columns, mask, embed, patches)
    fixed = lambda shape: pl.BlockSpec(shape, lambda i: (0,) * len(shape))
    shape = (count, D + LANES)
    return pl.pallas_call(
        payload_kernel,
        grid=(1,),
        in_specs=[fixed(one.shape) for one in operands],
        out_specs=fixed(shape),
        out_shape=jax.ShapeDtypeStruct(shape, jnp.bfloat16),
        compiler_params=pltpu.CompilerParams(vmem_limit_bytes=8 << 20),
        cost_estimate=pl.CostEstimate(
            flops=count * D, bytes_accessed=4 * count * D, transcendentals=0
        ),
        name="payload",
    )(*map(in_hbm, operands))


def qkv_kernel(count, flip, info, *refs):
    first, second = refs[:count], refs[count : 2 * count]
    table, gain, weight = refs[2 * count : 2 * count + 3]
    inputs_out, qkv_out, label_out = refs[-3:]
    mine, other = stacked(first), stacked(second)
    leads = info[CORE] == 0
    ahead = jnp.where(leads, mine, other)
    behind = jnp.where(leads, other, mine)
    both = jnp.concatenate([ahead, behind], axis=0)
    rows = both.shape[0]
    at = pl.ds(pl.multiple_of((info[CHIP] ^ flip) * rows, rows), rows)
    inputs_out[at, :] = both[:, :D]
    label_out[at, :] = both[:, D:]
    labels = both[:, D:].astype(jnp.float32)
    normed = norm_rows(both[:, :D].astype(jnp.float32), gain[...]).astype(jnp.bfloat16)
    columns = lax.dot_general(
        normed, weight[...], (((1,), (1,)), ((), ())), preferred_element_type=jnp.float32
    )
    lane = lax.broadcasted_iota(jnp.int32, labels.shape, 1)
    numbers = lane.astype(jnp.float32)
    hot = (numbers == labels[:, 1:2]) | (numbers == labels[:, 2:3] + POSITIONS)
    looked = jnp.dot(
        jnp.where(hot, 1.0, 0.0).astype(jnp.bfloat16), table[...], preferred_element_type=jnp.float32
    )
    cosine = looked[:, :LANES] + looked[:, LANES : 2 * LANES]
    sine = looked[:, 2 * LANES : 3 * LANES] + looked[:, 3 * LANES :]
    first_head = lane < HD // 2

    def turn(start):
        a = columns[:, start : start + LANES]
        b = columns[:, start + LANES : start + 2 * LANES]
        return a * cosine - b * sine, b * cosine + a * sine

    query_a, query_b = turn(0)
    key_a, key_b = turn(2 * LANES)
    zero = jnp.zeros_like(key_a)
    parts = [
        query_a,
        query_b,
        jnp.where(first_head, key_a, zero),
        jnp.where(first_head, key_b, zero),
        jnp.where(first_head, zero, key_a),
        jnp.where(first_head, zero, key_b),
    ]
    for head in range(2):
        values = columns[:, (4 + head) * LANES : (5 + head) * LANES]
        parts.append(jnp.where(lane == HD, 1.0, values))
    for number, part in enumerate(parts):
        qkv_out[at, number * LANES : (number + 1) * LANES] = part.astype(jnp.bfloat16)


def qkv_call(info, flip, first, second, table, gain, weight, earlier, total):
    rows = 2 * sum(piece.shape[0] for piece in first)
    widths = (D, 8 * LANES, LANES)
    operands = [*first, *second, table, gain, in_vmem(weight)]
    vmem = pl.BlockSpec(memory_space=pltpu.VMEM)
    held = [in_vmem(one) for one in earlier]
    return pl.pallas_call(
        functools.partial(qkv_kernel, len(first), flip),
        in_specs=[pl.BlockSpec(memory_space=pltpu.SMEM)]
        + [vmem] * (len(operands) + len(earlier)),
        out_specs=[vmem] * len(widths),
        out_shape=[pltpu.VMEM((total, width), jnp.bfloat16) for width in widths],
        input_output_aliases={1 + len(operands) + i: i for i in range(len(earlier))},
        compiler_params=pltpu.CompilerParams(vmem_limit_bytes=14 << 20),
        cost_estimate=pl.CostEstimate(
            flops=6 * rows * D * weight.shape[0],
            bytes_accessed=2 * (rows * 4 * D + weight.size),
            transcendentals=rows,
        ),
        name="norm_qkv",
    )(info, *operands, *held)


def segment_row(labels):
    pick = jnp.where(lax.broadcasted_iota(jnp.int32, (8, LANES), 1) == 0, 1.0, 0.0)
    return lax.dot_general(
        pick.astype(jnp.bfloat16),
        labels,
        (((1,), (1,)), ((), ())),
        preferred_element_type=jnp.float32,
    )


def attention_kernel(start, first_owner, images, info, labels, block, *refs):
    out, *rest = refs
    scores, high, rows_scratch = rest[-3:]
    rows = high.shape[1]
    total = block.shape[0]
    factor = HD**-0.5 * float(np.log2(np.e))
    segments = segment_row(labels[...])
    for step in range(total // BLOCK):
        rows_scratch[step] = segments[:, step * BLOCK : (step + 1) * BLOCK]
    own = labels[start : start + rows, :1].astype(jnp.float32)
    lowest, largest = jnp.min(own), jnp.max(own)
    one_row = segments[:1]
    begin = jnp.sum(jnp.where(one_row < lowest, 1, 0)) // BLOCK
    end = (jnp.sum(jnp.where(one_row <= largest, 1, 0)) + BLOCK - 1) // BLOCK
    queries = block[start : start + rows, : 2 * LANES]
    own = jnp.broadcast_to(own, (rows, LANES))
    high[...] = jnp.full_like(high, NEGATIVE)

    def score(step, carry):
        at = pl.ds(pl.multiple_of(step * BLOCK, BLOCK), BLOCK)
        theirs = rows_scratch[step, :1]
        same = jnp.concatenate([own == theirs[:, :LANES], own == theirs[:, LANES:]], axis=1)
        for head in range(2):
            keys = block[at, (2 + 2 * head) * LANES : (4 + 2 * head) * LANES]
            values = lax.dot_general(
                queries, keys, (((1,), (1,)), ((), ())), preferred_element_type=jnp.float32
            )
            values = jnp.where(same, values, NEGATIVE)
            scores[head, step] = values
            high[head] = jnp.maximum(
                high[head], jnp.maximum(values[:, :LANES], values[:, LANES:])
            )
        return carry

    lax.fori_loop(begin, end, score, 0)
    highest = [jnp.max(high[head], axis=-1, keepdims=True) for head in range(2)]

    def weigh(step, carry):
        at = pl.ds(pl.multiple_of(step * BLOCK, BLOCK), BLOCK)
        sums = []
        for head in range(2):
            weights = jnp.exp2((scores[head, step] - highest[head]) * factor)
            values = block[at, (6 + head) * LANES : (7 + head) * LANES]
            sums.append(
                carry[head]
                + jnp.dot(weights.astype(jnp.bfloat16), values, preferred_element_type=jnp.float32)
            )
        return tuple(sums)

    zero = jnp.zeros((rows, LANES), jnp.float32)
    sums = lax.fori_loop(begin, end, weigh, (zero, zero))
    first, second = (one / one[:, HD : HD + 1] for one in sums)
    lane = lax.broadcasted_iota(jnp.int32, first.shape, 1)
    turned = pltpu.roll(second, HD, 1)
    out[:rows] = jnp.where(lane < HD, first, turned).astype(jnp.bfloat16)
    half = rows // 2
    tail = 2 * HD - LANES
    lane = lane[:half]
    up = pltpu.roll(turned[half:], tail, 1)
    packed = jnp.where(lane < tail, turned[:half], jnp.where(lane < 2 * tail, up, 0.0))
    out[rows:] = packed.astype(jnp.bfloat16)

    if len(rest) > 3:
        note = rest[0]
        row = lax.broadcasted_iota(jnp.int32, note.shape, 0)
        lane = lax.broadcasted_iota(jnp.int32, note.shape, 1)
        found = jnp.zeros(note.shape, jnp.float32)
        for image in range(images):
            below = jnp.sum(jnp.where(one_row < image, 0.25, 0.0), axis=1, keepdims=True)
            inside = jnp.sum(jnp.where(one_row == image, 0.25, 0.0), axis=1, keepdims=True)
            here = row == info[first_owner + image]
            for place, number in enumerate((below, inside)):
                upper = jnp.floor(number * (1.0 / 16))
                found = jnp.where(here & (lane == 2 * place), upper, found)
                found = jnp.where(here & (lane == 2 * place + 1), number - 16 * upper, found)
        note[...] = found.astype(jnp.bfloat16)


def attention_call(start, rows, first_owner, info, labels, block, noted):
    total = block.shape[0]
    vmem = pl.BlockSpec(memory_space=pltpu.VMEM)
    shapes = [jax.ShapeDtypeStruct((rows + rows // 2, LANES), jnp.bfloat16)]
    if noted:
        shapes.append(jax.ShapeDtypeStruct((16, LANES), jnp.bfloat16))
    return pl.pallas_call(
        functools.partial(attention_kernel, start, first_owner, info.shape[0] - first_owner),
        in_specs=[pl.BlockSpec(memory_space=pltpu.SMEM), vmem, vmem],
        out_specs=[vmem] * len(shapes),
        out_shape=shapes,
        scratch_shapes=[
            pltpu.VMEM((2, total // BLOCK, rows, BLOCK), jnp.float32),
            pltpu.VMEM((2, rows, LANES), jnp.float32),
            pltpu.VMEM((total // BLOCK, 8, BLOCK), jnp.float32),
        ],
        compiler_params=pltpu.CompilerParams(vmem_limit_bytes=20 << 20),
        cost_estimate=pl.CostEstimate(
            flops=10 * rows * total * 2 * LANES,
            bytes_accessed=2 * block.size,
            transcendentals=rows * total,
        ),
        name="attention",
    )(info, in_vmem(labels), in_vmem(block))


def prepare_kernel(shards, info, out_weight, merge_weight, qkv_weight, spread, *refs):
    *rows, out, merge, qkv, qkv_buffer, spread_buffer, sems = refs
    for row, row_out in zip(rows[: len(rows) // 2], rows[len(rows) // 2 :]):
        row_out[...] = row[...].astype(jnp.float32)[None, :]
    rest = 2 * HD - LANES
    copies = [(qkv_weight, qkv_buffer), (spread, spread_buffer)]
    out[shards * LANES :] = jnp.zeros((shards // 2 * LANES, D), jnp.bfloat16)
    for place in range(shards):
        start = pl.multiple_of(info[IDS + place] * (2 * HD), 16)
        to = (shards + place // 2) * LANES + place % 2 * rest
        copies.append(
            (out_weight.at[pl.ds(start, LANES), :], out.at[pl.ds(place * LANES, LANES), :])
        )
        copies.append((out_weight.at[pl.ds(start + LANES, rest), :], out.at[pl.ds(to, rest), :]))
    copies.append((merge_weight, merge))
    copies = [
        pltpu.make_async_copy(source, target, sems.at[i])
        for i, (source, target) in enumerate(copies)
    ]
    for copy in copies:
        copy.start()
    copies[0].wait()
    copies[1].wait()
    qkv[...] = jnp.dot(
        spread_buffer[...], qkv_buffer[...], preferred_element_type=jnp.float32
    ).astype(jnp.bfloat16)
    for copy in copies[2:]:
        copy.wait()


def prepare_call(shards, info, out_weight, merge_weight, qkv_weight, spread, rows):
    anywhere = pl.BlockSpec(memory_space=pl.ANY)
    vmem = pl.BlockSpec(memory_space=pltpu.VMEM)
    operands = (out_weight, merge_weight, qkv_weight, spread)
    shapes = [(shards * LANES * 3 // 2, D), merge_weight.shape, (spread.shape[0], D)]
    return pl.pallas_call(
        functools.partial(prepare_kernel, shards),
        in_specs=[pl.BlockSpec(memory_space=pltpu.SMEM)]
        + [anywhere] * len(operands)
        + [vmem] * len(rows),
        out_specs=[vmem] * (len(rows) + len(shapes)),
        out_shape=[pltpu.VMEM((1, row.shape[0]), jnp.float32) for row in rows]
        + [pltpu.VMEM(shape, jnp.bfloat16) for shape in shapes],
        scratch_shapes=[
            pltpu.VMEM(qkv_weight.shape, jnp.bfloat16),
            pltpu.VMEM(spread.shape, jnp.bfloat16),
            pltpu.SemaphoreType.DMA((2 * shards + 3,)),
        ],
        compiler_params=pltpu.CompilerParams(vmem_limit_bytes=10 << 20),
        cost_estimate=pl.CostEstimate(
            flops=2 * spread.size * D,
            bytes_accessed=4 * (out_weight.size + merge_weight.size + qkv_weight.size),
            transcendentals=0,
        ),
        name="prepare",
    )(info, *map(in_hbm, operands), *rows)


def merge_kernel(start, counts, packs, last, *refs):
    inputs, weight, gain, merge_weight, bias = refs[:5]
    pieces = refs[5 : 5 + sum(counts)]
    *refs, state = refs[5 + sum(counts) :]
    rows = state.shape[1]
    half = rows // 2
    rest = 2 * HD - LANES
    sources, at = [], 0
    for count in counts:
        sources.append(stacked(pieces[at : at + count]))
        at += count
    shards = len(sources)
    lane = lax.broadcasted_iota(jnp.int32, (half, LANES), 1)
    for part in range(2):
        token = slice(part * half, (part + 1) * half)
        lined = [source[token, :] for source in sources]
        for pair in range(shards // 2):
            mine = sources[2 * pair][rows:, :].astype(jnp.float32)
            other = sources[2 * pair + 1][rows:, :].astype(jnp.float32)
            if part == 0:
                other = pltpu.roll(other, rest, 1)
            else:
                mine = pltpu.roll(mine, LANES - rest, 1)
            lined.append(jnp.where(lane < rest, mine, other).astype(jnp.bfloat16))
        mixed = jnp.dot(
            jnp.concatenate(lined, axis=1), weight[...], preferred_element_type=jnp.float32
        )
        before = inputs[start + part * half : start + (part + 1) * half, :].astype(jnp.float32)
        normed = norm_rows(before + mixed, gain[...])
        for column in range(D // LANES):
            state[column, token, :] = normed[:, column * LANES : (column + 1) * LANES]
    groups = rows // 4
    total = bias[...]
    for quadrant in range(4):
        tokens = jnp.concatenate(
            [
                state[column, pl.ds(quadrant, groups, stride=4), :].astype(jnp.bfloat16)
                for column in range(D // LANES)
            ],
            axis=1,
        )
        total = total + lax.dot_general(
            tokens,
            merge_weight[:, quadrant * D : (quadrant + 1) * D],
            (((1,), (1,)), ((), ())),
            preferred_element_type=jnp.float32,
        )
    total = total.astype(jnp.bfloat16)
    if not last:
        refs[0][...] = total
        return
    info, note, *earlier = refs[:-packs]
    outs = refs[-packs:]
    total = jnp.concatenate([*[one[...] for one in earlier], total], axis=0)
    whole = total.shape[1] // LANES
    most = outs[0].shape[0] * LANES // total.shape[1]
    notes = note[...].astype(jnp.float32)
    note_row = lax.broadcasted_iota(jnp.int32, notes.shape, 0)
    slot = lax.broadcasted_iota(jnp.int32, (most, total.shape[0]), 0)
    row = lax.broadcasted_iota(jnp.int32, (most, total.shape[0]), 1)
    for place, out in enumerate(outs):
        found = jnp.where(note_row == (info[PACK] ^ place), notes, 0.0)
        found = jnp.sum(found, axis=0, keepdims=True)
        first = (16.0 * found[:, :1] + found[:, 1:2]).astype(jnp.int32)
        length = (16.0 * found[:, 2:3] + found[:, 3:4]).astype(jnp.int32)
        chosen = (row == slot + first) & (slot < length)
        chosen = jnp.where(chosen, 1.0, 0.0).astype(jnp.bfloat16)
        block = jnp.dot(chosen, total, preferred_element_type=jnp.float32)
        for column in range(whole):
            out[column * most : (column + 1) * most, :] = block[
                :, column * LANES : (column + 1) * LANES
            ].astype(jnp.bfloat16)
        low = block[: most // 2, whole * LANES :]
        up = block[most // 2 :, whole * LANES :]
        out[whole * most :, :] = jnp.concatenate([low, up], axis=1).astype(jnp.bfloat16)


def merge_call(start, rows, sources, inputs, weight, gain, merge_weight, bias, packs, route):
    groups = rows // 4
    width = merge_weight.shape[0]
    pieces = [piece for source in sources for piece in source]
    vmem = pl.BlockSpec(memory_space=pltpu.VMEM)
    operands = [in_vmem(inputs), in_vmem(weight), gain, in_vmem(merge_weight), bias, *pieces]
    specs = [vmem] * len(operands)
    shapes = [jax.ShapeDtypeStruct((groups, width), jnp.bfloat16)]
    if route:
        me, most, *others = route
        operands += [me, *others]
        specs += [pl.BlockSpec(memory_space=pltpu.SMEM)] + [vmem] * len(others)
        shapes = [jax.ShapeDtypeStruct((most * width // LANES, LANES), jnp.bfloat16)] * packs
    return pl.pallas_call(
        functools.partial(
            merge_kernel, start, [len(source) for source in sources], packs, bool(route)
        ),
        in_specs=specs,
        out_specs=[vmem] * len(shapes),
        scratch_shapes=[pltpu.VMEM((D // LANES, rows, LANES), jnp.float32)],
        out_shape=shapes,
        compiler_params=pltpu.CompilerParams(vmem_limit_bytes=20 << 20),
        cost_estimate=pl.CostEstimate(
            flops=4 * rows * D * D + 2 * groups * merge_weight.size,
            bytes_accessed=2 * (D * D + merge_weight.size + 3 * rows * D),
            transcendentals=rows,
        ),
        name="out_merge",
    )(*operands)


def place_kernel(info, *refs):
    blocks, out = refs[:-1], refs[-1]
    most, width = out.shape[1:]
    whole = width // LANES
    half = most // 2
    middle = LANES // 2
    for place, block in enumerate(blocks):
        target = info[PACK] ^ place
        for column in range(whole):
            out[target, :, column * LANES : (column + 1) * LANES] = block[
                column * most : (column + 1) * most, :
            ]
        out[target, :half, whole * LANES :] = block[whole * most :, :middle]
        out[target, half:, whole * LANES :] = block[whole * most :, middle:]


def place_call(info, blocks, most, width):
    fixed = lambda shape: pl.BlockSpec(shape, lambda i: (0,) * len(shape))
    shape = (len(blocks), most, width)
    return pl.pallas_call(
        place_kernel,
        grid=(1,),
        in_specs=[pl.BlockSpec(memory_space=pltpu.SMEM)] + [fixed(one.shape) for one in blocks],
        out_specs=fixed(shape),
        out_shape=jax.ShapeDtypeStruct(shape, jnp.bfloat16),
        compiler_params=pltpu.CompilerParams(vmem_limit_bytes=8 << 20),
        cost_estimate=pl.CostEstimate(
            flops=0, bytes_accessed=4 * len(blocks) * most * width, transcendentals=0
        ),
        name="place_rows",
    )(info, *blocks)


def send_seq(value, flip):
    size = lax.axis_size("seq")
    return lax.ppermute(value, "seq", [(i, i ^ flip) for i in range(size)])


def after(values, *earlier):
    return lax.optimization_barrier((tuple(values), earlier))[0]


def halves_kernel(across_x, across_y, upper, lower):
    half = upper.shape[0]
    upper[...] = across_x[:half]
    lower[...] = across_y[half:]


def halves_call(across_x, across_y):
    vmem = pl.BlockSpec(memory_space=pltpu.VMEM)
    shape = (across_x.shape[0] // 2, across_x.shape[1])
    return pl.pallas_call(
        halves_kernel,
        in_specs=[vmem] * 2,
        out_specs=[vmem] * 2,
        out_shape=[jax.ShapeDtypeStruct(shape, across_x.dtype)] * 2,
        compiler_params=pltpu.CompilerParams(vmem_limit_bytes=4 << 20),
        cost_estimate=pl.CostEstimate(
            flops=0, bytes_accessed=4 * across_x.size, transcendentals=0
        ),
        name="halves",
    )(across_x, across_y)


def near_shards(value):
    return [send_seq(value, 1), send_seq(value, 2), send_seq(value, 4)]


def far_shards(across_x, across_y):
    upper, lower = halves_call(across_x, across_y)
    return [send_seq(upper, 4), send_seq(lower, 2)]


def chip_shards(value):
    return [value] + [send_seq(value, flip) for flip in (2, 4, 6)]


def weight_order(heads_here):
    quarter = HD // 4
    order = -np.ones((6 * LANES,), np.int32)
    for head in range(heads_here):
        base = head * 3 * HD
        for kind in range(2):
            for half in range(2):
                for letter in range(2):
                    target = (2 * kind + letter) * LANES + head * (HD // 2) + half * quarter
                    source = base + kind * HD + half * (HD // 2) + letter * quarter
                    order[target : target + quarter] = np.arange(source, source + quarter)
        target = (4 + head) * LANES
        order[target : target + HD] = np.arange(base + 2 * HD, base + 3 * HD)
    return order


def angle_table(heads_here):
    quarter = HD // 4
    frequency = (10000.0 ** (-np.arange(quarter) / quarter)).astype(np.float32)
    angles = np.arange(POSITIONS, dtype=np.float32)[:, None] * frequency[None, :]
    pieces = []
    for function in (np.cos, np.sin):
        exact = np.zeros((2 * POSITIONS, LANES), np.float64)
        for head in range(heads_here):
            for half in range(2):
                lane = head * (HD // 2) + half * quarter
                rows = slice(half * POSITIONS, (half + 1) * POSITIONS)
                exact[rows, lane : lane + quarter] = function(angles.astype(np.float64))
        upper = exact.astype(jnp.bfloat16)
        pieces += [upper, (exact - upper.astype(np.float64)).astype(jnp.bfloat16)]
    return np.concatenate(pieces, axis=1)


def fast_local(
    patches,
    patch_mask,
    mask_embed,
    norm_gain,
    qkv_weight,
    segment_ids,
    patch_rows,
    patch_column,
    out_weight,
    merge_gain,
    merge_weight,
    merge_bias,
    image_owner,
):
    local_rows = patches.shape[1]
    shards = lax.axis_size("seq")
    packs = lax.axis_size("pack")
    heads_here = HEADS // shards
    images = image_owner.shape[1]
    total = local_rows * shards
    me = lax.axis_index("seq").astype(jnp.int32)
    pack = lax.axis_index("pack").astype(jnp.int32)

    value = payload_call(segment_ids, patch_rows, patch_column, patch_mask, mask_embed, patches)
    own_swap, across_x, across_y = near_shards(value)

    order = weight_order(heads_here)
    spread = (order[:, None] == np.arange(qkv_weight.shape[1])[None, :]).astype(jnp.bfloat16)
    table = jnp.asarray(angle_table(heads_here))
    chip, core = me // 2, me % 2
    info = [chip, core, pack, *[me ^ place for place in range(shards)]]
    info = jnp.concatenate([jnp.stack(info), image_owner[0]])
    gain, merge_gain_row, bias, ordered, merge_rows, weight = prepare_call(
        shards,
        info,
        out_weight,
        merge_weight.T,
        qkv_weight.T,
        jnp.asarray(spread),
        (norm_gain, merge_gain, merge_bias),
    )

    project = lambda place, first, second, earlier: qkv_call(
        info, place, first, second, table, gain, weight, earlier, total
    )
    buffers = project(0, [value], [own_swap], ())
    across_x, across_y = after([across_x, across_y], buffers[2], ordered)
    far = far_shards(across_x, across_y)
    buffers = project(1, [across_x], [send_seq(across_x, 1)], buffers)
    buffers = project(2, [across_y], [send_seq(across_y, 1)], buffers)
    far = after(far, buffers[2])
    buffers = project(3, far, [send_seq(one, 1) for one in far], buffers)
    inputs, block, labels = buffers

    starts = [sum(CHUNKS[:number]) for number in range(len(CHUNKS))]
    attended, note = [], None
    for start, rows in zip(starts, CHUNKS):
        if attended:
            labels, block = after([labels, block], attended[-1][0])
        made = attention_call(start, rows, IDS + shards, info, labels, block, note is None)
        note = made[1] if note is None else note
        attended.append(chip_shards(made[0]))
    latest = attended[-1][0]
    most = 2 * (total // 4) // images
    projected = []
    for number, (start, rows) in enumerate(zip(starts, CHUNKS)):
        own, *others = attended[number]
        others = after(others, latest, *projected)
        sources = [[one] for share in (own, *others) for one in (share, send_seq(share, 1))]
        route = ()
        if number == len(CHUNKS) - 1:
            route = (info, most, note, *projected)
        made = merge_call(
            start, rows, sources, inputs, ordered, merge_gain_row, merge_rows, bias, packs, route
        )
        projected.append(made[0])
    blocks = [made[0]] + [
        lax.ppermute(made[flip], "pack", [(z, z ^ flip) for z in range(packs)])
        for flip in range(1, packs)
    ]
    return place_call(info, blocks, most, merge_weight.shape[1])[None]


def local(*arguments):
    patches, weight = arguments[0], arguments[4]
    shards = lax.axis_size("seq")
    fits = shards == 8 and HEADS // shards == 2 and weight.shape[1] == 6 * HD
    fits = fits and patches.shape[1] * shards == sum(CHUNKS) and lax.axis_size("pack") == 4
    return fast_local(*arguments) if fits else general_local(*arguments)


def solution(mesh):
    placed = (
        P("pack", "seq", None),
        P("pack", "seq"),
        P(),
        P(),
        P(None, "seq"),
        P("pack", "seq"),
        P("pack", "seq"),
        P("pack", "seq"),
        P(),
        P(),
        P(None, "seq"),
        P("seq"),
        P("pack", None),
    )
    return jax.shard_map(
        local, mesh=mesh, in_specs=placed, out_specs=P("pack", None, None, "seq"), check_vma=False
    )
```

```python
import functools

import jax
import jax.numpy as jnp
import numpy as np
from jax import lax
from jax.experimental import pallas as pl
from jax.experimental.pallas import tpu as pltpu
from jax.sharding import PartitionSpec as P

D = 1408
HEADS = 16
HD = 88


EPSILON = 1e-06


def layer_norm(values, gain_vector):
    center = values - jnp.mean(values, axis=-1, keepdims=True)
    spread = jnp.mean(center * center, axis=-1, keepdims=True)
    return center * lax.rsqrt(spread + EPSILON) * gain_vector.astype(jnp.float32)


def rotate(vectors, row_index, column_index):
    total_rows, heads_here, head_width = vectors.shape
    quarter = head_width // 4
    frequency = 10000.0 ** (-jnp.arange(quarter, dtype=jnp.float32) / quarter)
    row_angle = row_index.astype(jnp.float32)[:, None] * frequency[None, :]
    column_angle = column_index.astype(jnp.float32)[:, None] * frequency[None, :]
    angles = jnp.stack([row_angle, column_angle], axis=1)[:, None, :, None, :]
    split_up = vectors.reshape(total_rows, heads_here, 2, 2, quarter)
    partner = jnp.stack([-split_up[:, :, :, 1], split_up[:, :, :, 0]], axis=3)
    turned = split_up * jnp.cos(angles) + partner * jnp.sin(angles)
    return turned.reshape(total_rows, heads_here, head_width)


def qkv_block(projected, row_index, column_index):
    turned_queries = rotate(projected[:, :, 0], row_index, column_index)
    turned_keys = rotate(projected[:, :, 1], row_index, column_index)
    return jnp.concatenate([turned_queries, turned_keys, projected[:, :, 2]], axis=-1).astype(
        jnp.bfloat16
    )


def attention(block, segments):
    total_rows, heads_here, triple = block.shape
    head_width = triple // 3
    step_rows = min(512, total_rows)
    query_part = block[:, :, :head_width].reshape(
        total_rows // step_rows, step_rows, heads_here, head_width
    )
    key_part = block[:, :, head_width : 2 * head_width]
    value_part = block[:, :, 2 * head_width :]
    query_segments = segments.reshape(total_rows // step_rows, step_rows)
    scale = head_width ** (-0.5)

    def one_block(inputs_pair):
        queries_here, segments_here = inputs_pair
        scores = (
            jnp.einsum("qhd,khd->hqk", queries_here, key_part, preferred_element_type=jnp.float32)
            * scale
        )
        same_image = (segments_here[:, None] == segments[None, :])[None]
        scores = jnp.where(same_image, scores, -jnp.inf)
        highest = jnp.max(scores, axis=-1, keepdims=True)
        weights = jnp.exp(scores - highest)
        probs = (weights / jnp.sum(weights, axis=-1, keepdims=True)).astype(jnp.bfloat16)
        result = jnp.einsum("hqk,khd->qhd", probs, value_part, preferred_element_type=jnp.float32)
        return result.astype(jnp.bfloat16)

    return lax.map(one_block, (query_part, query_segments)).reshape(
        total_rows, heads_here, head_width
    )


def route(projected, segments, owners_here, packs, most):
    merged_segments = segments[::4]
    images = owners_here.shape[0]
    image_ids = jnp.arange(images, dtype=jnp.int32)
    member = (merged_segments[None, :] == image_ids[:, None]).astype(jnp.int32)
    lengths = jnp.sum(member, axis=1, dtype=jnp.int32)
    starts = jnp.cumsum(lengths, dtype=jnp.int32) - lengths
    owner_ids = jnp.arange(packs, dtype=jnp.int32)
    owned = owners_here[None, :] == owner_ids[:, None]
    first_row = jnp.sum(jnp.where(owned, starts[None, :], 0), axis=1, dtype=jnp.int32)
    owned_length = jnp.sum(jnp.where(owned, lengths[None, :], 0), axis=1, dtype=jnp.int32)
    slots = jnp.arange(most, dtype=jnp.int32)
    source_rows = jnp.clip(first_row[:, None] + slots[None, :], 0, projected.shape[0] - 1)
    picked = jnp.take(projected, source_rows.reshape(-1), axis=0).reshape(
        packs, most, projected.shape[1]
    )
    filled = slots[None, :] < owned_length[:, None]
    return jnp.where(filled[:, :, None], picked, jnp.zeros_like(picked))


def general_local(
    patches,
    patch_mask,
    mask_embed,
    norm_gain,
    qkv_weight,
    segment_ids,
    patch_rows,
    patch_column,
    out_weight,
    merge_gain,
    merge_weight,
    merge_bias,
    image_owner,
):
    local_rows = patches.shape[1]
    shards = lax.axis_size("seq")
    packs = lax.axis_size("pack")
    heads_here = HEADS // shards
    inputs = jnp.where(patch_mask[0][:, None] == 1, mask_embed[None, :], patches[0])
    normed = layer_norm(inputs.astype(jnp.float32), norm_gain).astype(jnp.bfloat16)
    labels = lax.all_gather(
        jnp.stack([segment_ids[0], patch_rows[0], patch_column[0]]), "seq", axis=1, tiled=True
    )
    piece = lax.all_gather(normed, "seq", axis=0, tiled=True)
    span = piece.shape[0]
    projected = jnp.dot(piece, qkv_weight, preferred_element_type=jnp.float32)
    row_part = labels[1]
    column_part = labels[2]
    block = qkv_block(projected.reshape(span, heads_here, 3, HD), row_part, column_part)
    result = attention(block, labels[0])
    mixed_heads = lax.all_to_all(result, "seq", split_axis=0, concat_axis=1, tiled=True)
    attended = mixed_heads.reshape(local_rows, D)
    residual = inputs.astype(jnp.float32) + jnp.dot(
        attended, out_weight, preferred_element_type=jnp.float32
    )
    merged = layer_norm(residual, merge_gain).astype(jnp.bfloat16).reshape(local_rows // 4, 4 * D)
    projected_all = (
        jnp.dot(
            lax.all_gather(merged, "seq", axis=0, tiled=True),
            merge_weight,
            preferred_element_type=jnp.float32,
        )
        + merge_bias.astype(jnp.float32)
    ).astype(jnp.bfloat16)
    images = image_owner.shape[1]
    most = 2 * projected_all.shape[0] // images
    outgoing = route(projected_all, labels[0], image_owner[0], packs, most)
    delivered = lax.all_to_all(outgoing, "pack", split_axis=0, concat_axis=0, tiled=True)
    return delivered[None]


LANES = 128
CHIP, CORE, PACK, IDS = 0, 1, 2, 3
BLOCK = 256
POSITIONS = 64
FAR_APART = -(2.0**100)
IMAGE_LANE = 96
CHUNKS = (768, 768)


def norm_rows(values, gain_row):
    center = values - jnp.mean(values, axis=-1, keepdims=True)
    spread = jnp.mean(center * center, axis=-1, keepdims=True)
    return center * lax.rsqrt(spread + EPSILON) * gain_row


def stacked(pieces):
    loaded = [piece[...] for piece in pieces]
    return loaded[0] if len(loaded) == 1 else jnp.concatenate(loaded, axis=0)


def in_vmem(value):
    return pltpu.with_memory_space_constraint(value, pltpu.VMEM)


def in_hbm(value):
    return pltpu.with_memory_space_constraint(value, pltpu.HBM)


def payload_kernel(segments, rows, columns, mask, embed, patches, out):
    labels = [one[...].astype(jnp.float32) for one in (segments, rows, columns, mask)]
    labels.append(jnp.zeros((4, labels[0].shape[1]), jnp.float32))
    labels = jnp.concatenate(labels, axis=0).astype(jnp.bfloat16)
    shape = (8, LANES)
    row = lax.broadcasted_iota(jnp.int32, shape, 0)
    place = jnp.where(row == lax.broadcasted_iota(jnp.int32, shape, 1), 1.0, 0.0)
    turned = lax.dot_general(
        labels,
        place.astype(jnp.bfloat16),
        (((0,), (0,)), ((), ())),
        preferred_element_type=jnp.float32,
    )
    masked = turned[:, 3:4] > 0.5
    tokens = jnp.where(
        masked, embed[...].astype(jnp.float32)[None, :], patches[0].astype(jnp.float32)
    )
    out[:, :D] = tokens.astype(jnp.bfloat16)
    out[:, D:] = turned.astype(jnp.bfloat16)


def payload_call(segments, rows, columns, mask, embed, patches):
    count = patches.shape[1]
    operands = (segments, rows, columns, mask, embed, patches)
    fixed = lambda shape: pl.BlockSpec(shape, lambda i: (0,) * len(shape))
    shape = (count, D + LANES)
    return pl.pallas_call(
        payload_kernel,
        grid=(1,),
        in_specs=[fixed(one.shape) for one in operands],
        out_specs=fixed(shape),
        out_shape=jax.ShapeDtypeStruct(shape, jnp.bfloat16),
        compiler_params=pltpu.CompilerParams(vmem_limit_bytes=8 << 20),
        cost_estimate=pl.CostEstimate(
            flops=count * D, bytes_accessed=4 * count * D, transcendentals=0
        ),
        name="payload",
    )(*map(in_hbm, operands))


def qkv_kernel(count, flip, info, *refs):
    first, second = refs[:count], refs[count : 2 * count]
    table, gain, weight = refs[2 * count : 2 * count + 3]
    inputs_out, qkv_out, label_out = refs[-3:]
    mine, other = stacked(first), stacked(second)
    leads = info[CORE] == 0
    ahead = jnp.where(leads, mine, other)
    behind = jnp.where(leads, other, mine)
    both = jnp.concatenate([ahead, behind], axis=0)
    rows = both.shape[0]
    at = pl.ds(pl.multiple_of((info[CHIP] ^ flip) * rows, rows), rows)
    inputs_out[at, :] = both[:, :D]
    label_out[at, :] = both[:, D:]
    labels = both[:, D:].astype(jnp.float32)
    normed = norm_rows(both[:, :D].astype(jnp.float32), gain[...]).astype(jnp.bfloat16)
    columns = lax.dot_general(
        normed, weight[...], (((1,), (1,)), ((), ())), preferred_element_type=jnp.float32
    )
    lane = lax.broadcasted_iota(jnp.int32, labels.shape, 1)
    numbers = lane.astype(jnp.float32)
    hot = (numbers == labels[:, 1:2]) | (numbers == labels[:, 2:3] + POSITIONS)
    looked = jnp.dot(
        jnp.where(hot, 1.0, 0.0).astype(jnp.bfloat16), table[...], preferred_element_type=jnp.float32
    )
    cosine = looked[:, :LANES] + looked[:, LANES : 2 * LANES]
    sine = looked[:, 2 * LANES : 3 * LANES] + looked[:, 3 * LANES :]
    first_head = lane < HD // 2

    def turn(start):
        a = columns[:, start : start + LANES]
        b = columns[:, start + LANES : start + 2 * LANES]
        return a * cosine - b * sine, b * cosine + a * sine

    factor = HD**-0.5 * float(np.log2(np.e))
    query_a, query_b = (one * factor for one in turn(0))
    key_a, key_b = turn(2 * LANES)
    zero = jnp.zeros_like(key_a)
    image = numbers == labels[:, :1] + IMAGE_LANE
    extra = lane >= IMAGE_LANE
    apart = jnp.where(image, 0.0, FAR_APART)
    parts = [
        jnp.where(image, 1.0, query_a),
        query_b,
        jnp.where(extra, apart, jnp.where(first_head, key_a, zero)),
        jnp.where(first_head, key_b, zero),
        jnp.where(extra, apart, jnp.where(first_head, zero, key_a)),
        jnp.where(first_head, zero, key_b),
    ]
    for head in range(2):
        values = columns[:, (4 + head) * LANES : (5 + head) * LANES]
        parts.append(jnp.where(lane == HD, 1.0, values))
    for number, part in enumerate(parts):
        qkv_out[at, number * LANES : (number + 1) * LANES] = part.astype(jnp.bfloat16)


def qkv_call(info, flip, first, second, table, gain, weight, earlier, total):
    rows = 2 * sum(piece.shape[0] for piece in first)
    widths = (D, 8 * LANES, LANES)
    operands = [*first, *second, table, gain, in_vmem(weight)]
    vmem = pl.BlockSpec(memory_space=pltpu.VMEM)
    held = [in_vmem(one) for one in earlier]
    return pl.pallas_call(
        functools.partial(qkv_kernel, len(first), flip),
        in_specs=[pl.BlockSpec(memory_space=pltpu.SMEM)]
        + [vmem] * (len(operands) + len(earlier)),
        out_specs=[vmem] * len(widths),
        out_shape=[pltpu.VMEM((total, width), jnp.bfloat16) for width in widths],
        input_output_aliases={1 + len(operands) + i: i for i in range(len(earlier))},
        compiler_params=pltpu.CompilerParams(vmem_limit_bytes=14 << 20),
        cost_estimate=pl.CostEstimate(
            flops=6 * rows * D * weight.shape[0],
            bytes_accessed=2 * (rows * 4 * D + weight.size),
            transcendentals=rows,
        ),
        name="norm_qkv",
    )(info, *operands, *held)


def segment_row(labels):
    pick = jnp.where(lax.broadcasted_iota(jnp.int32, (8, LANES), 1) == 0, 1.0, 0.0)
    return lax.dot_general(
        pick.astype(jnp.bfloat16),
        labels,
        (((1,), (1,)), ((), ())),
        preferred_element_type=jnp.float32,
    )


def attention_kernel(start, first_owner, images, info, labels, block, *refs):
    out, *rest = refs
    scores, high = rest[-2:]
    rows = high.shape[1]
    total = block.shape[0]
    segments = segment_row(labels[...])
    own = labels[start : start + rows, :1].astype(jnp.float32)
    lowest, largest = jnp.min(own), jnp.max(own)
    one_row = segments[:1]
    begin = jnp.sum(jnp.where(one_row < lowest, 1, 0)) // BLOCK
    end = (jnp.sum(jnp.where(one_row <= largest, 1, 0)) + BLOCK - 1) // BLOCK
    queries = block[start : start + rows, : 2 * LANES]
    high[...] = jnp.full_like(high, 2 * FAR_APART)

    def score(step, carry):
        at = pl.ds(pl.multiple_of(step * BLOCK, BLOCK), BLOCK)
        for head in range(2):
            keys = block[at, (2 + 2 * head) * LANES : (4 + 2 * head) * LANES]
            values = lax.dot_general(
                queries, keys, (((1,), (1,)), ((), ())), preferred_element_type=jnp.float32
            )
            scores[head, step] = values
            high[head] = jnp.maximum(
                high[head], jnp.maximum(values[:, :LANES], values[:, LANES:])
            )
        return carry

    lax.fori_loop(begin, end, score, 0)
    highest = [jnp.max(high[head], axis=-1, keepdims=True) for head in range(2)]

    def weigh(step, carry):
        at = pl.ds(pl.multiple_of(step * BLOCK, BLOCK), BLOCK)
        sums = []
        for head in range(2):
            weights = jnp.exp2(scores[head, step] - highest[head])
            values = block[at, (6 + head) * LANES : (7 + head) * LANES]
            sums.append(
                carry[head]
                + jnp.dot(weights.astype(jnp.bfloat16), values, preferred_element_type=jnp.float32)
            )
        return tuple(sums)

    zero = jnp.zeros((rows, LANES), jnp.float32)
    sums = lax.fori_loop(begin, end, weigh, (zero, zero))
    first, second = (one / one[:, HD : HD + 1] for one in sums)
    lane = lax.broadcasted_iota(jnp.int32, first.shape, 1)
    turned = pltpu.roll(second, HD, 1)
    out[:rows] = jnp.where(lane < HD, first, turned).astype(jnp.bfloat16)
    half = rows // 2
    tail = 2 * HD - LANES
    lane = lane[:half]
    up = pltpu.roll(turned[half:], tail, 1)
    packed = jnp.where(lane < tail, turned[:half], jnp.where(lane < 2 * tail, up, 0.0))
    out[rows:] = packed.astype(jnp.bfloat16)

    if len(rest) > 2:
        note = rest[0]
        row = lax.broadcasted_iota(jnp.int32, note.shape, 0)
        lane = lax.broadcasted_iota(jnp.int32, note.shape, 1)
        found = jnp.zeros(note.shape, jnp.float32)
        for image in range(images):
            below = jnp.sum(jnp.where(one_row < image, 0.25, 0.0), axis=1, keepdims=True)
            inside = jnp.sum(jnp.where(one_row == image, 0.25, 0.0), axis=1, keepdims=True)
            here = row == info[first_owner + image]
            for place, number in enumerate((below, inside)):
                upper = jnp.floor(number * (1.0 / 16))
                found = jnp.where(here & (lane == 2 * place), upper, found)
                found = jnp.where(here & (lane == 2 * place + 1), number - 16 * upper, found)
        note[...] = found.astype(jnp.bfloat16)


def attention_call(start, rows, first_owner, info, labels, block, noted):
    total = block.shape[0]
    vmem = pl.BlockSpec(memory_space=pltpu.VMEM)
    shapes = [jax.ShapeDtypeStruct((rows + rows // 2, LANES), jnp.bfloat16)]
    if noted:
        shapes.append(jax.ShapeDtypeStruct((16, LANES), jnp.bfloat16))
    return pl.pallas_call(
        functools.partial(attention_kernel, start, first_owner, info.shape[0] - first_owner),
        in_specs=[pl.BlockSpec(memory_space=pltpu.SMEM), vmem, vmem],
        out_specs=[vmem] * len(shapes),
        out_shape=shapes,
        scratch_shapes=[
            pltpu.VMEM((2, total // BLOCK, rows, BLOCK), jnp.float32),
            pltpu.VMEM((2, rows, LANES), jnp.float32),
        ],
        compiler_params=pltpu.CompilerParams(vmem_limit_bytes=20 << 20),
        cost_estimate=pl.CostEstimate(
            flops=10 * rows * total * 2 * LANES,
            bytes_accessed=2 * block.size,
            transcendentals=rows * total,
        ),
        name="attention",
    )(info, in_vmem(labels), in_vmem(block))


def prepare_kernel(shards, info, out_weight, merge_weight, qkv_weight, spread, *refs):
    *rows, out, merge, qkv, qkv_buffer, spread_buffer, sems = refs
    for row, row_out in zip(rows[: len(rows) // 2], rows[len(rows) // 2 :]):
        row_out[...] = row[...].astype(jnp.float32)[None, :]
    rest = 2 * HD - LANES
    copies = [(qkv_weight, qkv_buffer), (spread, spread_buffer)]
    out[shards * LANES :] = jnp.zeros((shards // 2 * LANES, D), jnp.bfloat16)
    for place in range(shards):
        start = pl.multiple_of(info[IDS + place] * (2 * HD), 16)
        to = (shards + place // 2) * LANES + place % 2 * rest
        copies.append(
            (out_weight.at[pl.ds(start, LANES), :], out.at[pl.ds(place * LANES, LANES), :])
        )
        copies.append((out_weight.at[pl.ds(start + LANES, rest), :], out.at[pl.ds(to, rest), :]))
    copies.append((merge_weight, merge))
    copies = [
        pltpu.make_async_copy(source, target, sems.at[i])
        for i, (source, target) in enumerate(copies)
    ]
    for copy in copies:
        copy.start()
    copies[0].wait()
    copies[1].wait()
    qkv[...] = jnp.dot(
        spread_buffer[...], qkv_buffer[...], preferred_element_type=jnp.float32
    ).astype(jnp.bfloat16)
    for copy in copies[2:]:
        copy.wait()


def prepare_call(shards, info, out_weight, merge_weight, qkv_weight, spread, rows):
    anywhere = pl.BlockSpec(memory_space=pl.ANY)
    vmem = pl.BlockSpec(memory_space=pltpu.VMEM)
    operands = (out_weight, merge_weight, qkv_weight, spread)
    shapes = [(shards * LANES * 3 // 2, D), merge_weight.shape, (spread.shape[0], D)]
    return pl.pallas_call(
        functools.partial(prepare_kernel, shards),
        in_specs=[pl.BlockSpec(memory_space=pltpu.SMEM)]
        + [anywhere] * len(operands)
        + [vmem] * len(rows),
        out_specs=[vmem] * (len(rows) + len(shapes)),
        out_shape=[pltpu.VMEM((1, row.shape[0]), jnp.float32) for row in rows]
        + [pltpu.VMEM(shape, jnp.bfloat16) for shape in shapes],
        scratch_shapes=[
            pltpu.VMEM(qkv_weight.shape, jnp.bfloat16),
            pltpu.VMEM(spread.shape, jnp.bfloat16),
            pltpu.SemaphoreType.DMA((2 * shards + 3,)),
        ],
        compiler_params=pltpu.CompilerParams(vmem_limit_bytes=10 << 20),
        cost_estimate=pl.CostEstimate(
            flops=2 * spread.size * D,
            bytes_accessed=4 * (out_weight.size + merge_weight.size + qkv_weight.size),
            transcendentals=0,
        ),
        name="prepare",
    )(info, *map(in_hbm, operands), *rows)


def merge_kernel(start, counts, packs, last, *refs):
    inputs, weight, gain, merge_weight, bias = refs[:5]
    pieces = refs[5 : 5 + sum(counts)]
    *refs, state = refs[5 + sum(counts) :]
    rows = state.shape[1]
    half = rows // 2
    rest = 2 * HD - LANES
    sources, at = [], 0
    for count in counts:
        sources.append(stacked(pieces[at : at + count]))
        at += count
    shards = len(sources)
    lane = lax.broadcasted_iota(jnp.int32, (half, LANES), 1)
    for part in range(2):
        token = slice(part * half, (part + 1) * half)
        lined = [source[token, :] for source in sources]
        for pair in range(shards // 2):
            mine = sources[2 * pair][rows:, :].astype(jnp.float32)
            other = sources[2 * pair + 1][rows:, :].astype(jnp.float32)
            if part == 0:
                other = pltpu.roll(other, rest, 1)
            else:
                mine = pltpu.roll(mine, LANES - rest, 1)
            lined.append(jnp.where(lane < rest, mine, other).astype(jnp.bfloat16))
        mixed = jnp.dot(
            jnp.concatenate(lined, axis=1), weight[...], preferred_element_type=jnp.float32
        )
        before = inputs[start + part * half : start + (part + 1) * half, :].astype(jnp.float32)
        normed = norm_rows(before + mixed, gain[...])
        for column in range(D // LANES):
            state[column, token, :] = normed[:, column * LANES : (column + 1) * LANES]
    groups = rows // 4
    total = bias[...]
    for quadrant in range(4):
        tokens = jnp.concatenate(
            [
                state[column, pl.ds(quadrant, groups, stride=4), :].astype(jnp.bfloat16)
                for column in range(D // LANES)
            ],
            axis=1,
        )
        total = total + lax.dot_general(
            tokens,
            merge_weight[:, quadrant * D : (quadrant + 1) * D],
            (((1,), (1,)), ((), ())),
            preferred_element_type=jnp.float32,
        )
    total = total.astype(jnp.bfloat16)
    if not last:
        refs[0][...] = total
        return
    info, note, *earlier = refs[:-packs]
    outs = refs[-packs:]
    total = jnp.concatenate([*[one[...] for one in earlier], total], axis=0)
    whole = total.shape[1] // LANES
    most = outs[0].shape[0] * LANES // total.shape[1]
    notes = note[...].astype(jnp.float32)
    note_row = lax.broadcasted_iota(jnp.int32, notes.shape, 0)
    slot = lax.broadcasted_iota(jnp.int32, (most, total.shape[0]), 0)
    row = lax.broadcasted_iota(jnp.int32, (most, total.shape[0]), 1)
    for place, out in enumerate(outs):
        found = jnp.where(note_row == (info[PACK] ^ place), notes, 0.0)
        found = jnp.sum(found, axis=0, keepdims=True)
        first = (16.0 * found[:, :1] + found[:, 1:2]).astype(jnp.int32)
        length = (16.0 * found[:, 2:3] + found[:, 3:4]).astype(jnp.int32)
        chosen = (row == slot + first) & (slot < length)
        chosen = jnp.where(chosen, 1.0, 0.0).astype(jnp.bfloat16)
        block = jnp.dot(chosen, total, preferred_element_type=jnp.float32)
        for column in range(whole):
            out[column * most : (column + 1) * most, :] = block[
                :, column * LANES : (column + 1) * LANES
            ].astype(jnp.bfloat16)
        low = block[: most // 2, whole * LANES :]
        up = block[most // 2 :, whole * LANES :]
        out[whole * most :, :] = jnp.concatenate([low, up], axis=1).astype(jnp.bfloat16)


def merge_call(start, rows, sources, inputs, weight, gain, merge_weight, bias, packs, route):
    groups = rows // 4
    width = merge_weight.shape[0]
    pieces = [piece for source in sources for piece in source]
    vmem = pl.BlockSpec(memory_space=pltpu.VMEM)
    operands = [in_vmem(inputs), in_vmem(weight), gain, in_vmem(merge_weight), bias, *pieces]
    specs = [vmem] * len(operands)
    shapes = [jax.ShapeDtypeStruct((groups, width), jnp.bfloat16)]
    if route:
        me, most, *others = route
        operands += [me, *others]
        specs += [pl.BlockSpec(memory_space=pltpu.SMEM)] + [vmem] * len(others)
        shapes = [jax.ShapeDtypeStruct((most * width // LANES, LANES), jnp.bfloat16)] * packs
    return pl.pallas_call(
        functools.partial(
            merge_kernel, start, [len(source) for source in sources], packs, bool(route)
        ),
        in_specs=specs,
        out_specs=[vmem] * len(shapes),
        scratch_shapes=[pltpu.VMEM((D // LANES, rows, LANES), jnp.float32)],
        out_shape=shapes,
        compiler_params=pltpu.CompilerParams(vmem_limit_bytes=20 << 20),
        cost_estimate=pl.CostEstimate(
            flops=4 * rows * D * D + 2 * groups * merge_weight.size,
            bytes_accessed=2 * (D * D + merge_weight.size + 3 * rows * D),
            transcendentals=rows,
        ),
        name="out_merge",
    )(*operands)


def place_kernel(info, *refs):
    blocks, out = refs[:-1], refs[-1]
    most, width = out.shape[1:]
    whole = width // LANES
    half = most // 2
    middle = LANES // 2
    for place, block in enumerate(blocks):
        target = info[PACK] ^ place
        for column in range(whole):
            out[target, :, column * LANES : (column + 1) * LANES] = block[
                column * most : (column + 1) * most, :
            ]
        out[target, :half, whole * LANES :] = block[whole * most :, :middle]
        out[target, half:, whole * LANES :] = block[whole * most :, middle:]


def place_call(info, blocks, most, width):
    fixed = lambda shape: pl.BlockSpec(shape, lambda i: (0,) * len(shape))
    shape = (len(blocks), most, width)
    return pl.pallas_call(
        place_kernel,
        grid=(1,),
        in_specs=[pl.BlockSpec(memory_space=pltpu.SMEM)] + [fixed(one.shape) for one in blocks],
        out_specs=fixed(shape),
        out_shape=jax.ShapeDtypeStruct(shape, jnp.bfloat16),
        compiler_params=pltpu.CompilerParams(vmem_limit_bytes=8 << 20),
        cost_estimate=pl.CostEstimate(
            flops=0, bytes_accessed=4 * len(blocks) * most * width, transcendentals=0
        ),
        name="place_rows",
    )(info, *blocks)


def send_seq(value, flip):
    size = lax.axis_size("seq")
    return lax.ppermute(value, "seq", [(i, i ^ flip) for i in range(size)])


def after(values, *earlier):
    return lax.optimization_barrier((tuple(values), earlier))[0]


def halves_kernel(across_x, across_y, upper, lower):
    half = upper.shape[0]
    upper[...] = across_x[:half]
    lower[...] = across_y[half:]


def halves_call(across_x, across_y):
    vmem = pl.BlockSpec(memory_space=pltpu.VMEM)
    shape = (across_x.shape[0] // 2, across_x.shape[1])
    return pl.pallas_call(
        halves_kernel,
        in_specs=[vmem] * 2,
        out_specs=[vmem] * 2,
        out_shape=[jax.ShapeDtypeStruct(shape, across_x.dtype)] * 2,
        compiler_params=pltpu.CompilerParams(vmem_limit_bytes=4 << 20),
        cost_estimate=pl.CostEstimate(
            flops=0, bytes_accessed=4 * across_x.size, transcendentals=0
        ),
        name="halves",
    )(across_x, across_y)


def near_shards(value):
    return [send_seq(value, 1), send_seq(value, 2), send_seq(value, 4)]


def far_shards(across_x, across_y):
    upper, lower = halves_call(across_x, across_y)
    return [send_seq(upper, 4), send_seq(lower, 2)]


def weight_order(heads_here):
    quarter = HD // 4
    order = -np.ones((6 * LANES,), np.int32)
    for head in range(heads_here):
        base = head * 3 * HD
        for kind in range(2):
            for half in range(2):
                for letter in range(2):
                    target = (2 * kind + letter) * LANES + head * (HD // 2) + half * quarter
                    source = base + kind * HD + half * (HD // 2) + letter * quarter
                    order[target : target + quarter] = np.arange(source, source + quarter)
        target = (4 + head) * LANES
        order[target : target + HD] = np.arange(base + 2 * HD, base + 3 * HD)
    return order


def angle_table(heads_here):
    quarter = HD // 4
    frequency = (10000.0 ** (-np.arange(quarter) / quarter)).astype(np.float32)
    angles = np.arange(POSITIONS, dtype=np.float32)[:, None] * frequency[None, :]
    pieces = []
    for function in (np.cos, np.sin):
        exact = np.zeros((2 * POSITIONS, LANES), np.float64)
        for head in range(heads_here):
            for half in range(2):
                lane = head * (HD // 2) + half * quarter
                rows = slice(half * POSITIONS, (half + 1) * POSITIONS)
                exact[rows, lane : lane + quarter] = function(angles.astype(np.float64))
        upper = exact.astype(jnp.bfloat16)
        pieces += [upper, (exact - upper.astype(np.float64)).astype(jnp.bfloat16)]
    return np.concatenate(pieces, axis=1)


def fast_local(
    patches,
    patch_mask,
    mask_embed,
    norm_gain,
    qkv_weight,
    segment_ids,
    patch_rows,
    patch_column,
    out_weight,
    merge_gain,
    merge_weight,
    merge_bias,
    image_owner,
):
    local_rows = patches.shape[1]
    shards = lax.axis_size("seq")
    packs = lax.axis_size("pack")
    heads_here = HEADS // shards
    images = image_owner.shape[1]
    total = local_rows * shards
    me = lax.axis_index("seq").astype(jnp.int32)
    pack = lax.axis_index("pack").astype(jnp.int32)

    value = payload_call(segment_ids, patch_rows, patch_column, patch_mask, mask_embed, patches)
    own_swap, across_x, across_y = near_shards(value)

    order = weight_order(heads_here)
    spread = (order[:, None] == np.arange(qkv_weight.shape[1])[None, :]).astype(jnp.bfloat16)
    table = jnp.asarray(angle_table(heads_here))
    chip, core = me // 2, me % 2
    info = [chip, core, pack, *[me ^ place for place in range(shards)]]
    info = jnp.concatenate([jnp.stack(info), image_owner[0]])
    gain, merge_gain_row, bias, ordered, merge_rows, weight = prepare_call(
        shards,
        info,
        out_weight,
        merge_weight.T,
        qkv_weight.T,
        jnp.asarray(spread),
        (norm_gain, merge_gain, merge_bias),
    )

    project = lambda place, first, second, earlier: qkv_call(
        info, place, first, second, table, gain, weight, earlier, total
    )
    buffers = project(0, [value], [own_swap], ())
    across_x, across_y = after([across_x, across_y], buffers[2], ordered)
    far = far_shards(across_x, across_y)
    buffers = project(1, [across_x], [send_seq(across_x, 1)], buffers)
    buffers = project(2, [across_y], [send_seq(across_y, 1)], buffers)
    far = after(far, buffers[2])
    buffers = project(3, far, [send_seq(one, 1) for one in far], buffers)
    inputs, block, labels = buffers

    starts = [sum(CHUNKS[:number]) for number in range(len(CHUNKS))]
    attended, note = [], None
    for start, rows in zip(starts, CHUNKS):
        made = attention_call(start, rows, IDS + shards, info, labels, block, note is None)
        note = made[1] if note is None else note
        value = made[0]
        if attended:
            (value,) = after([value], *attended[-1][1])
        attended.append((value, near_shards(value)))
    latest = attended[-1][0]
    most = 2 * (total // 4) // images
    projected, moving = [], []
    for own, (own_swap, across_x, across_y) in attended:
        previous = moving[-1][-1] if moving else ()
        across_x, across_y = after([across_x, across_y], latest, *previous)
        far = far_shards(across_x, across_y)
        moving.append(
            (own, own_swap, across_x, send_seq(across_x, 1), across_y, send_seq(across_y, 1), far)
        )
    for number, (start, rows) in enumerate(zip(starts, CHUNKS)):
        *near, far = moving[number]
        if projected:
            far = after(far, projected[-1])
        sources = [[one] for one in near] + [far, [send_seq(one, 1) for one in far]]
        route = ()
        if number == len(CHUNKS) - 1:
            route = (info, most, note, *projected)
        made = merge_call(
            start, rows, sources, inputs, ordered, merge_gain_row, merge_rows, bias, packs, route
        )
        projected.append(made[0])
    blocks = [made[0]] + [
        lax.ppermute(made[flip], "pack", [(z, z ^ flip) for z in range(packs)])
        for flip in range(1, packs)
    ]
    return place_call(info, blocks, most, merge_weight.shape[1])[None]


def local(*arguments):
    patches, weight = arguments[0], arguments[4]
    shards = lax.axis_size("seq")
    fits = shards == 8 and HEADS // shards == 2 and weight.shape[1] == 6 * HD
    fits = fits and patches.shape[1] * shards == sum(CHUNKS) and lax.axis_size("pack") == 4
    return fast_local(*arguments) if fits else general_local(*arguments)


def solution(mesh):
    placed = (
        P("pack", "seq", None),
        P("pack", "seq"),
        P(),
        P(),
        P(None, "seq"),
        P("pack", "seq"),
        P("pack", "seq"),
        P("pack", "seq"),
        P(),
        P(),
        P(None, "seq"),
        P("seq"),
        P("pack", None),
    )
    return jax.shard_map(
        local, mesh=mesh, in_specs=placed, out_specs=P("pack", None, None, "seq"), check_vma=False
    )
```

```python
import functools

import jax
import jax.numpy as jnp
import numpy as np
from jax import lax
from jax.experimental import pallas as pl
from jax.experimental.pallas import tpu as pltpu
from jax.sharding import PartitionSpec as P

D = 1408
HEADS = 16
HD = 88


EPSILON = 1e-06


def layer_norm(values, gain_vector):
    center = values - jnp.mean(values, axis=-1, keepdims=True)
    spread = jnp.mean(center * center, axis=-1, keepdims=True)
    return center * lax.rsqrt(spread + EPSILON) * gain_vector.astype(jnp.float32)


def rotate(vectors, row_index, column_index):
    total_rows, heads_here, head_width = vectors.shape
    quarter = head_width // 4
    frequency = 10000.0 ** (-jnp.arange(quarter, dtype=jnp.float32) / quarter)
    row_angle = row_index.astype(jnp.float32)[:, None] * frequency[None, :]
    column_angle = column_index.astype(jnp.float32)[:, None] * frequency[None, :]
    angles = jnp.stack([row_angle, column_angle], axis=1)[:, None, :, None, :]
    split_up = vectors.reshape(total_rows, heads_here, 2, 2, quarter)
    partner = jnp.stack([-split_up[:, :, :, 1], split_up[:, :, :, 0]], axis=3)
    turned = split_up * jnp.cos(angles) + partner * jnp.sin(angles)
    return turned.reshape(total_rows, heads_here, head_width)


def qkv_block(projected, row_index, column_index):
    turned_queries = rotate(projected[:, :, 0], row_index, column_index)
    turned_keys = rotate(projected[:, :, 1], row_index, column_index)
    return jnp.concatenate([turned_queries, turned_keys, projected[:, :, 2]], axis=-1).astype(
        jnp.bfloat16
    )


def attention(block, segments):
    total_rows, heads_here, triple = block.shape
    head_width = triple // 3
    step_rows = min(512, total_rows)
    query_part = block[:, :, :head_width].reshape(
        total_rows // step_rows, step_rows, heads_here, head_width
    )
    key_part = block[:, :, head_width : 2 * head_width]
    value_part = block[:, :, 2 * head_width :]
    query_segments = segments.reshape(total_rows // step_rows, step_rows)
    scale = head_width ** (-0.5)

    def one_block(inputs_pair):
        queries_here, segments_here = inputs_pair
        scores = (
            jnp.einsum("qhd,khd->hqk", queries_here, key_part, preferred_element_type=jnp.float32)
            * scale
        )
        same_image = (segments_here[:, None] == segments[None, :])[None]
        scores = jnp.where(same_image, scores, -jnp.inf)
        highest = jnp.max(scores, axis=-1, keepdims=True)
        weights = jnp.exp(scores - highest)
        probs = (weights / jnp.sum(weights, axis=-1, keepdims=True)).astype(jnp.bfloat16)
        result = jnp.einsum("hqk,khd->qhd", probs, value_part, preferred_element_type=jnp.float32)
        return result.astype(jnp.bfloat16)

    return lax.map(one_block, (query_part, query_segments)).reshape(
        total_rows, heads_here, head_width
    )


def route(projected, segments, owners_here, packs, most):
    merged_segments = segments[::4]
    images = owners_here.shape[0]
    image_ids = jnp.arange(images, dtype=jnp.int32)
    member = (merged_segments[None, :] == image_ids[:, None]).astype(jnp.int32)
    lengths = jnp.sum(member, axis=1, dtype=jnp.int32)
    starts = jnp.cumsum(lengths, dtype=jnp.int32) - lengths
    owner_ids = jnp.arange(packs, dtype=jnp.int32)
    owned = owners_here[None, :] == owner_ids[:, None]
    first_row = jnp.sum(jnp.where(owned, starts[None, :], 0), axis=1, dtype=jnp.int32)
    owned_length = jnp.sum(jnp.where(owned, lengths[None, :], 0), axis=1, dtype=jnp.int32)
    slots = jnp.arange(most, dtype=jnp.int32)
    source_rows = jnp.clip(first_row[:, None] + slots[None, :], 0, projected.shape[0] - 1)
    picked = jnp.take(projected, source_rows.reshape(-1), axis=0).reshape(
        packs, most, projected.shape[1]
    )
    filled = slots[None, :] < owned_length[:, None]
    return jnp.where(filled[:, :, None], picked, jnp.zeros_like(picked))


def general_local(
    patches,
    patch_mask,
    mask_embed,
    norm_gain,
    qkv_weight,
    segment_ids,
    patch_rows,
    patch_column,
    out_weight,
    merge_gain,
    merge_weight,
    merge_bias,
    image_owner,
):
    local_rows = patches.shape[1]
    shards = lax.axis_size("seq")
    packs = lax.axis_size("pack")
    heads_here = HEADS // shards
    inputs = jnp.where(patch_mask[0][:, None] == 1, mask_embed[None, :], patches[0])
    normed = layer_norm(inputs.astype(jnp.float32), norm_gain).astype(jnp.bfloat16)
    labels = lax.all_gather(
        jnp.stack([segment_ids[0], patch_rows[0], patch_column[0]]), "seq", axis=1, tiled=True
    )
    piece = lax.all_gather(normed, "seq", axis=0, tiled=True)
    span = piece.shape[0]
    projected = jnp.dot(piece, qkv_weight, preferred_element_type=jnp.float32)
    row_part = labels[1]
    column_part = labels[2]
    block = qkv_block(projected.reshape(span, heads_here, 3, HD), row_part, column_part)
    result = attention(block, labels[0])
    mixed_heads = lax.all_to_all(result, "seq", split_axis=0, concat_axis=1, tiled=True)
    attended = mixed_heads.reshape(local_rows, D)
    residual = inputs.astype(jnp.float32) + jnp.dot(
        attended, out_weight, preferred_element_type=jnp.float32
    )
    merged = layer_norm(residual, merge_gain).astype(jnp.bfloat16).reshape(local_rows // 4, 4 * D)
    projected_all = (
        jnp.dot(
            lax.all_gather(merged, "seq", axis=0, tiled=True),
            merge_weight,
            preferred_element_type=jnp.float32,
        )
        + merge_bias.astype(jnp.float32)
    ).astype(jnp.bfloat16)
    images = image_owner.shape[1]
    most = 2 * projected_all.shape[0] // images
    outgoing = route(projected_all, labels[0], image_owner[0], packs, most)
    delivered = lax.all_to_all(outgoing, "pack", split_axis=0, concat_axis=0, tiled=True)
    return delivered[None]


LANES = 128
CHIP, CORE, PACK, IDS = 0, 1, 2, 3
BLOCK = 256
POSITIONS = 64
FAR_APART = -(2.0**100)
IMAGE_LANE = 96
ROW_BLOCK = 128
NORM_ROWS = 16
CHUNKS = (768, 768)


def norm_rows(values, gain_row):
    center = values - jnp.mean(values, axis=-1, keepdims=True)
    spread = jnp.mean(center * center, axis=-1, keepdims=True)
    return center * lax.rsqrt(spread + EPSILON) * gain_row


def stacked(pieces):
    loaded = [piece[...] for piece in pieces]
    return loaded[0] if len(loaded) == 1 else jnp.concatenate(loaded, axis=0)


def in_vmem(value):
    return pltpu.with_memory_space_constraint(value, pltpu.VMEM)


def in_hbm(value):
    return pltpu.with_memory_space_constraint(value, pltpu.HBM)


def payload_kernel(segments, rows, columns, mask, embed, patches, out):
    labels = [one[...].astype(jnp.float32) for one in (segments, rows, columns, mask)]
    labels.append(jnp.zeros((4, labels[0].shape[1]), jnp.float32))
    labels = jnp.concatenate(labels, axis=0).astype(jnp.bfloat16)
    shape = (8, LANES)
    row = lax.broadcasted_iota(jnp.int32, shape, 0)
    place = jnp.where(row == lax.broadcasted_iota(jnp.int32, shape, 1), 1.0, 0.0)
    turned = lax.dot_general(
        labels,
        place.astype(jnp.bfloat16),
        (((0,), (0,)), ((), ())),
        preferred_element_type=jnp.float32,
    )
    masked = turned[:, 3:4] > 0.5
    tokens = jnp.where(
        masked, embed[...].astype(jnp.float32)[None, :], patches[0].astype(jnp.float32)
    )
    out[:, :D] = tokens.astype(jnp.bfloat16)
    out[:, D:] = turned.astype(jnp.bfloat16)


def payload_call(segments, rows, columns, mask, embed, patches):
    count = patches.shape[1]
    operands = (segments, rows, columns, mask, embed, patches)
    fixed = lambda shape: pl.BlockSpec(shape, lambda i: (0,) * len(shape))
    shape = (count, D + LANES)
    return pl.pallas_call(
        payload_kernel,
        grid=(1,),
        in_specs=[fixed(one.shape) for one in operands],
        out_specs=fixed(shape),
        out_shape=jax.ShapeDtypeStruct(shape, jnp.bfloat16),
        compiler_params=pltpu.CompilerParams(vmem_limit_bytes=8 << 20),
        cost_estimate=pl.CostEstimate(
            flops=count * D, bytes_accessed=4 * count * D, transcendentals=0
        ),
        name="payload",
    )(*map(in_hbm, operands))


def qkv_kernel(count, flip, info, *refs):
    first, second = refs[:count], refs[count : 2 * count]
    table, gain, weight = refs[2 * count : 2 * count + 3]
    inputs_out, qkv_out, label_out, normed = refs[-4:]
    leads = info[CORE] == 0
    half = sum(piece.shape[0] for piece in first)
    rows = 2 * half
    base = pl.multiple_of((info[CHIP] ^ flip) * rows, rows)
    at = pl.ds(base, rows)
    for behind, pieces in ((~leads, first), (leads, second)):
        done = jnp.where(behind, half, 0)
        for piece in pieces:
            size = piece.shape[0]
            target = pl.ds(pl.multiple_of(base + done, NORM_ROWS), size)
            inputs_out[target, :] = piece[:, :D]
            label_out[target, :] = piece[:, D:]
            for block in range(0, size, NORM_ROWS):
                values = piece[block : block + NORM_ROWS, :D].astype(jnp.float32)
                target = pl.ds(pl.multiple_of(done + block, NORM_ROWS), NORM_ROWS)
                normed[target, :] = norm_rows(values, gain[...]).astype(jnp.bfloat16)
            done += size
    labels = label_out[at, :].astype(jnp.float32)
    columns = lax.dot_general(
        normed[...], weight[...], (((1,), (1,)), ((), ())), preferred_element_type=jnp.float32
    )
    lane = lax.broadcasted_iota(jnp.int32, labels.shape, 1)
    numbers = lane.astype(jnp.float32)
    hot = (numbers == labels[:, 1:2]) | (numbers == labels[:, 2:3] + POSITIONS)
    looked = jnp.dot(
        jnp.where(hot, 1.0, 0.0).astype(jnp.bfloat16), table[...], preferred_element_type=jnp.float32
    )
    cosine = looked[:, :LANES] + looked[:, LANES : 2 * LANES]
    sine = looked[:, 2 * LANES : 3 * LANES] + looked[:, 3 * LANES :]
    first_head = lane < HD // 2

    def turn(start):
        a = columns[:, start : start + LANES]
        b = columns[:, start + LANES : start + 2 * LANES]
        return a * cosine - b * sine, b * cosine + a * sine

    factor = HD**-0.5 * float(np.log2(np.e))
    query_a, query_b = (one * factor for one in turn(0))
    key_a, key_b = turn(2 * LANES)
    zero = jnp.zeros_like(key_a)
    image = numbers == labels[:, :1] + IMAGE_LANE
    extra = lane >= IMAGE_LANE
    apart = jnp.where(image, 0.0, FAR_APART)
    parts = [
        jnp.where(image, 1.0, query_a),
        query_b,
        jnp.where(extra, apart, jnp.where(first_head, key_a, zero)),
        jnp.where(first_head, key_b, zero),
        jnp.where(extra, apart, jnp.where(first_head, zero, key_a)),
        jnp.where(first_head, zero, key_b),
    ]
    for head in range(2):
        values = columns[:, (4 + head) * LANES : (5 + head) * LANES]
        parts.append(jnp.where(lane == HD, 1.0, values))
    for number, part in enumerate(parts):
        qkv_out[at, number * LANES : (number + 1) * LANES] = part.astype(jnp.bfloat16)


def qkv_call(info, flip, first, second, table, gain, weight, earlier, total):
    rows = 2 * sum(piece.shape[0] for piece in first)
    widths = (D, 8 * LANES, LANES)
    operands = [*first, *second, table, gain, in_vmem(weight)]
    vmem = pl.BlockSpec(memory_space=pltpu.VMEM)
    held = [in_vmem(one) for one in earlier]
    return pl.pallas_call(
        functools.partial(qkv_kernel, len(first), flip),
        in_specs=[pl.BlockSpec(memory_space=pltpu.SMEM)]
        + [vmem] * (len(operands) + len(earlier)),
        out_specs=[vmem] * len(widths),
        scratch_shapes=[pltpu.VMEM((rows, D), jnp.bfloat16)],
        out_shape=[pltpu.VMEM((total, width), jnp.bfloat16) for width in widths],
        input_output_aliases={1 + len(operands) + i: i for i in range(len(earlier))},
        compiler_params=pltpu.CompilerParams(vmem_limit_bytes=14 << 20),
        cost_estimate=pl.CostEstimate(
            flops=6 * rows * D * weight.shape[0],
            bytes_accessed=2 * (rows * 4 * D + weight.size),
            transcendentals=rows,
        ),
        name="norm_qkv",
    )(info, *operands, *held)


def segment_row(labels):
    pick = jnp.where(lax.broadcasted_iota(jnp.int32, (8, LANES), 1) == 0, 1.0, 0.0)
    return lax.dot_general(
        pick.astype(jnp.bfloat16),
        labels,
        (((1,), (1,)), ((), ())),
        preferred_element_type=jnp.float32,
    )


def attention_kernel(start, first_owner, images, info, labels, block, *refs):
    out, *rest = refs
    high, sums = rest[-2:]
    rows = high.shape[1]
    total = block.shape[0]
    segments = segment_row(labels[...])
    own = labels[start : start + rows, :1].astype(jnp.float32)
    lowest, largest = jnp.min(own), jnp.max(own)
    one_row = segments[:1]
    begin = jnp.sum(jnp.where(one_row < lowest, 1, 0)) // BLOCK
    end = (jnp.sum(jnp.where(one_row <= largest, 1, 0)) + BLOCK - 1) // BLOCK
    high[...] = jnp.full_like(high, 2 * FAR_APART)
    sums[...] = jnp.zeros_like(sums)

    def attend(step, carry):
        at = pl.ds(pl.multiple_of(step * BLOCK, BLOCK), BLOCK)
        for part in range(rows // ROW_BLOCK):
            for head in range(2):
                rows_here = slice(part * ROW_BLOCK, (part + 1) * ROW_BLOCK)
                queries = block[
                    start + part * ROW_BLOCK : start + (part + 1) * ROW_BLOCK, : 2 * LANES
                ]
                keys = block[at, (2 + 2 * head) * LANES : (4 + 2 * head) * LANES]
                scores = lax.dot_general(
                    queries, keys, (((1,), (1,)), ((), ())), preferred_element_type=jnp.float32
                )
                low, up = scores[:, :LANES], scores[:, LANES:]
                before = high[head, rows_here, :]
                top = jnp.max(jnp.maximum(low, up), axis=-1, keepdims=True)
                now = jnp.maximum(before, top)
                weights = jnp.concatenate([jnp.exp2(low - now), jnp.exp2(up - now)], axis=1)
                values = block[at, (6 + head) * LANES : (7 + head) * LANES]
                term = jnp.dot(
                    weights.astype(jnp.bfloat16), values, preferred_element_type=jnp.float32
                )
                sums[head, rows_here, :] = sums[head, rows_here, :] * jnp.exp2(before - now) + term
                high[head, rows_here, :] = now
        return carry

    lax.fori_loop(begin, end, attend, 0)
    first, second = (sums[head] / sums[head, :, HD : HD + 1] for head in range(2))
    lane = lax.broadcasted_iota(jnp.int32, first.shape, 1)
    turned = pltpu.roll(second, HD, 1)
    out[:rows] = jnp.where(lane < HD, first, turned).astype(jnp.bfloat16)
    half = rows // 2
    tail = 2 * HD - LANES
    lane = lane[:half]
    up = pltpu.roll(turned[half:], tail, 1)
    packed = jnp.where(lane < tail, turned[:half], jnp.where(lane < 2 * tail, up, 0.0))
    out[rows:] = packed.astype(jnp.bfloat16)

    if len(rest) > 2:
        note = rest[0]
        row = lax.broadcasted_iota(jnp.int32, note.shape, 0)
        lane = lax.broadcasted_iota(jnp.int32, note.shape, 1)
        found = jnp.zeros(note.shape, jnp.float32)
        for image in range(images):
            below = jnp.sum(jnp.where(one_row < image, 0.25, 0.0), axis=1, keepdims=True)
            inside = jnp.sum(jnp.where(one_row == image, 0.25, 0.0), axis=1, keepdims=True)
            here = row == info[first_owner + image]
            for place, number in enumerate((below, inside)):
                upper = jnp.floor(number * (1.0 / 16))
                found = jnp.where(here & (lane == 2 * place), upper, found)
                found = jnp.where(here & (lane == 2 * place + 1), number - 16 * upper, found)
        note[...] = found.astype(jnp.bfloat16)


def attention_call(start, rows, first_owner, info, labels, block, noted):
    total = block.shape[0]
    vmem = pl.BlockSpec(memory_space=pltpu.VMEM)
    shapes = [jax.ShapeDtypeStruct((rows + rows // 2, LANES), jnp.bfloat16)]
    if noted:
        shapes.append(jax.ShapeDtypeStruct((16, LANES), jnp.bfloat16))
    return pl.pallas_call(
        functools.partial(attention_kernel, start, first_owner, info.shape[0] - first_owner),
        in_specs=[pl.BlockSpec(memory_space=pltpu.SMEM), vmem, vmem],
        out_specs=[vmem] * len(shapes),
        out_shape=shapes,
        scratch_shapes=[
            pltpu.VMEM((2, rows, LANES), jnp.float32),
            pltpu.VMEM((2, rows, LANES), jnp.float32),
        ],
        compiler_params=pltpu.CompilerParams(vmem_limit_bytes=12 << 20),
        cost_estimate=pl.CostEstimate(
            flops=10 * rows * total * 2 * LANES,
            bytes_accessed=2 * block.size,
            transcendentals=rows * total,
        ),
        name="attention",
    )(info, in_vmem(labels), in_vmem(block))


def prepare_kernel(shards, info, out_weight, merge_weight, qkv_weight, spread, *refs):
    *rows, out, merge, qkv, qkv_buffer, spread_buffer, sems = refs
    for row, row_out in zip(rows[: len(rows) // 2], rows[len(rows) // 2 :]):
        row_out[...] = row[...].astype(jnp.float32)[None, :]
    rest = 2 * HD - LANES
    copies = [(qkv_weight, qkv_buffer), (spread, spread_buffer)]
    out[shards * LANES :] = jnp.zeros((shards // 2 * LANES, D), jnp.bfloat16)
    for place in range(shards):
        start = pl.multiple_of(info[IDS + place] * (2 * HD), 16)
        to = (shards + place // 2) * LANES + place % 2 * rest
        copies.append(
            (out_weight.at[pl.ds(start, LANES), :], out.at[pl.ds(place * LANES, LANES), :])
        )
        copies.append((out_weight.at[pl.ds(start + LANES, rest), :], out.at[pl.ds(to, rest), :]))
    copies.append((merge_weight, merge))
    copies = [
        pltpu.make_async_copy(source, target, sems.at[i])
        for i, (source, target) in enumerate(copies)
    ]
    for copy in copies:
        copy.start()
    copies[0].wait()
    copies[1].wait()
    qkv[...] = jnp.dot(
        spread_buffer[...], qkv_buffer[...], preferred_element_type=jnp.float32
    ).astype(jnp.bfloat16)
    for copy in copies[2:]:
        copy.wait()


def prepare_call(shards, info, out_weight, merge_weight, qkv_weight, spread, rows):
    anywhere = pl.BlockSpec(memory_space=pl.ANY)
    vmem = pl.BlockSpec(memory_space=pltpu.VMEM)
    operands = (out_weight, merge_weight, qkv_weight, spread)
    shapes = [(shards * LANES * 3 // 2, D), merge_weight.shape, (spread.shape[0], D)]
    return pl.pallas_call(
        functools.partial(prepare_kernel, shards),
        in_specs=[pl.BlockSpec(memory_space=pltpu.SMEM)]
        + [anywhere] * len(operands)
        + [vmem] * len(rows),
        out_specs=[vmem] * (len(rows) + len(shapes)),
        out_shape=[pltpu.VMEM((1, row.shape[0]), jnp.float32) for row in rows]
        + [pltpu.VMEM(shape, jnp.bfloat16) for shape in shapes],
        scratch_shapes=[
            pltpu.VMEM(qkv_weight.shape, jnp.bfloat16),
            pltpu.VMEM(spread.shape, jnp.bfloat16),
            pltpu.SemaphoreType.DMA((2 * shards + 3,)),
        ],
        compiler_params=pltpu.CompilerParams(vmem_limit_bytes=10 << 20),
        cost_estimate=pl.CostEstimate(
            flops=2 * spread.size * D,
            bytes_accessed=4 * (out_weight.size + merge_weight.size + qkv_weight.size),
            transcendentals=0,
        ),
        name="prepare",
    )(info, *map(in_hbm, operands), *rows)


def merge_kernel(start, counts, packs, last, *refs):
    inputs, weight, gain, merge_weight, bias = refs[:5]
    pieces = refs[5 : 5 + sum(counts)]
    *refs, state, tokens = refs[5 + sum(counts) :]
    rows = state.shape[1]
    half = rows // 2
    rest = 2 * HD - LANES
    sources, at = [], 0
    for count in counts:
        sources.append(stacked(pieces[at : at + count]))
        at += count
    shards = len(sources)
    lane = lax.broadcasted_iota(jnp.int32, (half, LANES), 1)
    for part in range(2):
        token = slice(part * half, (part + 1) * half)
        lined = [source[token, :] for source in sources]
        for pair in range(shards // 2):
            mine = sources[2 * pair][rows:, :].astype(jnp.float32)
            other = sources[2 * pair + 1][rows:, :].astype(jnp.float32)
            if part == 0:
                other = pltpu.roll(other, rest, 1)
            else:
                mine = pltpu.roll(mine, LANES - rest, 1)
            lined.append(jnp.where(lane < rest, mine, other).astype(jnp.bfloat16))
        mixed = jnp.dot(
            jnp.concatenate(lined, axis=1), weight[...], preferred_element_type=jnp.float32
        )
        for column in range(D // LANES):
            lanes = slice(column * LANES, (column + 1) * LANES)
            before = inputs[start + part * half : start + (part + 1) * half, lanes]
            state[column, token, :] = before.astype(jnp.float32) + mixed[:, lanes]
    groups = rows // 4
    for block in range(0, groups, NORM_ROWS):
        for quadrant in range(4):
            at = pl.ds(4 * block + quadrant, NORM_ROWS, stride=4)
            residual = jnp.concatenate(
                [state[column, at, :] for column in range(D // LANES)], axis=1
            )
            tokens[block : block + NORM_ROWS, quadrant * D : (quadrant + 1) * D] = norm_rows(
                residual, gain[...]
            ).astype(jnp.bfloat16)
    total = bias[...] + lax.dot_general(
        tokens[...], merge_weight[...], (((1,), (1,)), ((), ())), preferred_element_type=jnp.float32
    )
    total = total.astype(jnp.bfloat16)
    if not last:
        refs[0][...] = total
        return
    info, note, *earlier = refs[:-packs]
    outs = refs[-packs:]
    total = jnp.concatenate([*[one[...] for one in earlier], total], axis=0)
    whole = total.shape[1] // LANES
    most = outs[0].shape[0] * LANES // total.shape[1]
    notes = note[...].astype(jnp.float32)
    note_row = lax.broadcasted_iota(jnp.int32, notes.shape, 0)
    slot = lax.broadcasted_iota(jnp.int32, (most, total.shape[0]), 0)
    row = lax.broadcasted_iota(jnp.int32, (most, total.shape[0]), 1)
    for place, out in enumerate(outs):
        found = jnp.where(note_row == (info[PACK] ^ place), notes, 0.0)
        found = jnp.sum(found, axis=0, keepdims=True)
        first = (16.0 * found[:, :1] + found[:, 1:2]).astype(jnp.int32)
        length = (16.0 * found[:, 2:3] + found[:, 3:4]).astype(jnp.int32)
        chosen = (row == slot + first) & (slot < length)
        chosen = jnp.where(chosen, 1.0, 0.0).astype(jnp.bfloat16)
        block = jnp.dot(chosen, total, preferred_element_type=jnp.float32)
        for column in range(whole):
            out[column * most : (column + 1) * most, :] = block[
                :, column * LANES : (column + 1) * LANES
            ].astype(jnp.bfloat16)
        low = block[: most // 2, whole * LANES :]
        up = block[most // 2 :, whole * LANES :]
        out[whole * most :, :] = jnp.concatenate([low, up], axis=1).astype(jnp.bfloat16)


def merge_call(start, rows, sources, inputs, weight, gain, merge_weight, bias, packs, route):
    groups = rows // 4
    width = merge_weight.shape[0]
    pieces = [piece for source in sources for piece in source]
    vmem = pl.BlockSpec(memory_space=pltpu.VMEM)
    operands = [in_vmem(inputs), in_vmem(weight), gain, in_vmem(merge_weight), bias, *pieces]
    specs = [vmem] * len(operands)
    shapes = [jax.ShapeDtypeStruct((groups, width), jnp.bfloat16)]
    if route:
        me, most, *others = route
        operands += [me, *others]
        specs += [pl.BlockSpec(memory_space=pltpu.SMEM)] + [vmem] * len(others)
        shapes = [jax.ShapeDtypeStruct((most * width // LANES, LANES), jnp.bfloat16)] * packs
    return pl.pallas_call(
        functools.partial(
            merge_kernel, start, [len(source) for source in sources], packs, bool(route)
        ),
        in_specs=specs,
        out_specs=[vmem] * len(shapes),
        scratch_shapes=[
            pltpu.VMEM((D // LANES, rows, LANES), jnp.float32),
            pltpu.VMEM((groups, 4 * D), jnp.bfloat16),
        ],
        out_shape=shapes,
        compiler_params=pltpu.CompilerParams(vmem_limit_bytes=20 << 20),
        cost_estimate=pl.CostEstimate(
            flops=4 * rows * D * D + 2 * groups * merge_weight.size,
            bytes_accessed=2 * (D * D + merge_weight.size + 3 * rows * D),
            transcendentals=rows,
        ),
        name="out_merge",
    )(*operands)


def place_kernel(info, *refs):
    blocks, out = refs[:-1], refs[-1]
    most, width = out.shape[1:]
    whole = width // LANES
    half = most // 2
    middle = LANES // 2
    for place, block in enumerate(blocks):
        target = info[PACK] ^ place
        for column in range(whole):
            out[target, :, column * LANES : (column + 1) * LANES] = block[
                column * most : (column + 1) * most, :
            ]
        out[target, :half, whole * LANES :] = block[whole * most :, :middle]
        out[target, half:, whole * LANES :] = block[whole * most :, middle:]


def place_call(info, blocks, most, width):
    fixed = lambda shape: pl.BlockSpec(shape, lambda i: (0,) * len(shape))
    shape = (len(blocks), most, width)
    return pl.pallas_call(
        place_kernel,
        grid=(1,),
        in_specs=[pl.BlockSpec(memory_space=pltpu.SMEM)] + [fixed(one.shape) for one in blocks],
        out_specs=fixed(shape),
        out_shape=jax.ShapeDtypeStruct(shape, jnp.bfloat16),
        compiler_params=pltpu.CompilerParams(vmem_limit_bytes=8 << 20),
        cost_estimate=pl.CostEstimate(
            flops=0, bytes_accessed=4 * len(blocks) * most * width, transcendentals=0
        ),
        name="place_rows",
    )(info, *blocks)


def send_seq(value, flip):
    size = lax.axis_size("seq")
    return lax.ppermute(value, "seq", [(i, i ^ flip) for i in range(size)])


def after(values, *earlier):
    return lax.optimization_barrier((tuple(values), earlier))[0]


def halves_kernel(across_x, across_y, upper, lower):
    half = upper.shape[0]
    upper[...] = across_x[:half]
    lower[...] = across_y[half:]


def halves_call(across_x, across_y):
    vmem = pl.BlockSpec(memory_space=pltpu.VMEM)
    shape = (across_x.shape[0] // 2, across_x.shape[1])
    return pl.pallas_call(
        halves_kernel,
        in_specs=[vmem] * 2,
        out_specs=[vmem] * 2,
        out_shape=[jax.ShapeDtypeStruct(shape, across_x.dtype)] * 2,
        compiler_params=pltpu.CompilerParams(vmem_limit_bytes=4 << 20),
        cost_estimate=pl.CostEstimate(
            flops=0, bytes_accessed=4 * across_x.size, transcendentals=0
        ),
        name="halves",
    )(across_x, across_y)


def near_shards(value):
    return [send_seq(value, 1), send_seq(value, 2), send_seq(value, 4)]


def far_shards(across_x, across_y):
    upper, lower = halves_call(across_x, across_y)
    return [send_seq(upper, 4), send_seq(lower, 2)]


def weight_order(heads_here):
    quarter = HD // 4
    order = -np.ones((6 * LANES,), np.int32)
    for head in range(heads_here):
        base = head * 3 * HD
        for kind in range(2):
            for half in range(2):
                for letter in range(2):
                    target = (2 * kind + letter) * LANES + head * (HD // 2) + half * quarter
                    source = base + kind * HD + half * (HD // 2) + letter * quarter
                    order[target : target + quarter] = np.arange(source, source + quarter)
        target = (4 + head) * LANES
        order[target : target + HD] = np.arange(base + 2 * HD, base + 3 * HD)
    return order


def angle_table(heads_here):
    quarter = HD // 4
    frequency = (10000.0 ** (-np.arange(quarter) / quarter)).astype(np.float32)
    angles = np.arange(POSITIONS, dtype=np.float32)[:, None] * frequency[None, :]
    pieces = []
    for function in (np.cos, np.sin):
        exact = np.zeros((2 * POSITIONS, LANES), np.float64)
        for head in range(heads_here):
            for half in range(2):
                lane = head * (HD // 2) + half * quarter
                rows = slice(half * POSITIONS, (half + 1) * POSITIONS)
                exact[rows, lane : lane + quarter] = function(angles.astype(np.float64))
        upper = exact.astype(jnp.bfloat16)
        pieces += [upper, (exact - upper.astype(np.float64)).astype(jnp.bfloat16)]
    return np.concatenate(pieces, axis=1)


def fast_local(
    patches,
    patch_mask,
    mask_embed,
    norm_gain,
    qkv_weight,
    segment_ids,
    patch_rows,
    patch_column,
    out_weight,
    merge_gain,
    merge_weight,
    merge_bias,
    image_owner,
):
    local_rows = patches.shape[1]
    shards = lax.axis_size("seq")
    packs = lax.axis_size("pack")
    heads_here = HEADS // shards
    images = image_owner.shape[1]
    total = local_rows * shards
    me = lax.axis_index("seq").astype(jnp.int32)
    pack = lax.axis_index("pack").astype(jnp.int32)

    value = payload_call(segment_ids, patch_rows, patch_column, patch_mask, mask_embed, patches)
    own_swap, across_x, across_y = near_shards(value)

    order = weight_order(heads_here)
    spread = (order[:, None] == np.arange(qkv_weight.shape[1])[None, :]).astype(jnp.bfloat16)
    table = jnp.asarray(angle_table(heads_here))
    chip, core = me // 2, me % 2
    info = [chip, core, pack, *[me ^ place for place in range(shards)]]
    info = jnp.concatenate([jnp.stack(info), image_owner[0]])
    gain, merge_gain_row, bias, ordered, merge_rows, weight = prepare_call(
        shards,
        info,
        out_weight,
        merge_weight.T,
        qkv_weight.T,
        jnp.asarray(spread),
        (norm_gain, merge_gain, merge_bias),
    )

    project = lambda place, first, second, earlier: qkv_call(
        info, place, first, second, table, gain, weight, earlier, total
    )
    buffers = project(0, [value], [own_swap], ())
    across_x, across_y = after([across_x, across_y], buffers[2], ordered)
    far = far_shards(across_x, across_y)
    buffers = project(1, [across_x], [send_seq(across_x, 1)], buffers)
    buffers = project(2, [across_y], [send_seq(across_y, 1)], buffers)
    far = after(far, buffers[2])
    buffers = project(3, far, [send_seq(one, 1) for one in far], buffers)
    inputs, block, labels = buffers

    starts = [sum(CHUNKS[:number]) for number in range(len(CHUNKS))]
    attended, note = [], None
    for start, rows in zip(starts, CHUNKS):
        made = attention_call(start, rows, IDS + shards, info, labels, block, note is None)
        note = made[1] if note is None else note
        value = made[0]
        if attended:
            (value,) = after([value], *attended[-1][1])
        attended.append((value, near_shards(value)))
    latest = attended[-1][0]
    most = 2 * (total // 4) // images
    projected, moving = [], []
    for own, (own_swap, across_x, across_y) in attended:
        previous = moving[-1][-1] if moving else ()
        across_x, across_y = after([across_x, across_y], latest, *previous)
        far = far_shards(across_x, across_y)
        moving.append(
            (own, own_swap, across_x, send_seq(across_x, 1), across_y, send_seq(across_y, 1), far)
        )
    for number, (start, rows) in enumerate(zip(starts, CHUNKS)):
        *near, far = moving[number]
        if projected:
            far = after(far, projected[-1])
        sources = [[one] for one in near] + [far, [send_seq(one, 1) for one in far]]
        route = ()
        if number == len(CHUNKS) - 1:
            route = (info, most, note, *projected)
        made = merge_call(
            start, rows, sources, inputs, ordered, merge_gain_row, merge_rows, bias, packs, route
        )
        projected.append(made[0])
    blocks = [made[0]] + [
        lax.ppermute(made[flip], "pack", [(z, z ^ flip) for z in range(packs)])
        for flip in range(1, packs)
    ]
    return place_call(info, blocks, most, merge_weight.shape[1])[None]


def local(*arguments):
    patches, weight = arguments[0], arguments[4]
    shards = lax.axis_size("seq")
    fits = shards == 8 and HEADS // shards == 2 and weight.shape[1] == 6 * HD
    fits = fits and patches.shape[1] * shards == sum(CHUNKS) and lax.axis_size("pack") == 4
    return fast_local(*arguments) if fits else general_local(*arguments)


def solution(mesh):
    placed = (
        P("pack", "seq", None),
        P("pack", "seq"),
        P(),
        P(),
        P(None, "seq"),
        P("pack", "seq"),
        P("pack", "seq"),
        P("pack", "seq"),
        P(),
        P(),
        P(None, "seq"),
        P("seq"),
        P("pack", None),
    )
    return jax.shard_map(
        local, mesh=mesh, in_specs=placed, out_specs=P("pack", None, None, "seq"), check_vma=False
    )
```

```python
import functools

import jax
import jax.numpy as jnp
import numpy as np
from jax import lax
from jax.experimental import pallas as pl
from jax.experimental.pallas import tpu as pltpu
from jax.sharding import PartitionSpec as P

D = 1408
HEADS = 16
HD = 88


EPSILON = 1e-06


def layer_norm(values, gain_vector):
    center = values - jnp.mean(values, axis=-1, keepdims=True)
    spread = jnp.mean(center * center, axis=-1, keepdims=True)
    return center * lax.rsqrt(spread + EPSILON) * gain_vector.astype(jnp.float32)


def rotate(vectors, row_index, column_index):
    total_rows, heads_here, head_width = vectors.shape
    quarter = head_width // 4
    frequency = 10000.0 ** (-jnp.arange(quarter, dtype=jnp.float32) / quarter)
    row_angle = row_index.astype(jnp.float32)[:, None] * frequency[None, :]
    column_angle = column_index.astype(jnp.float32)[:, None] * frequency[None, :]
    angles = jnp.stack([row_angle, column_angle], axis=1)[:, None, :, None, :]
    split_up = vectors.reshape(total_rows, heads_here, 2, 2, quarter)
    partner = jnp.stack([-split_up[:, :, :, 1], split_up[:, :, :, 0]], axis=3)
    turned = split_up * jnp.cos(angles) + partner * jnp.sin(angles)
    return turned.reshape(total_rows, heads_here, head_width)


def qkv_block(projected, row_index, column_index):
    turned_queries = rotate(projected[:, :, 0], row_index, column_index)
    turned_keys = rotate(projected[:, :, 1], row_index, column_index)
    return jnp.concatenate([turned_queries, turned_keys, projected[:, :, 2]], axis=-1).astype(
        jnp.bfloat16
    )


def attention(block, segments):
    total_rows, heads_here, triple = block.shape
    head_width = triple // 3
    step_rows = min(512, total_rows)
    query_part = block[:, :, :head_width].reshape(
        total_rows // step_rows, step_rows, heads_here, head_width
    )
    key_part = block[:, :, head_width : 2 * head_width]
    value_part = block[:, :, 2 * head_width :]
    query_segments = segments.reshape(total_rows // step_rows, step_rows)
    scale = head_width ** (-0.5)

    def one_block(inputs_pair):
        queries_here, segments_here = inputs_pair
        scores = (
            jnp.einsum("qhd,khd->hqk", queries_here, key_part, preferred_element_type=jnp.float32)
            * scale
        )
        same_image = (segments_here[:, None] == segments[None, :])[None]
        scores = jnp.where(same_image, scores, -jnp.inf)
        highest = jnp.max(scores, axis=-1, keepdims=True)
        weights = jnp.exp(scores - highest)
        probs = (weights / jnp.sum(weights, axis=-1, keepdims=True)).astype(jnp.bfloat16)
        result = jnp.einsum("hqk,khd->qhd", probs, value_part, preferred_element_type=jnp.float32)
        return result.astype(jnp.bfloat16)

    return lax.map(one_block, (query_part, query_segments)).reshape(
        total_rows, heads_here, head_width
    )


def route(projected, segments, owners_here, packs, most):
    merged_segments = segments[::4]
    images = owners_here.shape[0]
    image_ids = jnp.arange(images, dtype=jnp.int32)
    member = (merged_segments[None, :] == image_ids[:, None]).astype(jnp.int32)
    lengths = jnp.sum(member, axis=1, dtype=jnp.int32)
    starts = jnp.cumsum(lengths, dtype=jnp.int32) - lengths
    owner_ids = jnp.arange(packs, dtype=jnp.int32)
    owned = owners_here[None, :] == owner_ids[:, None]
    first_row = jnp.sum(jnp.where(owned, starts[None, :], 0), axis=1, dtype=jnp.int32)
    owned_length = jnp.sum(jnp.where(owned, lengths[None, :], 0), axis=1, dtype=jnp.int32)
    slots = jnp.arange(most, dtype=jnp.int32)
    source_rows = jnp.clip(first_row[:, None] + slots[None, :], 0, projected.shape[0] - 1)
    picked = jnp.take(projected, source_rows.reshape(-1), axis=0).reshape(
        packs, most, projected.shape[1]
    )
    filled = slots[None, :] < owned_length[:, None]
    return jnp.where(filled[:, :, None], picked, jnp.zeros_like(picked))


def general_local(
    patches,
    patch_mask,
    mask_embed,
    norm_gain,
    qkv_weight,
    segment_ids,
    patch_rows,
    patch_column,
    out_weight,
    merge_gain,
    merge_weight,
    merge_bias,
    image_owner,
):
    local_rows = patches.shape[1]
    shards = lax.axis_size("seq")
    packs = lax.axis_size("pack")
    heads_here = HEADS // shards
    inputs = jnp.where(patch_mask[0][:, None] == 1, mask_embed[None, :], patches[0])
    normed = layer_norm(inputs.astype(jnp.float32), norm_gain).astype(jnp.bfloat16)
    labels = lax.all_gather(
        jnp.stack([segment_ids[0], patch_rows[0], patch_column[0]]), "seq", axis=1, tiled=True
    )
    piece = lax.all_gather(normed, "seq", axis=0, tiled=True)
    span = piece.shape[0]
    projected = jnp.dot(piece, qkv_weight, preferred_element_type=jnp.float32)
    row_part = labels[1]
    column_part = labels[2]
    block = qkv_block(projected.reshape(span, heads_here, 3, HD), row_part, column_part)
    result = attention(block, labels[0])
    mixed_heads = lax.all_to_all(result, "seq", split_axis=0, concat_axis=1, tiled=True)
    attended = mixed_heads.reshape(local_rows, D)
    residual = inputs.astype(jnp.float32) + jnp.dot(
        attended, out_weight, preferred_element_type=jnp.float32
    )
    merged = layer_norm(residual, merge_gain).astype(jnp.bfloat16).reshape(local_rows // 4, 4 * D)
    projected_all = (
        jnp.dot(
            lax.all_gather(merged, "seq", axis=0, tiled=True),
            merge_weight,
            preferred_element_type=jnp.float32,
        )
        + merge_bias.astype(jnp.float32)
    ).astype(jnp.bfloat16)
    images = image_owner.shape[1]
    most = 2 * projected_all.shape[0] // images
    outgoing = route(projected_all, labels[0], image_owner[0], packs, most)
    delivered = lax.all_to_all(outgoing, "pack", split_axis=0, concat_axis=0, tiled=True)
    return delivered[None]


LANES = 128
CHIP, CORE, PACK, IDS = 0, 1, 2, 3
BLOCK = 256
POSITIONS = 64
FAR_APART = -(2.0**100)
IMAGE_LANE = 96
NORM_ROWS = 16
CHUNKS = (768, 768)


def norm_rows(values, gain_row):
    center = values - jnp.mean(values, axis=-1, keepdims=True)
    spread = jnp.mean(center * center, axis=-1, keepdims=True)
    return center * lax.rsqrt(spread + EPSILON) * gain_row


def stacked(pieces):
    loaded = [piece[...] for piece in pieces]
    return loaded[0] if len(loaded) == 1 else jnp.concatenate(loaded, axis=0)


def in_vmem(value):
    return pltpu.with_memory_space_constraint(value, pltpu.VMEM)


def in_hbm(value):
    return pltpu.with_memory_space_constraint(value, pltpu.HBM)


def payload_kernel(segments, rows, columns, mask, embed, patches, out):
    labels = [one[...].astype(jnp.float32) for one in (segments, rows, columns, mask)]
    labels.append(jnp.zeros((4, labels[0].shape[1]), jnp.float32))
    labels = jnp.concatenate(labels, axis=0).astype(jnp.bfloat16)
    shape = (8, LANES)
    row = lax.broadcasted_iota(jnp.int32, shape, 0)
    place = jnp.where(row == lax.broadcasted_iota(jnp.int32, shape, 1), 1.0, 0.0)
    turned = lax.dot_general(
        labels,
        place.astype(jnp.bfloat16),
        (((0,), (0,)), ((), ())),
        preferred_element_type=jnp.float32,
    )
    masked = turned[:, 3:4] > 0.5
    tokens = jnp.where(
        masked, embed[...].astype(jnp.float32)[None, :], patches[0].astype(jnp.float32)
    )
    out[:, :D] = tokens.astype(jnp.bfloat16)
    out[:, D:] = turned.astype(jnp.bfloat16)


def payload_call(segments, rows, columns, mask, embed, patches):
    count = patches.shape[1]
    operands = (segments, rows, columns, mask, embed, patches)
    fixed = lambda shape: pl.BlockSpec(shape, lambda i: (0,) * len(shape))
    shape = (count, D + LANES)
    return pl.pallas_call(
        payload_kernel,
        grid=(1,),
        in_specs=[fixed(one.shape) for one in operands],
        out_specs=fixed(shape),
        out_shape=jax.ShapeDtypeStruct(shape, jnp.bfloat16),
        compiler_params=pltpu.CompilerParams(vmem_limit_bytes=8 << 20),
        cost_estimate=pl.CostEstimate(
            flops=count * D, bytes_accessed=4 * count * D, transcendentals=0
        ),
        name="payload",
    )(*map(in_hbm, operands))


def qkv_kernel(count, flip, info, *refs):
    first, second = refs[:count], refs[count : 2 * count]
    table, gain, weight = refs[2 * count : 2 * count + 3]
    inputs_out, qkv_out, label_out = refs[-3:]
    mine, other = stacked(first), stacked(second)
    leads = info[CORE] == 0
    ahead = jnp.where(leads, mine, other)
    behind = jnp.where(leads, other, mine)
    both = jnp.concatenate([ahead, behind], axis=0)
    rows = both.shape[0]
    at = pl.ds(pl.multiple_of((info[CHIP] ^ flip) * rows, rows), rows)
    inputs_out[at, :] = both[:, :D]
    label_out[at, :] = both[:, D:]
    labels = both[:, D:].astype(jnp.float32)
    normed = norm_rows(both[:, :D].astype(jnp.float32), gain[...]).astype(jnp.bfloat16)
    columns = lax.dot_general(
        normed, weight[...], (((1,), (1,)), ((), ())), preferred_element_type=jnp.float32
    )
    lane = lax.broadcasted_iota(jnp.int32, labels.shape, 1)
    numbers = lane.astype(jnp.float32)
    hot = (numbers == labels[:, 1:2]) | (numbers == labels[:, 2:3] + POSITIONS)
    looked = jnp.dot(
        jnp.where(hot, 1.0, 0.0).astype(jnp.bfloat16), table[...], preferred_element_type=jnp.float32
    )
    cosine = looked[:, :LANES] + looked[:, LANES : 2 * LANES]
    sine = looked[:, 2 * LANES : 3 * LANES] + looked[:, 3 * LANES :]
    first_head = lane < HD // 2

    def turn(start):
        a = columns[:, start : start + LANES]
        b = columns[:, start + LANES : start + 2 * LANES]
        return a * cosine - b * sine, b * cosine + a * sine

    factor = HD**-0.5 * float(np.log2(np.e))
    query_a, query_b = (one * factor for one in turn(0))
    key_a, key_b = turn(2 * LANES)
    zero = jnp.zeros_like(key_a)
    image = numbers == labels[:, :1] + IMAGE_LANE
    extra = lane >= IMAGE_LANE
    apart = jnp.where(image, 0.0, FAR_APART)
    parts = [
        jnp.where(image, 1.0, query_a),
        query_b,
        jnp.where(extra, apart, jnp.where(first_head, key_a, zero)),
        jnp.where(first_head, key_b, zero),
        jnp.where(extra, apart, jnp.where(first_head, zero, key_a)),
        jnp.where(first_head, zero, key_b),
    ]
    for head in range(2):
        values = columns[:, (4 + head) * LANES : (5 + head) * LANES]
        parts.append(jnp.where(lane == HD, 1.0, values))
    for number, part in enumerate(parts):
        qkv_out[at, number * LANES : (number + 1) * LANES] = part.astype(jnp.bfloat16)


def qkv_call(info, flip, first, second, table, gain, weight, earlier, total):
    rows = 2 * sum(piece.shape[0] for piece in first)
    widths = (D, 8 * LANES, LANES)
    operands = [*first, *second, table, gain, in_vmem(weight)]
    vmem = pl.BlockSpec(memory_space=pltpu.VMEM)
    held = [in_vmem(one) for one in earlier]
    return pl.pallas_call(
        functools.partial(qkv_kernel, len(first), flip),
        in_specs=[pl.BlockSpec(memory_space=pltpu.SMEM)]
        + [vmem] * (len(operands) + len(earlier)),
        out_specs=[vmem] * len(widths),
        out_shape=[pltpu.VMEM((total, width), jnp.bfloat16) for width in widths],
        input_output_aliases={1 + len(operands) + i: i for i in range(len(earlier))},
        compiler_params=pltpu.CompilerParams(vmem_limit_bytes=14 << 20),
        cost_estimate=pl.CostEstimate(
            flops=6 * rows * D * weight.shape[0],
            bytes_accessed=2 * (rows * 4 * D + weight.size),
            transcendentals=rows,
        ),
        name="norm_qkv",
    )(info, *operands, *held)


def segment_row(labels):
    pick = jnp.where(lax.broadcasted_iota(jnp.int32, (8, LANES), 1) == 0, 1.0, 0.0)
    return lax.dot_general(
        pick.astype(jnp.bfloat16),
        labels,
        (((1,), (1,)), ((), ())),
        preferred_element_type=jnp.float32,
    )


def attention_kernel(start, first_owner, images, info, labels, block, *refs):
    out, *rest = refs
    scores, high = rest[-2:]
    rows = high.shape[1]
    total = block.shape[0]
    segments = segment_row(labels[...])
    own = labels[start : start + rows, :1].astype(jnp.float32)
    lowest, largest = jnp.min(own), jnp.max(own)
    one_row = segments[:1]
    begin = jnp.sum(jnp.where(one_row < lowest, 1, 0)) // BLOCK
    end = (jnp.sum(jnp.where(one_row <= largest, 1, 0)) + BLOCK - 1) // BLOCK
    queries = block[start : start + rows, : 2 * LANES]
    high[...] = jnp.full_like(high, 2 * FAR_APART)

    def score(step, carry):
        at = pl.ds(pl.multiple_of(step * BLOCK, BLOCK), BLOCK)
        for head in range(2):
            keys = block[at, (2 + 2 * head) * LANES : (4 + 2 * head) * LANES]
            values = lax.dot_general(
                queries, keys, (((1,), (1,)), ((), ())), preferred_element_type=jnp.float32
            )
            scores[head, step] = values
            high[head] = jnp.maximum(
                high[head], jnp.maximum(values[:, :LANES], values[:, LANES:])
            )
        return carry

    lax.fori_loop(begin, end, score, 0)
    highest = [jnp.max(high[head], axis=-1, keepdims=True) for head in range(2)]

    def weigh(step, carry):
        at = pl.ds(pl.multiple_of(step * BLOCK, BLOCK), BLOCK)
        sums = []
        for head in range(2):
            weights = jnp.exp2(scores[head, step] - highest[head])
            values = block[at, (6 + head) * LANES : (7 + head) * LANES]
            sums.append(
                carry[head]
                + jnp.dot(weights.astype(jnp.bfloat16), values, preferred_element_type=jnp.float32)
            )
        return tuple(sums)

    zero = jnp.zeros((rows, LANES), jnp.float32)
    sums = lax.fori_loop(begin, end, weigh, (zero, zero))
    first, second = (one / one[:, HD : HD + 1] for one in sums)
    lane = lax.broadcasted_iota(jnp.int32, first.shape, 1)
    turned = pltpu.roll(second, HD, 1)
    out[:rows] = jnp.where(lane < HD, first, turned).astype(jnp.bfloat16)
    half = rows // 2
    tail = 2 * HD - LANES
    lane = lane[:half]
    up = pltpu.roll(turned[half:], tail, 1)
    packed = jnp.where(lane < tail, turned[:half], jnp.where(lane < 2 * tail, up, 0.0))
    out[rows:] = packed.astype(jnp.bfloat16)

    if len(rest) > 2:
        note = rest[0]
        row = lax.broadcasted_iota(jnp.int32, note.shape, 0)
        lane = lax.broadcasted_iota(jnp.int32, note.shape, 1)
        found = jnp.zeros(note.shape, jnp.float32)
        for image in range(images):
            below = jnp.sum(jnp.where(one_row < image, 0.25, 0.0), axis=1, keepdims=True)
            inside = jnp.sum(jnp.where(one_row == image, 0.25, 0.0), axis=1, keepdims=True)
            here = row == info[first_owner + image]
            for place, number in enumerate((below, inside)):
                upper = jnp.floor(number * (1.0 / 16))
                found = jnp.where(here & (lane == 2 * place), upper, found)
                found = jnp.where(here & (lane == 2 * place + 1), number - 16 * upper, found)
        note[...] = found.astype(jnp.bfloat16)


def attention_call(start, rows, first_owner, info, labels, block, noted):
    total = block.shape[0]
    vmem = pl.BlockSpec(memory_space=pltpu.VMEM)
    shapes = [jax.ShapeDtypeStruct((rows + rows // 2, LANES), jnp.bfloat16)]
    if noted:
        shapes.append(jax.ShapeDtypeStruct((16, LANES), jnp.bfloat16))
    return pl.pallas_call(
        functools.partial(attention_kernel, start, first_owner, info.shape[0] - first_owner),
        in_specs=[pl.BlockSpec(memory_space=pltpu.SMEM), vmem, vmem],
        out_specs=[vmem] * len(shapes),
        out_shape=shapes,
        scratch_shapes=[
            pltpu.VMEM((2, total // BLOCK, rows, BLOCK), jnp.float32),
            pltpu.VMEM((2, rows, LANES), jnp.float32),
        ],
        compiler_params=pltpu.CompilerParams(vmem_limit_bytes=20 << 20),
        cost_estimate=pl.CostEstimate(
            flops=10 * rows * total * 2 * LANES,
            bytes_accessed=2 * block.size,
            transcendentals=rows * total,
        ),
        name="attention",
    )(info, in_vmem(labels), in_vmem(block))


def prepare_kernel(shards, info, out_weight, merge_weight, qkv_weight, spread, *refs):
    *rows, out, merge, qkv, qkv_buffer, spread_buffer, sems = refs
    for row, row_out in zip(rows[: len(rows) // 2], rows[len(rows) // 2 :]):
        row_out[...] = row[...].astype(jnp.float32)[None, :]
    rest = 2 * HD - LANES
    copies = [(qkv_weight, qkv_buffer), (spread, spread_buffer)]
    out[shards * LANES :] = jnp.zeros((shards // 2 * LANES, D), jnp.bfloat16)
    for place in range(shards):
        start = pl.multiple_of(info[IDS + place] * (2 * HD), 16)
        to = (shards + place // 2) * LANES + place % 2 * rest
        copies.append(
            (out_weight.at[pl.ds(start, LANES), :], out.at[pl.ds(place * LANES, LANES), :])
        )
        copies.append((out_weight.at[pl.ds(start + LANES, rest), :], out.at[pl.ds(to, rest), :]))
    copies.append((merge_weight, merge))
    copies = [
        pltpu.make_async_copy(source, target, sems.at[i])
        for i, (source, target) in enumerate(copies)
    ]
    for copy in copies:
        copy.start()
    copies[0].wait()
    copies[1].wait()
    qkv[...] = jnp.dot(
        spread_buffer[...], qkv_buffer[...], preferred_element_type=jnp.float32
    ).astype(jnp.bfloat16)
    for copy in copies[2:]:
        copy.wait()


def prepare_call(shards, info, out_weight, merge_weight, qkv_weight, spread, rows):
    anywhere = pl.BlockSpec(memory_space=pl.ANY)
    vmem = pl.BlockSpec(memory_space=pltpu.VMEM)
    operands = (out_weight, merge_weight, qkv_weight, spread)
    shapes = [(shards * LANES * 3 // 2, D), merge_weight.shape, (spread.shape[0], D)]
    return pl.pallas_call(
        functools.partial(prepare_kernel, shards),
        in_specs=[pl.BlockSpec(memory_space=pltpu.SMEM)]
        + [anywhere] * len(operands)
        + [vmem] * len(rows),
        out_specs=[vmem] * (len(rows) + len(shapes)),
        out_shape=[pltpu.VMEM((1, row.shape[0]), jnp.float32) for row in rows]
        + [pltpu.VMEM(shape, jnp.bfloat16) for shape in shapes],
        scratch_shapes=[
            pltpu.VMEM(qkv_weight.shape, jnp.bfloat16),
            pltpu.VMEM(spread.shape, jnp.bfloat16),
            pltpu.SemaphoreType.DMA((2 * shards + 3,)),
        ],
        compiler_params=pltpu.CompilerParams(vmem_limit_bytes=10 << 20),
        cost_estimate=pl.CostEstimate(
            flops=2 * spread.size * D,
            bytes_accessed=4 * (out_weight.size + merge_weight.size + qkv_weight.size),
            transcendentals=0,
        ),
        name="prepare",
    )(info, *map(in_hbm, operands), *rows)


def merge_kernel(start, counts, packs, last, *refs):
    inputs, weight, gain, merge_weight, bias = refs[:5]
    pieces = refs[5 : 5 + sum(counts)]
    *refs, state, tokens = refs[5 + sum(counts) :]
    rows = state.shape[1]
    half = rows // 2
    rest = 2 * HD - LANES
    sources, at = [], 0
    for count in counts:
        sources.append(stacked(pieces[at : at + count]))
        at += count
    shards = len(sources)
    lane = lax.broadcasted_iota(jnp.int32, (half, LANES), 1)
    for part in range(2):
        token = slice(part * half, (part + 1) * half)
        lined = [source[token, :] for source in sources]
        for pair in range(shards // 2):
            mine = sources[2 * pair][rows:, :].astype(jnp.float32)
            other = sources[2 * pair + 1][rows:, :].astype(jnp.float32)
            if part == 0:
                other = pltpu.roll(other, rest, 1)
            else:
                mine = pltpu.roll(mine, LANES - rest, 1)
            lined.append(jnp.where(lane < rest, mine, other).astype(jnp.bfloat16))
        mixed = jnp.dot(
            jnp.concatenate(lined, axis=1), weight[...], preferred_element_type=jnp.float32
        )
        for column in range(D // LANES):
            lanes = slice(column * LANES, (column + 1) * LANES)
            before = inputs[start + part * half : start + (part + 1) * half, lanes]
            state[column, token, :] = before.astype(jnp.float32) + mixed[:, lanes]
    groups = rows // 4
    for block in range(0, groups, NORM_ROWS):
        for quadrant in range(4):
            at = pl.ds(4 * block + quadrant, NORM_ROWS, stride=4)
            residual = jnp.concatenate(
                [state[column, at, :] for column in range(D // LANES)], axis=1
            )
            tokens[block : block + NORM_ROWS, quadrant * D : (quadrant + 1) * D] = norm_rows(
                residual, gain[...]
            ).astype(jnp.bfloat16)
    total = bias[...] + lax.dot_general(
        tokens[...], merge_weight[...], (((1,), (1,)), ((), ())), preferred_element_type=jnp.float32
    )
    total = total.astype(jnp.bfloat16)
    if not last:
        refs[0][...] = total
        return
    info, note, *earlier = refs[:-packs]
    outs = refs[-packs:]
    total = jnp.concatenate([*[one[...] for one in earlier], total], axis=0)
    whole = total.shape[1] // LANES
    most = outs[0].shape[0] * LANES // total.shape[1]
    notes = note[...].astype(jnp.float32)
    note_row = lax.broadcasted_iota(jnp.int32, notes.shape, 0)
    slot = lax.broadcasted_iota(jnp.int32, (most, total.shape[0]), 0)
    row = lax.broadcasted_iota(jnp.int32, (most, total.shape[0]), 1)
    for place, out in enumerate(outs):
        found = jnp.where(note_row == (info[PACK] ^ place), notes, 0.0)
        found = jnp.sum(found, axis=0, keepdims=True)
        first = (16.0 * found[:, :1] + found[:, 1:2]).astype(jnp.int32)
        length = (16.0 * found[:, 2:3] + found[:, 3:4]).astype(jnp.int32)
        chosen = (row == slot + first) & (slot < length)
        chosen = jnp.where(chosen, 1.0, 0.0).astype(jnp.bfloat16)
        block = jnp.dot(chosen, total, preferred_element_type=jnp.float32)
        for column in range(whole):
            out[column * most : (column + 1) * most, :] = block[
                :, column * LANES : (column + 1) * LANES
            ].astype(jnp.bfloat16)
        low = block[: most // 2, whole * LANES :]
        up = block[most // 2 :, whole * LANES :]
        out[whole * most :, :] = jnp.concatenate([low, up], axis=1).astype(jnp.bfloat16)


def merge_call(start, rows, sources, inputs, weight, gain, merge_weight, bias, packs, route):
    groups = rows // 4
    width = merge_weight.shape[0]
    pieces = [piece for source in sources for piece in source]
    vmem = pl.BlockSpec(memory_space=pltpu.VMEM)
    operands = [in_vmem(inputs), in_vmem(weight), gain, in_vmem(merge_weight), bias, *pieces]
    specs = [vmem] * len(operands)
    shapes = [jax.ShapeDtypeStruct((groups, width), jnp.bfloat16)]
    if route:
        me, most, *others = route
        operands += [me, *others]
        specs += [pl.BlockSpec(memory_space=pltpu.SMEM)] + [vmem] * len(others)
        shapes = [jax.ShapeDtypeStruct((most * width // LANES, LANES), jnp.bfloat16)] * packs
    return pl.pallas_call(
        functools.partial(
            merge_kernel, start, [len(source) for source in sources], packs, bool(route)
        ),
        in_specs=specs,
        out_specs=[vmem] * len(shapes),
        scratch_shapes=[
            pltpu.VMEM((D // LANES, rows, LANES), jnp.float32),
            pltpu.VMEM((groups, 4 * D), jnp.bfloat16),
        ],
        out_shape=shapes,
        compiler_params=pltpu.CompilerParams(vmem_limit_bytes=20 << 20),
        cost_estimate=pl.CostEstimate(
            flops=4 * rows * D * D + 2 * groups * merge_weight.size,
            bytes_accessed=2 * (D * D + merge_weight.size + 3 * rows * D),
            transcendentals=rows,
        ),
        name="out_merge",
    )(*operands)


def place_kernel(info, *refs):
    blocks, out = refs[:-1], refs[-1]
    most, width = out.shape[1:]
    whole = width // LANES
    half = most // 2
    middle = LANES // 2
    for place, block in enumerate(blocks):
        target = info[PACK] ^ place
        for column in range(whole):
            out[target, :, column * LANES : (column + 1) * LANES] = block[
                column * most : (column + 1) * most, :
            ]
        out[target, :half, whole * LANES :] = block[whole * most :, :middle]
        out[target, half:, whole * LANES :] = block[whole * most :, middle:]


def place_call(info, blocks, most, width):
    fixed = lambda shape: pl.BlockSpec(shape, lambda i: (0,) * len(shape))
    shape = (len(blocks), most, width)
    return pl.pallas_call(
        place_kernel,
        grid=(1,),
        in_specs=[pl.BlockSpec(memory_space=pltpu.SMEM)] + [fixed(one.shape) for one in blocks],
        out_specs=fixed(shape),
        out_shape=jax.ShapeDtypeStruct(shape, jnp.bfloat16),
        compiler_params=pltpu.CompilerParams(vmem_limit_bytes=8 << 20),
        cost_estimate=pl.CostEstimate(
            flops=0, bytes_accessed=4 * len(blocks) * most * width, transcendentals=0
        ),
        name="place_rows",
    )(info, *blocks)


def send_seq(value, flip):
    size = lax.axis_size("seq")
    return lax.ppermute(value, "seq", [(i, i ^ flip) for i in range(size)])


def after(values, *earlier):
    return lax.optimization_barrier((tuple(values), earlier))[0]


def halves_kernel(across_x, across_y, upper, lower):
    half = upper.shape[0]
    upper[...] = across_x[:half]
    lower[...] = across_y[half:]


def halves_call(across_x, across_y):
    vmem = pl.BlockSpec(memory_space=pltpu.VMEM)
    shape = (across_x.shape[0] // 2, across_x.shape[1])
    return pl.pallas_call(
        halves_kernel,
        in_specs=[vmem] * 2,
        out_specs=[vmem] * 2,
        out_shape=[jax.ShapeDtypeStruct(shape, across_x.dtype)] * 2,
        compiler_params=pltpu.CompilerParams(vmem_limit_bytes=4 << 20),
        cost_estimate=pl.CostEstimate(
            flops=0, bytes_accessed=4 * across_x.size, transcendentals=0
        ),
        name="halves",
    )(across_x, across_y)


def near_shards(value):
    return [send_seq(value, 1), send_seq(value, 2), send_seq(value, 4)]


def far_shards(across_x, across_y):
    upper, lower = halves_call(across_x, across_y)
    return [send_seq(upper, 4), send_seq(lower, 2)]


def weight_order(heads_here):
    quarter = HD // 4
    order = -np.ones((6 * LANES,), np.int32)
    for head in range(heads_here):
        base = head * 3 * HD
        for kind in range(2):
            for half in range(2):
                for letter in range(2):
                    target = (2 * kind + letter) * LANES + head * (HD // 2) + half * quarter
                    source = base + kind * HD + half * (HD // 2) + letter * quarter
                    order[target : target + quarter] = np.arange(source, source + quarter)
        target = (4 + head) * LANES
        order[target : target + HD] = np.arange(base + 2 * HD, base + 3 * HD)
    return order


def angle_table(heads_here):
    quarter = HD // 4
    frequency = (10000.0 ** (-np.arange(quarter) / quarter)).astype(np.float32)
    angles = np.arange(POSITIONS, dtype=np.float32)[:, None] * frequency[None, :]
    pieces = []
    for function in (np.cos, np.sin):
        exact = np.zeros((2 * POSITIONS, LANES), np.float64)
        for head in range(heads_here):
            for half in range(2):
                lane = head * (HD // 2) + half * quarter
                rows = slice(half * POSITIONS, (half + 1) * POSITIONS)
                exact[rows, lane : lane + quarter] = function(angles.astype(np.float64))
        upper = exact.astype(jnp.bfloat16)
        pieces += [upper, (exact - upper.astype(np.float64)).astype(jnp.bfloat16)]
    return np.concatenate(pieces, axis=1)


def fast_local(
    patches,
    patch_mask,
    mask_embed,
    norm_gain,
    qkv_weight,
    segment_ids,
    patch_rows,
    patch_column,
    out_weight,
    merge_gain,
    merge_weight,
    merge_bias,
    image_owner,
):
    local_rows = patches.shape[1]
    shards = lax.axis_size("seq")
    packs = lax.axis_size("pack")
    heads_here = HEADS // shards
    images = image_owner.shape[1]
    total = local_rows * shards
    me = lax.axis_index("seq").astype(jnp.int32)
    pack = lax.axis_index("pack").astype(jnp.int32)

    value = payload_call(segment_ids, patch_rows, patch_column, patch_mask, mask_embed, patches)
    own_swap, across_x, across_y = near_shards(value)

    order = weight_order(heads_here)
    spread = (order[:, None] == np.arange(qkv_weight.shape[1])[None, :]).astype(jnp.bfloat16)
    table = jnp.asarray(angle_table(heads_here))
    chip, core = me // 2, me % 2
    info = [chip, core, pack, *[me ^ place for place in range(shards)]]
    info = jnp.concatenate([jnp.stack(info), image_owner[0]])
    gain, merge_gain_row, bias, ordered, merge_rows, weight = prepare_call(
        shards,
        info,
        out_weight,
        merge_weight.T,
        qkv_weight.T,
        jnp.asarray(spread),
        (norm_gain, merge_gain, merge_bias),
    )

    project = lambda place, first, second, earlier: qkv_call(
        info, place, first, second, table, gain, weight, earlier, total
    )
    buffers = project(0, [value], [own_swap], ())
    across_x, across_y = after([across_x, across_y], buffers[2], ordered)
    far = far_shards(across_x, across_y)
    buffers = project(1, [across_x], [send_seq(across_x, 1)], buffers)
    buffers = project(2, [across_y], [send_seq(across_y, 1)], buffers)
    far = after(far, buffers[2])
    buffers = project(3, far, [send_seq(one, 1) for one in far], buffers)
    inputs, block, labels = buffers

    starts = [sum(CHUNKS[:number]) for number in range(len(CHUNKS))]
    attended, note = [], None
    for start, rows in zip(starts, CHUNKS):
        made = attention_call(start, rows, IDS + shards, info, labels, block, note is None)
        note = made[1] if note is None else note
        value = made[0]
        if attended:
            (value,) = after([value], *attended[-1][1])
        attended.append((value, near_shards(value)))
    latest = attended[-1][0]
    most = 2 * (total // 4) // images
    projected, moving = [], []
    for own, (own_swap, across_x, across_y) in attended:
        previous = moving[-1][-1] if moving else ()
        across_x, across_y = after([across_x, across_y], latest, *previous)
        far = far_shards(across_x, across_y)
        swapped = [across_x, across_y]
        if len(moving) < len(attended) - 1:
            swapped = after(swapped, *far)
        swap_x, swap_y = (send_seq(one, 1) for one in swapped)
        moving.append((own, own_swap, across_x, swap_x, across_y, swap_y, far))
    for number, (start, rows) in enumerate(zip(starts, CHUNKS)):
        *near, far = moving[number]
        if projected:
            far = after(far, projected[-1])
        sources = [[one] for one in near] + [far, [send_seq(one, 1) for one in far]]
        route = ()
        if number == len(CHUNKS) - 1:
            route = (info, most, note, *projected)
        made = merge_call(
            start, rows, sources, inputs, ordered, merge_gain_row, merge_rows, bias, packs, route
        )
        projected.append(made[0])
    blocks = [made[0]] + [
        lax.ppermute(made[flip], "pack", [(z, z ^ flip) for z in range(packs)])
        for flip in range(1, packs)
    ]
    return place_call(info, blocks, most, merge_weight.shape[1])[None]


def local(*arguments):
    patches, weight = arguments[0], arguments[4]
    shards = lax.axis_size("seq")
    fits = shards == 8 and HEADS // shards == 2 and weight.shape[1] == 6 * HD
    fits = fits and patches.shape[1] * shards == sum(CHUNKS) and lax.axis_size("pack") == 4
    return fast_local(*arguments) if fits else general_local(*arguments)


def solution(mesh):
    placed = (
        P("pack", "seq", None),
        P("pack", "seq"),
        P(),
        P(),
        P(None, "seq"),
        P("pack", "seq"),
        P("pack", "seq"),
        P("pack", "seq"),
        P(),
        P(),
        P(None, "seq"),
        P("seq"),
        P("pack", None),
    )
    return jax.shard_map(
        local, mesh=mesh, in_specs=placed, out_specs=P("pack", None, None, "seq"), check_vma=False
    )
```

```python
import functools

import jax
import jax.numpy as jnp
import numpy as np
from jax import lax
from jax.experimental import pallas as pl
from jax.experimental.pallas import tpu as pltpu
from jax.sharding import PartitionSpec as P

D = 1408
HEADS = 16
HD = 88


EPSILON = 1e-06


def layer_norm(values, gain_vector):
    center = values - jnp.mean(values, axis=-1, keepdims=True)
    spread = jnp.mean(center * center, axis=-1, keepdims=True)
    return center * lax.rsqrt(spread + EPSILON) * gain_vector.astype(jnp.float32)


def rotate(vectors, row_index, column_index):
    total_rows, heads_here, head_width = vectors.shape
    quarter = head_width // 4
    frequency = 10000.0 ** (-jnp.arange(quarter, dtype=jnp.float32) / quarter)
    row_angle = row_index.astype(jnp.float32)[:, None] * frequency[None, :]
    column_angle = column_index.astype(jnp.float32)[:, None] * frequency[None, :]
    angles = jnp.stack([row_angle, column_angle], axis=1)[:, None, :, None, :]
    split_up = vectors.reshape(total_rows, heads_here, 2, 2, quarter)
    partner = jnp.stack([-split_up[:, :, :, 1], split_up[:, :, :, 0]], axis=3)
    turned = split_up * jnp.cos(angles) + partner * jnp.sin(angles)
    return turned.reshape(total_rows, heads_here, head_width)


def qkv_block(projected, row_index, column_index):
    turned_queries = rotate(projected[:, :, 0], row_index, column_index)
    turned_keys = rotate(projected[:, :, 1], row_index, column_index)
    return jnp.concatenate([turned_queries, turned_keys, projected[:, :, 2]], axis=-1).astype(
        jnp.bfloat16
    )


def attention(block, segments):
    total_rows, heads_here, triple = block.shape
    head_width = triple // 3
    step_rows = min(512, total_rows)
    query_part = block[:, :, :head_width].reshape(
        total_rows // step_rows, step_rows, heads_here, head_width
    )
    key_part = block[:, :, head_width : 2 * head_width]
    value_part = block[:, :, 2 * head_width :]
    query_segments = segments.reshape(total_rows // step_rows, step_rows)
    scale = head_width ** (-0.5)

    def one_block(inputs_pair):
        queries_here, segments_here = inputs_pair
        scores = (
            jnp.einsum("qhd,khd->hqk", queries_here, key_part, preferred_element_type=jnp.float32)
            * scale
        )
        same_image = (segments_here[:, None] == segments[None, :])[None]
        scores = jnp.where(same_image, scores, -jnp.inf)
        highest = jnp.max(scores, axis=-1, keepdims=True)
        weights = jnp.exp(scores - highest)
        probs = (weights / jnp.sum(weights, axis=-1, keepdims=True)).astype(jnp.bfloat16)
        result = jnp.einsum("hqk,khd->qhd", probs, value_part, preferred_element_type=jnp.float32)
        return result.astype(jnp.bfloat16)

    return lax.map(one_block, (query_part, query_segments)).reshape(
        total_rows, heads_here, head_width
    )


def route(projected, segments, owners_here, packs, most):
    merged_segments = segments[::4]
    images = owners_here.shape[0]
    image_ids = jnp.arange(images, dtype=jnp.int32)
    member = (merged_segments[None, :] == image_ids[:, None]).astype(jnp.int32)
    lengths = jnp.sum(member, axis=1, dtype=jnp.int32)
    starts = jnp.cumsum(lengths, dtype=jnp.int32) - lengths
    owner_ids = jnp.arange(packs, dtype=jnp.int32)
    owned = owners_here[None, :] == owner_ids[:, None]
    first_row = jnp.sum(jnp.where(owned, starts[None, :], 0), axis=1, dtype=jnp.int32)
    owned_length = jnp.sum(jnp.where(owned, lengths[None, :], 0), axis=1, dtype=jnp.int32)
    slots = jnp.arange(most, dtype=jnp.int32)
    source_rows = jnp.clip(first_row[:, None] + slots[None, :], 0, projected.shape[0] - 1)
    picked = jnp.take(projected, source_rows.reshape(-1), axis=0).reshape(
        packs, most, projected.shape[1]
    )
    filled = slots[None, :] < owned_length[:, None]
    return jnp.where(filled[:, :, None], picked, jnp.zeros_like(picked))


def general_local(
    patches,
    patch_mask,
    mask_embed,
    norm_gain,
    qkv_weight,
    segment_ids,
    patch_rows,
    patch_column,
    out_weight,
    merge_gain,
    merge_weight,
    merge_bias,
    image_owner,
):
    local_rows = patches.shape[1]
    shards = lax.axis_size("seq")
    packs = lax.axis_size("pack")
    heads_here = HEADS // shards
    inputs = jnp.where(patch_mask[0][:, None] == 1, mask_embed[None, :], patches[0])
    normed = layer_norm(inputs.astype(jnp.float32), norm_gain).astype(jnp.bfloat16)
    labels = lax.all_gather(
        jnp.stack([segment_ids[0], patch_rows[0], patch_column[0]]), "seq", axis=1, tiled=True
    )
    piece = lax.all_gather(normed, "seq", axis=0, tiled=True)
    span = piece.shape[0]
    projected = jnp.dot(piece, qkv_weight, preferred_element_type=jnp.float32)
    row_part = labels[1]
    column_part = labels[2]
    block = qkv_block(projected.reshape(span, heads_here, 3, HD), row_part, column_part)
    result = attention(block, labels[0])
    mixed_heads = lax.all_to_all(result, "seq", split_axis=0, concat_axis=1, tiled=True)
    attended = mixed_heads.reshape(local_rows, D)
    residual = inputs.astype(jnp.float32) + jnp.dot(
        attended, out_weight, preferred_element_type=jnp.float32
    )
    merged = layer_norm(residual, merge_gain).astype(jnp.bfloat16).reshape(local_rows // 4, 4 * D)
    projected_all = (
        jnp.dot(
            lax.all_gather(merged, "seq", axis=0, tiled=True),
            merge_weight,
            preferred_element_type=jnp.float32,
        )
        + merge_bias.astype(jnp.float32)
    ).astype(jnp.bfloat16)
    images = image_owner.shape[1]
    most = 2 * projected_all.shape[0] // images
    outgoing = route(projected_all, labels[0], image_owner[0], packs, most)
    delivered = lax.all_to_all(outgoing, "pack", split_axis=0, concat_axis=0, tiled=True)
    return delivered[None]


LANES = 128
CHIP, CORE, PACK, IDS = 0, 1, 2, 3
BLOCK = 512
POSITIONS = 64
FAR_APART = -(2.0**100)
IMAGE_LANE = 96
NORM_ROWS = 16
CHUNKS = (768, 768)


def norm_rows(values, gain_row):
    center = values - jnp.mean(values, axis=-1, keepdims=True)
    spread = jnp.mean(center * center, axis=-1, keepdims=True)
    return center * lax.rsqrt(spread + EPSILON) * gain_row


def stacked(pieces):
    loaded = [piece[...] for piece in pieces]
    return loaded[0] if len(loaded) == 1 else jnp.concatenate(loaded, axis=0)


def in_vmem(value):
    return pltpu.with_memory_space_constraint(value, pltpu.VMEM)


def in_hbm(value):
    return pltpu.with_memory_space_constraint(value, pltpu.HBM)


def payload_kernel(segments, rows, columns, mask, embed, patches, out):
    labels = [one[...].astype(jnp.float32) for one in (segments, rows, columns, mask)]
    labels.append(jnp.zeros((4, labels[0].shape[1]), jnp.float32))
    labels = jnp.concatenate(labels, axis=0).astype(jnp.bfloat16)
    shape = (8, LANES)
    row = lax.broadcasted_iota(jnp.int32, shape, 0)
    place = jnp.where(row == lax.broadcasted_iota(jnp.int32, shape, 1), 1.0, 0.0)
    turned = lax.dot_general(
        labels,
        place.astype(jnp.bfloat16),
        (((0,), (0,)), ((), ())),
        preferred_element_type=jnp.float32,
    )
    masked = turned[:, 3:4] > 0.5
    tokens = jnp.where(
        masked, embed[...].astype(jnp.float32)[None, :], patches[0].astype(jnp.float32)
    )
    out[:, :D] = tokens.astype(jnp.bfloat16)
    out[:, D:] = turned.astype(jnp.bfloat16)


def payload_call(segments, rows, columns, mask, embed, patches):
    count = patches.shape[1]
    operands = (segments, rows, columns, mask, embed, patches)
    fixed = lambda shape: pl.BlockSpec(shape, lambda i: (0,) * len(shape))
    shape = (count, D + LANES)
    return pl.pallas_call(
        payload_kernel,
        grid=(1,),
        in_specs=[fixed(one.shape) for one in operands],
        out_specs=fixed(shape),
        out_shape=jax.ShapeDtypeStruct(shape, jnp.bfloat16),
        compiler_params=pltpu.CompilerParams(vmem_limit_bytes=8 << 20),
        cost_estimate=pl.CostEstimate(
            flops=count * D, bytes_accessed=4 * count * D, transcendentals=0
        ),
        name="payload",
    )(*map(in_hbm, operands))


def qkv_kernel(count, flip, info, *refs):
    first, second = refs[:count], refs[count : 2 * count]
    table, gain, weight = refs[2 * count : 2 * count + 3]
    inputs_out, qkv_out, label_out = refs[-3:]
    mine, other = stacked(first), stacked(second)
    leads = info[CORE] == 0
    ahead = jnp.where(leads, mine, other)
    behind = jnp.where(leads, other, mine)
    both = jnp.concatenate([ahead, behind], axis=0)
    rows = both.shape[0]
    at = pl.ds(pl.multiple_of((info[CHIP] ^ flip) * rows, rows), rows)
    inputs_out[at, :] = both[:, :D]
    label_out[at, :] = both[:, D:]
    labels = both[:, D:].astype(jnp.float32)
    normed = norm_rows(both[:, :D].astype(jnp.float32), gain[...]).astype(jnp.bfloat16)
    columns = lax.dot_general(
        normed, weight[...], (((1,), (1,)), ((), ())), preferred_element_type=jnp.float32
    )
    lane = lax.broadcasted_iota(jnp.int32, labels.shape, 1)
    numbers = lane.astype(jnp.float32)
    hot = (numbers == labels[:, 1:2]) | (numbers == labels[:, 2:3] + POSITIONS)
    looked = jnp.dot(
        jnp.where(hot, 1.0, 0.0).astype(jnp.bfloat16), table[...], preferred_element_type=jnp.float32
    )
    cosine = looked[:, :LANES] + looked[:, LANES : 2 * LANES]
    sine = looked[:, 2 * LANES : 3 * LANES] + looked[:, 3 * LANES :]
    first_head = lane < HD // 2

    def turn(start):
        a = columns[:, start : start + LANES]
        b = columns[:, start + LANES : start + 2 * LANES]
        return a * cosine - b * sine, b * cosine + a * sine

    factor = HD**-0.5 * float(np.log2(np.e))
    query_a, query_b = (one * factor for one in turn(0))
    key_a, key_b = turn(2 * LANES)
    zero = jnp.zeros_like(key_a)
    image = numbers == labels[:, :1] + IMAGE_LANE
    extra = lane >= IMAGE_LANE
    apart = jnp.where(image, 0.0, FAR_APART)
    parts = [
        jnp.where(image, 1.0, query_a),
        query_b,
        jnp.where(extra, apart, jnp.where(first_head, key_a, zero)),
        jnp.where(first_head, key_b, zero),
        jnp.where(extra, apart, jnp.where(first_head, zero, key_a)),
        jnp.where(first_head, zero, key_b),
    ]
    for head in range(2):
        values = columns[:, (4 + head) * LANES : (5 + head) * LANES]
        parts.append(jnp.where(lane == HD, 1.0, values))
    for number, part in enumerate(parts):
        qkv_out[at, number * LANES : (number + 1) * LANES] = part.astype(jnp.bfloat16)


def qkv_call(info, flip, first, second, table, gain, weight, earlier, total):
    rows = 2 * sum(piece.shape[0] for piece in first)
    widths = (D, 8 * LANES, LANES)
    operands = [*first, *second, table, gain, in_vmem(weight)]
    vmem = pl.BlockSpec(memory_space=pltpu.VMEM)
    held = [in_vmem(one) for one in earlier]
    return pl.pallas_call(
        functools.partial(qkv_kernel, len(first), flip),
        in_specs=[pl.BlockSpec(memory_space=pltpu.SMEM)]
        + [vmem] * (len(operands) + len(earlier)),
        out_specs=[vmem] * len(widths),
        out_shape=[pltpu.VMEM((total, width), jnp.bfloat16) for width in widths],
        input_output_aliases={1 + len(operands) + i: i for i in range(len(earlier))},
        compiler_params=pltpu.CompilerParams(vmem_limit_bytes=14 << 20),
        cost_estimate=pl.CostEstimate(
            flops=6 * rows * D * weight.shape[0],
            bytes_accessed=2 * (rows * 4 * D + weight.size),
            transcendentals=rows,
        ),
        name="norm_qkv",
    )(info, *operands, *held)


def segment_row(labels):
    pick = jnp.where(lax.broadcasted_iota(jnp.int32, (8, LANES), 1) == 0, 1.0, 0.0)
    return lax.dot_general(
        pick.astype(jnp.bfloat16),
        labels,
        (((1,), (1,)), ((), ())),
        preferred_element_type=jnp.float32,
    )


def attention_kernel(start, first_owner, images, info, labels, block, *refs):
    out, *rest = refs
    scores, high = rest[-2:]
    rows = high.shape[1]
    total = block.shape[0]
    segments = segment_row(labels[...])
    own = labels[start : start + rows, :1].astype(jnp.float32)
    lowest, largest = jnp.min(own), jnp.max(own)
    one_row = segments[:1]
    begin = jnp.sum(jnp.where(one_row < lowest, 1, 0)) // BLOCK
    end = (jnp.sum(jnp.where(one_row <= largest, 1, 0)) + BLOCK - 1) // BLOCK
    queries = block[start : start + rows, : 2 * LANES]
    high[...] = jnp.full_like(high, 2 * FAR_APART)

    def score(step, carry):
        at = pl.ds(pl.multiple_of(step * BLOCK, BLOCK), BLOCK)
        for head in range(2):
            keys = block[at, (2 + 2 * head) * LANES : (4 + 2 * head) * LANES]
            values = lax.dot_general(
                queries, keys, (((1,), (1,)), ((), ())), preferred_element_type=jnp.float32
            )
            scores[head, step] = values
            tops = [values[:, lane : lane + LANES] for lane in range(0, BLOCK, LANES)]
            high[head] = functools.reduce(jnp.maximum, tops, high[head])
        return carry

    lax.fori_loop(begin, end, score, 0)
    highest = [jnp.max(high[head], axis=-1, keepdims=True) for head in range(2)]

    def weigh(step, carry):
        at = pl.ds(pl.multiple_of(step * BLOCK, BLOCK), BLOCK)
        sums = []
        for head in range(2):
            weights = jnp.exp2(scores[head, step] - highest[head])
            values = block[at, (6 + head) * LANES : (7 + head) * LANES]
            sums.append(
                carry[head]
                + jnp.dot(weights.astype(jnp.bfloat16), values, preferred_element_type=jnp.float32)
            )
        return tuple(sums)

    zero = jnp.zeros((rows, LANES), jnp.float32)
    sums = lax.fori_loop(begin, end, weigh, (zero, zero))
    first, second = (one / one[:, HD : HD + 1] for one in sums)
    lane = lax.broadcasted_iota(jnp.int32, first.shape, 1)
    turned = pltpu.roll(second, HD, 1)
    out[:rows] = jnp.where(lane < HD, first, turned).astype(jnp.bfloat16)
    half = rows // 2
    tail = 2 * HD - LANES
    lane = lane[:half]
    up = pltpu.roll(turned[half:], tail, 1)
    packed = jnp.where(lane < tail, turned[:half], jnp.where(lane < 2 * tail, up, 0.0))
    out[rows:] = packed.astype(jnp.bfloat16)

    if len(rest) > 2:
        note = rest[0]
        row = lax.broadcasted_iota(jnp.int32, note.shape, 0)
        lane = lax.broadcasted_iota(jnp.int32, note.shape, 1)
        found = jnp.zeros(note.shape, jnp.float32)
        for image in range(images):
            below = jnp.sum(jnp.where(one_row < image, 0.25, 0.0), axis=1, keepdims=True)
            inside = jnp.sum(jnp.where(one_row == image, 0.25, 0.0), axis=1, keepdims=True)
            here = row == info[first_owner + image]
            for place, number in enumerate((below, inside)):
                upper = jnp.floor(number * (1.0 / 16))
                found = jnp.where(here & (lane == 2 * place), upper, found)
                found = jnp.where(here & (lane == 2 * place + 1), number - 16 * upper, found)
        note[...] = found.astype(jnp.bfloat16)


def attention_call(start, rows, first_owner, info, labels, block, noted):
    total = block.shape[0]
    vmem = pl.BlockSpec(memory_space=pltpu.VMEM)
    shapes = [jax.ShapeDtypeStruct((rows + rows // 2, LANES), jnp.bfloat16)]
    if noted:
        shapes.append(jax.ShapeDtypeStruct((16, LANES), jnp.bfloat16))
    return pl.pallas_call(
        functools.partial(attention_kernel, start, first_owner, info.shape[0] - first_owner),
        in_specs=[pl.BlockSpec(memory_space=pltpu.SMEM), vmem, vmem],
        out_specs=[vmem] * len(shapes),
        out_shape=shapes,
        scratch_shapes=[
            pltpu.VMEM((2, total // BLOCK, rows, BLOCK), jnp.float32),
            pltpu.VMEM((2, rows, LANES), jnp.float32),
        ],
        compiler_params=pltpu.CompilerParams(vmem_limit_bytes=20 << 20),
        cost_estimate=pl.CostEstimate(
            flops=10 * rows * total * 2 * LANES,
            bytes_accessed=2 * block.size,
            transcendentals=rows * total,
        ),
        name="attention",
    )(info, in_vmem(labels), in_vmem(block))


def prepare_kernel(shards, info, out_weight, merge_weight, qkv_weight, spread, *refs):
    *rows, out, merge, qkv, qkv_buffer, spread_buffer, sems = refs
    for row, row_out in zip(rows[: len(rows) // 2], rows[len(rows) // 2 :]):
        row_out[...] = row[...].astype(jnp.float32)[None, :]
    rest = 2 * HD - LANES
    copies = [(qkv_weight, qkv_buffer), (spread, spread_buffer)]
    out[shards * LANES :] = jnp.zeros((shards // 2 * LANES, D), jnp.bfloat16)
    for place in range(shards):
        start = pl.multiple_of(info[IDS + place] * (2 * HD), 16)
        to = (shards + place // 2) * LANES + place % 2 * rest
        copies.append(
            (out_weight.at[pl.ds(start, LANES), :], out.at[pl.ds(place * LANES, LANES), :])
        )
        copies.append((out_weight.at[pl.ds(start + LANES, rest), :], out.at[pl.ds(to, rest), :]))
    copies.append((merge_weight, merge))
    copies = [
        pltpu.make_async_copy(source, target, sems.at[i])
        for i, (source, target) in enumerate(copies)
    ]
    for copy in copies:
        copy.start()
    copies[0].wait()
    copies[1].wait()
    qkv[...] = jnp.dot(
        spread_buffer[...], qkv_buffer[...], preferred_element_type=jnp.float32
    ).astype(jnp.bfloat16)
    for copy in copies[2:]:
        copy.wait()


def prepare_call(shards, info, out_weight, merge_weight, qkv_weight, spread, rows):
    anywhere = pl.BlockSpec(memory_space=pl.ANY)
    vmem = pl.BlockSpec(memory_space=pltpu.VMEM)
    operands = (out_weight, merge_weight, qkv_weight, spread)
    shapes = [(shards * LANES * 3 // 2, D), merge_weight.shape, (spread.shape[0], D)]
    return pl.pallas_call(
        functools.partial(prepare_kernel, shards),
        in_specs=[pl.BlockSpec(memory_space=pltpu.SMEM)]
        + [anywhere] * len(operands)
        + [vmem] * len(rows),
        out_specs=[vmem] * (len(rows) + len(shapes)),
        out_shape=[pltpu.VMEM((1, row.shape[0]), jnp.float32) for row in rows]
        + [pltpu.VMEM(shape, jnp.bfloat16) for shape in shapes],
        scratch_shapes=[
            pltpu.VMEM(qkv_weight.shape, jnp.bfloat16),
            pltpu.VMEM(spread.shape, jnp.bfloat16),
            pltpu.SemaphoreType.DMA((2 * shards + 3,)),
        ],
        compiler_params=pltpu.CompilerParams(vmem_limit_bytes=10 << 20),
        cost_estimate=pl.CostEstimate(
            flops=2 * spread.size * D,
            bytes_accessed=4 * (out_weight.size + merge_weight.size + qkv_weight.size),
            transcendentals=0,
        ),
        name="prepare",
    )(info, *map(in_hbm, operands), *rows)


def merge_kernel(start, counts, packs, last, *refs):
    inputs, weight, gain, merge_weight, bias = refs[:5]
    pieces = refs[5 : 5 + sum(counts)]
    *refs, state, tokens = refs[5 + sum(counts) :]
    rows = state.shape[1]
    half = rows // 2
    rest = 2 * HD - LANES
    sources, at = [], 0
    for count in counts:
        sources.append(stacked(pieces[at : at + count]))
        at += count
    shards = len(sources)
    lane = lax.broadcasted_iota(jnp.int32, (half, LANES), 1)
    for part in range(2):
        token = slice(part * half, (part + 1) * half)
        lined = [source[token, :] for source in sources]
        for pair in range(shards // 2):
            mine = sources[2 * pair][rows:, :].astype(jnp.float32)
            other = sources[2 * pair + 1][rows:, :].astype(jnp.float32)
            if part == 0:
                other = pltpu.roll(other, rest, 1)
            else:
                mine = pltpu.roll(mine, LANES - rest, 1)
            lined.append(jnp.where(lane < rest, mine, other).astype(jnp.bfloat16))
        mixed = jnp.dot(
            jnp.concatenate(lined, axis=1), weight[...], preferred_element_type=jnp.float32
        )
        for column in range(D // LANES):
            lanes = slice(column * LANES, (column + 1) * LANES)
            before = inputs[start + part * half : start + (part + 1) * half, lanes]
            state[column, token, :] = before.astype(jnp.float32) + mixed[:, lanes]
    groups = rows // 4
    for block in range(0, groups, NORM_ROWS):
        for quadrant in range(4):
            at = pl.ds(4 * block + quadrant, NORM_ROWS, stride=4)
            residual = jnp.concatenate(
                [state[column, at, :] for column in range(D // LANES)], axis=1
            )
            tokens[block : block + NORM_ROWS, quadrant * D : (quadrant + 1) * D] = norm_rows(
                residual, gain[...]
            ).astype(jnp.bfloat16)
    total = bias[...] + lax.dot_general(
        tokens[...], merge_weight[...], (((1,), (1,)), ((), ())), preferred_element_type=jnp.float32
    )
    total = total.astype(jnp.bfloat16)
    if not last:
        refs[0][...] = total
        return
    info, note, *earlier = refs[:-packs]
    outs = refs[-packs:]
    total = jnp.concatenate([*[one[...] for one in earlier], total], axis=0)
    whole = total.shape[1] // LANES
    most = outs[0].shape[0] * LANES // total.shape[1]
    notes = note[...].astype(jnp.float32)
    note_row = lax.broadcasted_iota(jnp.int32, notes.shape, 0)
    slot = lax.broadcasted_iota(jnp.int32, (most, total.shape[0]), 0)
    row = lax.broadcasted_iota(jnp.int32, (most, total.shape[0]), 1)
    for place, out in enumerate(outs):
        found = jnp.where(note_row == (info[PACK] ^ place), notes, 0.0)
        found = jnp.sum(found, axis=0, keepdims=True)
        first = (16.0 * found[:, :1] + found[:, 1:2]).astype(jnp.int32)
        length = (16.0 * found[:, 2:3] + found[:, 3:4]).astype(jnp.int32)
        chosen = (row == slot + first) & (slot < length)
        chosen = jnp.where(chosen, 1.0, 0.0).astype(jnp.bfloat16)
        block = jnp.dot(chosen, total, preferred_element_type=jnp.float32)
        for column in range(whole):
            out[column * most : (column + 1) * most, :] = block[
                :, column * LANES : (column + 1) * LANES
            ].astype(jnp.bfloat16)
        low = block[: most // 2, whole * LANES :]
        up = block[most // 2 :, whole * LANES :]
        out[whole * most :, :] = jnp.concatenate([low, up], axis=1).astype(jnp.bfloat16)


def merge_call(start, rows, sources, inputs, weight, gain, merge_weight, bias, packs, route):
    groups = rows // 4
    width = merge_weight.shape[0]
    pieces = [piece for source in sources for piece in source]
    vmem = pl.BlockSpec(memory_space=pltpu.VMEM)
    operands = [in_vmem(inputs), in_vmem(weight), gain, in_vmem(merge_weight), bias, *pieces]
    specs = [vmem] * len(operands)
    shapes = [jax.ShapeDtypeStruct((groups, width), jnp.bfloat16)]
    if route:
        me, most, *others = route
        operands += [me, *others]
        specs += [pl.BlockSpec(memory_space=pltpu.SMEM)] + [vmem] * len(others)
        shapes = [jax.ShapeDtypeStruct((most * width // LANES, LANES), jnp.bfloat16)] * packs
    return pl.pallas_call(
        functools.partial(
            merge_kernel, start, [len(source) for source in sources], packs, bool(route)
        ),
        in_specs=specs,
        out_specs=[vmem] * len(shapes),
        scratch_shapes=[
            pltpu.VMEM((D // LANES, rows, LANES), jnp.float32),
            pltpu.VMEM((groups, 4 * D), jnp.bfloat16),
        ],
        out_shape=shapes,
        compiler_params=pltpu.CompilerParams(vmem_limit_bytes=20 << 20),
        cost_estimate=pl.CostEstimate(
            flops=4 * rows * D * D + 2 * groups * merge_weight.size,
            bytes_accessed=2 * (D * D + merge_weight.size + 3 * rows * D),
            transcendentals=rows,
        ),
        name="out_merge",
    )(*operands)


def place_kernel(info, *refs):
    blocks, out = refs[:-1], refs[-1]
    most, width = out.shape[1:]
    whole = width // LANES
    half = most // 2
    middle = LANES // 2
    for place, block in enumerate(blocks):
        target = info[PACK] ^ place
        for column in range(whole):
            out[target, :, column * LANES : (column + 1) * LANES] = block[
                column * most : (column + 1) * most, :
            ]
        out[target, :half, whole * LANES :] = block[whole * most :, :middle]
        out[target, half:, whole * LANES :] = block[whole * most :, middle:]


def place_call(info, blocks, most, width):
    fixed = lambda shape: pl.BlockSpec(shape, lambda i: (0,) * len(shape))
    shape = (len(blocks), most, width)
    return pl.pallas_call(
        place_kernel,
        grid=(1,),
        in_specs=[pl.BlockSpec(memory_space=pltpu.SMEM)] + [fixed(one.shape) for one in blocks],
        out_specs=fixed(shape),
        out_shape=jax.ShapeDtypeStruct(shape, jnp.bfloat16),
        compiler_params=pltpu.CompilerParams(vmem_limit_bytes=8 << 20),
        cost_estimate=pl.CostEstimate(
            flops=0, bytes_accessed=4 * len(blocks) * most * width, transcendentals=0
        ),
        name="place_rows",
    )(info, *blocks)


def send_seq(value, flip):
    size = lax.axis_size("seq")
    return lax.ppermute(value, "seq", [(i, i ^ flip) for i in range(size)])


def after(values, *earlier):
    return lax.optimization_barrier((tuple(values), earlier))[0]


def halves_kernel(across_x, across_y, upper, lower):
    half = upper.shape[0]
    upper[...] = across_x[:half]
    lower[...] = across_y[half:]


def halves_call(across_x, across_y):
    vmem = pl.BlockSpec(memory_space=pltpu.VMEM)
    shape = (across_x.shape[0] // 2, across_x.shape[1])
    return pl.pallas_call(
        halves_kernel,
        in_specs=[vmem] * 2,
        out_specs=[vmem] * 2,
        out_shape=[jax.ShapeDtypeStruct(shape, across_x.dtype)] * 2,
        compiler_params=pltpu.CompilerParams(vmem_limit_bytes=4 << 20),
        cost_estimate=pl.CostEstimate(
            flops=0, bytes_accessed=4 * across_x.size, transcendentals=0
        ),
        name="halves",
    )(across_x, across_y)


def near_shards(value):
    return [send_seq(value, 1), send_seq(value, 2), send_seq(value, 4)]


def far_shards(across_x, across_y):
    upper, lower = halves_call(across_x, across_y)
    return [send_seq(upper, 4), send_seq(lower, 2)]


def weight_order(heads_here):
    quarter = HD // 4
    order = -np.ones((6 * LANES,), np.int32)
    for head in range(heads_here):
        base = head * 3 * HD
        for kind in range(2):
            for half in range(2):
                for letter in range(2):
                    target = (2 * kind + letter) * LANES + head * (HD // 2) + half * quarter
                    source = base + kind * HD + half * (HD // 2) + letter * quarter
                    order[target : target + quarter] = np.arange(source, source + quarter)
        target = (4 + head) * LANES
        order[target : target + HD] = np.arange(base + 2 * HD, base + 3 * HD)
    return order


def angle_table(heads_here):
    quarter = HD // 4
    frequency = (10000.0 ** (-np.arange(quarter) / quarter)).astype(np.float32)
    angles = np.arange(POSITIONS, dtype=np.float32)[:, None] * frequency[None, :]
    pieces = []
    for function in (np.cos, np.sin):
        exact = np.zeros((2 * POSITIONS, LANES), np.float64)
        for head in range(heads_here):
            for half in range(2):
                lane = head * (HD // 2) + half * quarter
                rows = slice(half * POSITIONS, (half + 1) * POSITIONS)
                exact[rows, lane : lane + quarter] = function(angles.astype(np.float64))
        upper = exact.astype(jnp.bfloat16)
        pieces += [upper, (exact - upper.astype(np.float64)).astype(jnp.bfloat16)]
    return np.concatenate(pieces, axis=1)


def fast_local(
    patches,
    patch_mask,
    mask_embed,
    norm_gain,
    qkv_weight,
    segment_ids,
    patch_rows,
    patch_column,
    out_weight,
    merge_gain,
    merge_weight,
    merge_bias,
    image_owner,
):
    local_rows = patches.shape[1]
    shards = lax.axis_size("seq")
    packs = lax.axis_size("pack")
    heads_here = HEADS // shards
    images = image_owner.shape[1]
    total = local_rows * shards
    me = lax.axis_index("seq").astype(jnp.int32)
    pack = lax.axis_index("pack").astype(jnp.int32)

    value = payload_call(segment_ids, patch_rows, patch_column, patch_mask, mask_embed, patches)
    own_swap, across_x, across_y = near_shards(value)

    order = weight_order(heads_here)
    spread = (order[:, None] == np.arange(qkv_weight.shape[1])[None, :]).astype(jnp.bfloat16)
    table = jnp.asarray(angle_table(heads_here))
    chip, core = me // 2, me % 2
    info = [chip, core, pack, *[me ^ place for place in range(shards)]]
    info = jnp.concatenate([jnp.stack(info), image_owner[0]])
    gain, merge_gain_row, bias, ordered, merge_rows, weight = prepare_call(
        shards,
        info,
        out_weight,
        merge_weight.T,
        qkv_weight.T,
        jnp.asarray(spread),
        (norm_gain, merge_gain, merge_bias),
    )

    project = lambda place, first, second, earlier: qkv_call(
        info, place, first, second, table, gain, weight, earlier, total
    )
    buffers = project(0, [value], [own_swap], ())
    across_x, across_y = after([across_x, across_y], buffers[2], ordered)
    far = far_shards(across_x, across_y)
    buffers = project(1, [across_x], [send_seq(across_x, 1)], buffers)
    buffers = project(2, [across_y], [send_seq(across_y, 1)], buffers)
    far = after(far, buffers[2])
    buffers = project(3, far, [send_seq(one, 1) for one in far], buffers)
    inputs, block, labels = buffers

    starts = [sum(CHUNKS[:number]) for number in range(len(CHUNKS))]
    attended, note = [], None
    for start, rows in zip(starts, CHUNKS):
        made = attention_call(start, rows, IDS + shards, info, labels, block, note is None)
        note = made[1] if note is None else note
        value = made[0]
        if attended:
            (value,) = after([value], *attended[-1][1])
        attended.append((value, near_shards(value)))
    latest = attended[-1][0]
    most = 2 * (total // 4) // images
    projected, moving = [], []
    for own, (own_swap, across_x, across_y) in attended:
        previous = moving[-1][-1] if moving else ()
        across_x, across_y = after([across_x, across_y], latest, *previous)
        swapped = [across_x, across_y]
        if len(moving) < len(attended) - 1:
            far = far_shards(across_x, across_y)
            swapped = after(swapped, *far)
        else:
            far = [send_seq(own, 6)]
        swap_x, swap_y = (send_seq(one, 1) for one in swapped)
        moving.append((own, own_swap, across_x, swap_x, across_y, swap_y, far))
    for number, (start, rows) in enumerate(zip(starts, CHUNKS)):
        *near, far = moving[number]
        if projected:
            far = after(far, projected[-1])
        sources = [[one] for one in near] + [far, [send_seq(one, 1) for one in far]]
        route = ()
        if number == len(CHUNKS) - 1:
            route = (info, most, note, *projected)
        made = merge_call(
            start, rows, sources, inputs, ordered, merge_gain_row, merge_rows, bias, packs, route
        )
        projected.append(made[0])
    blocks = [made[0]] + [
        lax.ppermute(made[flip], "pack", [(z, z ^ flip) for z in range(packs)])
        for flip in range(1, packs)
    ]
    return place_call(info, blocks, most, merge_weight.shape[1])[None]


def local(*arguments):
    patches, weight = arguments[0], arguments[4]
    shards = lax.axis_size("seq")
    fits = shards == 8 and HEADS // shards == 2 and weight.shape[1] == 6 * HD
    fits = fits and patches.shape[1] * shards == sum(CHUNKS) and lax.axis_size("pack") == 4
    return fast_local(*arguments) if fits else general_local(*arguments)


def solution(mesh):
    placed = (
        P("pack", "seq", None),
        P("pack", "seq"),
        P(),
        P(),
        P(None, "seq"),
        P("pack", "seq"),
        P("pack", "seq"),
        P("pack", "seq"),
        P(),
        P(),
        P(None, "seq"),
        P("seq"),
        P("pack", None),
    )
    return jax.shard_map(
        local, mesh=mesh, in_specs=placed, out_specs=P("pack", None, None, "seq"), check_vma=False
    )
```

```python
import functools

import jax
import jax.numpy as jnp
import numpy as np
from jax import lax
from jax.experimental import pallas as pl
from jax.experimental.pallas import tpu as pltpu
from jax.sharding import PartitionSpec as P

D = 1408
HEADS = 16
HD = 88


EPSILON = 1e-06


def layer_norm(values, gain_vector):
    center = values - jnp.mean(values, axis=-1, keepdims=True)
    spread = jnp.mean(center * center, axis=-1, keepdims=True)
    return center * lax.rsqrt(spread + EPSILON) * gain_vector.astype(jnp.float32)


def rotate(vectors, row_index, column_index):
    total_rows, heads_here, head_width = vectors.shape
    quarter = head_width // 4
    frequency = 10000.0 ** (-jnp.arange(quarter, dtype=jnp.float32) / quarter)
    row_angle = row_index.astype(jnp.float32)[:, None] * frequency[None, :]
    column_angle = column_index.astype(jnp.float32)[:, None] * frequency[None, :]
    angles = jnp.stack([row_angle, column_angle], axis=1)[:, None, :, None, :]
    split_up = vectors.reshape(total_rows, heads_here, 2, 2, quarter)
    partner = jnp.stack([-split_up[:, :, :, 1], split_up[:, :, :, 0]], axis=3)
    turned = split_up * jnp.cos(angles) + partner * jnp.sin(angles)
    return turned.reshape(total_rows, heads_here, head_width)


def qkv_block(projected, row_index, column_index):
    turned_queries = rotate(projected[:, :, 0], row_index, column_index)
    turned_keys = rotate(projected[:, :, 1], row_index, column_index)
    return jnp.concatenate([turned_queries, turned_keys, projected[:, :, 2]], axis=-1).astype(
        jnp.bfloat16
    )


def attention(block, segments):
    total_rows, heads_here, triple = block.shape
    head_width = triple // 3
    step_rows = min(512, total_rows)
    query_part = block[:, :, :head_width].reshape(
        total_rows // step_rows, step_rows, heads_here, head_width
    )
    key_part = block[:, :, head_width : 2 * head_width]
    value_part = block[:, :, 2 * head_width :]
    query_segments = segments.reshape(total_rows // step_rows, step_rows)
    scale = head_width ** (-0.5)

    def one_block(inputs_pair):
        queries_here, segments_here = inputs_pair
        scores = (
            jnp.einsum("qhd,khd->hqk", queries_here, key_part, preferred_element_type=jnp.float32)
            * scale
        )
        same_image = (segments_here[:, None] == segments[None, :])[None]
        scores = jnp.where(same_image, scores, -jnp.inf)
        highest = jnp.max(scores, axis=-1, keepdims=True)
        weights = jnp.exp(scores - highest)
        probs = (weights / jnp.sum(weights, axis=-1, keepdims=True)).astype(jnp.bfloat16)
        result = jnp.einsum("hqk,khd->qhd", probs, value_part, preferred_element_type=jnp.float32)
        return result.astype(jnp.bfloat16)

    return lax.map(one_block, (query_part, query_segments)).reshape(
        total_rows, heads_here, head_width
    )


def route(projected, segments, owners_here, packs, most):
    merged_segments = segments[::4]
    images = owners_here.shape[0]
    image_ids = jnp.arange(images, dtype=jnp.int32)
    member = (merged_segments[None, :] == image_ids[:, None]).astype(jnp.int32)
    lengths = jnp.sum(member, axis=1, dtype=jnp.int32)
    starts = jnp.cumsum(lengths, dtype=jnp.int32) - lengths
    owner_ids = jnp.arange(packs, dtype=jnp.int32)
    owned = owners_here[None, :] == owner_ids[:, None]
    first_row = jnp.sum(jnp.where(owned, starts[None, :], 0), axis=1, dtype=jnp.int32)
    owned_length = jnp.sum(jnp.where(owned, lengths[None, :], 0), axis=1, dtype=jnp.int32)
    slots = jnp.arange(most, dtype=jnp.int32)
    source_rows = jnp.clip(first_row[:, None] + slots[None, :], 0, projected.shape[0] - 1)
    picked = jnp.take(projected, source_rows.reshape(-1), axis=0).reshape(
        packs, most, projected.shape[1]
    )
    filled = slots[None, :] < owned_length[:, None]
    return jnp.where(filled[:, :, None], picked, jnp.zeros_like(picked))


def general_local(
    patches,
    patch_mask,
    mask_embed,
    norm_gain,
    qkv_weight,
    segment_ids,
    patch_rows,
    patch_column,
    out_weight,
    merge_gain,
    merge_weight,
    merge_bias,
    image_owner,
):
    local_rows = patches.shape[1]
    shards = lax.axis_size("seq")
    packs = lax.axis_size("pack")
    heads_here = HEADS // shards
    inputs = jnp.where(patch_mask[0][:, None] == 1, mask_embed[None, :], patches[0])
    normed = layer_norm(inputs.astype(jnp.float32), norm_gain).astype(jnp.bfloat16)
    labels = lax.all_gather(
        jnp.stack([segment_ids[0], patch_rows[0], patch_column[0]]), "seq", axis=1, tiled=True
    )
    piece = lax.all_gather(normed, "seq", axis=0, tiled=True)
    span = piece.shape[0]
    projected = jnp.dot(piece, qkv_weight, preferred_element_type=jnp.float32)
    row_part = labels[1]
    column_part = labels[2]
    block = qkv_block(projected.reshape(span, heads_here, 3, HD), row_part, column_part)
    result = attention(block, labels[0])
    mixed_heads = lax.all_to_all(result, "seq", split_axis=0, concat_axis=1, tiled=True)
    attended = mixed_heads.reshape(local_rows, D)
    residual = inputs.astype(jnp.float32) + jnp.dot(
        attended, out_weight, preferred_element_type=jnp.float32
    )
    merged = layer_norm(residual, merge_gain).astype(jnp.bfloat16).reshape(local_rows // 4, 4 * D)
    projected_all = (
        jnp.dot(
            lax.all_gather(merged, "seq", axis=0, tiled=True),
            merge_weight,
            preferred_element_type=jnp.float32,
        )
        + merge_bias.astype(jnp.float32)
    ).astype(jnp.bfloat16)
    images = image_owner.shape[1]
    most = 2 * projected_all.shape[0] // images
    outgoing = route(projected_all, labels[0], image_owner[0], packs, most)
    delivered = lax.all_to_all(outgoing, "pack", split_axis=0, concat_axis=0, tiled=True)
    return delivered[None]


LANES = 128
CHIP, CORE, PACK, IDS = 0, 1, 2, 3
BLOCK = 512
POSITIONS = 64
FAR_APART = -(2.0**100)
IMAGE_LANE = 96
NORM_ROWS = 16
CHUNKS = (768, 768)


def norm_rows(values, gain_row):
    center = values - jnp.mean(values, axis=-1, keepdims=True)
    spread = jnp.mean(center * center, axis=-1, keepdims=True)
    return center * lax.rsqrt(spread + EPSILON) * gain_row


def stacked(pieces):
    loaded = [piece[...] for piece in pieces]
    return loaded[0] if len(loaded) == 1 else jnp.concatenate(loaded, axis=0)


def in_vmem(value):
    return pltpu.with_memory_space_constraint(value, pltpu.VMEM)


def in_hbm(value):
    return pltpu.with_memory_space_constraint(value, pltpu.HBM)


def payload_kernel(segments, rows, columns, mask, embed, patches, out):
    labels = [one[...].astype(jnp.float32) for one in (segments, rows, columns, mask)]
    labels.append(jnp.zeros((4, labels[0].shape[1]), jnp.float32))
    labels = jnp.concatenate(labels, axis=0).astype(jnp.bfloat16)
    shape = (8, LANES)
    row = lax.broadcasted_iota(jnp.int32, shape, 0)
    place = jnp.where(row == lax.broadcasted_iota(jnp.int32, shape, 1), 1.0, 0.0)
    turned = lax.dot_general(
        labels,
        place.astype(jnp.bfloat16),
        (((0,), (0,)), ((), ())),
        preferred_element_type=jnp.float32,
    )
    masked = turned[:, 3:4] > 0.5
    tokens = jnp.where(
        masked, embed[...].astype(jnp.float32)[None, :], patches[0].astype(jnp.float32)
    )
    out[:, :D] = tokens.astype(jnp.bfloat16)
    out[:, D:] = turned.astype(jnp.bfloat16)


def payload_call(segments, rows, columns, mask, embed, patches):
    count = patches.shape[1]
    operands = (segments, rows, columns, mask, embed, patches)
    fixed = lambda shape: pl.BlockSpec(shape, lambda i: (0,) * len(shape))
    shape = (count, D + LANES)
    return pl.pallas_call(
        payload_kernel,
        grid=(1,),
        in_specs=[fixed(one.shape) for one in operands],
        out_specs=fixed(shape),
        out_shape=jax.ShapeDtypeStruct(shape, jnp.bfloat16),
        compiler_params=pltpu.CompilerParams(vmem_limit_bytes=8 << 20),
        cost_estimate=pl.CostEstimate(
            flops=count * D, bytes_accessed=4 * count * D, transcendentals=0
        ),
        name="payload",
    )(*map(in_hbm, operands))


def qkv_kernel(count, flip, info, *refs):
    first, second = refs[:count], refs[count : 2 * count]
    table, gain, weight = refs[2 * count : 2 * count + 3]
    inputs_out, qkv_out, label_out = refs[-3:]
    mine, other = stacked(first), stacked(second)
    leads = info[CORE] == 0
    ahead = jnp.where(leads, mine, other)
    behind = jnp.where(leads, other, mine)
    both = jnp.concatenate([ahead, behind], axis=0)
    rows = both.shape[0]
    at = pl.ds(pl.multiple_of((info[CHIP] ^ flip) * rows, rows), rows)
    inputs_out[at, :] = both[:, :D]
    label_out[at, :] = both[:, D:]
    labels = both[:, D:].astype(jnp.float32)
    normed = norm_rows(both[:, :D].astype(jnp.float32), gain[...]).astype(jnp.bfloat16)
    columns = lax.dot_general(
        normed, weight[...], (((1,), (1,)), ((), ())), preferred_element_type=jnp.float32
    )
    lane = lax.broadcasted_iota(jnp.int32, labels.shape, 1)
    numbers = lane.astype(jnp.float32)
    hot = (numbers == labels[:, 1:2]) | (numbers == labels[:, 2:3] + POSITIONS)
    looked = jnp.dot(
        jnp.where(hot, 1.0, 0.0).astype(jnp.bfloat16), table[...], preferred_element_type=jnp.float32
    )
    cosine = looked[:, :LANES] + looked[:, LANES : 2 * LANES]
    sine = looked[:, 2 * LANES : 3 * LANES] + looked[:, 3 * LANES :]
    first_head = lane < HD // 2

    def turn(start):
        a = columns[:, start : start + LANES]
        b = columns[:, start + LANES : start + 2 * LANES]
        return a * cosine - b * sine, b * cosine + a * sine

    factor = HD**-0.5 * float(np.log2(np.e))
    query_a, query_b = (one * factor for one in turn(0))
    key_a, key_b = turn(2 * LANES)
    zero = jnp.zeros_like(key_a)
    image = numbers == labels[:, :1] + IMAGE_LANE
    extra = lane >= IMAGE_LANE
    apart = jnp.where(image, 0.0, FAR_APART)
    parts = [
        jnp.where(image, 1.0, query_a),
        query_b,
        jnp.where(extra, apart, jnp.where(first_head, key_a, zero)),
        jnp.where(first_head, key_b, zero),
        jnp.where(extra, apart, jnp.where(first_head, zero, key_a)),
        jnp.where(first_head, zero, key_b),
    ]
    for head in range(2):
        values = columns[:, (4 + head) * LANES : (5 + head) * LANES]
        parts.append(jnp.where(lane == HD, 1.0, values))
    for number, part in enumerate(parts):
        qkv_out[at, number * LANES : (number + 1) * LANES] = part.astype(jnp.bfloat16)


def qkv_call(info, flip, first, second, table, gain, weight, earlier, total):
    rows = 2 * sum(piece.shape[0] for piece in first)
    widths = (D, 8 * LANES, LANES)
    operands = [*first, *second, table, gain, in_vmem(weight)]
    vmem = pl.BlockSpec(memory_space=pltpu.VMEM)
    held = [in_vmem(one) for one in earlier]
    return pl.pallas_call(
        functools.partial(qkv_kernel, len(first), flip),
        in_specs=[pl.BlockSpec(memory_space=pltpu.SMEM)]
        + [vmem] * (len(operands) + len(earlier)),
        out_specs=[vmem] * len(widths),
        out_shape=[pltpu.VMEM((total, width), jnp.bfloat16) for width in widths],
        input_output_aliases={1 + len(operands) + i: i for i in range(len(earlier))},
        compiler_params=pltpu.CompilerParams(vmem_limit_bytes=14 << 20),
        cost_estimate=pl.CostEstimate(
            flops=6 * rows * D * weight.shape[0],
            bytes_accessed=2 * (rows * 4 * D + weight.size),
            transcendentals=rows,
        ),
        name="norm_qkv",
    )(info, *operands, *held)


def segment_row(labels):
    pick = jnp.where(lax.broadcasted_iota(jnp.int32, (8, LANES), 1) == 0, 1.0, 0.0)
    return lax.dot_general(
        pick.astype(jnp.bfloat16),
        labels,
        (((1,), (1,)), ((), ())),
        preferred_element_type=jnp.float32,
    )


def attention_kernel(start, first_owner, images, info, labels, block, *refs):
    out, *rest = refs
    scores, high = rest[-2:]
    rows = high.shape[1]
    total = block.shape[0]
    segments = segment_row(labels[...])
    own = labels[start : start + rows, :1].astype(jnp.float32)
    lowest, largest = jnp.min(own), jnp.max(own)
    one_row = segments[:1]
    begin = jnp.sum(jnp.where(one_row < lowest, 1, 0)) // BLOCK
    end = (jnp.sum(jnp.where(one_row <= largest, 1, 0)) + BLOCK - 1) // BLOCK
    queries = block[start : start + rows, : 2 * LANES]
    high[...] = jnp.full_like(high, 2 * FAR_APART)

    def score(step, carry):
        at = pl.ds(pl.multiple_of(step * BLOCK, BLOCK), BLOCK)
        for head in range(2):
            keys = block[at, (2 + 2 * head) * LANES : (4 + 2 * head) * LANES]
            values = lax.dot_general(
                queries, keys, (((1,), (1,)), ((), ())), preferred_element_type=jnp.float32
            )
            scores[head, step] = values
            tops = [values[:, lane : lane + LANES] for lane in range(0, BLOCK, LANES)]
            high[head] = functools.reduce(jnp.maximum, tops, high[head])
        return carry

    lax.fori_loop(begin, end, score, 0)
    highest = [jnp.max(high[head], axis=-1, keepdims=True) for head in range(2)]

    def weigh(step, carry):
        at = pl.ds(pl.multiple_of(step * BLOCK, BLOCK), BLOCK)
        sums = []
        for head in range(2):
            weights = jnp.exp2(scores[head, step] - highest[head])
            values = block[at, (6 + head) * LANES : (7 + head) * LANES]
            sums.append(
                carry[head]
                + jnp.dot(weights.astype(jnp.bfloat16), values, preferred_element_type=jnp.float32)
            )
        return tuple(sums)

    zero = jnp.zeros((rows, LANES), jnp.float32)
    sums = lax.fori_loop(begin, end, weigh, (zero, zero))
    first, second = (one / one[:, HD : HD + 1] for one in sums)
    lane = lax.broadcasted_iota(jnp.int32, first.shape, 1)
    turned = pltpu.roll(second, HD, 1)
    out[:rows] = jnp.where(lane < HD, first, turned).astype(jnp.bfloat16)
    half = rows // 2
    tail = 2 * HD - LANES
    lane = lane[:half]
    up = pltpu.roll(turned[half:], tail, 1)
    packed = jnp.where(lane < tail, turned[:half], jnp.where(lane < 2 * tail, up, 0.0))
    out[rows:] = packed.astype(jnp.bfloat16)

    if len(rest) > 2:
        note = rest[0]
        row = lax.broadcasted_iota(jnp.int32, note.shape, 0)
        lane = lax.broadcasted_iota(jnp.int32, note.shape, 1)
        found = jnp.zeros(note.shape, jnp.float32)
        for image in range(images):
            below = jnp.sum(jnp.where(one_row < image, 0.25, 0.0), axis=1, keepdims=True)
            inside = jnp.sum(jnp.where(one_row == image, 0.25, 0.0), axis=1, keepdims=True)
            here = row == info[first_owner + image]
            for place, number in enumerate((below, inside)):
                upper = jnp.floor(number * (1.0 / 16))
                found = jnp.where(here & (lane == 2 * place), upper, found)
                found = jnp.where(here & (lane == 2 * place + 1), number - 16 * upper, found)
        note[...] = found.astype(jnp.bfloat16)


def attention_call(start, rows, first_owner, info, labels, block, noted):
    total = block.shape[0]
    vmem = pl.BlockSpec(memory_space=pltpu.VMEM)
    shapes = [jax.ShapeDtypeStruct((rows + rows // 2, LANES), jnp.bfloat16)]
    if noted:
        shapes.append(jax.ShapeDtypeStruct((16, LANES), jnp.bfloat16))
    return pl.pallas_call(
        functools.partial(attention_kernel, start, first_owner, info.shape[0] - first_owner),
        in_specs=[pl.BlockSpec(memory_space=pltpu.SMEM), vmem, vmem],
        out_specs=[vmem] * len(shapes),
        out_shape=shapes,
        scratch_shapes=[
            pltpu.VMEM((2, total // BLOCK, rows, BLOCK), jnp.float32),
            pltpu.VMEM((2, rows, LANES), jnp.float32),
        ],
        compiler_params=pltpu.CompilerParams(vmem_limit_bytes=20 << 20),
        cost_estimate=pl.CostEstimate(
            flops=10 * rows * total * 2 * LANES,
            bytes_accessed=2 * block.size,
            transcendentals=rows * total,
        ),
        name="attention",
    )(info, in_vmem(labels), in_vmem(block))


def prepare_kernel(shards, info, out_weight, merge_weight, qkv_weight, spread, *refs):
    *rows, out, merge, qkv, qkv_buffer, spread_buffer, sems = refs
    for row, row_out in zip(rows[: len(rows) // 2], rows[len(rows) // 2 :]):
        row_out[...] = row[...].astype(jnp.float32)[None, :]
    rest = 2 * HD - LANES
    copies = [(qkv_weight, qkv_buffer), (spread, spread_buffer)]
    out[shards * LANES :] = jnp.zeros((shards // 2 * LANES, D), jnp.bfloat16)
    for place in range(shards):
        start = pl.multiple_of(info[IDS + place] * (2 * HD), 16)
        to = (shards + place // 2) * LANES + place % 2 * rest
        copies.append(
            (out_weight.at[pl.ds(start, LANES), :], out.at[pl.ds(place * LANES, LANES), :])
        )
        copies.append((out_weight.at[pl.ds(start + LANES, rest), :], out.at[pl.ds(to, rest), :]))
    copies.append((merge_weight, merge))
    copies = [
        pltpu.make_async_copy(source, target, sems.at[i])
        for i, (source, target) in enumerate(copies)
    ]
    for copy in copies:
        copy.start()
    copies[0].wait()
    copies[1].wait()
    qkv[...] = jnp.dot(
        spread_buffer[...], qkv_buffer[...], preferred_element_type=jnp.float32
    ).astype(jnp.bfloat16)
    for copy in copies[2:]:
        copy.wait()


def prepare_call(shards, info, out_weight, merge_weight, qkv_weight, spread, rows):
    anywhere = pl.BlockSpec(memory_space=pl.ANY)
    vmem = pl.BlockSpec(memory_space=pltpu.VMEM)
    operands = (out_weight, merge_weight, qkv_weight, spread)
    shapes = [(shards * LANES * 3 // 2, D), merge_weight.shape, (spread.shape[0], D)]
    return pl.pallas_call(
        functools.partial(prepare_kernel, shards),
        in_specs=[pl.BlockSpec(memory_space=pltpu.SMEM)]
        + [anywhere] * len(operands)
        + [vmem] * len(rows),
        out_specs=[vmem] * (len(rows) + len(shapes)),
        out_shape=[pltpu.VMEM((1, row.shape[0]), jnp.float32) for row in rows]
        + [pltpu.VMEM(shape, jnp.bfloat16) for shape in shapes],
        scratch_shapes=[
            pltpu.VMEM(qkv_weight.shape, jnp.bfloat16),
            pltpu.VMEM(spread.shape, jnp.bfloat16),
            pltpu.SemaphoreType.DMA((2 * shards + 3,)),
        ],
        compiler_params=pltpu.CompilerParams(vmem_limit_bytes=10 << 20),
        cost_estimate=pl.CostEstimate(
            flops=2 * spread.size * D,
            bytes_accessed=4 * (out_weight.size + merge_weight.size + qkv_weight.size),
            transcendentals=0,
        ),
        name="prepare",
    )(info, *map(in_hbm, operands), *rows)


def merge_kernel(start, counts, packs, last, *refs):
    inputs, weight, gain, merge_weight, bias = refs[:5]
    pieces = refs[5 : 5 + sum(counts)]
    *refs, state, tokens = refs[5 + sum(counts) :]
    rows = state.shape[1]
    half = rows // 2
    rest = 2 * HD - LANES
    sources, at = [], 0
    for count in counts:
        sources.append(stacked(pieces[at : at + count]))
        at += count
    shards = len(sources)
    lane = lax.broadcasted_iota(jnp.int32, (half, LANES), 1)
    for part in range(2):
        token = slice(part * half, (part + 1) * half)
        lined = [source[token, :] for source in sources]
        for pair in range(shards // 2):
            mine = sources[2 * pair][rows:, :].astype(jnp.float32)
            other = sources[2 * pair + 1][rows:, :].astype(jnp.float32)
            if part == 0:
                other = pltpu.roll(other, rest, 1)
            else:
                mine = pltpu.roll(mine, LANES - rest, 1)
            lined.append(jnp.where(lane < rest, mine, other).astype(jnp.bfloat16))
        mixed = jnp.dot(
            jnp.concatenate(lined, axis=1), weight[...], preferred_element_type=jnp.float32
        )
        for column in range(D // LANES):
            lanes = slice(column * LANES, (column + 1) * LANES)
            before = inputs[start + part * half : start + (part + 1) * half, lanes]
            state[column, token, :] = before.astype(jnp.float32) + mixed[:, lanes]
    groups = rows // 4
    for block in range(0, groups, NORM_ROWS):
        for quadrant in range(4):
            at = pl.ds(4 * block + quadrant, NORM_ROWS, stride=4)
            residual = jnp.concatenate(
                [state[column, at, :] for column in range(D // LANES)], axis=1
            )
            tokens[block : block + NORM_ROWS, quadrant * D : (quadrant + 1) * D] = norm_rows(
                residual, gain[...]
            ).astype(jnp.bfloat16)
    total = bias[...] + lax.dot_general(
        tokens[...], merge_weight[...], (((1,), (1,)), ((), ())), preferred_element_type=jnp.float32
    )
    total = total.astype(jnp.bfloat16)
    if not last:
        refs[0][...] = total
        return
    info, note, *earlier = refs[:-packs]
    outs = refs[-packs:]
    total = jnp.concatenate([*[one[...] for one in earlier], total], axis=0)
    whole = total.shape[1] // LANES
    most = outs[0].shape[0] * LANES // total.shape[1]
    notes = note[...].astype(jnp.float32)
    note_row = lax.broadcasted_iota(jnp.int32, notes.shape, 0)
    slot = lax.broadcasted_iota(jnp.int32, (most, total.shape[0]), 0)
    row = lax.broadcasted_iota(jnp.int32, (most, total.shape[0]), 1)
    for place, out in enumerate(outs):
        found = jnp.where(note_row == (info[PACK] ^ place), notes, 0.0)
        found = jnp.sum(found, axis=0, keepdims=True)
        first = (16.0 * found[:, :1] + found[:, 1:2]).astype(jnp.int32)
        length = (16.0 * found[:, 2:3] + found[:, 3:4]).astype(jnp.int32)
        chosen = (row == slot + first) & (slot < length)
        chosen = jnp.where(chosen, 1.0, 0.0).astype(jnp.bfloat16)
        block = jnp.dot(chosen, total, preferred_element_type=jnp.float32)
        for column in range(whole):
            out[column * most : (column + 1) * most, :] = block[
                :, column * LANES : (column + 1) * LANES
            ].astype(jnp.bfloat16)
        low = block[: most // 2, whole * LANES :]
        up = block[most // 2 :, whole * LANES :]
        out[whole * most :, :] = jnp.concatenate([low, up], axis=1).astype(jnp.bfloat16)


def merge_call(start, rows, sources, inputs, weight, gain, merge_weight, bias, packs, route):
    groups = rows // 4
    width = merge_weight.shape[0]
    pieces = [piece for source in sources for piece in source]
    vmem = pl.BlockSpec(memory_space=pltpu.VMEM)
    operands = [in_vmem(inputs), in_vmem(weight), gain, in_vmem(merge_weight), bias, *pieces]
    specs = [vmem] * len(operands)
    shapes = [jax.ShapeDtypeStruct((groups, width), jnp.bfloat16)]
    if route:
        me, most, *others = route
        operands += [me, *others]
        specs += [pl.BlockSpec(memory_space=pltpu.SMEM)] + [vmem] * len(others)
        shapes = [jax.ShapeDtypeStruct((most * width // LANES, LANES), jnp.bfloat16)] * packs
    return pl.pallas_call(
        functools.partial(
            merge_kernel, start, [len(source) for source in sources], packs, bool(route)
        ),
        in_specs=specs,
        out_specs=[vmem] * len(shapes),
        scratch_shapes=[
            pltpu.VMEM((D // LANES, rows, LANES), jnp.float32),
            pltpu.VMEM((groups, 4 * D), jnp.bfloat16),
        ],
        out_shape=shapes,
        compiler_params=pltpu.CompilerParams(vmem_limit_bytes=20 << 20),
        cost_estimate=pl.CostEstimate(
            flops=4 * rows * D * D + 2 * groups * merge_weight.size,
            bytes_accessed=2 * (D * D + merge_weight.size + 3 * rows * D),
            transcendentals=rows,
        ),
        name="out_merge",
    )(*operands)


def place_kernel(info, *refs):
    blocks, out = refs[:-1], refs[-1]
    most, width = out.shape[1:]
    whole = width // LANES
    half = most // 2
    middle = LANES // 2
    for place, block in enumerate(blocks):
        target = info[PACK] ^ place
        for column in range(whole):
            out[target, :, column * LANES : (column + 1) * LANES] = block[
                column * most : (column + 1) * most, :
            ]
        out[target, :half, whole * LANES :] = block[whole * most :, :middle]
        out[target, half:, whole * LANES :] = block[whole * most :, middle:]


def place_call(info, blocks, most, width):
    fixed = lambda shape: pl.BlockSpec(shape, lambda i: (0,) * len(shape))
    shape = (len(blocks), most, width)
    return pl.pallas_call(
        place_kernel,
        grid=(1,),
        in_specs=[pl.BlockSpec(memory_space=pltpu.SMEM)] + [fixed(one.shape) for one in blocks],
        out_specs=fixed(shape),
        out_shape=jax.ShapeDtypeStruct(shape, jnp.bfloat16),
        compiler_params=pltpu.CompilerParams(vmem_limit_bytes=8 << 20),
        cost_estimate=pl.CostEstimate(
            flops=0, bytes_accessed=4 * len(blocks) * most * width, transcendentals=0
        ),
        name="place_rows",
    )(info, *blocks)


def send_seq(value, flip):
    size = lax.axis_size("seq")
    return lax.ppermute(value, "seq", [(i, i ^ flip) for i in range(size)])


def after(values, *earlier):
    return lax.optimization_barrier((tuple(values), earlier))[0]


def halves_kernel(across_x, across_y, upper, lower):
    half = upper.shape[0]
    upper[...] = across_x[:half]
    lower[...] = across_y[half:]


def halves_call(across_x, across_y):
    vmem = pl.BlockSpec(memory_space=pltpu.VMEM)
    shape = (across_x.shape[0] // 2, across_x.shape[1])
    return pl.pallas_call(
        halves_kernel,
        in_specs=[vmem] * 2,
        out_specs=[vmem] * 2,
        out_shape=[jax.ShapeDtypeStruct(shape, across_x.dtype)] * 2,
        compiler_params=pltpu.CompilerParams(vmem_limit_bytes=4 << 20),
        cost_estimate=pl.CostEstimate(
            flops=0, bytes_accessed=4 * across_x.size, transcendentals=0
        ),
        name="halves",
    )(across_x, across_y)


def near_shards(value):
    return [send_seq(value, 1), send_seq(value, 2), send_seq(value, 4)]


def far_shards(across_x, across_y):
    upper, lower = halves_call(across_x, across_y)
    return [send_seq(upper, 4), send_seq(lower, 2)]


def weight_order(heads_here):
    quarter = HD // 4
    order = -np.ones((6 * LANES,), np.int32)
    for head in range(heads_here):
        base = head * 3 * HD
        for kind in range(2):
            for half in range(2):
                for letter in range(2):
                    target = (2 * kind + letter) * LANES + head * (HD // 2) + half * quarter
                    source = base + kind * HD + half * (HD // 2) + letter * quarter
                    order[target : target + quarter] = np.arange(source, source + quarter)
        target = (4 + head) * LANES
        order[target : target + HD] = np.arange(base + 2 * HD, base + 3 * HD)
    return order


def angle_table(heads_here):
    quarter = HD // 4
    frequency = (10000.0 ** (-np.arange(quarter) / quarter)).astype(np.float32)
    angles = np.arange(POSITIONS, dtype=np.float32)[:, None] * frequency[None, :]
    pieces = []
    for function in (np.cos, np.sin):
        exact = np.zeros((2 * POSITIONS, LANES), np.float64)
        for head in range(heads_here):
            for half in range(2):
                lane = head * (HD // 2) + half * quarter
                rows = slice(half * POSITIONS, (half + 1) * POSITIONS)
                exact[rows, lane : lane + quarter] = function(angles.astype(np.float64))
        upper = exact.astype(jnp.bfloat16)
        pieces += [upper, (exact - upper.astype(np.float64)).astype(jnp.bfloat16)]
    return np.concatenate(pieces, axis=1)


def fast_local(
    patches,
    patch_mask,
    mask_embed,
    norm_gain,
    qkv_weight,
    segment_ids,
    patch_rows,
    patch_column,
    out_weight,
    merge_gain,
    merge_weight,
    merge_bias,
    image_owner,
):
    local_rows = patches.shape[1]
    shards = lax.axis_size("seq")
    packs = lax.axis_size("pack")
    heads_here = HEADS // shards
    images = image_owner.shape[1]
    total = local_rows * shards
    me = lax.axis_index("seq").astype(jnp.int32)
    pack = lax.axis_index("pack").astype(jnp.int32)

    value = payload_call(segment_ids, patch_rows, patch_column, patch_mask, mask_embed, patches)
    own_swap, across_x, across_y = near_shards(value)

    order = weight_order(heads_here)
    spread = (order[:, None] == np.arange(qkv_weight.shape[1])[None, :]).astype(jnp.bfloat16)
    table = jnp.asarray(angle_table(heads_here))
    chip, core = me // 2, me % 2
    info = [chip, core, pack, *[me ^ place for place in range(shards)]]
    info = jnp.concatenate([jnp.stack(info), image_owner[0]])
    gain, merge_gain_row, bias, ordered, merge_rows, weight = prepare_call(
        shards,
        info,
        out_weight,
        merge_weight.T,
        qkv_weight.T,
        jnp.asarray(spread),
        (norm_gain, merge_gain, merge_bias),
    )

    project = lambda place, first, second, earlier: qkv_call(
        info, place, first, second, table, gain, weight, earlier, total
    )
    buffers = project(0, [value], [own_swap], ())
    across_x, across_y = after([across_x, across_y], buffers[2], ordered)
    far = far_shards(across_x, across_y)
    buffers = project(1, [across_x], [send_seq(across_x, 1)], buffers)
    buffers = project(2, [across_y], [send_seq(across_y, 1)], buffers)
    far = after(far, buffers[2])
    buffers = project(3, far, [send_seq(one, 1) for one in far], buffers)
    inputs, block, labels = buffers

    most = 2 * (total // 4) // images
    first_rows, last_rows = CHUNKS
    attend = functools.partial(attention_call, first_owner=IDS + shards, info=info)
    own, note = attend(0, first_rows, labels=labels, block=block, noted=True)
    own_swap, across_x, across_y = near_shards(own)
    labels, block = after([labels, block], own)
    (late,) = attend(first_rows, last_rows, labels=labels, block=block, noted=False)
    across_x, across_y = after([across_x, across_y], late)
    halves = halves_call(across_x, across_y)
    far = [send_seq(halves[0], 4), send_seq(halves[1], 2)]
    (late,) = after([late], *halves)
    late_shares = [late] + [send_seq(late, flip) for flip in (2, 4, 6)]
    near = [send_seq(one, 1) for one in after([across_x, across_y], *far)]
    merge = lambda start, rows, sources, route: merge_call(
        start, rows, sources, inputs, ordered, merge_gain_row, merge_rows, bias, packs, route
    )
    sources = [[own], [own_swap], [across_x], near[:1], [across_y], near[1:], far]
    (projected,) = merge(0, first_rows, sources + [[send_seq(one, 1) for one in far]], ())
    late_shares[3:] = after(late_shares[3:], projected)
    sources = [[one] for share in late_shares for one in (share, send_seq(share, 1))]
    made = merge(first_rows, last_rows, sources, (info, most, note, projected))
    blocks = [made[0]] + [
        lax.ppermute(made[flip], "pack", [(z, z ^ flip) for z in range(packs)])
        for flip in range(1, packs)
    ]
    return place_call(info, blocks, most, merge_weight.shape[1])[None]


def local(*arguments):
    patches, weight = arguments[0], arguments[4]
    shards = lax.axis_size("seq")
    fits = shards == 8 and HEADS // shards == 2 and weight.shape[1] == 6 * HD
    fits = fits and patches.shape[1] * shards == sum(CHUNKS) and lax.axis_size("pack") == 4
    return fast_local(*arguments) if fits else general_local(*arguments)


def solution(mesh):
    placed = (
        P("pack", "seq", None),
        P("pack", "seq"),
        P(),
        P(),
        P(None, "seq"),
        P("pack", "seq"),
        P("pack", "seq"),
        P("pack", "seq"),
        P(),
        P(),
        P(None, "seq"),
        P("seq"),
        P("pack", None),
    )
    return jax.shard_map(
        local, mesh=mesh, in_specs=placed, out_specs=P("pack", None, None, "seq"), check_vma=False
    )
```

```python
import functools

import jax
import jax.numpy as jnp
import numpy as np
from jax import lax
from jax.experimental import pallas as pl
from jax.experimental.pallas import tpu as pltpu
from jax.sharding import PartitionSpec as P

D = 1408
HEADS = 16
HD = 88


EPSILON = 1e-06


def layer_norm(values, gain_vector):
    center = values - jnp.mean(values, axis=-1, keepdims=True)
    spread = jnp.mean(center * center, axis=-1, keepdims=True)
    return center * lax.rsqrt(spread + EPSILON) * gain_vector.astype(jnp.float32)


def rotate(vectors, row_index, column_index):
    total_rows, heads_here, head_width = vectors.shape
    quarter = head_width // 4
    frequency = 10000.0 ** (-jnp.arange(quarter, dtype=jnp.float32) / quarter)
    row_angle = row_index.astype(jnp.float32)[:, None] * frequency[None, :]
    column_angle = column_index.astype(jnp.float32)[:, None] * frequency[None, :]
    angles = jnp.stack([row_angle, column_angle], axis=1)[:, None, :, None, :]
    split_up = vectors.reshape(total_rows, heads_here, 2, 2, quarter)
    partner = jnp.stack([-split_up[:, :, :, 1], split_up[:, :, :, 0]], axis=3)
    turned = split_up * jnp.cos(angles) + partner * jnp.sin(angles)
    return turned.reshape(total_rows, heads_here, head_width)


def qkv_block(projected, row_index, column_index):
    turned_queries = rotate(projected[:, :, 0], row_index, column_index)
    turned_keys = rotate(projected[:, :, 1], row_index, column_index)
    return jnp.concatenate([turned_queries, turned_keys, projected[:, :, 2]], axis=-1).astype(
        jnp.bfloat16
    )


def attention(block, segments):
    total_rows, heads_here, triple = block.shape
    head_width = triple // 3
    step_rows = min(512, total_rows)
    query_part = block[:, :, :head_width].reshape(
        total_rows // step_rows, step_rows, heads_here, head_width
    )
    key_part = block[:, :, head_width : 2 * head_width]
    value_part = block[:, :, 2 * head_width :]
    query_segments = segments.reshape(total_rows // step_rows, step_rows)
    scale = head_width ** (-0.5)

    def one_block(inputs_pair):
        queries_here, segments_here = inputs_pair
        scores = (
            jnp.einsum("qhd,khd->hqk", queries_here, key_part, preferred_element_type=jnp.float32)
            * scale
        )
        same_image = (segments_here[:, None] == segments[None, :])[None]
        scores = jnp.where(same_image, scores, -jnp.inf)
        highest = jnp.max(scores, axis=-1, keepdims=True)
        weights = jnp.exp(scores - highest)
        probs = (weights / jnp.sum(weights, axis=-1, keepdims=True)).astype(jnp.bfloat16)
        result = jnp.einsum("hqk,khd->qhd", probs, value_part, preferred_element_type=jnp.float32)
        return result.astype(jnp.bfloat16)

    return lax.map(one_block, (query_part, query_segments)).reshape(
        total_rows, heads_here, head_width
    )


def route(projected, segments, owners_here, packs, most):
    merged_segments = segments[::4]
    images = owners_here.shape[0]
    image_ids = jnp.arange(images, dtype=jnp.int32)
    member = (merged_segments[None, :] == image_ids[:, None]).astype(jnp.int32)
    lengths = jnp.sum(member, axis=1, dtype=jnp.int32)
    starts = jnp.cumsum(lengths, dtype=jnp.int32) - lengths
    owner_ids = jnp.arange(packs, dtype=jnp.int32)
    owned = owners_here[None, :] == owner_ids[:, None]
    first_row = jnp.sum(jnp.where(owned, starts[None, :], 0), axis=1, dtype=jnp.int32)
    owned_length = jnp.sum(jnp.where(owned, lengths[None, :], 0), axis=1, dtype=jnp.int32)
    slots = jnp.arange(most, dtype=jnp.int32)
    source_rows = jnp.clip(first_row[:, None] + slots[None, :], 0, projected.shape[0] - 1)
    picked = jnp.take(projected, source_rows.reshape(-1), axis=0).reshape(
        packs, most, projected.shape[1]
    )
    filled = slots[None, :] < owned_length[:, None]
    return jnp.where(filled[:, :, None], picked, jnp.zeros_like(picked))


def general_local(
    patches,
    patch_mask,
    mask_embed,
    norm_gain,
    qkv_weight,
    segment_ids,
    patch_rows,
    patch_column,
    out_weight,
    merge_gain,
    merge_weight,
    merge_bias,
    image_owner,
):
    local_rows = patches.shape[1]
    shards = lax.axis_size("seq")
    packs = lax.axis_size("pack")
    heads_here = HEADS // shards
    inputs = jnp.where(patch_mask[0][:, None] == 1, mask_embed[None, :], patches[0])
    normed = layer_norm(inputs.astype(jnp.float32), norm_gain).astype(jnp.bfloat16)
    labels = lax.all_gather(
        jnp.stack([segment_ids[0], patch_rows[0], patch_column[0]]), "seq", axis=1, tiled=True
    )
    piece = lax.all_gather(normed, "seq", axis=0, tiled=True)
    span = piece.shape[0]
    projected = jnp.dot(piece, qkv_weight, preferred_element_type=jnp.float32)
    row_part = labels[1]
    column_part = labels[2]
    block = qkv_block(projected.reshape(span, heads_here, 3, HD), row_part, column_part)
    result = attention(block, labels[0])
    mixed_heads = lax.all_to_all(result, "seq", split_axis=0, concat_axis=1, tiled=True)
    attended = mixed_heads.reshape(local_rows, D)
    residual = inputs.astype(jnp.float32) + jnp.dot(
        attended, out_weight, preferred_element_type=jnp.float32
    )
    merged = layer_norm(residual, merge_gain).astype(jnp.bfloat16).reshape(local_rows // 4, 4 * D)
    projected_all = (
        jnp.dot(
            lax.all_gather(merged, "seq", axis=0, tiled=True),
            merge_weight,
            preferred_element_type=jnp.float32,
        )
        + merge_bias.astype(jnp.float32)
    ).astype(jnp.bfloat16)
    images = image_owner.shape[1]
    most = 2 * projected_all.shape[0] // images
    outgoing = route(projected_all, labels[0], image_owner[0], packs, most)
    delivered = lax.all_to_all(outgoing, "pack", split_axis=0, concat_axis=0, tiled=True)
    return delivered[None]


LANES = 128
CHIP, CORE, PACK, IDS = 0, 1, 2, 3
BLOCK = 512
POSITIONS = 64
FAR_APART = -(2.0**100)
IMAGE_LANE = 96
NORM_ROWS = 16
CHUNKS = (768, 768)


def norm_rows(values, gain_row):
    center = values - jnp.mean(values, axis=-1, keepdims=True)
    spread = jnp.mean(center * center, axis=-1, keepdims=True)
    return center * lax.rsqrt(spread + EPSILON) * gain_row


def stacked(pieces):
    loaded = [piece[...] for piece in pieces]
    return loaded[0] if len(loaded) == 1 else jnp.concatenate(loaded, axis=0)


def in_vmem(value):
    return pltpu.with_memory_space_constraint(value, pltpu.VMEM)


def in_hbm(value):
    return pltpu.with_memory_space_constraint(value, pltpu.HBM)


def payload_kernel(segments, rows, columns, mask, embed, patches, out):
    labels = [one[...].astype(jnp.float32) for one in (segments, rows, columns, mask)]
    labels.append(jnp.zeros((4, labels[0].shape[1]), jnp.float32))
    labels = jnp.concatenate(labels, axis=0).astype(jnp.bfloat16)
    shape = (8, LANES)
    row = lax.broadcasted_iota(jnp.int32, shape, 0)
    place = jnp.where(row == lax.broadcasted_iota(jnp.int32, shape, 1), 1.0, 0.0)
    turned = lax.dot_general(
        labels,
        place.astype(jnp.bfloat16),
        (((0,), (0,)), ((), ())),
        preferred_element_type=jnp.float32,
    )
    masked = turned[:, 3:4] > 0.5
    tokens = jnp.where(
        masked, embed[...].astype(jnp.float32)[None, :], patches[0].astype(jnp.float32)
    )
    out[:, :D] = tokens.astype(jnp.bfloat16)
    out[:, D:] = turned.astype(jnp.bfloat16)


def payload_call(segments, rows, columns, mask, embed, patches):
    count = patches.shape[1]
    operands = (segments, rows, columns, mask, embed, patches)
    fixed = lambda shape: pl.BlockSpec(shape, lambda i: (0,) * len(shape))
    shape = (count, D + LANES)
    return pl.pallas_call(
        payload_kernel,
        grid=(1,),
        in_specs=[fixed(one.shape) for one in operands],
        out_specs=fixed(shape),
        out_shape=jax.ShapeDtypeStruct(shape, jnp.bfloat16),
        compiler_params=pltpu.CompilerParams(vmem_limit_bytes=8 << 20),
        cost_estimate=pl.CostEstimate(
            flops=count * D, bytes_accessed=4 * count * D, transcendentals=0
        ),
        name="payload",
    )(*map(in_hbm, operands))


def qkv_kernel(count, flip, info, *refs):
    first, second = refs[:count], refs[count : 2 * count]
    table, gain, weight = refs[2 * count : 2 * count + 3]
    inputs_out, qkv_out, label_out = refs[-3:]
    mine, other = stacked(first), stacked(second)
    leads = info[CORE] == 0
    ahead = jnp.where(leads, mine, other)
    behind = jnp.where(leads, other, mine)
    both = jnp.concatenate([ahead, behind], axis=0)
    rows = both.shape[0]
    at = pl.ds(pl.multiple_of((info[CHIP] ^ flip) * rows, rows), rows)
    inputs_out[at, :] = both[:, :D]
    label_out[at, :] = both[:, D:]
    labels = both[:, D:].astype(jnp.float32)
    normed = norm_rows(both[:, :D].astype(jnp.float32), gain[...]).astype(jnp.bfloat16)
    columns = lax.dot_general(
        normed, weight[...], (((1,), (1,)), ((), ())), preferred_element_type=jnp.float32
    )
    lane = lax.broadcasted_iota(jnp.int32, labels.shape, 1)
    numbers = lane.astype(jnp.float32)
    hot = (numbers == labels[:, 1:2]) | (numbers == labels[:, 2:3] + POSITIONS)
    looked = jnp.dot(
        jnp.where(hot, 1.0, 0.0).astype(jnp.bfloat16), table[...], preferred_element_type=jnp.float32
    )
    cosine = looked[:, :LANES] + looked[:, LANES : 2 * LANES]
    sine = looked[:, 2 * LANES : 3 * LANES] + looked[:, 3 * LANES :]
    first_head = lane < HD // 2

    def turn(start):
        a = columns[:, start : start + LANES]
        b = columns[:, start + LANES : start + 2 * LANES]
        return a * cosine - b * sine, b * cosine + a * sine

    factor = HD**-0.5 * float(np.log2(np.e))
    query_a, query_b = (one * factor for one in turn(0))
    key_a, key_b = turn(2 * LANES)
    zero = jnp.zeros_like(key_a)
    image = numbers == labels[:, :1] + IMAGE_LANE
    extra = lane >= IMAGE_LANE
    apart = jnp.where(image, 0.0, FAR_APART)
    parts = [
        jnp.where(image, 1.0, query_a),
        query_b,
        jnp.where(extra, apart, jnp.where(first_head, key_a, zero)),
        jnp.where(first_head, key_b, zero),
        jnp.where(extra, apart, jnp.where(first_head, zero, key_a)),
        jnp.where(first_head, zero, key_b),
    ]
    for head in range(2):
        values = columns[:, (4 + head) * LANES : (5 + head) * LANES]
        parts.append(jnp.where(lane == HD, 1.0, values))
    for number, part in enumerate(parts):
        qkv_out[at, number * LANES : (number + 1) * LANES] = part.astype(jnp.bfloat16)


def qkv_call(info, flip, first, second, table, gain, weight, earlier, total):
    rows = 2 * sum(piece.shape[0] for piece in first)
    widths = (D, 8 * LANES, LANES)
    operands = [*first, *second, table, gain, in_vmem(weight)]
    vmem = pl.BlockSpec(memory_space=pltpu.VMEM)
    held = [in_vmem(one) for one in earlier]
    return pl.pallas_call(
        functools.partial(qkv_kernel, len(first), flip),
        in_specs=[pl.BlockSpec(memory_space=pltpu.SMEM)]
        + [vmem] * (len(operands) + len(earlier)),
        out_specs=[vmem] * len(widths),
        out_shape=[pltpu.VMEM((total, width), jnp.bfloat16) for width in widths],
        input_output_aliases={1 + len(operands) + i: i for i in range(len(earlier))},
        compiler_params=pltpu.CompilerParams(vmem_limit_bytes=14 << 20),
        cost_estimate=pl.CostEstimate(
            flops=6 * rows * D * weight.shape[0],
            bytes_accessed=2 * (rows * 4 * D + weight.size),
            transcendentals=rows,
        ),
        name="norm_qkv",
    )(info, *operands, *held)


def segment_row(labels):
    pick = jnp.where(lax.broadcasted_iota(jnp.int32, (8, LANES), 1) == 0, 1.0, 0.0)
    return lax.dot_general(
        pick.astype(jnp.bfloat16),
        labels,
        (((1,), (1,)), ((), ())),
        preferred_element_type=jnp.float32,
    )


def attention_kernel(start, first_owner, images, info, labels, block, *refs):
    out, *rest = refs
    scores, high = rest[-2:]
    rows = high.shape[1]
    total = block.shape[0]
    segments = segment_row(labels[...])
    one_row = segments[:1]
    lowest = jnp.min(labels[start : start + 16, :1].astype(jnp.float32), axis=0, keepdims=True)
    largest = labels[start + rows - 16 : start + rows, :1].astype(jnp.float32)
    largest = jnp.max(largest, axis=0, keepdims=True)
    begin = jnp.sum(jnp.where(one_row < lowest, 1, 0)) // BLOCK
    end = (jnp.sum(jnp.where(one_row <= largest, 1, 0)) + BLOCK - 1) // BLOCK
    queries = block[start : start + rows, : 2 * LANES]
    high[...] = jnp.full_like(high, 2 * FAR_APART)

    def score(step, carry):
        at = pl.ds(pl.multiple_of(step * BLOCK, BLOCK), BLOCK)
        for head in range(2):
            keys = block[at, (2 + 2 * head) * LANES : (4 + 2 * head) * LANES]
            values = lax.dot_general(
                queries, keys, (((1,), (1,)), ((), ())), preferred_element_type=jnp.float32
            )
            scores[head, step] = values
            tops = [values[:, lane : lane + LANES] for lane in range(0, BLOCK, LANES)]
            high[head] = functools.reduce(jnp.maximum, tops, high[head])
        return carry

    lax.fori_loop(begin, end, score, 0)
    highest = [jnp.max(high[head], axis=-1, keepdims=True) for head in range(2)]

    def weigh(step, carry):
        at = pl.ds(pl.multiple_of(step * BLOCK, BLOCK), BLOCK)
        sums = []
        for head in range(2):
            weights = jnp.exp2(scores[head, step] - highest[head])
            values = block[at, (6 + head) * LANES : (7 + head) * LANES]
            sums.append(
                carry[head]
                + jnp.dot(weights.astype(jnp.bfloat16), values, preferred_element_type=jnp.float32)
            )
        return tuple(sums)

    zero = jnp.zeros((rows, LANES), jnp.float32)
    sums = lax.fori_loop(begin, end, weigh, (zero, zero))
    first, second = (one / one[:, HD : HD + 1] for one in sums)
    lane = lax.broadcasted_iota(jnp.int32, first.shape, 1)
    turned = pltpu.roll(second, HD, 1)
    out[:rows] = jnp.where(lane < HD, first, turned).astype(jnp.bfloat16)
    half = rows // 2
    tail = 2 * HD - LANES
    lane = lane[:half]
    up = pltpu.roll(turned[half:], tail, 1)
    packed = jnp.where(lane < tail, turned[:half], jnp.where(lane < 2 * tail, up, 0.0))
    out[rows:] = packed.astype(jnp.bfloat16)

    if len(rest) > 2:
        note = rest[0]
        row = lax.broadcasted_iota(jnp.int32, note.shape, 0)
        lane = lax.broadcasted_iota(jnp.int32, note.shape, 1)
        found = jnp.zeros(note.shape, jnp.float32)
        for image in range(images):
            below = jnp.sum(jnp.where(one_row < image, 0.25, 0.0), axis=1, keepdims=True)
            inside = jnp.sum(jnp.where(one_row == image, 0.25, 0.0), axis=1, keepdims=True)
            here = row == info[first_owner + image]
            for place, number in enumerate((below, inside)):
                upper = jnp.floor(number * (1.0 / 16))
                found = jnp.where(here & (lane == 2 * place), upper, found)
                found = jnp.where(here & (lane == 2 * place + 1), number - 16 * upper, found)
        note[...] = found.astype(jnp.bfloat16)


def attention_call(start, rows, first_owner, info, labels, block, noted):
    total = block.shape[0]
    vmem = pl.BlockSpec(memory_space=pltpu.VMEM)
    shapes = [jax.ShapeDtypeStruct((rows + rows // 2, LANES), jnp.bfloat16)]
    if noted:
        shapes.append(jax.ShapeDtypeStruct((16, LANES), jnp.bfloat16))
    return pl.pallas_call(
        functools.partial(attention_kernel, start, first_owner, info.shape[0] - first_owner),
        in_specs=[pl.BlockSpec(memory_space=pltpu.SMEM), vmem, vmem],
        out_specs=[vmem] * len(shapes),
        out_shape=shapes,
        scratch_shapes=[
            pltpu.VMEM((2, total // BLOCK, rows, BLOCK), jnp.float32),
            pltpu.VMEM((2, rows, LANES), jnp.float32),
        ],
        compiler_params=pltpu.CompilerParams(vmem_limit_bytes=20 << 20),
        cost_estimate=pl.CostEstimate(
            flops=10 * rows * total * 2 * LANES,
            bytes_accessed=2 * block.size,
            transcendentals=rows * total,
        ),
        name="attention",
    )(info, in_vmem(labels), in_vmem(block))


def prepare_kernel(shards, info, out_weight, merge_weight, qkv_weight, spread, *refs):
    *rows, out, merge, qkv, qkv_buffer, spread_buffer, sems = refs
    for row, row_out in zip(rows[: len(rows) // 2], rows[len(rows) // 2 :]):
        row_out[...] = row[...].astype(jnp.float32)[None, :]
    rest = 2 * HD - LANES
    copies = [(qkv_weight, qkv_buffer), (spread, spread_buffer)]
    out[shards * LANES :] = jnp.zeros((shards // 2 * LANES, D), jnp.bfloat16)
    for place in range(shards):
        start = pl.multiple_of(info[IDS + place] * (2 * HD), 16)
        to = (shards + place // 2) * LANES + place % 2 * rest
        copies.append(
            (out_weight.at[pl.ds(start, LANES), :], out.at[pl.ds(place * LANES, LANES), :])
        )
        copies.append((out_weight.at[pl.ds(start + LANES, rest), :], out.at[pl.ds(to, rest), :]))
    copies.append((merge_weight, merge))
    copies = [
        pltpu.make_async_copy(source, target, sems.at[i])
        for i, (source, target) in enumerate(copies)
    ]
    for copy in copies:
        copy.start()
    copies[0].wait()
    copies[1].wait()
    qkv[...] = jnp.dot(
        spread_buffer[...], qkv_buffer[...], preferred_element_type=jnp.float32
    ).astype(jnp.bfloat16)
    for copy in copies[2:]:
        copy.wait()


def prepare_call(shards, info, out_weight, merge_weight, qkv_weight, spread, rows):
    anywhere = pl.BlockSpec(memory_space=pl.ANY)
    vmem = pl.BlockSpec(memory_space=pltpu.VMEM)
    operands = (out_weight, merge_weight, qkv_weight, spread)
    shapes = [(shards * LANES * 3 // 2, D), merge_weight.shape, (spread.shape[0], D)]
    return pl.pallas_call(
        functools.partial(prepare_kernel, shards),
        in_specs=[pl.BlockSpec(memory_space=pltpu.SMEM)]
        + [anywhere] * len(operands)
        + [vmem] * len(rows),
        out_specs=[vmem] * (len(rows) + len(shapes)),
        out_shape=[pltpu.VMEM((1, row.shape[0]), jnp.float32) for row in rows]
        + [pltpu.VMEM(shape, jnp.bfloat16) for shape in shapes],
        scratch_shapes=[
            pltpu.VMEM(qkv_weight.shape, jnp.bfloat16),
            pltpu.VMEM(spread.shape, jnp.bfloat16),
            pltpu.SemaphoreType.DMA((2 * shards + 3,)),
        ],
        compiler_params=pltpu.CompilerParams(vmem_limit_bytes=10 << 20),
        cost_estimate=pl.CostEstimate(
            flops=2 * spread.size * D,
            bytes_accessed=4 * (out_weight.size + merge_weight.size + qkv_weight.size),
            transcendentals=0,
        ),
        name="prepare",
    )(info, *map(in_hbm, operands), *rows)


def merge_kernel(start, counts, packs, last, *refs):
    inputs, weight, gain, merge_weight, bias = refs[:5]
    pieces = refs[5 : 5 + sum(counts)]
    *refs, state, tokens = refs[5 + sum(counts) :]
    rows = state.shape[1]
    half = rows // 2
    rest = 2 * HD - LANES
    sources, at = [], 0
    for count in counts:
        sources.append(stacked(pieces[at : at + count]))
        at += count
    shards = len(sources)
    lane = lax.broadcasted_iota(jnp.int32, (half, LANES), 1)
    for part in range(2):
        token = slice(part * half, (part + 1) * half)
        lined = [source[token, :] for source in sources]
        for pair in range(shards // 2):
            mine = sources[2 * pair][rows:, :].astype(jnp.float32)
            other = sources[2 * pair + 1][rows:, :].astype(jnp.float32)
            if part == 0:
                other = pltpu.roll(other, rest, 1)
            else:
                mine = pltpu.roll(mine, LANES - rest, 1)
            lined.append(jnp.where(lane < rest, mine, other).astype(jnp.bfloat16))
        mixed = jnp.dot(
            jnp.concatenate(lined, axis=1), weight[...], preferred_element_type=jnp.float32
        )
        for column in range(D // LANES):
            lanes = slice(column * LANES, (column + 1) * LANES)
            before = inputs[start + part * half : start + (part + 1) * half, lanes]
            state[column, token, :] = before.astype(jnp.float32) + mixed[:, lanes]
    groups = rows // 4
    for block in range(0, groups, NORM_ROWS):
        for quadrant in range(4):
            at = pl.ds(4 * block + quadrant, NORM_ROWS, stride=4)
            residual = jnp.concatenate(
                [state[column, at, :] for column in range(D // LANES)], axis=1
            )
            tokens[block : block + NORM_ROWS, quadrant * D : (quadrant + 1) * D] = norm_rows(
                residual, gain[...]
            ).astype(jnp.bfloat16)
    total = bias[...] + lax.dot_general(
        tokens[...], merge_weight[...], (((1,), (1,)), ((), ())), preferred_element_type=jnp.float32
    )
    total = total.astype(jnp.bfloat16)
    if not last:
        refs[0][...] = total
        return
    info, note, *earlier = refs[:-packs]
    outs = refs[-packs:]
    total = jnp.concatenate([*[one[...] for one in earlier], total], axis=0)
    whole = total.shape[1] // LANES
    most = outs[0].shape[0] * LANES // total.shape[1]
    notes = note[...].astype(jnp.float32)
    note_row = lax.broadcasted_iota(jnp.int32, notes.shape, 0)
    slot = lax.broadcasted_iota(jnp.int32, (most, total.shape[0]), 0)
    row = lax.broadcasted_iota(jnp.int32, (most, total.shape[0]), 1)
    for place, out in enumerate(outs):
        found = jnp.where(note_row == (info[PACK] ^ place), notes, 0.0)
        found = jnp.sum(found, axis=0, keepdims=True)
        first = (16.0 * found[:, :1] + found[:, 1:2]).astype(jnp.int32)
        length = (16.0 * found[:, 2:3] + found[:, 3:4]).astype(jnp.int32)
        chosen = (row == slot + first) & (slot < length)
        chosen = jnp.where(chosen, 1.0, 0.0).astype(jnp.bfloat16)
        block = jnp.dot(chosen, total, preferred_element_type=jnp.float32)
        for column in range(whole):
            out[column * most : (column + 1) * most, :] = block[
                :, column * LANES : (column + 1) * LANES
            ].astype(jnp.bfloat16)
        low = block[: most // 2, whole * LANES :]
        up = block[most // 2 :, whole * LANES :]
        out[whole * most :, :] = jnp.concatenate([low, up], axis=1).astype(jnp.bfloat16)


def merge_call(start, rows, sources, inputs, weight, gain, merge_weight, bias, packs, route):
    groups = rows // 4
    width = merge_weight.shape[0]
    pieces = [piece for source in sources for piece in source]
    vmem = pl.BlockSpec(memory_space=pltpu.VMEM)
    operands = [in_vmem(inputs), in_vmem(weight), gain, in_vmem(merge_weight), bias, *pieces]
    specs = [vmem] * len(operands)
    shapes = [jax.ShapeDtypeStruct((groups, width), jnp.bfloat16)]
    if route:
        me, most, *others = route
        operands += [me, *others]
        specs += [pl.BlockSpec(memory_space=pltpu.SMEM)] + [vmem] * len(others)
        shapes = [jax.ShapeDtypeStruct((most * width // LANES, LANES), jnp.bfloat16)] * packs
    return pl.pallas_call(
        functools.partial(
            merge_kernel, start, [len(source) for source in sources], packs, bool(route)
        ),
        in_specs=specs,
        out_specs=[vmem] * len(shapes),
        scratch_shapes=[
            pltpu.VMEM((D // LANES, rows, LANES), jnp.float32),
            pltpu.VMEM((groups, 4 * D), jnp.bfloat16),
        ],
        out_shape=shapes,
        compiler_params=pltpu.CompilerParams(vmem_limit_bytes=20 << 20),
        cost_estimate=pl.CostEstimate(
            flops=0,
            bytes_accessed=1024,
            transcendentals=rows,
        ),
        name="out_merge",
    )(*operands)


def place_kernel(info, *refs):
    blocks, out = refs[:-1], refs[-1]
    most, width = out.shape[1:]
    whole = width // LANES
    half = most // 2
    middle = LANES // 2
    for place, block in enumerate(blocks):
        target = info[PACK] ^ (-place % len(blocks))
        for column in range(whole):
            out[target, :, column * LANES : (column + 1) * LANES] = block[
                column * most : (column + 1) * most, :
            ]
        out[target, :half, whole * LANES :] = block[whole * most :, :middle]
        out[target, half:, whole * LANES :] = block[whole * most :, middle:]


def place_call(info, blocks, most, width):
    fixed = lambda shape: pl.BlockSpec(shape, lambda i: (0,) * len(shape))
    shape = (len(blocks), most, width)
    return pl.pallas_call(
        place_kernel,
        grid=(1,),
        in_specs=[pl.BlockSpec(memory_space=pltpu.SMEM)] + [fixed(one.shape) for one in blocks],
        out_specs=fixed(shape),
        out_shape=jax.ShapeDtypeStruct(shape, jnp.bfloat16),
        compiler_params=pltpu.CompilerParams(vmem_limit_bytes=8 << 20),
        cost_estimate=pl.CostEstimate(
            flops=0, bytes_accessed=4 * len(blocks) * most * width, transcendentals=0
        ),
        name="place_rows",
    )(info, *blocks)


def send_seq(value, flip):
    size = lax.axis_size("seq")
    return lax.ppermute(value, "seq", [(i, i ^ flip) for i in range(size)])


def after(values, *earlier):
    return lax.optimization_barrier((tuple(values), earlier))[0]


def halves_kernel(across_x, across_y, upper, lower):
    half = upper.shape[0]
    upper[...] = across_x[:half]
    lower[...] = across_y[half:]


def halves_call(across_x, across_y):
    vmem = pl.BlockSpec(memory_space=pltpu.VMEM)
    shape = (across_x.shape[0] // 2, across_x.shape[1])
    return pl.pallas_call(
        halves_kernel,
        in_specs=[vmem] * 2,
        out_specs=[vmem] * 2,
        out_shape=[jax.ShapeDtypeStruct(shape, across_x.dtype)] * 2,
        compiler_params=pltpu.CompilerParams(vmem_limit_bytes=4 << 20),
        cost_estimate=pl.CostEstimate(
            flops=0, bytes_accessed=4 * across_x.size, transcendentals=0
        ),
        name="halves",
    )(across_x, across_y)


def near_shards(value):
    return [send_seq(value, 1), send_seq(value, 2), send_seq(value, 4)]


def far_shards(across_x, across_y):
    upper, lower = halves_call(across_x, across_y)
    return [send_seq(upper, 4), send_seq(lower, 2)]


def weight_order(heads_here):
    quarter = HD // 4
    order = -np.ones((6 * LANES,), np.int32)
    for head in range(heads_here):
        base = head * 3 * HD
        for kind in range(2):
            for half in range(2):
                for letter in range(2):
                    target = (2 * kind + letter) * LANES + head * (HD // 2) + half * quarter
                    source = base + kind * HD + half * (HD // 2) + letter * quarter
                    order[target : target + quarter] = np.arange(source, source + quarter)
        target = (4 + head) * LANES
        order[target : target + HD] = np.arange(base + 2 * HD, base + 3 * HD)
    return order


def angle_table(heads_here):
    quarter = HD // 4
    frequency = (10000.0 ** (-np.arange(quarter) / quarter)).astype(np.float32)
    angles = np.arange(POSITIONS, dtype=np.float32)[:, None] * frequency[None, :]
    pieces = []
    for function in (np.cos, np.sin):
        exact = np.zeros((2 * POSITIONS, LANES), np.float64)
        for head in range(heads_here):
            for half in range(2):
                lane = head * (HD // 2) + half * quarter
                rows = slice(half * POSITIONS, (half + 1) * POSITIONS)
                exact[rows, lane : lane + quarter] = function(angles.astype(np.float64))
        upper = exact.astype(jnp.bfloat16)
        pieces += [upper, (exact - upper.astype(np.float64)).astype(jnp.bfloat16)]
    return np.concatenate(pieces, axis=1)


def fast_local(
    patches,
    patch_mask,
    mask_embed,
    norm_gain,
    qkv_weight,
    segment_ids,
    patch_rows,
    patch_column,
    out_weight,
    merge_gain,
    merge_weight,
    merge_bias,
    image_owner,
):
    local_rows = patches.shape[1]
    shards = lax.axis_size("seq")
    packs = lax.axis_size("pack")
    heads_here = HEADS // shards
    images = image_owner.shape[1]
    total = local_rows * shards
    me = lax.axis_index("seq").astype(jnp.int32)
    pack = lax.axis_index("pack").astype(jnp.int32)

    value = payload_call(segment_ids, patch_rows, patch_column, patch_mask, mask_embed, patches)
    own_swap, across_x, across_y = near_shards(value)

    order = weight_order(heads_here)
    spread = (order[:, None] == np.arange(qkv_weight.shape[1])[None, :]).astype(jnp.bfloat16)
    table = jnp.asarray(angle_table(heads_here))
    chip, core = me // 2, me % 2
    info = [chip, core, pack, *[me ^ place for place in range(shards)]]
    info = jnp.concatenate([jnp.stack(info), image_owner[0]])
    gain, merge_gain_row, bias, ordered, merge_rows, weight = prepare_call(
        shards,
        info,
        out_weight,
        merge_weight.T,
        qkv_weight.T,
        jnp.asarray(spread),
        (norm_gain, merge_gain, merge_bias),
    )

    project = lambda place, first, second, earlier: qkv_call(
        info, place, first, second, table, gain, weight, earlier, total
    )
    buffers = project(0, [value], [own_swap], ())
    across_x, across_y = after([across_x, across_y], buffers[2], ordered)
    far = far_shards(across_x, across_y)
    buffers = project(1, [across_x], [send_seq(across_x, 1)], buffers)
    buffers = project(2, [across_y], [send_seq(across_y, 1)], buffers)
    far = after(far, buffers[2])
    buffers = project(3, far, [send_seq(one, 1) for one in far], buffers)
    inputs, block, labels = buffers

    most = 2 * (total // 4) // images
    first_rows, last_rows = CHUNKS
    attend = functools.partial(attention_call, first_owner=IDS + shards, info=info)
    own, note = attend(0, first_rows, labels=labels, block=block, noted=True)
    own_swap, across_x, across_y = near_shards(own)
    labels, block = after([labels, block], own)
    (late,) = attend(first_rows, last_rows, labels=labels, block=block, noted=False)
    across_x, across_y = after([across_x, across_y], late)
    halves = halves_call(across_x, across_y)
    far = [send_seq(halves[0], 4), send_seq(halves[1], 2)]
    (late,) = after([late], *halves)
    late_shares = [late] + [send_seq(late, flip) for flip in (2, 4, 6)]
    near = [send_seq(one, 1) for one in (across_x, across_y)]
    merge = lambda start, rows, sources, route: merge_call(
        start, rows, sources, inputs, ordered, merge_gain_row, merge_rows, bias, packs, route
    )
    sources = [[own], [own_swap], [across_x], near[:1], [across_y], near[1:], far]
    (projected,) = merge(0, first_rows, sources + [[send_seq(one, 1) for one in far]], ())
    late_shares[1:] = [after([one], projected)[0] for one in late_shares[1:]]
    sources = [[one] for share in late_shares for one in (share, send_seq(share, 1))]
    made = merge(first_rows, last_rows, sources, (info, most, note, projected))
    blocks = [made[0]] + [
        lax.ppermute(made[flip], "pack", [(z, z ^ flip) for z in range(packs)])
        for flip in range(packs - 1, 0, -1)
    ]
    return place_call(info, blocks, most, merge_weight.shape[1])[None]


def local(*arguments):
    patches, weight = arguments[0], arguments[4]
    shards = lax.axis_size("seq")
    fits = shards == 8 and HEADS // shards == 2 and weight.shape[1] == 6 * HD
    fits = fits and patches.shape[1] * shards == sum(CHUNKS) and lax.axis_size("pack") == 4
    return fast_local(*arguments) if fits else general_local(*arguments)


def solution(mesh):
    placed = (
        P("pack", "seq", None),
        P("pack", "seq"),
        P(),
        P(),
        P(None, "seq"),
        P("pack", "seq"),
        P("pack", "seq"),
        P("pack", "seq"),
        P(),
        P(),
        P(None, "seq"),
        P("seq"),
        P("pack", None),
    )
    return jax.shard_map(
        local, mesh=mesh, in_specs=placed, out_specs=P("pack", None, None, "seq"), check_vma=False
    )
```

```python
import functools

import jax
import jax.numpy as jnp
import numpy as np
from jax import lax
from jax.experimental import pallas as pl
from jax.experimental.pallas import tpu as pltpu
from jax.sharding import PartitionSpec as P

D = 1408
HEADS = 16
HD = 88


EPSILON = 1e-06


def layer_norm(values, gain_vector):
    center = values - jnp.mean(values, axis=-1, keepdims=True)
    spread = jnp.mean(center * center, axis=-1, keepdims=True)
    return center * lax.rsqrt(spread + EPSILON) * gain_vector.astype(jnp.float32)


def rotate(vectors, row_index, column_index):
    total_rows, heads_here, head_width = vectors.shape
    quarter = head_width // 4
    frequency = 10000.0 ** (-jnp.arange(quarter, dtype=jnp.float32) / quarter)
    row_angle = row_index.astype(jnp.float32)[:, None] * frequency[None, :]
    column_angle = column_index.astype(jnp.float32)[:, None] * frequency[None, :]
    angles = jnp.stack([row_angle, column_angle], axis=1)[:, None, :, None, :]
    split_up = vectors.reshape(total_rows, heads_here, 2, 2, quarter)
    partner = jnp.stack([-split_up[:, :, :, 1], split_up[:, :, :, 0]], axis=3)
    turned = split_up * jnp.cos(angles) + partner * jnp.sin(angles)
    return turned.reshape(total_rows, heads_here, head_width)


def qkv_block(projected, row_index, column_index):
    turned_queries = rotate(projected[:, :, 0], row_index, column_index)
    turned_keys = rotate(projected[:, :, 1], row_index, column_index)
    return jnp.concatenate([turned_queries, turned_keys, projected[:, :, 2]], axis=-1).astype(
        jnp.bfloat16
    )


def attention(block, segments):
    total_rows, heads_here, triple = block.shape
    head_width = triple // 3
    step_rows = min(512, total_rows)
    query_part = block[:, :, :head_width].reshape(
        total_rows // step_rows, step_rows, heads_here, head_width
    )
    key_part = block[:, :, head_width : 2 * head_width]
    value_part = block[:, :, 2 * head_width :]
    query_segments = segments.reshape(total_rows // step_rows, step_rows)
    scale = head_width ** (-0.5)

    def one_block(inputs_pair):
        queries_here, segments_here = inputs_pair
        scores = (
            jnp.einsum("qhd,khd->hqk", queries_here, key_part, preferred_element_type=jnp.float32)
            * scale
        )
        same_image = (segments_here[:, None] == segments[None, :])[None]
        scores = jnp.where(same_image, scores, -jnp.inf)
        highest = jnp.max(scores, axis=-1, keepdims=True)
        weights = jnp.exp(scores - highest)
        probs = (weights / jnp.sum(weights, axis=-1, keepdims=True)).astype(jnp.bfloat16)
        result = jnp.einsum("hqk,khd->qhd", probs, value_part, preferred_element_type=jnp.float32)
        return result.astype(jnp.bfloat16)

    return lax.map(one_block, (query_part, query_segments)).reshape(
        total_rows, heads_here, head_width
    )


def route(projected, segments, owners_here, packs, most):
    merged_segments = segments[::4]
    images = owners_here.shape[0]
    image_ids = jnp.arange(images, dtype=jnp.int32)
    member = (merged_segments[None, :] == image_ids[:, None]).astype(jnp.int32)
    lengths = jnp.sum(member, axis=1, dtype=jnp.int32)
    starts = jnp.cumsum(lengths, dtype=jnp.int32) - lengths
    owner_ids = jnp.arange(packs, dtype=jnp.int32)
    owned = owners_here[None, :] == owner_ids[:, None]
    first_row = jnp.sum(jnp.where(owned, starts[None, :], 0), axis=1, dtype=jnp.int32)
    owned_length = jnp.sum(jnp.where(owned, lengths[None, :], 0), axis=1, dtype=jnp.int32)
    slots = jnp.arange(most, dtype=jnp.int32)
    source_rows = jnp.clip(first_row[:, None] + slots[None, :], 0, projected.shape[0] - 1)
    picked = jnp.take(projected, source_rows.reshape(-1), axis=0).reshape(
        packs, most, projected.shape[1]
    )
    filled = slots[None, :] < owned_length[:, None]
    return jnp.where(filled[:, :, None], picked, jnp.zeros_like(picked))


def general_local(
    patches,
    patch_mask,
    mask_embed,
    norm_gain,
    qkv_weight,
    segment_ids,
    patch_rows,
    patch_column,
    out_weight,
    merge_gain,
    merge_weight,
    merge_bias,
    image_owner,
):
    local_rows = patches.shape[1]
    shards = lax.axis_size("seq")
    packs = lax.axis_size("pack")
    heads_here = HEADS // shards
    inputs = jnp.where(patch_mask[0][:, None] == 1, mask_embed[None, :], patches[0])
    normed = layer_norm(inputs.astype(jnp.float32), norm_gain).astype(jnp.bfloat16)
    labels = lax.all_gather(
        jnp.stack([segment_ids[0], patch_rows[0], patch_column[0]]), "seq", axis=1, tiled=True
    )
    piece = lax.all_gather(normed, "seq", axis=0, tiled=True)
    span = piece.shape[0]
    projected = jnp.dot(piece, qkv_weight, preferred_element_type=jnp.float32)
    row_part = labels[1]
    column_part = labels[2]
    block = qkv_block(projected.reshape(span, heads_here, 3, HD), row_part, column_part)
    result = attention(block, labels[0])
    mixed_heads = lax.all_to_all(result, "seq", split_axis=0, concat_axis=1, tiled=True)
    attended = mixed_heads.reshape(local_rows, D)
    residual = inputs.astype(jnp.float32) + jnp.dot(
        attended, out_weight, preferred_element_type=jnp.float32
    )
    merged = layer_norm(residual, merge_gain).astype(jnp.bfloat16).reshape(local_rows // 4, 4 * D)
    projected_all = (
        jnp.dot(
            lax.all_gather(merged, "seq", axis=0, tiled=True),
            merge_weight,
            preferred_element_type=jnp.float32,
        )
        + merge_bias.astype(jnp.float32)
    ).astype(jnp.bfloat16)
    images = image_owner.shape[1]
    most = 2 * projected_all.shape[0] // images
    outgoing = route(projected_all, labels[0], image_owner[0], packs, most)
    delivered = lax.all_to_all(outgoing, "pack", split_axis=0, concat_axis=0, tiled=True)
    return delivered[None]


LANES = 128
CHIP, CORE, PACK, IDS = 0, 1, 2, 3
BLOCK = 512
POSITIONS = 64
FAR_APART = -(2.0**100)
IMAGE_LANE = 96
NORM_ROWS = 16
CHUNKS = (768, 768)


def norm_rows(values, gain_row):
    center = values - jnp.mean(values, axis=-1, keepdims=True)
    spread = jnp.mean(center * center, axis=-1, keepdims=True)
    return center * lax.rsqrt(spread + EPSILON) * gain_row


def stacked(pieces):
    loaded = [piece[...] for piece in pieces]
    return loaded[0] if len(loaded) == 1 else jnp.concatenate(loaded, axis=0)


def in_vmem(value):
    return pltpu.with_memory_space_constraint(value, pltpu.VMEM)


def in_hbm(value):
    return pltpu.with_memory_space_constraint(value, pltpu.HBM)


def payload_kernel(segments, rows, columns, mask, embed, patches, out):
    labels = [one[...].astype(jnp.float32) for one in (segments, rows, columns, mask)]
    labels.append(jnp.zeros((4, labels[0].shape[1]), jnp.float32))
    labels = jnp.concatenate(labels, axis=0).astype(jnp.bfloat16)
    shape = (8, LANES)
    row = lax.broadcasted_iota(jnp.int32, shape, 0)
    place = jnp.where(row == lax.broadcasted_iota(jnp.int32, shape, 1), 1.0, 0.0)
    turned = lax.dot_general(
        labels,
        place.astype(jnp.bfloat16),
        (((0,), (0,)), ((), ())),
        preferred_element_type=jnp.float32,
    )
    masked = turned[:, 3:4] > 0.5
    tokens = jnp.where(
        masked, embed[...].astype(jnp.float32)[None, :], patches[0].astype(jnp.float32)
    )
    out[:, :D] = tokens.astype(jnp.bfloat16)
    out[:, D:] = turned.astype(jnp.bfloat16)


def payload_call(segments, rows, columns, mask, embed, patches):
    count = patches.shape[1]
    operands = (segments, rows, columns, mask, embed, patches)
    fixed = lambda shape: pl.BlockSpec(shape, lambda i: (0,) * len(shape))
    shape = (count, D + LANES)
    return pl.pallas_call(
        payload_kernel,
        grid=(1,),
        in_specs=[fixed(one.shape) for one in operands],
        out_specs=fixed(shape),
        out_shape=jax.ShapeDtypeStruct(shape, jnp.bfloat16),
        compiler_params=pltpu.CompilerParams(vmem_limit_bytes=8 << 20),
        cost_estimate=pl.CostEstimate(
            flops=count * D, bytes_accessed=4 * count * D, transcendentals=0
        ),
        name="payload",
    )(*map(in_hbm, operands))


def qkv_kernel(count, flip, info, *refs):
    first, second = refs[:count], refs[count : 2 * count]
    table, gain, weight = refs[2 * count : 2 * count + 3]
    inputs_out, qkv_out, label_out = refs[-3:]
    mine, other = stacked(first), stacked(second)
    leads = info[CORE] == 0
    ahead = jnp.where(leads, mine, other)
    behind = jnp.where(leads, other, mine)
    both = jnp.concatenate([ahead, behind], axis=0)
    rows = both.shape[0]
    at = pl.ds(pl.multiple_of((info[CHIP] ^ flip) * rows, rows), rows)
    inputs_out[at, :] = both[:, :D]
    label_out[at, :] = both[:, D:]
    labels = both[:, D:].astype(jnp.float32)
    normed = norm_rows(both[:, :D].astype(jnp.float32), gain[...]).astype(jnp.bfloat16)
    columns = lax.dot_general(
        normed, weight[...], (((1,), (1,)), ((), ())), preferred_element_type=jnp.float32
    )
    lane = lax.broadcasted_iota(jnp.int32, labels.shape, 1)
    numbers = lane.astype(jnp.float32)
    hot = (numbers == labels[:, 1:2]) | (numbers == labels[:, 2:3] + POSITIONS)
    looked = jnp.dot(
        jnp.where(hot, 1.0, 0.0).astype(jnp.bfloat16), table[...], preferred_element_type=jnp.float32
    )
    cosine = looked[:, :LANES] + looked[:, LANES : 2 * LANES]
    sine = looked[:, 2 * LANES : 3 * LANES] + looked[:, 3 * LANES :]
    first_head = lane < HD // 2

    def turn(start):
        a = columns[:, start : start + LANES]
        b = columns[:, start + LANES : start + 2 * LANES]
        return a * cosine - b * sine, b * cosine + a * sine

    factor = HD**-0.5 * float(np.log2(np.e))
    query_a, query_b = (one * factor for one in turn(0))
    key_a, key_b = turn(2 * LANES)
    zero = jnp.zeros_like(key_a)
    image = numbers == labels[:, :1] + IMAGE_LANE
    extra = lane >= IMAGE_LANE
    apart = jnp.where(image, 0.0, FAR_APART)
    parts = [
        jnp.where(image, 1.0, query_a),
        query_b,
        jnp.where(extra, apart, jnp.where(first_head, key_a, zero)),
        jnp.where(first_head, key_b, zero),
        jnp.where(extra, apart, jnp.where(first_head, zero, key_a)),
        jnp.where(first_head, zero, key_b),
    ]
    for head in range(2):
        values = columns[:, (4 + head) * LANES : (5 + head) * LANES]
        parts.append(jnp.where(lane == HD, 1.0, values))
    for number, part in enumerate(parts):
        qkv_out[at, number * LANES : (number + 1) * LANES] = part.astype(jnp.bfloat16)


def qkv_call(info, flip, first, second, table, gain, weight, earlier, total):
    rows = 2 * sum(piece.shape[0] for piece in first)
    widths = (D, 8 * LANES, LANES)
    operands = [*first, *second, table, gain, in_vmem(weight)]
    vmem = pl.BlockSpec(memory_space=pltpu.VMEM)
    held = [in_vmem(one) for one in earlier]
    return pl.pallas_call(
        functools.partial(qkv_kernel, len(first), flip),
        in_specs=[pl.BlockSpec(memory_space=pltpu.SMEM)]
        + [vmem] * (len(operands) + len(earlier)),
        out_specs=[vmem] * len(widths),
        out_shape=[pltpu.VMEM((total, width), jnp.bfloat16) for width in widths],
        input_output_aliases={1 + len(operands) + i: i for i in range(len(earlier))},
        compiler_params=pltpu.CompilerParams(vmem_limit_bytes=14 << 20),
        cost_estimate=pl.CostEstimate(
            flops=6 * rows * D * weight.shape[0],
            bytes_accessed=2 * (rows * 4 * D + weight.size),
            transcendentals=rows,
        ),
        name="norm_qkv",
    )(info, *operands, *held)


def segment_row(labels):
    pick = jnp.where(lax.broadcasted_iota(jnp.int32, (8, LANES), 1) == 0, 1.0, 0.0)
    return lax.dot_general(
        pick.astype(jnp.bfloat16),
        labels,
        (((1,), (1,)), ((), ())),
        preferred_element_type=jnp.float32,
    )


def attention_kernel(start, first_owner, images, info, labels, block, *refs):
    out, *rest = refs
    scores, high = rest[-2:]
    rows = high.shape[1]
    total = block.shape[0]
    segments = segment_row(labels[...])
    one_row = segments[:1]
    lowest = jnp.min(labels[start : start + 16, :1].astype(jnp.float32), axis=0, keepdims=True)
    largest = labels[start + rows - 16 : start + rows, :1].astype(jnp.float32)
    largest = jnp.max(largest, axis=0, keepdims=True)
    begin = jnp.sum(jnp.where(one_row < lowest, 1, 0)) // BLOCK
    end = (jnp.sum(jnp.where(one_row <= largest, 1, 0)) + BLOCK - 1) // BLOCK
    queries = block[start : start + rows, : 2 * LANES]
    high[...] = jnp.full_like(high, 2 * FAR_APART)

    def score(step, carry):
        at = pl.ds(pl.multiple_of(step * BLOCK, BLOCK), BLOCK)
        for head in range(2):
            keys = block[at, (2 + 2 * head) * LANES : (4 + 2 * head) * LANES]
            values = lax.dot_general(
                queries, keys, (((1,), (1,)), ((), ())), preferred_element_type=jnp.float32
            )
            scores[head, step] = values
            tops = [values[:, lane : lane + LANES] for lane in range(0, BLOCK, LANES)]
            high[head] = functools.reduce(jnp.maximum, tops, high[head])
        return carry

    lax.fori_loop(begin, end, score, 0)
    highest = [jnp.max(high[head], axis=-1, keepdims=True) for head in range(2)]

    def weigh(step, carry):
        at = pl.ds(pl.multiple_of(step * BLOCK, BLOCK), BLOCK)
        sums = []
        for head in range(2):
            weights = jnp.exp2(scores[head, step] - highest[head])
            values = block[at, (6 + head) * LANES : (7 + head) * LANES]
            sums.append(
                carry[head]
                + jnp.dot(weights.astype(jnp.bfloat16), values, preferred_element_type=jnp.float32)
            )
        return tuple(sums)

    zero = jnp.zeros((rows, LANES), jnp.float32)
    sums = lax.fori_loop(begin, end, weigh, (zero, zero))
    first, second = (one / one[:, HD : HD + 1] for one in sums)
    lane = lax.broadcasted_iota(jnp.int32, first.shape, 1)
    turned = pltpu.roll(second, HD, 1)
    out[:rows] = jnp.where(lane < HD, first, turned).astype(jnp.bfloat16)
    half = rows // 2
    tail = 2 * HD - LANES
    lane = lane[:half]
    up = pltpu.roll(turned[half:], tail, 1)
    packed = jnp.where(lane < tail, turned[:half], jnp.where(lane < 2 * tail, up, 0.0))
    out[rows:] = packed.astype(jnp.bfloat16)

    if len(rest) > 2:
        note = rest[0]
        row = lax.broadcasted_iota(jnp.int32, note.shape, 0)
        lane = lax.broadcasted_iota(jnp.int32, note.shape, 1)
        found = jnp.zeros(note.shape, jnp.float32)
        for image in range(images):
            below = jnp.sum(jnp.where(one_row < image, 0.25, 0.0), axis=1, keepdims=True)
            inside = jnp.sum(jnp.where(one_row == image, 0.25, 0.0), axis=1, keepdims=True)
            here = row == info[first_owner + image]
            for place, number in enumerate((below, inside)):
                upper = jnp.floor(number * (1.0 / 16))
                found = jnp.where(here & (lane == 2 * place), upper, found)
                found = jnp.where(here & (lane == 2 * place + 1), number - 16 * upper, found)
        note[...] = found.astype(jnp.bfloat16)


def attention_call(start, rows, first_owner, info, labels, block, noted):
    total = block.shape[0]
    vmem = pl.BlockSpec(memory_space=pltpu.VMEM)
    shapes = [jax.ShapeDtypeStruct((rows + rows // 2, LANES), jnp.bfloat16)]
    if noted:
        shapes.append(jax.ShapeDtypeStruct((16, LANES), jnp.bfloat16))
    return pl.pallas_call(
        functools.partial(attention_kernel, start, first_owner, info.shape[0] - first_owner),
        in_specs=[pl.BlockSpec(memory_space=pltpu.SMEM), vmem, vmem],
        out_specs=[vmem] * len(shapes),
        out_shape=shapes,
        scratch_shapes=[
            pltpu.VMEM((2, total // BLOCK, rows, BLOCK), jnp.float32),
            pltpu.VMEM((2, rows, LANES), jnp.float32),
        ],
        compiler_params=pltpu.CompilerParams(vmem_limit_bytes=20 << 20),
        cost_estimate=pl.CostEstimate(
            flops=10 * rows * total * 2 * LANES,
            bytes_accessed=2 * block.size,
            transcendentals=rows * total,
        ),
        name="attention",
    )(info, in_vmem(labels), in_vmem(block))


def prepare_kernel(shards, info, out_weight, merge_weight, qkv_weight, spread, *refs):
    *rows, out, merge, qkv, qkv_buffer, spread_buffer, sems = refs
    for row, row_out in zip(rows[: len(rows) // 2], rows[len(rows) // 2 :]):
        row_out[...] = row[...].astype(jnp.float32)[None, :]
    rest = 2 * HD - LANES
    copies = [(qkv_weight, qkv_buffer), (spread, spread_buffer)]
    out[shards * LANES :] = jnp.zeros((shards // 2 * LANES, D), jnp.bfloat16)
    for place in range(shards):
        start = pl.multiple_of(info[IDS + place] * (2 * HD), 16)
        to = (shards + place // 2) * LANES + place % 2 * rest
        copies.append(
            (out_weight.at[pl.ds(start, LANES), :], out.at[pl.ds(place * LANES, LANES), :])
        )
        copies.append((out_weight.at[pl.ds(start + LANES, rest), :], out.at[pl.ds(to, rest), :]))
    copies.append((merge_weight, merge))
    copies = [
        pltpu.make_async_copy(source, target, sems.at[i])
        for i, (source, target) in enumerate(copies)
    ]
    for copy in copies:
        copy.start()
    copies[0].wait()
    copies[1].wait()
    qkv[...] = jnp.dot(
        spread_buffer[...], qkv_buffer[...], preferred_element_type=jnp.float32
    ).astype(jnp.bfloat16)
    for copy in copies[2:]:
        copy.wait()


def prepare_call(shards, info, out_weight, merge_weight, qkv_weight, spread, rows):
    anywhere = pl.BlockSpec(memory_space=pl.ANY)
    vmem = pl.BlockSpec(memory_space=pltpu.VMEM)
    operands = (out_weight, merge_weight, qkv_weight, spread)
    shapes = [(shards * LANES * 3 // 2, D), merge_weight.shape, (spread.shape[0], D)]
    return pl.pallas_call(
        functools.partial(prepare_kernel, shards),
        in_specs=[pl.BlockSpec(memory_space=pltpu.SMEM)]
        + [anywhere] * len(operands)
        + [vmem] * len(rows),
        out_specs=[vmem] * (len(rows) + len(shapes)),
        out_shape=[pltpu.VMEM((1, row.shape[0]), jnp.float32) for row in rows]
        + [pltpu.VMEM(shape, jnp.bfloat16) for shape in shapes],
        scratch_shapes=[
            pltpu.VMEM(qkv_weight.shape, jnp.bfloat16),
            pltpu.VMEM(spread.shape, jnp.bfloat16),
            pltpu.SemaphoreType.DMA((2 * shards + 3,)),
        ],
        compiler_params=pltpu.CompilerParams(vmem_limit_bytes=10 << 20),
        cost_estimate=pl.CostEstimate(
            flops=2 * spread.size * D,
            bytes_accessed=4 * (out_weight.size + merge_weight.size + qkv_weight.size),
            transcendentals=0,
        ),
        name="prepare",
    )(info, *map(in_hbm, operands), *rows)


def merge_kernel(start, counts, packs, last, *refs):
    inputs, weight, gain, merge_weight, bias = refs[:5]
    pieces = refs[5 : 5 + sum(counts)]
    *refs, state, tokens = refs[5 + sum(counts) :]
    rows = state.shape[1]
    half = rows // 2
    rest = 2 * HD - LANES
    sources, at = [], 0
    for count in counts:
        sources.append(stacked(pieces[at : at + count]))
        at += count
    shards = len(sources)
    lane = lax.broadcasted_iota(jnp.int32, (half, LANES), 1)
    lined = [source[:rows, :] for source in sources]
    for pair in range(shards // 2):
        mine = sources[2 * pair][rows:, :].astype(jnp.float32)
        other = sources[2 * pair + 1][rows:, :].astype(jnp.float32)
        upper = jnp.where(lane < rest, mine, pltpu.roll(other, rest, 1))
        lower = jnp.where(lane < rest, pltpu.roll(mine, LANES - rest, 1), other)
        lined.append(jnp.concatenate([upper, lower], axis=0).astype(jnp.bfloat16))
    mixed = jnp.dot(
        jnp.concatenate(lined, axis=1), weight[...], preferred_element_type=jnp.float32
    )
    for column in range(D // LANES):
        lanes = slice(column * LANES, (column + 1) * LANES)
        before = inputs[start : start + rows, lanes]
        state[column] = before.astype(jnp.float32) + mixed[:, lanes]
    groups = rows // 4
    for block in range(0, groups, NORM_ROWS):
        for quadrant in range(4):
            at = pl.ds(4 * block + quadrant, NORM_ROWS, stride=4)
            residual = jnp.concatenate(
                [state[column, at, :] for column in range(D // LANES)], axis=1
            )
            tokens[block : block + NORM_ROWS, quadrant * D : (quadrant + 1) * D] = norm_rows(
                residual, gain[...]
            ).astype(jnp.bfloat16)
    total = bias[...] + lax.dot_general(
        tokens[...], merge_weight[...], (((1,), (1,)), ((), ())), preferred_element_type=jnp.float32
    )
    total = total.astype(jnp.bfloat16)
    if not last:
        refs[0][...] = total
        return
    info, note, *earlier = refs[:-packs]
    outs = refs[-packs:]
    total = jnp.concatenate([*[one[...] for one in earlier], total], axis=0)
    whole = total.shape[1] // LANES
    most = outs[0].shape[0] * LANES // total.shape[1]
    notes = note[...].astype(jnp.float32)
    note_row = lax.broadcasted_iota(jnp.int32, notes.shape, 0)
    slot = lax.broadcasted_iota(jnp.int32, (most, total.shape[0]), 0)
    row = lax.broadcasted_iota(jnp.int32, (most, total.shape[0]), 1)
    for place, out in enumerate(outs):
        found = jnp.where(note_row == (info[PACK] ^ place), notes, 0.0)
        found = jnp.sum(found, axis=0, keepdims=True)
        first = (16.0 * found[:, :1] + found[:, 1:2]).astype(jnp.int32)
        length = (16.0 * found[:, 2:3] + found[:, 3:4]).astype(jnp.int32)
        chosen = (row == slot + first) & (slot < length)
        chosen = jnp.where(chosen, 1.0, 0.0).astype(jnp.bfloat16)
        block = jnp.dot(chosen, total, preferred_element_type=jnp.float32)
        for column in range(whole):
            out[column * most : (column + 1) * most, :] = block[
                :, column * LANES : (column + 1) * LANES
            ].astype(jnp.bfloat16)
        low = block[: most // 2, whole * LANES :]
        up = block[most // 2 :, whole * LANES :]
        out[whole * most :, :] = jnp.concatenate([low, up], axis=1).astype(jnp.bfloat16)


def merge_call(start, rows, sources, inputs, weight, gain, merge_weight, bias, packs, route):
    groups = rows // 4
    width = merge_weight.shape[0]
    pieces = [piece for source in sources for piece in source]
    vmem = pl.BlockSpec(memory_space=pltpu.VMEM)
    operands = [in_vmem(inputs), in_vmem(weight), gain, in_vmem(merge_weight), bias, *pieces]
    specs = [vmem] * len(operands)
    shapes = [jax.ShapeDtypeStruct((groups, width), jnp.bfloat16)]
    if route:
        me, most, *others = route
        operands += [me, *others]
        specs += [pl.BlockSpec(memory_space=pltpu.SMEM)] + [vmem] * len(others)
        shapes = [jax.ShapeDtypeStruct((most * width // LANES, LANES), jnp.bfloat16)] * packs
    return pl.pallas_call(
        functools.partial(
            merge_kernel, start, [len(source) for source in sources], packs, bool(route)
        ),
        in_specs=specs,
        out_specs=[vmem] * len(shapes),
        scratch_shapes=[
            pltpu.VMEM((D // LANES, rows, LANES), jnp.float32),
            pltpu.VMEM((groups, 4 * D), jnp.bfloat16),
        ],
        out_shape=shapes,
        compiler_params=pltpu.CompilerParams(vmem_limit_bytes=20 << 20),
        cost_estimate=pl.CostEstimate(
            flops=0,
            bytes_accessed=1024,
            transcendentals=rows,
        ),
        name="out_merge",
    )(*operands)


def place_kernel(place, info, block, *refs):
    out, rows, sem = refs[-3:]
    most, width = rows.shape
    whole = width // LANES
    half = most // 2
    middle = LANES // 2
    for column in range(whole):
        rows[:, column * LANES : (column + 1) * LANES] = block[
            column * most : (column + 1) * most, :
        ]
    rows[:half, whole * LANES :] = block[whole * most :, :middle]
    rows[half:, whole * LANES :] = block[whole * most :, middle:]
    copy = pltpu.make_async_copy(rows, out.at[info[PACK] ^ place], sem)
    copy.start()
    copy.wait()


def place_call(info, place, block, earlier, shape):
    anywhere = pl.BlockSpec(memory_space=pl.ANY)
    return pl.pallas_call(
        functools.partial(place_kernel, place),
        in_specs=[
            pl.BlockSpec(memory_space=pltpu.SMEM),
            pl.BlockSpec(memory_space=pltpu.VMEM),
        ]
        + [anywhere] * len(earlier),
        out_specs=anywhere,
        out_shape=pltpu.HBM(shape, jnp.bfloat16),
        scratch_shapes=[pltpu.VMEM(shape[1:], jnp.bfloat16), pltpu.SemaphoreType.DMA],
        input_output_aliases={2: 0} if earlier else {},
        compiler_params=pltpu.CompilerParams(vmem_limit_bytes=4 << 20),
        cost_estimate=pl.CostEstimate(
            flops=0, bytes_accessed=4 * shape[1] * shape[2], transcendentals=0
        ),
        name="place_rows",
    )(info, block, *map(in_hbm, earlier))


def send_seq(value, flip):
    size = lax.axis_size("seq")
    return lax.ppermute(value, "seq", [(i, i ^ flip) for i in range(size)])


def after(values, *earlier):
    return lax.optimization_barrier((tuple(values), earlier))[0]


def halves_kernel(across_x, across_y, upper, lower):
    half = upper.shape[0]
    upper[...] = across_x[:half]
    lower[...] = across_y[half:]


def halves_call(across_x, across_y):
    vmem = pl.BlockSpec(memory_space=pltpu.VMEM)
    shape = (across_x.shape[0] // 2, across_x.shape[1])
    return pl.pallas_call(
        halves_kernel,
        in_specs=[vmem] * 2,
        out_specs=[vmem] * 2,
        out_shape=[jax.ShapeDtypeStruct(shape, across_x.dtype)] * 2,
        compiler_params=pltpu.CompilerParams(vmem_limit_bytes=4 << 20),
        cost_estimate=pl.CostEstimate(
            flops=0, bytes_accessed=4 * across_x.size, transcendentals=0
        ),
        name="halves",
    )(across_x, across_y)


def near_shards(value):
    return [send_seq(value, 1), send_seq(value, 2), send_seq(value, 4)]


def far_shards(across_x, across_y):
    upper, lower = halves_call(across_x, across_y)
    return [send_seq(upper, 4), send_seq(lower, 2)]


def weight_order(heads_here):
    quarter = HD // 4
    order = -np.ones((6 * LANES,), np.int32)
    for head in range(heads_here):
        base = head * 3 * HD
        for kind in range(2):
            for half in range(2):
                for letter in range(2):
                    target = (2 * kind + letter) * LANES + head * (HD // 2) + half * quarter
                    source = base + kind * HD + half * (HD // 2) + letter * quarter
                    order[target : target + quarter] = np.arange(source, source + quarter)
        target = (4 + head) * LANES
        order[target : target + HD] = np.arange(base + 2 * HD, base + 3 * HD)
    return order


def angle_table(heads_here):
    quarter = HD // 4
    frequency = (10000.0 ** (-np.arange(quarter) / quarter)).astype(np.float32)
    angles = np.arange(POSITIONS, dtype=np.float32)[:, None] * frequency[None, :]
    pieces = []
    for function in (np.cos, np.sin):
        exact = np.zeros((2 * POSITIONS, LANES), np.float64)
        for head in range(heads_here):
            for half in range(2):
                lane = head * (HD // 2) + half * quarter
                rows = slice(half * POSITIONS, (half + 1) * POSITIONS)
                exact[rows, lane : lane + quarter] = function(angles.astype(np.float64))
        upper = exact.astype(jnp.bfloat16)
        pieces += [upper, (exact - upper.astype(np.float64)).astype(jnp.bfloat16)]
    return np.concatenate(pieces, axis=1)


def fast_local(
    patches,
    patch_mask,
    mask_embed,
    norm_gain,
    qkv_weight,
    segment_ids,
    patch_rows,
    patch_column,
    out_weight,
    merge_gain,
    merge_weight,
    merge_bias,
    image_owner,
):
    local_rows = patches.shape[1]
    shards = lax.axis_size("seq")
    packs = lax.axis_size("pack")
    heads_here = HEADS // shards
    images = image_owner.shape[1]
    total = local_rows * shards
    me = lax.axis_index("seq").astype(jnp.int32)
    pack = lax.axis_index("pack").astype(jnp.int32)

    value = payload_call(segment_ids, patch_rows, patch_column, patch_mask, mask_embed, patches)
    own_swap, across_x, across_y = near_shards(value)

    order = weight_order(heads_here)
    spread = (order[:, None] == np.arange(qkv_weight.shape[1])[None, :]).astype(jnp.bfloat16)
    table = jnp.asarray(angle_table(heads_here))
    chip, core = me // 2, me % 2
    info = [chip, core, pack, *[me ^ place for place in range(shards)]]
    info = jnp.concatenate([jnp.stack(info), image_owner[0]])
    gain, merge_gain_row, bias, ordered, merge_rows, weight = prepare_call(
        shards,
        info,
        out_weight,
        merge_weight.T,
        qkv_weight.T,
        jnp.asarray(spread),
        (norm_gain, merge_gain, merge_bias),
    )

    project = lambda place, first, second, earlier: qkv_call(
        info, place, first, second, table, gain, weight, earlier, total
    )
    buffers = project(0, [value], [own_swap], ())
    across_x, across_y = after([across_x, across_y], buffers[2], ordered)
    far = far_shards(across_x, across_y)
    buffers = project(1, [across_x], [send_seq(across_x, 1)], buffers)
    buffers = project(2, [across_y], [send_seq(across_y, 1)], buffers)
    far = after(far, buffers[2])
    buffers = project(3, far, [send_seq(one, 1) for one in far], buffers)
    inputs, block, labels = buffers

    most = 2 * (total // 4) // images
    first_rows, last_rows = CHUNKS
    attend = functools.partial(attention_call, first_owner=IDS + shards, info=info)
    own, note = attend(0, first_rows, labels=labels, block=block, noted=True)
    own_swap, across_x, across_y = near_shards(own)
    labels, block = after([labels, block], own)
    (late,) = attend(first_rows, last_rows, labels=labels, block=block, noted=False)
    across_x, across_y = after([across_x, across_y], late)
    halves = halves_call(across_x, across_y)
    far = [send_seq(halves[0], 4), send_seq(halves[1], 2)]
    (late,) = after([late], *halves)
    late_shares = [late] + [send_seq(late, flip) for flip in (2, 4, 6)]
    near = [send_seq(one, 1) for one in (across_x, across_y)]
    merge = lambda start, rows, sources, route: merge_call(
        start, rows, sources, inputs, ordered, merge_gain_row, merge_rows, bias, packs, route
    )
    sources = [[own], [own_swap], [across_x], near[:1], [across_y], near[1:], far]
    (projected,) = merge(0, first_rows, sources + [[send_seq(one, 1) for one in far]], ())
    late_shares[1:] = [after([one], projected)[0] for one in late_shares[1:]]
    sources = [[one] for share in late_shares for one in (share, send_seq(share, 1))]
    made = merge(first_rows, last_rows, sources, (info, most, note, projected))
    sent = {
        flip: lax.ppermute(made[flip], "pack", [(z, z ^ flip) for z in range(packs)])
        for flip in range(packs - 1, 0, -1)
    }
    shape = (packs, most, merge_weight.shape[1])
    routed = place_call(info, 0, made[0], (), shape)
    for flip in (3, 1, 2):
        routed = place_call(info, flip, sent[flip], (routed,), shape)
    return routed[None]


def local(*arguments):
    patches, weight = arguments[0], arguments[4]
    shards = lax.axis_size("seq")
    fits = shards == 8 and HEADS // shards == 2 and weight.shape[1] == 6 * HD
    fits = fits and patches.shape[1] * shards == sum(CHUNKS) and lax.axis_size("pack") == 4
    return fast_local(*arguments) if fits else general_local(*arguments)


def solution(mesh):
    placed = (
        P("pack", "seq", None),
        P("pack", "seq"),
        P(),
        P(),
        P(None, "seq"),
        P("pack", "seq"),
        P("pack", "seq"),
        P("pack", "seq"),
        P(),
        P(),
        P(None, "seq"),
        P("seq"),
        P("pack", None),
    )
    return jax.shard_map(
        local, mesh=mesh, in_specs=placed, out_specs=P("pack", None, None, "seq"), check_vma=False
    )
```

```python
import functools

import jax
import jax.numpy as jnp
import numpy as np
from jax import lax
from jax.experimental import pallas as pl
from jax.experimental.pallas import tpu as pltpu
from jax.sharding import PartitionSpec as P

D = 1408
HEADS = 16
HD = 88


EPSILON = 1e-06


def layer_norm(values, gain_vector):
    center = values - jnp.mean(values, axis=-1, keepdims=True)
    spread = jnp.mean(center * center, axis=-1, keepdims=True)
    return center * lax.rsqrt(spread + EPSILON) * gain_vector.astype(jnp.float32)


def rotate(vectors, row_index, column_index):
    total_rows, heads_here, head_width = vectors.shape
    quarter = head_width // 4
    frequency = 10000.0 ** (-jnp.arange(quarter, dtype=jnp.float32) / quarter)
    row_angle = row_index.astype(jnp.float32)[:, None] * frequency[None, :]
    column_angle = column_index.astype(jnp.float32)[:, None] * frequency[None, :]
    angles = jnp.stack([row_angle, column_angle], axis=1)[:, None, :, None, :]
    split_up = vectors.reshape(total_rows, heads_here, 2, 2, quarter)
    partner = jnp.stack([-split_up[:, :, :, 1], split_up[:, :, :, 0]], axis=3)
    turned = split_up * jnp.cos(angles) + partner * jnp.sin(angles)
    return turned.reshape(total_rows, heads_here, head_width)


def qkv_block(projected, row_index, column_index):
    turned_queries = rotate(projected[:, :, 0], row_index, column_index)
    turned_keys = rotate(projected[:, :, 1], row_index, column_index)
    return jnp.concatenate([turned_queries, turned_keys, projected[:, :, 2]], axis=-1).astype(
        jnp.bfloat16
    )


def attention(block, segments):
    total_rows, heads_here, triple = block.shape
    head_width = triple // 3
    step_rows = min(512, total_rows)
    query_part = block[:, :, :head_width].reshape(
        total_rows // step_rows, step_rows, heads_here, head_width
    )
    key_part = block[:, :, head_width : 2 * head_width]
    value_part = block[:, :, 2 * head_width :]
    query_segments = segments.reshape(total_rows // step_rows, step_rows)
    scale = head_width ** (-0.5)

    def one_block(inputs_pair):
        queries_here, segments_here = inputs_pair
        scores = (
            jnp.einsum("qhd,khd->hqk", queries_here, key_part, preferred_element_type=jnp.float32)
            * scale
        )
        same_image = (segments_here[:, None] == segments[None, :])[None]
        scores = jnp.where(same_image, scores, -jnp.inf)
        highest = jnp.max(scores, axis=-1, keepdims=True)
        weights = jnp.exp(scores - highest)
        probs = (weights / jnp.sum(weights, axis=-1, keepdims=True)).astype(jnp.bfloat16)
        result = jnp.einsum("hqk,khd->qhd", probs, value_part, preferred_element_type=jnp.float32)
        return result.astype(jnp.bfloat16)

    return lax.map(one_block, (query_part, query_segments)).reshape(
        total_rows, heads_here, head_width
    )


def route(projected, segments, owners_here, packs, most):
    merged_segments = segments[::4]
    images = owners_here.shape[0]
    image_ids = jnp.arange(images, dtype=jnp.int32)
    member = (merged_segments[None, :] == image_ids[:, None]).astype(jnp.int32)
    lengths = jnp.sum(member, axis=1, dtype=jnp.int32)
    starts = jnp.cumsum(lengths, dtype=jnp.int32) - lengths
    owner_ids = jnp.arange(packs, dtype=jnp.int32)
    owned = owners_here[None, :] == owner_ids[:, None]
    first_row = jnp.sum(jnp.where(owned, starts[None, :], 0), axis=1, dtype=jnp.int32)
    owned_length = jnp.sum(jnp.where(owned, lengths[None, :], 0), axis=1, dtype=jnp.int32)
    slots = jnp.arange(most, dtype=jnp.int32)
    source_rows = jnp.clip(first_row[:, None] + slots[None, :], 0, projected.shape[0] - 1)
    picked = jnp.take(projected, source_rows.reshape(-1), axis=0).reshape(
        packs, most, projected.shape[1]
    )
    filled = slots[None, :] < owned_length[:, None]
    return jnp.where(filled[:, :, None], picked, jnp.zeros_like(picked))


def general_local(
    patches,
    patch_mask,
    mask_embed,
    norm_gain,
    qkv_weight,
    segment_ids,
    patch_rows,
    patch_column,
    out_weight,
    merge_gain,
    merge_weight,
    merge_bias,
    image_owner,
):
    local_rows = patches.shape[1]
    shards = lax.axis_size("seq")
    packs = lax.axis_size("pack")
    heads_here = HEADS // shards
    inputs = jnp.where(patch_mask[0][:, None] == 1, mask_embed[None, :], patches[0])
    normed = layer_norm(inputs.astype(jnp.float32), norm_gain).astype(jnp.bfloat16)
    labels = lax.all_gather(
        jnp.stack([segment_ids[0], patch_rows[0], patch_column[0]]), "seq", axis=1, tiled=True
    )
    piece = lax.all_gather(normed, "seq", axis=0, tiled=True)
    span = piece.shape[0]
    projected = jnp.dot(piece, qkv_weight, preferred_element_type=jnp.float32)
    row_part = labels[1]
    column_part = labels[2]
    block = qkv_block(projected.reshape(span, heads_here, 3, HD), row_part, column_part)
    result = attention(block, labels[0])
    mixed_heads = lax.all_to_all(result, "seq", split_axis=0, concat_axis=1, tiled=True)
    attended = mixed_heads.reshape(local_rows, D)
    residual = inputs.astype(jnp.float32) + jnp.dot(
        attended, out_weight, preferred_element_type=jnp.float32
    )
    merged = layer_norm(residual, merge_gain).astype(jnp.bfloat16).reshape(local_rows // 4, 4 * D)
    projected_all = (
        jnp.dot(
            lax.all_gather(merged, "seq", axis=0, tiled=True),
            merge_weight,
            preferred_element_type=jnp.float32,
        )
        + merge_bias.astype(jnp.float32)
    ).astype(jnp.bfloat16)
    images = image_owner.shape[1]
    most = 2 * projected_all.shape[0] // images
    outgoing = route(projected_all, labels[0], image_owner[0], packs, most)
    delivered = lax.all_to_all(outgoing, "pack", split_axis=0, concat_axis=0, tiled=True)
    return delivered[None]


LANES = 128
BLOCK = 512
POSITIONS = 64
FAR_APART = -(2.0**100)
IMAGE_LANE = 96
NORM_ROWS = 16
CHUNKS = (768, 768)


def norm_rows(values, gain_row):
    center = values - jnp.mean(values, axis=-1, keepdims=True)
    spread = jnp.mean(center * center, axis=-1, keepdims=True)
    return center * lax.rsqrt(spread + EPSILON) * gain_row


def stacked(pieces):
    loaded = [piece[...] for piece in pieces]
    return loaded[0] if len(loaded) == 1 else jnp.concatenate(loaded, axis=0)


def in_vmem(value):
    return pltpu.with_memory_space_constraint(value, pltpu.VMEM)


def in_hbm(value):
    return pltpu.with_memory_space_constraint(value, pltpu.HBM)


def payload_kernel(segments, rows, columns, mask, embed, patches, out):
    labels = [one[...].astype(jnp.float32) for one in (segments, rows, columns, mask)]
    labels.append(jnp.zeros((4, labels[0].shape[1]), jnp.float32))
    labels = jnp.concatenate(labels, axis=0).astype(jnp.bfloat16)
    shape = (8, LANES)
    row = lax.broadcasted_iota(jnp.int32, shape, 0)
    place = jnp.where(row == lax.broadcasted_iota(jnp.int32, shape, 1), 1.0, 0.0)
    turned = lax.dot_general(
        labels,
        place.astype(jnp.bfloat16),
        (((0,), (0,)), ((), ())),
        preferred_element_type=jnp.float32,
    )
    masked = turned[:, 3:4] > 0.5
    tokens = jnp.where(
        masked, embed[...].astype(jnp.float32)[None, :], patches[0].astype(jnp.float32)
    )
    out[:, :D] = tokens.astype(jnp.bfloat16)
    out[:, D:] = turned.astype(jnp.bfloat16)


def payload_call(segments, rows, columns, mask, embed, patches):
    count = patches.shape[1]
    operands = (segments, rows, columns, mask, embed, patches)
    fixed = lambda shape: pl.BlockSpec(shape, lambda i: (0,) * len(shape))
    shape = (count, D + LANES)
    return pl.pallas_call(
        payload_kernel,
        grid=(1,),
        in_specs=[fixed(one.shape) for one in operands],
        out_specs=fixed(shape),
        out_shape=jax.ShapeDtypeStruct(shape, jnp.bfloat16),
        compiler_params=pltpu.CompilerParams(vmem_limit_bytes=8 << 20),
        cost_estimate=pl.CostEstimate(
            flops=count * D, bytes_accessed=4 * count * D, transcendentals=0
        ),
        name="payload",
    )(*map(in_hbm, operands))


def qkv_kernel(count, flip, *refs):
    me = lax.axis_index("seq")
    first, second = refs[:count], refs[count : 2 * count]
    table, gain, weight = refs[2 * count : 2 * count + 3]
    inputs_out, qkv_out, label_out = refs[-3:]
    mine, other = stacked(first), stacked(second)
    leads = me % 2 == 0
    ahead = jnp.where(leads, mine, other)
    behind = jnp.where(leads, other, mine)
    both = jnp.concatenate([ahead, behind], axis=0)
    rows = both.shape[0]
    at = pl.ds(pl.multiple_of((me // 2 ^ flip) * rows, rows), rows)
    inputs_out[at, :] = both[:, :D]
    label_out[at, :] = both[:, D:]
    labels = both[:, D:].astype(jnp.float32)
    normed = norm_rows(both[:, :D].astype(jnp.float32), gain[...]).astype(jnp.bfloat16)
    columns = lax.dot_general(
        normed, weight[...], (((1,), (1,)), ((), ())), preferred_element_type=jnp.float32
    )
    lane = lax.broadcasted_iota(jnp.int32, labels.shape, 1)
    numbers = lane.astype(jnp.float32)
    hot = (numbers == labels[:, 1:2]) | (numbers == labels[:, 2:3] + POSITIONS)
    looked = jnp.dot(
        jnp.where(hot, 1.0, 0.0).astype(jnp.bfloat16), table[...], preferred_element_type=jnp.float32
    )
    cosine = looked[:, :LANES] + looked[:, LANES : 2 * LANES]
    sine = looked[:, 2 * LANES : 3 * LANES] + looked[:, 3 * LANES :]
    first_head = lane < HD // 2

    def turn(start):
        a = columns[:, start : start + LANES]
        b = columns[:, start + LANES : start + 2 * LANES]
        return a * cosine - b * sine, b * cosine + a * sine

    factor = HD**-0.5 * float(np.log2(np.e))
    query_a, query_b = (one * factor for one in turn(0))
    key_a, key_b = turn(2 * LANES)
    zero = jnp.zeros_like(key_a)
    image = numbers == labels[:, :1] + IMAGE_LANE
    extra = lane >= IMAGE_LANE
    apart = jnp.where(image, 0.0, FAR_APART)
    parts = [
        jnp.where(image, 1.0, query_a),
        query_b,
        jnp.where(extra, apart, jnp.where(first_head, key_a, zero)),
        jnp.where(first_head, key_b, zero),
        jnp.where(extra, apart, jnp.where(first_head, zero, key_a)),
        jnp.where(first_head, zero, key_b),
    ]
    for head in range(2):
        values = columns[:, (4 + head) * LANES : (5 + head) * LANES]
        parts.append(jnp.where(lane == HD, 1.0, values))
    for number, part in enumerate(parts):
        qkv_out[at, number * LANES : (number + 1) * LANES] = part.astype(jnp.bfloat16)


def qkv_call(flip, first, second, table, gain, weight, earlier, total):
    rows = 2 * sum(piece.shape[0] for piece in first)
    widths = (D, 8 * LANES, LANES)
    operands = [*first, *second, table, gain, in_vmem(weight)]
    vmem = pl.BlockSpec(memory_space=pltpu.VMEM)
    held = [in_vmem(one) for one in earlier]
    return pl.pallas_call(
        functools.partial(qkv_kernel, len(first), flip),
        in_specs=[vmem] * (len(operands) + len(earlier)),
        out_specs=[vmem] * len(widths),
        out_shape=[pltpu.VMEM((total, width), jnp.bfloat16) for width in widths],
        input_output_aliases={len(operands) + i: i for i in range(len(earlier))},
        compiler_params=pltpu.CompilerParams(vmem_limit_bytes=14 << 20),
        cost_estimate=pl.CostEstimate(
            flops=6 * rows * D * weight.shape[0],
            bytes_accessed=2 * (rows * 4 * D + weight.size),
            transcendentals=rows,
        ),
        name="norm_qkv",
    )(*operands, *held)


def segment_row(labels):
    pick = jnp.where(lax.broadcasted_iota(jnp.int32, (8, LANES), 1) == 0, 1.0, 0.0)
    return lax.dot_general(
        pick.astype(jnp.bfloat16),
        labels,
        (((1,), (1,)), ((), ())),
        preferred_element_type=jnp.float32,
    )


def attention_kernel(start, images, labels, block, *refs):
    owners, refs = (refs[0], refs[1:]) if images else (None, refs)
    out, *rest = refs
    scores, high = rest[-2:]
    rows = high.shape[1]
    total = block.shape[0]
    segments = segment_row(labels[...])
    one_row = segments[:1]
    lowest = jnp.min(labels[start : start + 16, :1].astype(jnp.float32), axis=0, keepdims=True)
    largest = labels[start + rows - 16 : start + rows, :1].astype(jnp.float32)
    largest = jnp.max(largest, axis=0, keepdims=True)
    begin = jnp.sum(jnp.where(one_row < lowest, 1, 0)) // BLOCK
    end = (jnp.sum(jnp.where(one_row <= largest, 1, 0)) + BLOCK - 1) // BLOCK
    queries = block[start : start + rows, : 2 * LANES]
    high[...] = jnp.full_like(high, 2 * FAR_APART)

    def score(step, carry):
        at = pl.ds(pl.multiple_of(step * BLOCK, BLOCK), BLOCK)
        for head in range(2):
            keys = block[at, (2 + 2 * head) * LANES : (4 + 2 * head) * LANES]
            values = lax.dot_general(
                queries, keys, (((1,), (1,)), ((), ())), preferred_element_type=jnp.float32
            )
            scores[head, step] = values
            tops = [values[:, lane : lane + LANES] for lane in range(0, BLOCK, LANES)]
            high[head] = functools.reduce(jnp.maximum, tops, high[head])
        return carry

    lax.fori_loop(begin, end, score, 0)
    highest = [jnp.max(high[head], axis=-1, keepdims=True) for head in range(2)]

    def weigh(step, carry):
        at = pl.ds(pl.multiple_of(step * BLOCK, BLOCK), BLOCK)
        sums = []
        for head in range(2):
            weights = jnp.exp2(scores[head, step] - highest[head])
            values = block[at, (6 + head) * LANES : (7 + head) * LANES]
            sums.append(
                carry[head]
                + jnp.dot(weights.astype(jnp.bfloat16), values, preferred_element_type=jnp.float32)
            )
        return tuple(sums)

    zero = jnp.zeros((rows, LANES), jnp.float32)
    sums = lax.fori_loop(begin, end, weigh, (zero, zero))
    first, second = (one / one[:, HD : HD + 1] for one in sums)
    lane = lax.broadcasted_iota(jnp.int32, first.shape, 1)
    turned = pltpu.roll(second, HD, 1)
    out[:rows] = jnp.where(lane < HD, first, turned).astype(jnp.bfloat16)
    half = rows // 2
    tail = 2 * HD - LANES
    lane = lane[:half]
    up = pltpu.roll(turned[half:], tail, 1)
    packed = jnp.where(lane < tail, turned[:half], jnp.where(lane < 2 * tail, up, 0.0))
    out[rows:] = packed.astype(jnp.bfloat16)

    if len(rest) > 2:
        note = rest[0]
        row = lax.broadcasted_iota(jnp.int32, note.shape, 0)
        lane = lax.broadcasted_iota(jnp.int32, note.shape, 1)
        found = jnp.zeros(note.shape, jnp.float32)
        for image in range(images):
            below = jnp.sum(jnp.where(one_row < image, 0.25, 0.0), axis=1, keepdims=True)
            inside = jnp.sum(jnp.where(one_row == image, 0.25, 0.0), axis=1, keepdims=True)
            here = row == owners[0, image]
            for place, number in enumerate((below, inside)):
                upper = jnp.floor(number * (1.0 / 16))
                found = jnp.where(here & (lane == 2 * place), upper, found)
                found = jnp.where(here & (lane == 2 * place + 1), number - 16 * upper, found)
        note[...] = found.astype(jnp.bfloat16)


def attention_call(start, rows, labels, block, owners):
    total = block.shape[0]
    vmem = pl.BlockSpec(memory_space=pltpu.VMEM)
    shapes = [jax.ShapeDtypeStruct((rows + rows // 2, LANES), jnp.bfloat16)]
    if owners:
        shapes.append(jax.ShapeDtypeStruct((16, LANES), jnp.bfloat16))
    return pl.pallas_call(
        functools.partial(attention_kernel, start, owners[0].shape[1] if owners else 0),
        in_specs=[vmem, vmem] + [pl.BlockSpec(memory_space=pltpu.SMEM)] * len(owners),
        out_specs=[vmem] * len(shapes),
        out_shape=shapes,
        scratch_shapes=[
            pltpu.VMEM((2, total // BLOCK, rows, BLOCK), jnp.float32),
            pltpu.VMEM((2, rows, LANES), jnp.float32),
        ],
        compiler_params=pltpu.CompilerParams(vmem_limit_bytes=20 << 20),
        cost_estimate=pl.CostEstimate(
            flops=10 * rows * total * 2 * LANES,
            bytes_accessed=2 * block.size,
            transcendentals=rows * total,
        ),
        name="attention",
    )(in_vmem(labels), in_vmem(block), *owners)


def prepare_kernel(shards, ids, out_weight, merge_weight, qkv_weight, spread, *refs):
    *rows, out, merge, qkv, qkv_buffer, spread_buffer, sems = refs
    for row, row_out in zip(rows[: len(rows) // 2], rows[len(rows) // 2 :]):
        row_out[...] = row[...].astype(jnp.float32)[None, :]
    rest = 2 * HD - LANES
    copies = [(qkv_weight, qkv_buffer), (spread, spread_buffer)]
    out[shards * LANES :] = jnp.zeros((shards // 2 * LANES, D), jnp.bfloat16)
    for place in range(shards):
        start = pl.multiple_of(ids[place] * (2 * HD), 16)
        to = (shards + place // 2) * LANES + place % 2 * rest
        copies.append(
            (out_weight.at[pl.ds(start, LANES), :], out.at[pl.ds(place * LANES, LANES), :])
        )
        copies.append((out_weight.at[pl.ds(start + LANES, rest), :], out.at[pl.ds(to, rest), :]))
    copies.append((merge_weight, merge))
    copies = [
        pltpu.make_async_copy(source, target, sems.at[i])
        for i, (source, target) in enumerate(copies)
    ]
    for copy in copies:
        copy.start()
    copies[0].wait()
    copies[1].wait()
    qkv[...] = jnp.dot(
        spread_buffer[...], qkv_buffer[...], preferred_element_type=jnp.float32
    ).astype(jnp.bfloat16)
    for copy in copies[2:]:
        copy.wait()


def prepare_call(shards, ids, out_weight, merge_weight, qkv_weight, spread, rows):
    anywhere = pl.BlockSpec(memory_space=pl.ANY)
    vmem = pl.BlockSpec(memory_space=pltpu.VMEM)
    operands = (out_weight, merge_weight, qkv_weight, spread)
    shapes = [(shards * LANES * 3 // 2, D), merge_weight.shape, (spread.shape[0], D)]
    return pl.pallas_call(
        functools.partial(prepare_kernel, shards),
        in_specs=[pl.BlockSpec(memory_space=pltpu.SMEM)]
        + [anywhere] * len(operands)
        + [vmem] * len(rows),
        out_specs=[vmem] * (len(rows) + len(shapes)),
        out_shape=[pltpu.VMEM((1, row.shape[0]), jnp.float32) for row in rows]
        + [pltpu.VMEM(shape, jnp.bfloat16) for shape in shapes],
        scratch_shapes=[
            pltpu.VMEM(qkv_weight.shape, jnp.bfloat16),
            pltpu.VMEM(spread.shape, jnp.bfloat16),
            pltpu.SemaphoreType.DMA((2 * shards + 3,)),
        ],
        compiler_params=pltpu.CompilerParams(vmem_limit_bytes=10 << 20),
        cost_estimate=pl.CostEstimate(
            flops=2 * spread.size * D,
            bytes_accessed=4 * (out_weight.size + merge_weight.size + qkv_weight.size),
            transcendentals=0,
        ),
        name="prepare",
    )(ids, *map(in_hbm, operands), *rows)


def merge_kernel(start, counts, packs, last, *refs):
    inputs, weight, gain, merge_weight, bias = refs[:5]
    pieces = refs[5 : 5 + sum(counts)]
    *refs, state, tokens = refs[5 + sum(counts) :]
    rows = state.shape[1]
    half = rows // 2
    rest = 2 * HD - LANES
    sources, at = [], 0
    for count in counts:
        sources.append(stacked(pieces[at : at + count]))
        at += count
    shards = len(sources)
    lane = lax.broadcasted_iota(jnp.int32, (half, LANES), 1)
    lined = [source[:rows, :] for source in sources]
    for pair in range(shards // 2):
        mine = sources[2 * pair][rows:, :].astype(jnp.float32)
        other = sources[2 * pair + 1][rows:, :].astype(jnp.float32)
        upper = jnp.where(lane < rest, mine, pltpu.roll(other, rest, 1))
        lower = jnp.where(lane < rest, pltpu.roll(mine, LANES - rest, 1), other)
        lined.append(jnp.concatenate([upper, lower], axis=0).astype(jnp.bfloat16))
    mixed = jnp.dot(
        jnp.concatenate(lined, axis=1), weight[...], preferred_element_type=jnp.float32
    )
    for column in range(D // LANES):
        lanes = slice(column * LANES, (column + 1) * LANES)
        before = inputs[start : start + rows, lanes]
        state[column] = before.astype(jnp.float32) + mixed[:, lanes]
    groups = rows // 4
    for block in range(0, groups, NORM_ROWS):
        for quadrant in range(4):
            at = pl.ds(4 * block + quadrant, NORM_ROWS, stride=4)
            residual = jnp.concatenate(
                [state[column, at, :] for column in range(D // LANES)], axis=1
            )
            tokens[block : block + NORM_ROWS, quadrant * D : (quadrant + 1) * D] = norm_rows(
                residual, gain[...]
            ).astype(jnp.bfloat16)
    total = bias[...] + lax.dot_general(
        tokens[...], merge_weight[...], (((1,), (1,)), ((), ())), preferred_element_type=jnp.float32
    )
    total = total.astype(jnp.bfloat16)
    if not last:
        refs[0][...] = total
        return
    note, *earlier = refs[:-packs]
    me = lax.axis_index("pack")
    outs = refs[-packs:]
    total = jnp.concatenate([*[one[...] for one in earlier], total], axis=0)
    whole = total.shape[1] // LANES
    most = outs[0].shape[0] * LANES // total.shape[1]
    notes = note[...].astype(jnp.float32)
    note_row = lax.broadcasted_iota(jnp.int32, notes.shape, 0)
    slot = lax.broadcasted_iota(jnp.int32, (most, total.shape[0]), 0)
    row = lax.broadcasted_iota(jnp.int32, (most, total.shape[0]), 1)
    for place, out in enumerate(outs):
        found = jnp.where(note_row == (me ^ place), notes, 0.0)
        found = jnp.sum(found, axis=0, keepdims=True)
        first = (16.0 * found[:, :1] + found[:, 1:2]).astype(jnp.int32)
        length = (16.0 * found[:, 2:3] + found[:, 3:4]).astype(jnp.int32)
        chosen = (row == slot + first) & (slot < length)
        chosen = jnp.where(chosen, 1.0, 0.0).astype(jnp.bfloat16)
        block = jnp.dot(chosen, total, preferred_element_type=jnp.float32)
        for column in range(whole):
            out[column * most : (column + 1) * most, :] = block[
                :, column * LANES : (column + 1) * LANES
            ].astype(jnp.bfloat16)
        low = block[: most // 2, whole * LANES :]
        up = block[most // 2 :, whole * LANES :]
        out[whole * most :, :] = jnp.concatenate([low, up], axis=1).astype(jnp.bfloat16)


def merge_call(start, rows, sources, inputs, weight, gain, merge_weight, bias, packs, route):
    groups = rows // 4
    width = merge_weight.shape[0]
    pieces = [piece for source in sources for piece in source]
    vmem = pl.BlockSpec(memory_space=pltpu.VMEM)
    operands = [in_vmem(inputs), in_vmem(weight), gain, in_vmem(merge_weight), bias, *pieces]
    specs = [vmem] * len(operands)
    shapes = [jax.ShapeDtypeStruct((groups, width), jnp.bfloat16)]
    if route:
        most, *others = route
        operands += others
        specs += [vmem] * len(others)
        shapes = [jax.ShapeDtypeStruct((most * width // LANES, LANES), jnp.bfloat16)] * packs
    return pl.pallas_call(
        functools.partial(
            merge_kernel, start, [len(source) for source in sources], packs, bool(route)
        ),
        in_specs=specs,
        out_specs=[vmem] * len(shapes),
        scratch_shapes=[
            pltpu.VMEM((D // LANES, rows, LANES), jnp.float32),
            pltpu.VMEM((groups, 4 * D), jnp.bfloat16),
        ],
        out_shape=shapes,
        compiler_params=pltpu.CompilerParams(vmem_limit_bytes=20 << 20),
        cost_estimate=pl.CostEstimate(
            flops=0,
            bytes_accessed=1024,
            transcendentals=rows,
        ),
        name="out_merge",
    )(*operands)


def place_kernel(place, block, *refs):
    out, rows, sem = refs[-3:]
    most, width = rows.shape
    whole = width // LANES
    half = most // 2
    middle = LANES // 2
    for column in range(whole):
        rows[:, column * LANES : (column + 1) * LANES] = block[
            column * most : (column + 1) * most, :
        ]
    rows[:half, whole * LANES :] = block[whole * most :, :middle]
    rows[half:, whole * LANES :] = block[whole * most :, middle:]
    copy = pltpu.make_async_copy(rows, out.at[lax.axis_index("pack") ^ place], sem)
    copy.start()
    copy.wait()


def place_call(place, block, earlier, shape):
    anywhere = pl.BlockSpec(memory_space=pl.ANY)
    return pl.pallas_call(
        functools.partial(place_kernel, place),
        in_specs=[pl.BlockSpec(memory_space=pltpu.VMEM)] + [anywhere] * len(earlier),
        out_specs=anywhere,
        out_shape=pltpu.HBM(shape, jnp.bfloat16),
        scratch_shapes=[pltpu.VMEM(shape[1:], jnp.bfloat16), pltpu.SemaphoreType.DMA],
        input_output_aliases={1: 0} if earlier else {},
        compiler_params=pltpu.CompilerParams(vmem_limit_bytes=4 << 20),
        cost_estimate=pl.CostEstimate(
            flops=0, bytes_accessed=4 * shape[1] * shape[2], transcendentals=0
        ),
        name="place_rows",
    )(block, *map(in_hbm, earlier))


def send_seq(value, flip):
    size = lax.axis_size("seq")
    return lax.ppermute(value, "seq", [(i, i ^ flip) for i in range(size)])


def after(values, *earlier):
    return lax.optimization_barrier((tuple(values), earlier))[0]


def halves_kernel(across_x, across_y, upper, lower):
    half = upper.shape[0]
    upper[...] = across_x[:half]
    lower[...] = across_y[half:]


def halves_call(across_x, across_y):
    vmem = pl.BlockSpec(memory_space=pltpu.VMEM)
    shape = (across_x.shape[0] // 2, across_x.shape[1])
    return pl.pallas_call(
        halves_kernel,
        in_specs=[vmem] * 2,
        out_specs=[vmem] * 2,
        out_shape=[jax.ShapeDtypeStruct(shape, across_x.dtype)] * 2,
        compiler_params=pltpu.CompilerParams(vmem_limit_bytes=4 << 20),
        cost_estimate=pl.CostEstimate(
            flops=0, bytes_accessed=4 * across_x.size, transcendentals=0
        ),
        name="halves",
    )(across_x, across_y)


def near_shards(value):
    return [send_seq(value, 1), send_seq(value, 2), send_seq(value, 4)]


def far_shards(across_x, across_y):
    upper, lower = halves_call(across_x, across_y)
    return [send_seq(upper, 4), send_seq(lower, 2)]


def weight_order(heads_here):
    quarter = HD // 4
    order = -np.ones((6 * LANES,), np.int32)
    for head in range(heads_here):
        base = head * 3 * HD
        for kind in range(2):
            for half in range(2):
                for letter in range(2):
                    target = (2 * kind + letter) * LANES + head * (HD // 2) + half * quarter
                    source = base + kind * HD + half * (HD // 2) + letter * quarter
                    order[target : target + quarter] = np.arange(source, source + quarter)
        target = (4 + head) * LANES
        order[target : target + HD] = np.arange(base + 2 * HD, base + 3 * HD)
    return order


def angle_table(heads_here):
    quarter = HD // 4
    frequency = (10000.0 ** (-np.arange(quarter) / quarter)).astype(np.float32)
    angles = np.arange(POSITIONS, dtype=np.float32)[:, None] * frequency[None, :]
    pieces = []
    for function in (np.cos, np.sin):
        exact = np.zeros((2 * POSITIONS, LANES), np.float64)
        for head in range(heads_here):
            for half in range(2):
                lane = head * (HD // 2) + half * quarter
                rows = slice(half * POSITIONS, (half + 1) * POSITIONS)
                exact[rows, lane : lane + quarter] = function(angles.astype(np.float64))
        upper = exact.astype(jnp.bfloat16)
        pieces += [upper, (exact - upper.astype(np.float64)).astype(jnp.bfloat16)]
    return np.concatenate(pieces, axis=1)


def fast_local(
    patches,
    patch_mask,
    mask_embed,
    norm_gain,
    qkv_weight,
    segment_ids,
    patch_rows,
    patch_column,
    out_weight,
    merge_gain,
    merge_weight,
    merge_bias,
    image_owner,
):
    local_rows = patches.shape[1]
    shards = lax.axis_size("seq")
    packs = lax.axis_size("pack")
    heads_here = HEADS // shards
    images = image_owner.shape[1]
    total = local_rows * shards
    me = lax.axis_index("seq").astype(jnp.int32)

    value = payload_call(segment_ids, patch_rows, patch_column, patch_mask, mask_embed, patches)
    own_swap, across_x, across_y = near_shards(value)

    order = weight_order(heads_here)
    spread = (order[:, None] == np.arange(qkv_weight.shape[1])[None, :]).astype(jnp.bfloat16)
    table = jnp.asarray(angle_table(heads_here))
    ids = jnp.stack([me ^ place for place in range(shards)])
    gain, merge_gain_row, bias, ordered, merge_rows, weight = prepare_call(
        shards,
        ids,
        out_weight,
        merge_weight.T,
        qkv_weight.T,
        jnp.asarray(spread),
        (norm_gain, merge_gain, merge_bias),
    )

    project = lambda place, first, second, earlier: qkv_call(
        place, first, second, table, gain, weight, earlier, total
    )
    buffers = project(0, [value], [own_swap], ())
    across_x, across_y = after([across_x, across_y], buffers[2], ordered)
    far = far_shards(across_x, across_y)
    buffers = project(1, [across_x], [send_seq(across_x, 1)], buffers)
    buffers = project(2, [across_y], [send_seq(across_y, 1)], buffers)
    far = after(far, buffers[2])
    buffers = project(3, far, [send_seq(one, 1) for one in far], buffers)
    inputs, block, labels = buffers

    most = 2 * (total // 4) // images
    first_rows, last_rows = CHUNKS
    (own,) = attention_call(0, first_rows, labels, block, ())
    own_swap, across_x, across_y = near_shards(own)
    labels, block = after([labels, block], own)
    late, note = attention_call(first_rows, last_rows, labels, block, (image_owner,))
    across_x, across_y = after([across_x, across_y], late)
    halves = halves_call(across_x, across_y)
    far = [send_seq(halves[0], 4), send_seq(halves[1], 2)]
    (late,) = after([late], *halves)
    late_shares = [late] + [send_seq(late, flip) for flip in (2, 4, 6)]
    near = [send_seq(one, 1) for one in (across_x, across_y)]
    merge = lambda start, rows, sources, route: merge_call(
        start, rows, sources, inputs, ordered, merge_gain_row, merge_rows, bias, packs, route
    )
    sources = [[own], [own_swap], [across_x], near[:1], [across_y], near[1:], far]
    (projected,) = merge(0, first_rows, sources + [[send_seq(one, 1) for one in far]], ())
    late_shares[1:] = [after([one], projected)[0] for one in late_shares[1:]]
    sources = [[one] for share in late_shares for one in (share, send_seq(share, 1))]
    made = merge(first_rows, last_rows, sources, (most, note, projected))
    sent = {
        flip: lax.ppermute(made[flip], "pack", [(z, z ^ flip) for z in range(packs)])
        for flip in range(packs - 1, 0, -1)
    }
    shape = (packs, most, merge_weight.shape[1])
    routed = place_call(0, made[0], (), shape)
    for flip in (3, 1, 2):
        routed = place_call(flip, sent[flip], (routed,), shape)
    return routed[None]


def local(*arguments):
    patches, weight = arguments[0], arguments[4]
    shards = lax.axis_size("seq")
    fits = shards == 8 and HEADS // shards == 2 and weight.shape[1] == 6 * HD
    fits = fits and patches.shape[1] * shards == sum(CHUNKS) and lax.axis_size("pack") == 4
    return fast_local(*arguments) if fits else general_local(*arguments)


def solution(mesh):
    placed = (
        P("pack", "seq", None),
        P("pack", "seq"),
        P(),
        P(),
        P(None, "seq"),
        P("pack", "seq"),
        P("pack", "seq"),
        P("pack", "seq"),
        P(),
        P(),
        P(None, "seq"),
        P("seq"),
        P("pack", None),
    )
    return jax.shard_map(
        local, mesh=mesh, in_specs=placed, out_specs=P("pack", None, None, "seq"), check_vma=False
    )
```

```python
import functools

import jax
import jax.numpy as jnp
import numpy as np
from jax import lax
from jax.experimental import pallas as pl
from jax.experimental.pallas import tpu as pltpu
from jax.sharding import PartitionSpec as P

D = 1408
HEADS = 16
HD = 88


EPSILON = 1e-06


def layer_norm(values, gain_vector):
    center = values - jnp.mean(values, axis=-1, keepdims=True)
    spread = jnp.mean(center * center, axis=-1, keepdims=True)
    return center * lax.rsqrt(spread + EPSILON) * gain_vector.astype(jnp.float32)


def rotate(vectors, row_index, column_index):
    total_rows, heads_here, head_width = vectors.shape
    quarter = head_width // 4
    frequency = 10000.0 ** (-jnp.arange(quarter, dtype=jnp.float32) / quarter)
    row_angle = row_index.astype(jnp.float32)[:, None] * frequency[None, :]
    column_angle = column_index.astype(jnp.float32)[:, None] * frequency[None, :]
    angles = jnp.stack([row_angle, column_angle], axis=1)[:, None, :, None, :]
    split_up = vectors.reshape(total_rows, heads_here, 2, 2, quarter)
    partner = jnp.stack([-split_up[:, :, :, 1], split_up[:, :, :, 0]], axis=3)
    turned = split_up * jnp.cos(angles) + partner * jnp.sin(angles)
    return turned.reshape(total_rows, heads_here, head_width)


def qkv_block(projected, row_index, column_index):
    turned_queries = rotate(projected[:, :, 0], row_index, column_index)
    turned_keys = rotate(projected[:, :, 1], row_index, column_index)
    return jnp.concatenate([turned_queries, turned_keys, projected[:, :, 2]], axis=-1).astype(
        jnp.bfloat16
    )


def attention(block, segments):
    total_rows, heads_here, triple = block.shape
    head_width = triple // 3
    step_rows = min(512, total_rows)
    query_part = block[:, :, :head_width].reshape(
        total_rows // step_rows, step_rows, heads_here, head_width
    )
    key_part = block[:, :, head_width : 2 * head_width]
    value_part = block[:, :, 2 * head_width :]
    query_segments = segments.reshape(total_rows // step_rows, step_rows)
    scale = head_width ** (-0.5)

    def one_block(inputs_pair):
        queries_here, segments_here = inputs_pair
        scores = (
            jnp.einsum("qhd,khd->hqk", queries_here, key_part, preferred_element_type=jnp.float32)
            * scale
        )
        same_image = (segments_here[:, None] == segments[None, :])[None]
        scores = jnp.where(same_image, scores, -jnp.inf)
        highest = jnp.max(scores, axis=-1, keepdims=True)
        weights = jnp.exp(scores - highest)
        probs = (weights / jnp.sum(weights, axis=-1, keepdims=True)).astype(jnp.bfloat16)
        result = jnp.einsum("hqk,khd->qhd", probs, value_part, preferred_element_type=jnp.float32)
        return result.astype(jnp.bfloat16)

    return lax.map(one_block, (query_part, query_segments)).reshape(
        total_rows, heads_here, head_width
    )


def route(projected, segments, owners_here, packs, most):
    merged_segments = segments[::4]
    images = owners_here.shape[0]
    image_ids = jnp.arange(images, dtype=jnp.int32)
    member = (merged_segments[None, :] == image_ids[:, None]).astype(jnp.int32)
    lengths = jnp.sum(member, axis=1, dtype=jnp.int32)
    starts = jnp.cumsum(lengths, dtype=jnp.int32) - lengths
    owner_ids = jnp.arange(packs, dtype=jnp.int32)
    owned = owners_here[None, :] == owner_ids[:, None]
    first_row = jnp.sum(jnp.where(owned, starts[None, :], 0), axis=1, dtype=jnp.int32)
    owned_length = jnp.sum(jnp.where(owned, lengths[None, :], 0), axis=1, dtype=jnp.int32)
    slots = jnp.arange(most, dtype=jnp.int32)
    source_rows = jnp.clip(first_row[:, None] + slots[None, :], 0, projected.shape[0] - 1)
    picked = jnp.take(projected, source_rows.reshape(-1), axis=0).reshape(
        packs, most, projected.shape[1]
    )
    filled = slots[None, :] < owned_length[:, None]
    return jnp.where(filled[:, :, None], picked, jnp.zeros_like(picked))


def general_local(
    patches,
    patch_mask,
    mask_embed,
    norm_gain,
    qkv_weight,
    segment_ids,
    patch_rows,
    patch_column,
    out_weight,
    merge_gain,
    merge_weight,
    merge_bias,
    image_owner,
):
    local_rows = patches.shape[1]
    shards = lax.axis_size("seq")
    packs = lax.axis_size("pack")
    heads_here = HEADS // shards
    inputs = jnp.where(patch_mask[0][:, None] == 1, mask_embed[None, :], patches[0])
    normed = layer_norm(inputs.astype(jnp.float32), norm_gain).astype(jnp.bfloat16)
    labels = lax.all_gather(
        jnp.stack([segment_ids[0], patch_rows[0], patch_column[0]]), "seq", axis=1, tiled=True
    )
    piece = lax.all_gather(normed, "seq", axis=0, tiled=True)
    span = piece.shape[0]
    projected = jnp.dot(piece, qkv_weight, preferred_element_type=jnp.float32)
    row_part = labels[1]
    column_part = labels[2]
    block = qkv_block(projected.reshape(span, heads_here, 3, HD), row_part, column_part)
    result = attention(block, labels[0])
    mixed_heads = lax.all_to_all(result, "seq", split_axis=0, concat_axis=1, tiled=True)
    attended = mixed_heads.reshape(local_rows, D)
    residual = inputs.astype(jnp.float32) + jnp.dot(
        attended, out_weight, preferred_element_type=jnp.float32
    )
    merged = layer_norm(residual, merge_gain).astype(jnp.bfloat16).reshape(local_rows // 4, 4 * D)
    projected_all = (
        jnp.dot(
            lax.all_gather(merged, "seq", axis=0, tiled=True),
            merge_weight,
            preferred_element_type=jnp.float32,
        )
        + merge_bias.astype(jnp.float32)
    ).astype(jnp.bfloat16)
    images = image_owner.shape[1]
    most = 2 * projected_all.shape[0] // images
    outgoing = route(projected_all, labels[0], image_owner[0], packs, most)
    delivered = lax.all_to_all(outgoing, "pack", split_axis=0, concat_axis=0, tiled=True)
    return delivered[None]


LANES = 128
BLOCK = 512
POSITIONS = 64
FAR_APART = -(2.0**100)
IMAGE_LANE = 96
NORM_ROWS = 16
CHUNKS = (896, 640)


def norm_rows(values, gain_row):
    center = values - jnp.mean(values, axis=-1, keepdims=True)
    spread = jnp.mean(center * center, axis=-1, keepdims=True)
    return center * lax.rsqrt(spread + EPSILON) * gain_row


def stacked(pieces):
    loaded = [piece[...] for piece in pieces]
    return loaded[0] if len(loaded) == 1 else jnp.concatenate(loaded, axis=0)


def in_vmem(value):
    return pltpu.with_memory_space_constraint(value, pltpu.VMEM)


def in_hbm(value):
    return pltpu.with_memory_space_constraint(value, pltpu.HBM)


def payload_kernel(segments, rows, columns, mask, embed, patches, out):
    labels = [one[...].astype(jnp.float32) for one in (segments, rows, columns, mask)]
    labels.append(jnp.zeros((4, labels[0].shape[1]), jnp.float32))
    labels = jnp.concatenate(labels, axis=0).astype(jnp.bfloat16)
    shape = (8, LANES)
    row = lax.broadcasted_iota(jnp.int32, shape, 0)
    place = jnp.where(row == lax.broadcasted_iota(jnp.int32, shape, 1), 1.0, 0.0)
    turned = lax.dot_general(
        labels,
        place.astype(jnp.bfloat16),
        (((0,), (0,)), ((), ())),
        preferred_element_type=jnp.float32,
    )
    masked = turned[:, 3:4] > 0.5
    tokens = jnp.where(
        masked, embed[...].astype(jnp.float32)[None, :], patches[0].astype(jnp.float32)
    )
    out[:, :D] = tokens.astype(jnp.bfloat16)
    out[:, D:] = turned.astype(jnp.bfloat16)


def payload_call(segments, rows, columns, mask, embed, patches):
    count = patches.shape[1]
    operands = (segments, rows, columns, mask, embed, patches)
    fixed = lambda shape: pl.BlockSpec(shape, lambda i: (0,) * len(shape))
    shape = (count, D + LANES)
    return pl.pallas_call(
        payload_kernel,
        grid=(1,),
        in_specs=[fixed(one.shape) for one in operands],
        out_specs=fixed(shape),
        out_shape=jax.ShapeDtypeStruct(shape, jnp.bfloat16),
        compiler_params=pltpu.CompilerParams(vmem_limit_bytes=8 << 20),
        cost_estimate=pl.CostEstimate(
            flops=count * D, bytes_accessed=4 * count * D, transcendentals=0
        ),
        name="payload",
    )(*map(in_hbm, operands))


def qkv_kernel(count, flip, *refs):
    me = lax.axis_index("seq")
    first, second = refs[:count], refs[count : 2 * count]
    table, gain, weight = refs[2 * count : 2 * count + 3]
    inputs_out, qkv_out, label_out = refs[-3:]
    mine, other = stacked(first), stacked(second)
    leads = me % 2 == 0
    ahead = jnp.where(leads, mine, other)
    behind = jnp.where(leads, other, mine)
    both = jnp.concatenate([ahead, behind], axis=0)
    rows = both.shape[0]
    at = pl.ds(pl.multiple_of((me // 2 ^ flip) * rows, rows), rows)
    inputs_out[at, :] = both[:, :D]
    label_out[at, :] = both[:, D:]
    labels = both[:, D:].astype(jnp.float32)
    normed = norm_rows(both[:, :D].astype(jnp.float32), gain[...]).astype(jnp.bfloat16)
    columns = lax.dot_general(
        normed, weight[...], (((1,), (1,)), ((), ())), preferred_element_type=jnp.float32
    )
    lane = lax.broadcasted_iota(jnp.int32, labels.shape, 1)
    numbers = lane.astype(jnp.float32)
    hot = (numbers == labels[:, 1:2]) | (numbers == labels[:, 2:3] + POSITIONS)
    looked = jnp.dot(
        jnp.where(hot, 1.0, 0.0).astype(jnp.bfloat16), table[...], preferred_element_type=jnp.float32
    )
    cosine = looked[:, :LANES] + looked[:, LANES : 2 * LANES]
    sine = looked[:, 2 * LANES : 3 * LANES] + looked[:, 3 * LANES :]
    first_head = lane < HD // 2

    def turn(start):
        a = columns[:, start : start + LANES]
        b = columns[:, start + LANES : start + 2 * LANES]
        return a * cosine - b * sine, b * cosine + a * sine

    factor = HD**-0.5 * float(np.log2(np.e))
    query_a, query_b = (one * factor for one in turn(0))
    key_a, key_b = turn(2 * LANES)
    zero = jnp.zeros_like(key_a)
    image = numbers == labels[:, :1] + IMAGE_LANE
    extra = lane >= IMAGE_LANE
    apart = jnp.where(image, 0.0, FAR_APART)
    parts = [
        jnp.where(image, 1.0, query_a),
        query_b,
        jnp.where(extra, apart, jnp.where(first_head, key_a, zero)),
        jnp.where(first_head, key_b, zero),
        jnp.where(extra, apart, jnp.where(first_head, zero, key_a)),
        jnp.where(first_head, zero, key_b),
    ]
    for head in range(2):
        values = columns[:, (4 + head) * LANES : (5 + head) * LANES]
        parts.append(jnp.where(lane == HD, 1.0, values))
    for number, part in enumerate(parts):
        qkv_out[at, number * LANES : (number + 1) * LANES] = part.astype(jnp.bfloat16)


def qkv_call(flip, first, second, table, gain, weight, earlier, total):
    rows = 2 * sum(piece.shape[0] for piece in first)
    widths = (D, 8 * LANES, LANES)
    operands = [*first, *second, table, gain, in_vmem(weight)]
    vmem = pl.BlockSpec(memory_space=pltpu.VMEM)
    held = [in_vmem(one) for one in earlier]
    return pl.pallas_call(
        functools.partial(qkv_kernel, len(first), flip),
        in_specs=[vmem] * (len(operands) + len(earlier)),
        out_specs=[vmem] * len(widths),
        out_shape=[pltpu.VMEM((total, width), jnp.bfloat16) for width in widths],
        input_output_aliases={len(operands) + i: i for i in range(len(earlier))},
        compiler_params=pltpu.CompilerParams(vmem_limit_bytes=14 << 20),
        cost_estimate=pl.CostEstimate(
            flops=6 * rows * D * weight.shape[0],
            bytes_accessed=2 * (rows * 4 * D + weight.size),
            transcendentals=rows,
        ),
        name="norm_qkv",
    )(*operands, *held)


def segment_row(labels):
    pick = jnp.where(lax.broadcasted_iota(jnp.int32, (8, LANES), 1) == 0, 1.0, 0.0)
    return lax.dot_general(
        pick.astype(jnp.bfloat16),
        labels,
        (((1,), (1,)), ((), ())),
        preferred_element_type=jnp.float32,
    )


def attention_kernel(start, images, labels, block, *refs):
    owners, refs = (refs[0], refs[1:]) if images else (None, refs)
    out, *rest = refs
    scores, high = rest[-2:]
    rows = high.shape[1]
    total = block.shape[0]
    segments = segment_row(labels[...])
    one_row = segments[:1]
    lowest = jnp.min(labels[start : start + 16, :1].astype(jnp.float32), axis=0, keepdims=True)
    largest = labels[start + rows - 16 : start + rows, :1].astype(jnp.float32)
    largest = jnp.max(largest, axis=0, keepdims=True)
    begin = jnp.sum(jnp.where(one_row < lowest, 1, 0)) // BLOCK
    end = (jnp.sum(jnp.where(one_row <= largest, 1, 0)) + BLOCK - 1) // BLOCK
    queries = block[start : start + rows, : 2 * LANES]
    high[...] = jnp.full_like(high, 2 * FAR_APART)

    def score(step, carry):
        at = pl.ds(pl.multiple_of(step * BLOCK, BLOCK), BLOCK)
        for head in range(2):
            keys = block[at, (2 + 2 * head) * LANES : (4 + 2 * head) * LANES]
            values = lax.dot_general(
                queries, keys, (((1,), (1,)), ((), ())), preferred_element_type=jnp.float32
            )
            scores[head, step] = values
            tops = [values[:, lane : lane + LANES] for lane in range(0, BLOCK, LANES)]
            high[head] = functools.reduce(jnp.maximum, tops, high[head])
        return carry

    lax.fori_loop(begin, end, score, 0)
    highest = [jnp.max(high[head], axis=-1, keepdims=True) for head in range(2)]

    def weigh(step, carry):
        at = pl.ds(pl.multiple_of(step * BLOCK, BLOCK), BLOCK)
        sums = []
        for head in range(2):
            weights = jnp.exp2(scores[head, step] - highest[head])
            values = block[at, (6 + head) * LANES : (7 + head) * LANES]
            sums.append(
                carry[head]
                + jnp.dot(weights.astype(jnp.bfloat16), values, preferred_element_type=jnp.float32)
            )
        return tuple(sums)

    zero = jnp.zeros((rows, LANES), jnp.float32)
    sums = lax.fori_loop(begin, end, weigh, (zero, zero))
    first, second = (one / one[:, HD : HD + 1] for one in sums)
    lane = lax.broadcasted_iota(jnp.int32, first.shape, 1)
    turned = pltpu.roll(second, HD, 1)
    out[:rows] = jnp.where(lane < HD, first, turned).astype(jnp.bfloat16)
    half = rows // 2
    tail = 2 * HD - LANES
    lane = lane[:half]
    up = pltpu.roll(turned[half:], tail, 1)
    packed = jnp.where(lane < tail, turned[:half], jnp.where(lane < 2 * tail, up, 0.0))
    out[rows:] = packed.astype(jnp.bfloat16)

    if len(rest) > 2:
        note = rest[0]
        row = lax.broadcasted_iota(jnp.int32, note.shape, 0)
        lane = lax.broadcasted_iota(jnp.int32, note.shape, 1)
        found = jnp.zeros(note.shape, jnp.float32)
        for image in range(images):
            below = jnp.sum(jnp.where(one_row < image, 0.25, 0.0), axis=1, keepdims=True)
            inside = jnp.sum(jnp.where(one_row == image, 0.25, 0.0), axis=1, keepdims=True)
            here = row == owners[0, image]
            for place, number in enumerate((below, inside)):
                upper = jnp.floor(number * (1.0 / 16))
                found = jnp.where(here & (lane == 2 * place), upper, found)
                found = jnp.where(here & (lane == 2 * place + 1), number - 16 * upper, found)
        note[...] = found.astype(jnp.bfloat16)


def attention_call(start, rows, labels, block, owners):
    total = block.shape[0]
    vmem = pl.BlockSpec(memory_space=pltpu.VMEM)
    shapes = [jax.ShapeDtypeStruct((rows + rows // 2, LANES), jnp.bfloat16)]
    if owners:
        shapes.append(jax.ShapeDtypeStruct((16, LANES), jnp.bfloat16))
    return pl.pallas_call(
        functools.partial(attention_kernel, start, owners[0].shape[1] if owners else 0),
        in_specs=[vmem, vmem] + [pl.BlockSpec(memory_space=pltpu.SMEM)] * len(owners),
        out_specs=[vmem] * len(shapes),
        out_shape=shapes,
        scratch_shapes=[
            pltpu.VMEM((2, total // BLOCK, rows, BLOCK), jnp.float32),
            pltpu.VMEM((2, rows, LANES), jnp.float32),
        ],
        compiler_params=pltpu.CompilerParams(vmem_limit_bytes=20 << 20),
        cost_estimate=pl.CostEstimate(
            flops=10 * rows * total * 2 * LANES,
            bytes_accessed=2 * block.size,
            transcendentals=rows * total,
        ),
        name="attention",
    )(in_vmem(labels), in_vmem(block), *owners)


def prepare_kernel(shards, ids, out_weight, merge_weight, qkv_weight, spread, *refs):
    *rows, out, merge, qkv, qkv_buffer, spread_buffer, sems = refs
    for row, row_out in zip(rows[: len(rows) // 2], rows[len(rows) // 2 :]):
        row_out[...] = row[...].astype(jnp.float32)[None, :]
    rest = 2 * HD - LANES
    copies = [(qkv_weight, qkv_buffer), (spread, spread_buffer)]
    out[shards * LANES :] = jnp.zeros((shards // 2 * LANES, D), jnp.bfloat16)
    for place in range(shards):
        start = pl.multiple_of(ids[place] * (2 * HD), 16)
        to = (shards + place // 2) * LANES + place % 2 * rest
        copies.append(
            (out_weight.at[pl.ds(start, LANES), :], out.at[pl.ds(place * LANES, LANES), :])
        )
        copies.append((out_weight.at[pl.ds(start + LANES, rest), :], out.at[pl.ds(to, rest), :]))
    copies.append((merge_weight, merge))
    copies = [
        pltpu.make_async_copy(source, target, sems.at[i])
        for i, (source, target) in enumerate(copies)
    ]
    for copy in copies:
        copy.start()
    copies[0].wait()
    copies[1].wait()
    qkv[...] = jnp.dot(
        spread_buffer[...], qkv_buffer[...], preferred_element_type=jnp.float32
    ).astype(jnp.bfloat16)
    for copy in copies[2:]:
        copy.wait()


def prepare_call(shards, ids, out_weight, merge_weight, qkv_weight, spread, rows):
    anywhere = pl.BlockSpec(memory_space=pl.ANY)
    vmem = pl.BlockSpec(memory_space=pltpu.VMEM)
    operands = (out_weight, merge_weight, qkv_weight, spread)
    shapes = [(shards * LANES * 3 // 2, D), merge_weight.shape, (spread.shape[0], D)]
    return pl.pallas_call(
        functools.partial(prepare_kernel, shards),
        in_specs=[pl.BlockSpec(memory_space=pltpu.SMEM)]
        + [anywhere] * len(operands)
        + [vmem] * len(rows),
        out_specs=[vmem] * (len(rows) + len(shapes)),
        out_shape=[pltpu.VMEM((1, row.shape[0]), jnp.float32) for row in rows]
        + [pltpu.VMEM(shape, jnp.bfloat16) for shape in shapes],
        scratch_shapes=[
            pltpu.VMEM(qkv_weight.shape, jnp.bfloat16),
            pltpu.VMEM(spread.shape, jnp.bfloat16),
            pltpu.SemaphoreType.DMA((2 * shards + 3,)),
        ],
        compiler_params=pltpu.CompilerParams(vmem_limit_bytes=10 << 20),
        cost_estimate=pl.CostEstimate(
            flops=2 * spread.size * D,
            bytes_accessed=4 * (out_weight.size + merge_weight.size + qkv_weight.size),
            transcendentals=0,
        ),
        name="prepare",
    )(ids, *map(in_hbm, operands), *rows)


def merge_kernel(start, counts, packs, last, *refs):
    inputs, weight, gain, merge_weight, bias = refs[:5]
    pieces = refs[5 : 5 + sum(counts)]
    *refs, state, tokens = refs[5 + sum(counts) :]
    rows = state.shape[1]
    half = rows // 2
    rest = 2 * HD - LANES
    sources, at = [], 0
    for count in counts:
        sources.append(stacked(pieces[at : at + count]))
        at += count
    shards = len(sources)
    lane = lax.broadcasted_iota(jnp.int32, (half, LANES), 1)
    lined = [source[:rows, :] for source in sources]
    for pair in range(shards // 2):
        mine = sources[2 * pair][rows:, :].astype(jnp.float32)
        other = sources[2 * pair + 1][rows:, :].astype(jnp.float32)
        upper = jnp.where(lane < rest, mine, pltpu.roll(other, rest, 1))
        lower = jnp.where(lane < rest, pltpu.roll(mine, LANES - rest, 1), other)
        lined.append(jnp.concatenate([upper, lower], axis=0).astype(jnp.bfloat16))
    mixed = jnp.dot(
        jnp.concatenate(lined, axis=1), weight[...], preferred_element_type=jnp.float32
    )
    for column in range(D // LANES):
        lanes = slice(column * LANES, (column + 1) * LANES)
        before = inputs[start : start + rows, lanes]
        state[column] = before.astype(jnp.float32) + mixed[:, lanes]
    groups = rows // 4
    for block in range(0, groups, NORM_ROWS):
        for quadrant in range(4):
            at = pl.ds(4 * block + quadrant, NORM_ROWS, stride=4)
            residual = jnp.concatenate(
                [state[column, at, :] for column in range(D // LANES)], axis=1
            )
            tokens[block : block + NORM_ROWS, quadrant * D : (quadrant + 1) * D] = norm_rows(
                residual, gain[...]
            ).astype(jnp.bfloat16)
    total = bias[...] + lax.dot_general(
        tokens[...], merge_weight[...], (((1,), (1,)), ((), ())), preferred_element_type=jnp.float32
    )
    total = total.astype(jnp.bfloat16)
    if not last:
        refs[0][...] = total
        return
    note, *earlier = refs[:-packs]
    me = lax.axis_index("pack")
    outs = refs[-packs:]
    total = jnp.concatenate([*[one[...] for one in earlier], total], axis=0)
    whole = total.shape[1] // LANES
    most = outs[0].shape[0] * LANES // total.shape[1]
    notes = note[...].astype(jnp.float32)
    note_row = lax.broadcasted_iota(jnp.int32, notes.shape, 0)
    slot = lax.broadcasted_iota(jnp.int32, (most, total.shape[0]), 0)
    row = lax.broadcasted_iota(jnp.int32, (most, total.shape[0]), 1)
    for place, out in enumerate(outs):
        found = jnp.where(note_row == (me ^ place), notes, 0.0)
        found = jnp.sum(found, axis=0, keepdims=True)
        first = (16.0 * found[:, :1] + found[:, 1:2]).astype(jnp.int32)
        length = (16.0 * found[:, 2:3] + found[:, 3:4]).astype(jnp.int32)
        chosen = (row == slot + first) & (slot < length)
        chosen = jnp.where(chosen, 1.0, 0.0).astype(jnp.bfloat16)
        block = jnp.dot(chosen, total, preferred_element_type=jnp.float32)
        for column in range(whole):
            out[column * most : (column + 1) * most, :] = block[
                :, column * LANES : (column + 1) * LANES
            ].astype(jnp.bfloat16)
        low = block[: most // 2, whole * LANES :]
        up = block[most // 2 :, whole * LANES :]
        out[whole * most :, :] = jnp.concatenate([low, up], axis=1).astype(jnp.bfloat16)


def merge_call(start, rows, sources, inputs, weight, gain, merge_weight, bias, packs, route):
    groups = rows // 4
    width = merge_weight.shape[0]
    pieces = [piece for source in sources for piece in source]
    vmem = pl.BlockSpec(memory_space=pltpu.VMEM)
    operands = [in_vmem(inputs), in_vmem(weight), gain, in_vmem(merge_weight), bias, *pieces]
    specs = [vmem] * len(operands)
    shapes = [jax.ShapeDtypeStruct((groups, width), jnp.bfloat16)]
    if route:
        most, *others = route
        operands += others
        specs += [vmem] * len(others)
        shapes = [jax.ShapeDtypeStruct((most * width // LANES, LANES), jnp.bfloat16)] * packs
    return pl.pallas_call(
        functools.partial(
            merge_kernel, start, [len(source) for source in sources], packs, bool(route)
        ),
        in_specs=specs,
        out_specs=[vmem] * len(shapes),
        scratch_shapes=[
            pltpu.VMEM((D // LANES, rows, LANES), jnp.float32),
            pltpu.VMEM((groups, 4 * D), jnp.bfloat16),
        ],
        out_shape=shapes,
        compiler_params=pltpu.CompilerParams(vmem_limit_bytes=20 << 20),
        cost_estimate=pl.CostEstimate(
            flops=0,
            bytes_accessed=1024,
            transcendentals=rows,
        ),
        name="out_merge",
    )(*operands)


def place_kernel(place, block, *refs):
    out, rows, sem = refs[-3:]
    most, width = rows.shape
    whole = width // LANES
    half = most // 2
    middle = LANES // 2
    for column in range(whole):
        rows[:, column * LANES : (column + 1) * LANES] = block[
            column * most : (column + 1) * most, :
        ]
    rows[:half, whole * LANES :] = block[whole * most :, :middle]
    rows[half:, whole * LANES :] = block[whole * most :, middle:]
    copy = pltpu.make_async_copy(rows, out.at[lax.axis_index("pack") ^ place], sem)
    copy.start()
    copy.wait()


def place_call(place, block, earlier, shape):
    anywhere = pl.BlockSpec(memory_space=pl.ANY)
    return pl.pallas_call(
        functools.partial(place_kernel, place),
        in_specs=[pl.BlockSpec(memory_space=pltpu.VMEM)] + [anywhere] * len(earlier),
        out_specs=anywhere,
        out_shape=pltpu.HBM(shape, jnp.bfloat16),
        scratch_shapes=[pltpu.VMEM(shape[1:], jnp.bfloat16), pltpu.SemaphoreType.DMA],
        input_output_aliases={1: 0} if earlier else {},
        compiler_params=pltpu.CompilerParams(vmem_limit_bytes=4 << 20),
        cost_estimate=pl.CostEstimate(
            flops=0, bytes_accessed=4 * shape[1] * shape[2], transcendentals=0
        ),
        name="place_rows",
    )(block, *map(in_hbm, earlier))


def send_seq(value, flip):
    size = lax.axis_size("seq")
    return lax.ppermute(value, "seq", [(i, i ^ flip) for i in range(size)])


def after(values, *earlier):
    return lax.optimization_barrier((tuple(values), earlier))[0]


def halves_kernel(across_x, across_y, upper, lower):
    half = upper.shape[0]
    upper[...] = across_x[:half]
    lower[...] = across_y[half:]


def halves_call(across_x, across_y):
    vmem = pl.BlockSpec(memory_space=pltpu.VMEM)
    shape = (across_x.shape[0] // 2, across_x.shape[1])
    return pl.pallas_call(
        halves_kernel,
        in_specs=[vmem] * 2,
        out_specs=[vmem] * 2,
        out_shape=[jax.ShapeDtypeStruct(shape, across_x.dtype)] * 2,
        compiler_params=pltpu.CompilerParams(vmem_limit_bytes=4 << 20),
        cost_estimate=pl.CostEstimate(
            flops=0, bytes_accessed=4 * across_x.size, transcendentals=0
        ),
        name="halves",
    )(across_x, across_y)


def near_shards(value):
    return [send_seq(value, 1), send_seq(value, 2), send_seq(value, 4)]


def far_shards(across_x, across_y):
    upper, lower = halves_call(across_x, across_y)
    return [send_seq(upper, 4), send_seq(lower, 2)]


def weight_order(heads_here):
    quarter = HD // 4
    order = -np.ones((6 * LANES,), np.int32)
    for head in range(heads_here):
        base = head * 3 * HD
        for kind in range(2):
            for half in range(2):
                for letter in range(2):
                    target = (2 * kind + letter) * LANES + head * (HD // 2) + half * quarter
                    source = base + kind * HD + half * (HD // 2) + letter * quarter
                    order[target : target + quarter] = np.arange(source, source + quarter)
        target = (4 + head) * LANES
        order[target : target + HD] = np.arange(base + 2 * HD, base + 3 * HD)
    return order


def angle_table(heads_here):
    quarter = HD // 4
    frequency = (10000.0 ** (-np.arange(quarter) / quarter)).astype(np.float32)
    angles = np.arange(POSITIONS, dtype=np.float32)[:, None] * frequency[None, :]
    pieces = []
    for function in (np.cos, np.sin):
        exact = np.zeros((2 * POSITIONS, LANES), np.float64)
        for head in range(heads_here):
            for half in range(2):
                lane = head * (HD // 2) + half * quarter
                rows = slice(half * POSITIONS, (half + 1) * POSITIONS)
                exact[rows, lane : lane + quarter] = function(angles.astype(np.float64))
        upper = exact.astype(jnp.bfloat16)
        pieces += [upper, (exact - upper.astype(np.float64)).astype(jnp.bfloat16)]
    return np.concatenate(pieces, axis=1)


def fast_local(
    patches,
    patch_mask,
    mask_embed,
    norm_gain,
    qkv_weight,
    segment_ids,
    patch_rows,
    patch_column,
    out_weight,
    merge_gain,
    merge_weight,
    merge_bias,
    image_owner,
):
    local_rows = patches.shape[1]
    shards = lax.axis_size("seq")
    packs = lax.axis_size("pack")
    heads_here = HEADS // shards
    images = image_owner.shape[1]
    total = local_rows * shards
    me = lax.axis_index("seq").astype(jnp.int32)

    value = payload_call(segment_ids, patch_rows, patch_column, patch_mask, mask_embed, patches)
    own_swap, across_x, across_y = near_shards(value)

    order = weight_order(heads_here)
    spread = (order[:, None] == np.arange(qkv_weight.shape[1])[None, :]).astype(jnp.bfloat16)
    table = jnp.asarray(angle_table(heads_here))
    ids = jnp.stack([me ^ place for place in range(shards)])
    gain, merge_gain_row, bias, ordered, merge_rows, weight = prepare_call(
        shards,
        ids,
        out_weight,
        merge_weight.T,
        qkv_weight.T,
        jnp.asarray(spread),
        (norm_gain, merge_gain, merge_bias),
    )

    project = lambda place, first, second, earlier: qkv_call(
        place, first, second, table, gain, weight, earlier, total
    )
    buffers = project(0, [value], [own_swap], ())
    across_x, across_y = after([across_x, across_y], buffers[2], ordered)
    far = far_shards(across_x, across_y)
    buffers = project(1, [across_x], [send_seq(across_x, 1)], buffers)
    buffers = project(2, [across_y], [send_seq(across_y, 1)], buffers)
    far = after(far, buffers[2])
    buffers = project(3, far, [send_seq(one, 1) for one in far], buffers)
    inputs, block, labels = buffers

    most = 2 * (total // 4) // images
    first_rows, last_rows = CHUNKS
    (own,) = attention_call(0, first_rows, labels, block, ())
    own_swap, across_x, across_y = near_shards(own)
    labels, block = after([labels, block], own)
    late, note = attention_call(first_rows, last_rows, labels, block, (image_owner,))
    across_x, across_y = after([across_x, across_y], late)
    halves = halves_call(across_x, across_y)
    far = [send_seq(halves[0], 4), send_seq(halves[1], 2)]
    (late,) = after([late], *halves)
    late_shares = [late] + [send_seq(late, flip) for flip in (2, 4, 6)]
    near = [send_seq(one, 1) for one in (across_x, across_y)]
    merge = lambda start, rows, sources, route: merge_call(
        start, rows, sources, inputs, ordered, merge_gain_row, merge_rows, bias, packs, route
    )
    sources = [[own], [own_swap], [across_x], near[:1], [across_y], near[1:], far]
    (projected,) = merge(0, first_rows, sources + [[send_seq(one, 1) for one in far]], ())
    late_shares[1:] = [after([one], projected)[0] for one in late_shares[1:]]
    sources = [[one] for share in late_shares for one in (share, send_seq(share, 1))]
    made = merge(first_rows, last_rows, sources, (most, note, projected))
    sent = {
        flip: lax.ppermute(made[flip], "pack", [(z, z ^ flip) for z in range(packs)])
        for flip in range(packs - 1, 0, -1)
    }
    shape = (packs, most, merge_weight.shape[1])
    routed = place_call(0, made[0], (), shape)
    for flip in (3, 1, 2):
        routed = place_call(flip, sent[flip], (routed,), shape)
    return routed[None]


def local(*arguments):
    patches, weight = arguments[0], arguments[4]
    shards = lax.axis_size("seq")
    fits = shards == 8 and HEADS // shards == 2 and weight.shape[1] == 6 * HD
    fits = fits and patches.shape[1] * shards == sum(CHUNKS) and lax.axis_size("pack") == 4
    return fast_local(*arguments) if fits else general_local(*arguments)


def solution(mesh):
    placed = (
        P("pack", "seq", None),
        P("pack", "seq"),
        P(),
        P(),
        P(None, "seq"),
        P("pack", "seq"),
        P("pack", "seq"),
        P("pack", "seq"),
        P(),
        P(),
        P(None, "seq"),
        P("seq"),
        P("pack", None),
    )
    return jax.shard_map(
        local, mesh=mesh, in_specs=placed, out_specs=P("pack", None, None, "seq"), check_vma=False
    )
```

```python
import functools

import jax
import jax.numpy as jnp
import numpy as np
from jax import lax
from jax.experimental import pallas as pl
from jax.experimental.pallas import tpu as pltpu
from jax.sharding import PartitionSpec as P

D = 1408
HEADS = 16
HD = 88


EPSILON = 1e-06


def layer_norm(values, gain_vector):
    center = values - jnp.mean(values, axis=-1, keepdims=True)
    spread = jnp.mean(center * center, axis=-1, keepdims=True)
    return center * lax.rsqrt(spread + EPSILON) * gain_vector.astype(jnp.float32)


def rotate(vectors, row_index, column_index):
    total_rows, heads_here, head_width = vectors.shape
    quarter = head_width // 4
    frequency = 10000.0 ** (-jnp.arange(quarter, dtype=jnp.float32) / quarter)
    row_angle = row_index.astype(jnp.float32)[:, None] * frequency[None, :]
    column_angle = column_index.astype(jnp.float32)[:, None] * frequency[None, :]
    angles = jnp.stack([row_angle, column_angle], axis=1)[:, None, :, None, :]
    split_up = vectors.reshape(total_rows, heads_here, 2, 2, quarter)
    partner = jnp.stack([-split_up[:, :, :, 1], split_up[:, :, :, 0]], axis=3)
    turned = split_up * jnp.cos(angles) + partner * jnp.sin(angles)
    return turned.reshape(total_rows, heads_here, head_width)


def qkv_block(projected, row_index, column_index):
    turned_queries = rotate(projected[:, :, 0], row_index, column_index)
    turned_keys = rotate(projected[:, :, 1], row_index, column_index)
    return jnp.concatenate([turned_queries, turned_keys, projected[:, :, 2]], axis=-1).astype(
        jnp.bfloat16
    )


def attention(block, segments):
    total_rows, heads_here, triple = block.shape
    head_width = triple // 3
    step_rows = min(512, total_rows)
    query_part = block[:, :, :head_width].reshape(
        total_rows // step_rows, step_rows, heads_here, head_width
    )
    key_part = block[:, :, head_width : 2 * head_width]
    value_part = block[:, :, 2 * head_width :]
    query_segments = segments.reshape(total_rows // step_rows, step_rows)
    scale = head_width ** (-0.5)

    def one_block(inputs_pair):
        queries_here, segments_here = inputs_pair
        scores = (
            jnp.einsum("qhd,khd->hqk", queries_here, key_part, preferred_element_type=jnp.float32)
            * scale
        )
        same_image = (segments_here[:, None] == segments[None, :])[None]
        scores = jnp.where(same_image, scores, -jnp.inf)
        highest = jnp.max(scores, axis=-1, keepdims=True)
        weights = jnp.exp(scores - highest)
        probs = (weights / jnp.sum(weights, axis=-1, keepdims=True)).astype(jnp.bfloat16)
        result = jnp.einsum("hqk,khd->qhd", probs, value_part, preferred_element_type=jnp.float32)
        return result.astype(jnp.bfloat16)

    return lax.map(one_block, (query_part, query_segments)).reshape(
        total_rows, heads_here, head_width
    )


def route(projected, segments, owners_here, packs, most):
    merged_segments = segments[::4]
    images = owners_here.shape[0]
    image_ids = jnp.arange(images, dtype=jnp.int32)
    member = (merged_segments[None, :] == image_ids[:, None]).astype(jnp.int32)
    lengths = jnp.sum(member, axis=1, dtype=jnp.int32)
    starts = jnp.cumsum(lengths, dtype=jnp.int32) - lengths
    owner_ids = jnp.arange(packs, dtype=jnp.int32)
    owned = owners_here[None, :] == owner_ids[:, None]
    first_row = jnp.sum(jnp.where(owned, starts[None, :], 0), axis=1, dtype=jnp.int32)
    owned_length = jnp.sum(jnp.where(owned, lengths[None, :], 0), axis=1, dtype=jnp.int32)
    slots = jnp.arange(most, dtype=jnp.int32)
    source_rows = jnp.clip(first_row[:, None] + slots[None, :], 0, projected.shape[0] - 1)
    picked = jnp.take(projected, source_rows.reshape(-1), axis=0).reshape(
        packs, most, projected.shape[1]
    )
    filled = slots[None, :] < owned_length[:, None]
    return jnp.where(filled[:, :, None], picked, jnp.zeros_like(picked))


def general_local(
    patches,
    patch_mask,
    mask_embed,
    norm_gain,
    qkv_weight,
    segment_ids,
    patch_rows,
    patch_column,
    out_weight,
    merge_gain,
    merge_weight,
    merge_bias,
    image_owner,
):
    local_rows = patches.shape[1]
    shards = lax.axis_size("seq")
    packs = lax.axis_size("pack")
    heads_here = HEADS // shards
    inputs = jnp.where(patch_mask[0][:, None] == 1, mask_embed[None, :], patches[0])
    normed = layer_norm(inputs.astype(jnp.float32), norm_gain).astype(jnp.bfloat16)
    labels = lax.all_gather(
        jnp.stack([segment_ids[0], patch_rows[0], patch_column[0]]), "seq", axis=1, tiled=True
    )
    piece = lax.all_gather(normed, "seq", axis=0, tiled=True)
    span = piece.shape[0]
    projected = jnp.dot(piece, qkv_weight, preferred_element_type=jnp.float32)
    row_part = labels[1]
    column_part = labels[2]
    block = qkv_block(projected.reshape(span, heads_here, 3, HD), row_part, column_part)
    result = attention(block, labels[0])
    mixed_heads = lax.all_to_all(result, "seq", split_axis=0, concat_axis=1, tiled=True)
    attended = mixed_heads.reshape(local_rows, D)
    residual = inputs.astype(jnp.float32) + jnp.dot(
        attended, out_weight, preferred_element_type=jnp.float32
    )
    merged = layer_norm(residual, merge_gain).astype(jnp.bfloat16).reshape(local_rows // 4, 4 * D)
    projected_all = (
        jnp.dot(
            lax.all_gather(merged, "seq", axis=0, tiled=True),
            merge_weight,
            preferred_element_type=jnp.float32,
        )
        + merge_bias.astype(jnp.float32)
    ).astype(jnp.bfloat16)
    images = image_owner.shape[1]
    most = 2 * projected_all.shape[0] // images
    outgoing = route(projected_all, labels[0], image_owner[0], packs, most)
    delivered = lax.all_to_all(outgoing, "pack", split_axis=0, concat_axis=0, tiled=True)
    return delivered[None]


LANES = 128
BLOCK = 512
POSITIONS = 64
FAR_APART = -(2.0**100)
IMAGE_LANE = 96
PAIR_ROWS = 3 * LANES
PAIR_CHIPS = (0, 3, 1, 2)
NORM_ROWS = 16
CHUNKS = (768, 768)


def norm_rows(values, gain_row):
    center = values - jnp.mean(values, axis=-1, keepdims=True)
    spread = jnp.mean(center * center, axis=-1, keepdims=True)
    return center * lax.rsqrt(spread + EPSILON) * gain_row


def stacked(pieces):
    loaded = [piece[...] for piece in pieces]
    return loaded[0] if len(loaded) == 1 else jnp.concatenate(loaded, axis=0)


def in_vmem(value):
    return pltpu.with_memory_space_constraint(value, pltpu.VMEM)


def in_hbm(value):
    return pltpu.with_memory_space_constraint(value, pltpu.HBM)


def payload_kernel(segments, rows, columns, mask, embed, patches, out):
    labels = [one[...].astype(jnp.float32) for one in (segments, rows, columns, mask)]
    labels.append(jnp.zeros((4, labels[0].shape[1]), jnp.float32))
    labels = jnp.concatenate(labels, axis=0).astype(jnp.bfloat16)
    shape = (8, LANES)
    row = lax.broadcasted_iota(jnp.int32, shape, 0)
    place = jnp.where(row == lax.broadcasted_iota(jnp.int32, shape, 1), 1.0, 0.0)
    turned = lax.dot_general(
        labels,
        place.astype(jnp.bfloat16),
        (((0,), (0,)), ((), ())),
        preferred_element_type=jnp.float32,
    )
    masked = turned[:, 3:4] > 0.5
    tokens = jnp.where(
        masked, embed[...].astype(jnp.float32)[None, :], patches[0].astype(jnp.float32)
    )
    out[:, :D] = tokens.astype(jnp.bfloat16)
    out[:, D:] = turned.astype(jnp.bfloat16)


def payload_call(segments, rows, columns, mask, embed, patches):
    count = patches.shape[1]
    operands = (segments, rows, columns, mask, embed, patches)
    fixed = lambda shape: pl.BlockSpec(shape, lambda i: (0,) * len(shape))
    shape = (count, D + LANES)
    return pl.pallas_call(
        payload_kernel,
        grid=(1,),
        in_specs=[fixed(one.shape) for one in operands],
        out_specs=fixed(shape),
        out_shape=jax.ShapeDtypeStruct(shape, jnp.bfloat16),
        compiler_params=pltpu.CompilerParams(vmem_limit_bytes=8 << 20),
        cost_estimate=pl.CostEstimate(
            flops=count * D, bytes_accessed=4 * count * D, transcendentals=0
        ),
        name="payload",
    )(*map(in_hbm, operands))


def qkv_kernel(count, flip, *refs):
    me = lax.axis_index("seq")
    first, second = refs[:count], refs[count : 2 * count]
    table, gain, weight = refs[2 * count : 2 * count + 3]
    inputs_out, qkv_out, label_out = refs[-3:]
    mine, other = stacked(first), stacked(second)
    leads = me % 2 == 0
    ahead = jnp.where(leads, mine, other)
    behind = jnp.where(leads, other, mine)
    both = jnp.concatenate([ahead, behind], axis=0)
    rows = both.shape[0]
    at = pl.ds(pl.multiple_of((me // 2 ^ flip) * rows, rows), rows)
    inputs_out[at, :] = both[:, :D]
    label_out[at, :] = both[:, D:]
    labels = both[:, D:].astype(jnp.float32)
    normed = norm_rows(both[:, :D].astype(jnp.float32), gain[...]).astype(jnp.bfloat16)
    columns = lax.dot_general(
        normed, weight[...], (((1,), (1,)), ((), ())), preferred_element_type=jnp.float32
    )
    lane = lax.broadcasted_iota(jnp.int32, labels.shape, 1)
    numbers = lane.astype(jnp.float32)
    hot = (numbers == labels[:, 1:2]) | (numbers == labels[:, 2:3] + POSITIONS)
    looked = jnp.dot(
        jnp.where(hot, 1.0, 0.0).astype(jnp.bfloat16), table[...], preferred_element_type=jnp.float32
    )
    cosine = looked[:, :LANES] + looked[:, LANES : 2 * LANES]
    sine = looked[:, 2 * LANES : 3 * LANES] + looked[:, 3 * LANES :]
    first_head = lane < HD // 2

    def turn(start):
        a = columns[:, start : start + LANES]
        b = columns[:, start + LANES : start + 2 * LANES]
        return a * cosine - b * sine, b * cosine + a * sine

    factor = HD**-0.5 * float(np.log2(np.e))
    query_a, query_b = (one * factor for one in turn(0))
    key_a, key_b = turn(2 * LANES)
    zero = jnp.zeros_like(key_a)
    image = numbers == labels[:, :1] + IMAGE_LANE
    extra = lane >= IMAGE_LANE
    apart = jnp.where(image, 0.0, FAR_APART)
    parts = [
        jnp.where(image, 1.0, query_a),
        query_b,
        jnp.where(extra, apart, jnp.where(first_head, key_a, zero)),
        jnp.where(first_head, key_b, zero),
        jnp.where(extra, apart, jnp.where(first_head, zero, key_a)),
        jnp.where(first_head, zero, key_b),
    ]
    for head in range(2):
        values = columns[:, (4 + head) * LANES : (5 + head) * LANES]
        parts.append(jnp.where(lane == HD, 1.0, values))
    for number, part in enumerate(parts):
        qkv_out[at, number * LANES : (number + 1) * LANES] = part.astype(jnp.bfloat16)


def qkv_call(flip, first, second, table, gain, weight, earlier, total):
    rows = 2 * sum(piece.shape[0] for piece in first)
    widths = (D, 8 * LANES, LANES)
    operands = [*first, *second, table, gain, in_vmem(weight)]
    vmem = pl.BlockSpec(memory_space=pltpu.VMEM)
    held = [in_vmem(one) for one in earlier]
    return pl.pallas_call(
        functools.partial(qkv_kernel, len(first), flip),
        in_specs=[vmem] * (len(operands) + len(earlier)),
        out_specs=[vmem] * len(widths),
        out_shape=[pltpu.VMEM((total, width), jnp.bfloat16) for width in widths],
        input_output_aliases={len(operands) + i: i for i in range(len(earlier))},
        compiler_params=pltpu.CompilerParams(vmem_limit_bytes=14 << 20),
        cost_estimate=pl.CostEstimate(
            flops=6 * rows * D * weight.shape[0],
            bytes_accessed=2 * (rows * 4 * D + weight.size),
            transcendentals=rows,
        ),
        name="norm_qkv",
    )(*operands, *held)


def segment_row(labels):
    pick = jnp.where(lax.broadcasted_iota(jnp.int32, (8, LANES), 1) == 0, 1.0, 0.0)
    return lax.dot_general(
        pick.astype(jnp.bfloat16),
        labels,
        (((1,), (1,)), ((), ())),
        preferred_element_type=jnp.float32,
    )


def attention_kernel(start, images, labels, block, *refs):
    owners, refs = (refs[0], refs[1:]) if images else (None, refs)
    out, *rest = refs
    scores, high = rest[-2:]
    rows = high.shape[1]
    total = block.shape[0]
    segments = segment_row(labels[...])
    one_row = segments[:1]
    lowest = jnp.min(labels[start : start + 16, :1].astype(jnp.float32), axis=0, keepdims=True)
    largest = labels[start + rows - 16 : start + rows, :1].astype(jnp.float32)
    largest = jnp.max(largest, axis=0, keepdims=True)
    begin = jnp.sum(jnp.where(one_row < lowest, 1, 0)) // BLOCK
    end = (jnp.sum(jnp.where(one_row <= largest, 1, 0)) + BLOCK - 1) // BLOCK
    queries = block[start : start + rows, : 2 * LANES]
    high[...] = jnp.full_like(high, 2 * FAR_APART)

    def score(step, carry):
        at = pl.ds(pl.multiple_of(step * BLOCK, BLOCK), BLOCK)
        for head in range(2):
            keys = block[at, (2 + 2 * head) * LANES : (4 + 2 * head) * LANES]
            values = lax.dot_general(
                queries, keys, (((1,), (1,)), ((), ())), preferred_element_type=jnp.float32
            )
            scores[head, step] = values
            tops = [values[:, lane : lane + LANES] for lane in range(0, BLOCK, LANES)]
            high[head] = functools.reduce(jnp.maximum, tops, high[head])
        return carry

    lax.fori_loop(begin, end, score, 0)
    highest = [jnp.max(high[head], axis=-1, keepdims=True) for head in range(2)]

    def weigh(step, carry):
        at = pl.ds(pl.multiple_of(step * BLOCK, BLOCK), BLOCK)
        sums = []
        for head in range(2):
            weights = jnp.exp2(scores[head, step] - highest[head])
            values = block[at, (6 + head) * LANES : (7 + head) * LANES]
            sums.append(
                carry[head]
                + jnp.dot(weights.astype(jnp.bfloat16), values, preferred_element_type=jnp.float32)
            )
        return tuple(sums)

    zero = jnp.zeros((rows, LANES), jnp.float32)
    sums = lax.fori_loop(begin, end, weigh, (zero, zero))
    first, second = (one / one[:, HD : HD + 1] for one in sums)
    lane = lax.broadcasted_iota(jnp.int32, first.shape, 1)
    turned = pltpu.roll(second, HD, 1)
    out[:rows] = jnp.where(lane < HD, first, turned).astype(jnp.bfloat16)
    half = rows // 2
    tail = 2 * HD - LANES
    lane = lane[:half]
    up = pltpu.roll(turned[half:], tail, 1)
    packed = jnp.where(lane < tail, turned[:half], jnp.where(lane < 2 * tail, up, 0.0))
    out[rows:] = packed.astype(jnp.bfloat16)

    if len(rest) > 2:
        note = rest[0]
        row = lax.broadcasted_iota(jnp.int32, note.shape, 0)
        lane = lax.broadcasted_iota(jnp.int32, note.shape, 1)
        found = jnp.zeros(note.shape, jnp.float32)
        for image in range(images):
            below = jnp.sum(jnp.where(one_row < image, 0.25, 0.0), axis=1, keepdims=True)
            inside = jnp.sum(jnp.where(one_row == image, 0.25, 0.0), axis=1, keepdims=True)
            here = row == owners[0, image]
            for place, number in enumerate((below, inside)):
                upper = jnp.floor(number * (1.0 / 16))
                found = jnp.where(here & (lane == 2 * place), upper, found)
                found = jnp.where(here & (lane == 2 * place + 1), number - 16 * upper, found)
        note[...] = found.astype(jnp.bfloat16)


def attention_call(start, rows, labels, block, owners):
    total = block.shape[0]
    vmem = pl.BlockSpec(memory_space=pltpu.VMEM)
    shapes = [jax.ShapeDtypeStruct((rows + rows // 2, LANES), jnp.bfloat16)]
    if owners:
        shapes.append(jax.ShapeDtypeStruct((16, LANES), jnp.bfloat16))
    return pl.pallas_call(
        functools.partial(attention_kernel, start, owners[0].shape[1] if owners else 0),
        in_specs=[vmem, vmem] + [pl.BlockSpec(memory_space=pltpu.SMEM)] * len(owners),
        out_specs=[vmem] * len(shapes),
        out_shape=shapes,
        scratch_shapes=[
            pltpu.VMEM((2, total // BLOCK, rows, BLOCK), jnp.float32),
            pltpu.VMEM((2, rows, LANES), jnp.float32),
        ],
        compiler_params=pltpu.CompilerParams(vmem_limit_bytes=20 << 20),
        cost_estimate=pl.CostEstimate(
            flops=10 * rows * total * 2 * LANES,
            bytes_accessed=2 * block.size,
            transcendentals=rows * total,
        ),
        name="attention",
    )(in_vmem(labels), in_vmem(block), *owners)


def prepare_kernel(shards, ids, out_weight, merge_weight, qkv_weight, spread, *refs):
    *rows, out, merge, qkv, qkv_buffer, spread_buffer, sems = refs
    for row, row_out in zip(rows[: len(rows) // 2], rows[len(rows) // 2 :]):
        row_out[...] = row[...].astype(jnp.float32)[None, :]
    rest = 2 * HD - LANES
    copies = [(qkv_weight, qkv_buffer), (spread, spread_buffer)]
    for pair in range(shards // 2):
        low = pair * PAIR_ROWS + 2 * LANES
        out[low : low + LANES] = jnp.zeros((LANES, D), jnp.bfloat16)
    for place in range(shards):
        start = pl.multiple_of(ids[place] * (2 * HD), 16)
        base = place // 2 * PAIR_ROWS
        wide = base + place % 2 * LANES
        to = base + 2 * LANES + place % 2 * rest
        copies.append(
            (out_weight.at[pl.ds(start, LANES), :], out.at[pl.ds(wide, LANES), :])
        )
        copies.append((out_weight.at[pl.ds(start + LANES, rest), :], out.at[pl.ds(to, rest), :]))
    copies.append((merge_weight, merge))
    copies = [
        pltpu.make_async_copy(source, target, sems.at[i])
        for i, (source, target) in enumerate(copies)
    ]
    for copy in copies:
        copy.start()
    copies[0].wait()
    copies[1].wait()
    qkv[...] = jnp.dot(
        spread_buffer[...], qkv_buffer[...], preferred_element_type=jnp.float32
    ).astype(jnp.bfloat16)
    for copy in copies[2:]:
        copy.wait()


def prepare_call(shards, ids, out_weight, merge_weight, qkv_weight, spread, rows):
    anywhere = pl.BlockSpec(memory_space=pl.ANY)
    vmem = pl.BlockSpec(memory_space=pltpu.VMEM)
    operands = (out_weight, merge_weight, qkv_weight, spread)
    shapes = [(shards * LANES * 3 // 2, D), merge_weight.shape, (spread.shape[0], D)]
    return pl.pallas_call(
        functools.partial(prepare_kernel, shards),
        in_specs=[pl.BlockSpec(memory_space=pltpu.SMEM)]
        + [anywhere] * len(operands)
        + [vmem] * len(rows),
        out_specs=[vmem] * (len(rows) + len(shapes)),
        out_shape=[pltpu.VMEM((1, row.shape[0]), jnp.float32) for row in rows]
        + [pltpu.VMEM(shape, jnp.bfloat16) for shape in shapes],
        scratch_shapes=[
            pltpu.VMEM(qkv_weight.shape, jnp.bfloat16),
            pltpu.VMEM(spread.shape, jnp.bfloat16),
            pltpu.SemaphoreType.DMA((2 * shards + 3,)),
        ],
        compiler_params=pltpu.CompilerParams(vmem_limit_bytes=10 << 20),
        cost_estimate=pl.CostEstimate(
            flops=2 * spread.size * D,
            bytes_accessed=4 * (out_weight.size + merge_weight.size + qkv_weight.size),
            transcendentals=0,
        ),
        name="prepare",
    )(ids, *map(in_hbm, operands), *rows)


def out_product(sources, rows, weight, first_pair):
    half = rows // 2
    rest = 2 * HD - LANES
    lane = lax.broadcasted_iota(jnp.int32, (half, LANES), 1)
    lined = []
    for same, swapped in zip(sources[::2], sources[1::2]):
        mine, other = same[rows:, :].astype(jnp.float32), swapped[rows:, :].astype(jnp.float32)
        upper = jnp.where(lane < rest, mine, pltpu.roll(other, rest, 1))
        lower = jnp.where(lane < rest, pltpu.roll(mine, LANES - rest, 1), other)
        tail = jnp.concatenate([upper, lower], axis=0).astype(jnp.bfloat16)
        lined += [same[:rows, :], swapped[:rows, :], tail]
    low = first_pair * PAIR_ROWS
    high = low + len(sources) // 2 * PAIR_ROWS
    return jnp.dot(
        jnp.concatenate(lined, axis=1), weight[low:high, :], preferred_element_type=jnp.float32
    )


def merged_product(state, tokens, gain, merge_weight, bias):
    groups = tokens.shape[0]
    for block in range(0, groups, NORM_ROWS):
        for quadrant in range(4):
            at = pl.ds(4 * block + quadrant, NORM_ROWS, stride=4)
            residual = jnp.concatenate(
                [state[column, at, :] for column in range(D // LANES)], axis=1
            )
            tokens[block : block + NORM_ROWS, quadrant * D : (quadrant + 1) * D] = norm_rows(
                residual, gain[...]
            ).astype(jnp.bfloat16)
    total = bias[...] + lax.dot_general(
        tokens[...], merge_weight[...], (((1,), (1,)), ((), ())), preferred_element_type=jnp.float32
    )
    return total.astype(jnp.bfloat16)


def split(pieces, counts):
    sources, at = [], 0
    for count in counts:
        sources.append(stacked(pieces[at : at + count]))
        at += count
    return sources


def add_inputs(state, inputs, start, mixed):
    for column in range(D // LANES):
        lanes = slice(column * LANES, (column + 1) * LANES)
        before = inputs[start : start + mixed.shape[0], lanes]
        state[column] = before.astype(jnp.float32) + mixed[:, lanes]


def merge_kernel(start, counts, inputs, weight, gain, merge_weight, bias, *refs):
    *pieces, out, state, tokens = refs
    mixed = out_product(split(pieces, counts), state.shape[1], weight, 0)
    add_inputs(state, inputs, start, mixed)
    out[...] = merged_product(state, tokens, gain, merge_weight, bias)


def partial_kernel(start, counts, inputs, weight, *refs):
    *pieces, state = refs
    mixed = out_product(split(pieces, counts), state.shape[1], weight, 0)
    add_inputs(state, inputs, start, mixed)


def finish_kernel(
    first_pair, packs, partial, weight, gain, merge_weight, bias, *refs
):
    *refs, state, tokens = refs
    sources, refs = [one[...] for one in refs[:4]], refs[4:]
    mixed = out_product(sources, state.shape[1], weight, first_pair)
    for column in range(D // LANES):
        state[column] = partial[column] + mixed[:, column * LANES : (column + 1) * LANES]
    total = merged_product(state, tokens, gain, merge_weight, bias)
    note, *earlier = refs[:-packs]
    me = lax.axis_index("pack")
    outs = refs[-packs:]
    total = jnp.concatenate([*[one[...] for one in earlier], total], axis=0)
    whole = total.shape[1] // LANES
    most = outs[0].shape[0] * LANES // total.shape[1]
    notes = note[...].astype(jnp.float32)
    note_row = lax.broadcasted_iota(jnp.int32, notes.shape, 0)
    slot = lax.broadcasted_iota(jnp.int32, (most, total.shape[0]), 0)
    row = lax.broadcasted_iota(jnp.int32, (most, total.shape[0]), 1)
    for place, out in enumerate(outs):
        found = jnp.where(note_row == (me ^ place), notes, 0.0)
        found = jnp.sum(found, axis=0, keepdims=True)
        first = (16.0 * found[:, :1] + found[:, 1:2]).astype(jnp.int32)
        length = (16.0 * found[:, 2:3] + found[:, 3:4]).astype(jnp.int32)
        chosen = (row == slot + first) & (slot < length)
        chosen = jnp.where(chosen, 1.0, 0.0).astype(jnp.bfloat16)
        block = jnp.dot(chosen, total, preferred_element_type=jnp.float32)
        for column in range(whole):
            out[column * most : (column + 1) * most, :] = block[
                :, column * LANES : (column + 1) * LANES
            ].astype(jnp.bfloat16)
        low = block[: most // 2, whole * LANES :]
        up = block[most // 2 :, whole * LANES :]
        out[whole * most :, :] = jnp.concatenate([low, up], axis=1).astype(jnp.bfloat16)


def vmem_call(kernel, name, operands, shapes, scratch):
    vmem = pl.BlockSpec(memory_space=pltpu.VMEM)
    return pl.pallas_call(
        kernel,
        in_specs=[vmem] * len(operands),
        out_specs=[vmem] * len(shapes),
        scratch_shapes=scratch,
        out_shape=shapes,
        compiler_params=pltpu.CompilerParams(vmem_limit_bytes=20 << 20),
        cost_estimate=pl.CostEstimate(flops=0, bytes_accessed=1024, transcendentals=0),
        name=name,
    )(*operands)


def merge_scratch(rows):
    return [
        pltpu.VMEM((D // LANES, rows, LANES), jnp.float32),
        pltpu.VMEM((rows // 4, 4 * D), jnp.bfloat16),
    ]


def merge_call(start, rows, sources, inputs, weight, gain, merge_weight, bias):
    pieces = [piece for source in sources for piece in source]
    return vmem_call(
        functools.partial(merge_kernel, start, [len(source) for source in sources]),
        "out_merge",
        [in_vmem(inputs), in_vmem(weight), gain, in_vmem(merge_weight), bias, *pieces],
        [jax.ShapeDtypeStruct((rows // 4, merge_weight.shape[0]), jnp.bfloat16)],
        merge_scratch(rows),
    )[0]


def partial_call(start, rows, sources, inputs, weight):
    return vmem_call(
        functools.partial(partial_kernel, start, [1] * len(sources)),
        "out_near",
        [in_vmem(inputs), in_vmem(weight), *sources],
        [pltpu.VMEM((D // LANES, rows, LANES), jnp.float32)],
        [],
    )[0]


def finish_call(
    rows, partial, sources, first_pair, weight, gain, merge_weight, bias, packs, most, note, earlier
):
    shape = (most * merge_weight.shape[0] // LANES, LANES)
    return vmem_call(
        functools.partial(finish_kernel, first_pair, packs),
        "out_far_merge",
        [in_vmem(partial), in_vmem(weight), gain, in_vmem(merge_weight), bias, *sources]
        + [note, earlier],
        [jax.ShapeDtypeStruct(shape, jnp.bfloat16)] * packs,
        merge_scratch(rows),
    )


def place_kernel(place, block, *refs):
    out, rows, sem = refs[-3:]
    most, width = rows.shape
    whole = width // LANES
    half = most // 2
    middle = LANES // 2
    for column in range(whole):
        rows[:, column * LANES : (column + 1) * LANES] = block[
            column * most : (column + 1) * most, :
        ]
    rows[:half, whole * LANES :] = block[whole * most :, :middle]
    rows[half:, whole * LANES :] = block[whole * most :, middle:]
    copy = pltpu.make_async_copy(rows, out.at[lax.axis_index("pack") ^ place], sem)
    copy.start()
    copy.wait()


def place_call(place, block, earlier, shape):
    anywhere = pl.BlockSpec(memory_space=pl.ANY)
    return pl.pallas_call(
        functools.partial(place_kernel, place),
        in_specs=[pl.BlockSpec(memory_space=pltpu.VMEM)] + [anywhere] * len(earlier),
        out_specs=anywhere,
        out_shape=pltpu.HBM(shape, jnp.bfloat16),
        scratch_shapes=[pltpu.VMEM(shape[1:], jnp.bfloat16), pltpu.SemaphoreType.DMA],
        input_output_aliases={1: 0} if earlier else {},
        compiler_params=pltpu.CompilerParams(vmem_limit_bytes=4 << 20),
        cost_estimate=pl.CostEstimate(
            flops=0, bytes_accessed=4 * shape[1] * shape[2], transcendentals=0
        ),
        name="place_rows",
    )(block, *map(in_hbm, earlier))


def send_seq(value, flip):
    size = lax.axis_size("seq")
    return lax.ppermute(value, "seq", [(i, i ^ flip) for i in range(size)])


def after(values, *earlier):
    return lax.optimization_barrier((tuple(values), earlier))[0]


def halves_kernel(across_x, across_y, upper, lower):
    half = upper.shape[0]
    upper[...] = across_x[:half]
    lower[...] = across_y[half:]


def halves_call(across_x, across_y):
    vmem = pl.BlockSpec(memory_space=pltpu.VMEM)
    shape = (across_x.shape[0] // 2, across_x.shape[1])
    return pl.pallas_call(
        halves_kernel,
        in_specs=[vmem] * 2,
        out_specs=[vmem] * 2,
        out_shape=[jax.ShapeDtypeStruct(shape, across_x.dtype)] * 2,
        compiler_params=pltpu.CompilerParams(vmem_limit_bytes=4 << 20),
        cost_estimate=pl.CostEstimate(
            flops=0, bytes_accessed=4 * across_x.size, transcendentals=0
        ),
        name="halves",
    )(across_x, across_y)


def near_shards(value):
    return [send_seq(value, 1), send_seq(value, 2), send_seq(value, 4)]


def far_shards(across_x, across_y):
    upper, lower = halves_call(across_x, across_y)
    return [send_seq(upper, 4), send_seq(lower, 2)]


def weight_order(heads_here):
    quarter = HD // 4
    order = -np.ones((6 * LANES,), np.int32)
    for head in range(heads_here):
        base = head * 3 * HD
        for kind in range(2):
            for half in range(2):
                for letter in range(2):
                    target = (2 * kind + letter) * LANES + head * (HD // 2) + half * quarter
                    source = base + kind * HD + half * (HD // 2) + letter * quarter
                    order[target : target + quarter] = np.arange(source, source + quarter)
        target = (4 + head) * LANES
        order[target : target + HD] = np.arange(base + 2 * HD, base + 3 * HD)
    return order


def angle_table(heads_here):
    quarter = HD // 4
    frequency = (10000.0 ** (-np.arange(quarter) / quarter)).astype(np.float32)
    angles = np.arange(POSITIONS, dtype=np.float32)[:, None] * frequency[None, :]
    pieces = []
    for function in (np.cos, np.sin):
        exact = np.zeros((2 * POSITIONS, LANES), np.float64)
        for head in range(heads_here):
            for half in range(2):
                lane = head * (HD // 2) + half * quarter
                rows = slice(half * POSITIONS, (half + 1) * POSITIONS)
                exact[rows, lane : lane + quarter] = function(angles.astype(np.float64))
        upper = exact.astype(jnp.bfloat16)
        pieces += [upper, (exact - upper.astype(np.float64)).astype(jnp.bfloat16)]
    return np.concatenate(pieces, axis=1)


def fast_local(
    patches,
    patch_mask,
    mask_embed,
    norm_gain,
    qkv_weight,
    segment_ids,
    patch_rows,
    patch_column,
    out_weight,
    merge_gain,
    merge_weight,
    merge_bias,
    image_owner,
):
    local_rows = patches.shape[1]
    shards = lax.axis_size("seq")
    packs = lax.axis_size("pack")
    heads_here = HEADS // shards
    images = image_owner.shape[1]
    total = local_rows * shards
    me = lax.axis_index("seq").astype(jnp.int32)

    value = payload_call(segment_ids, patch_rows, patch_column, patch_mask, mask_embed, patches)
    own_swap, across_x, across_y = near_shards(value)

    order = weight_order(heads_here)
    spread = (order[:, None] == np.arange(qkv_weight.shape[1])[None, :]).astype(jnp.bfloat16)
    table = jnp.asarray(angle_table(heads_here))
    ids = jnp.stack([me ^ (2 * chip + core) for chip in PAIR_CHIPS for core in range(2)])
    gain, merge_gain_row, bias, ordered, merge_rows, weight = prepare_call(
        shards,
        ids,
        out_weight,
        merge_weight.T,
        qkv_weight.T,
        jnp.asarray(spread),
        (norm_gain, merge_gain, merge_bias),
    )

    project = lambda place, first, second, earlier: qkv_call(
        place, first, second, table, gain, weight, earlier, total
    )
    buffers = project(0, [value], [own_swap], ())
    across_x, across_y = after([across_x, across_y], buffers[2], ordered)
    far = far_shards(across_x, across_y)
    buffers = project(1, [across_x], [send_seq(across_x, 1)], buffers)
    buffers = project(2, [across_y], [send_seq(across_y, 1)], buffers)
    far = after(far, buffers[2])
    buffers = project(3, far, [send_seq(one, 1) for one in far], buffers)
    inputs, block, labels = buffers

    most = 2 * (total // 4) // images
    first_rows, last_rows = CHUNKS
    (own,) = attention_call(0, first_rows, labels, block, ())
    own_swap, across_x, across_y = near_shards(own)
    labels, block = after([labels, block], own)
    late, note = attention_call(first_rows, last_rows, labels, block, (image_owner,))
    across_x, across_y = after([across_x, across_y], late)
    halves = halves_call(across_x, across_y)
    far = [send_seq(halves[0], 4), send_seq(halves[1], 2)]
    (late,) = after([late], *halves)
    late_shares = [late] + [send_seq(late, flip) for flip in (2, 4, 6)]
    near = [send_seq(one, 1) for one in (across_x, across_y)]
    sources = [[own], [own_swap], far, [send_seq(one, 1) for one in far]]
    sources += [[across_x], near[:1], [across_y], near[1:]]
    projected = merge_call(
        0, first_rows, sources, inputs, ordered, merge_gain_row, merge_rows, bias
    )
    late_shares[1:] = [after([one], projected)[0] for one in late_shares[1:]]
    pairs = [[late_shares[chip], send_seq(late_shares[chip], 1)] for chip in PAIR_CHIPS]
    partial = partial_call(first_rows, last_rows, pairs[0] + pairs[1], inputs, ordered)
    made = finish_call(
        last_rows,
        partial,
        pairs[2] + pairs[3],
        2,
        ordered,
        merge_gain_row,
        merge_rows,
        bias,
        packs,
        most,
        note,
        projected,
    )
    sent = {
        flip: lax.ppermute(made[flip], "pack", [(z, z ^ flip) for z in range(packs)])
        for flip in range(packs - 1, 0, -1)
    }
    shape = (packs, most, merge_weight.shape[1])
    routed = place_call(0, made[0], (), shape)
    for flip in (3, 1, 2):
        routed = place_call(flip, sent[flip], (routed,), shape)
    return routed[None]


def local(*arguments):
    patches, weight = arguments[0], arguments[4]
    shards = lax.axis_size("seq")
    fits = shards == 8 and HEADS // shards == 2 and weight.shape[1] == 6 * HD
    fits = fits and patches.shape[1] * shards == sum(CHUNKS) and lax.axis_size("pack") == 4
    return fast_local(*arguments) if fits else general_local(*arguments)


def solution(mesh):
    placed = (
        P("pack", "seq", None),
        P("pack", "seq"),
        P(),
        P(),
        P(None, "seq"),
        P("pack", "seq"),
        P("pack", "seq"),
        P("pack", "seq"),
        P(),
        P(),
        P(None, "seq"),
        P("seq"),
        P("pack", None),
    )
    return jax.shard_map(
        local, mesh=mesh, in_specs=placed, out_specs=P("pack", None, None, "seq"), check_vma=False
    )
```

```python
import functools

import jax
import jax.numpy as jnp
import numpy as np
from jax import lax
from jax.experimental import pallas as pl
from jax.experimental.pallas import tpu as pltpu
from jax.sharding import PartitionSpec as P

D = 1408
HEADS = 16
HD = 88


EPSILON = 1e-06


def layer_norm(values, gain_vector):
    center = values - jnp.mean(values, axis=-1, keepdims=True)
    spread = jnp.mean(center * center, axis=-1, keepdims=True)
    return center * lax.rsqrt(spread + EPSILON) * gain_vector.astype(jnp.float32)


def rotate(vectors, row_index, column_index):
    total_rows, heads_here, head_width = vectors.shape
    quarter = head_width // 4
    frequency = 10000.0 ** (-jnp.arange(quarter, dtype=jnp.float32) / quarter)
    row_angle = row_index.astype(jnp.float32)[:, None] * frequency[None, :]
    column_angle = column_index.astype(jnp.float32)[:, None] * frequency[None, :]
    angles = jnp.stack([row_angle, column_angle], axis=1)[:, None, :, None, :]
    split_up = vectors.reshape(total_rows, heads_here, 2, 2, quarter)
    partner = jnp.stack([-split_up[:, :, :, 1], split_up[:, :, :, 0]], axis=3)
    turned = split_up * jnp.cos(angles) + partner * jnp.sin(angles)
    return turned.reshape(total_rows, heads_here, head_width)


def qkv_block(projected, row_index, column_index):
    turned_queries = rotate(projected[:, :, 0], row_index, column_index)
    turned_keys = rotate(projected[:, :, 1], row_index, column_index)
    return jnp.concatenate([turned_queries, turned_keys, projected[:, :, 2]], axis=-1).astype(
        jnp.bfloat16
    )


def attention(block, segments):
    total_rows, heads_here, triple = block.shape
    head_width = triple // 3
    step_rows = min(512, total_rows)
    query_part = block[:, :, :head_width].reshape(
        total_rows // step_rows, step_rows, heads_here, head_width
    )
    key_part = block[:, :, head_width : 2 * head_width]
    value_part = block[:, :, 2 * head_width :]
    query_segments = segments.reshape(total_rows // step_rows, step_rows)
    scale = head_width ** (-0.5)

    def one_block(inputs_pair):
        queries_here, segments_here = inputs_pair
        scores = (
            jnp.einsum("qhd,khd->hqk", queries_here, key_part, preferred_element_type=jnp.float32)
            * scale
        )
        same_image = (segments_here[:, None] == segments[None, :])[None]
        scores = jnp.where(same_image, scores, -jnp.inf)
        highest = jnp.max(scores, axis=-1, keepdims=True)
        weights = jnp.exp(scores - highest)
        probs = (weights / jnp.sum(weights, axis=-1, keepdims=True)).astype(jnp.bfloat16)
        result = jnp.einsum("hqk,khd->qhd", probs, value_part, preferred_element_type=jnp.float32)
        return result.astype(jnp.bfloat16)

    return lax.map(one_block, (query_part, query_segments)).reshape(
        total_rows, heads_here, head_width
    )


def route(projected, segments, owners_here, packs, most):
    merged_segments = segments[::4]
    images = owners_here.shape[0]
    image_ids = jnp.arange(images, dtype=jnp.int32)
    member = (merged_segments[None, :] == image_ids[:, None]).astype(jnp.int32)
    lengths = jnp.sum(member, axis=1, dtype=jnp.int32)
    starts = jnp.cumsum(lengths, dtype=jnp.int32) - lengths
    owner_ids = jnp.arange(packs, dtype=jnp.int32)
    owned = owners_here[None, :] == owner_ids[:, None]
    first_row = jnp.sum(jnp.where(owned, starts[None, :], 0), axis=1, dtype=jnp.int32)
    owned_length = jnp.sum(jnp.where(owned, lengths[None, :], 0), axis=1, dtype=jnp.int32)
    slots = jnp.arange(most, dtype=jnp.int32)
    source_rows = jnp.clip(first_row[:, None] + slots[None, :], 0, projected.shape[0] - 1)
    picked = jnp.take(projected, source_rows.reshape(-1), axis=0).reshape(
        packs, most, projected.shape[1]
    )
    filled = slots[None, :] < owned_length[:, None]
    return jnp.where(filled[:, :, None], picked, jnp.zeros_like(picked))


def general_local(
    patches,
    patch_mask,
    mask_embed,
    norm_gain,
    qkv_weight,
    segment_ids,
    patch_rows,
    patch_column,
    out_weight,
    merge_gain,
    merge_weight,
    merge_bias,
    image_owner,
):
    local_rows = patches.shape[1]
    shards = lax.axis_size("seq")
    packs = lax.axis_size("pack")
    heads_here = HEADS // shards
    inputs = jnp.where(patch_mask[0][:, None] == 1, mask_embed[None, :], patches[0])
    normed = layer_norm(inputs.astype(jnp.float32), norm_gain).astype(jnp.bfloat16)
    labels = lax.all_gather(
        jnp.stack([segment_ids[0], patch_rows[0], patch_column[0]]), "seq", axis=1, tiled=True
    )
    piece = lax.all_gather(normed, "seq", axis=0, tiled=True)
    span = piece.shape[0]
    projected = jnp.dot(piece, qkv_weight, preferred_element_type=jnp.float32)
    row_part = labels[1]
    column_part = labels[2]
    block = qkv_block(projected.reshape(span, heads_here, 3, HD), row_part, column_part)
    result = attention(block, labels[0])
    mixed_heads = lax.all_to_all(result, "seq", split_axis=0, concat_axis=1, tiled=True)
    attended = mixed_heads.reshape(local_rows, D)
    residual = inputs.astype(jnp.float32) + jnp.dot(
        attended, out_weight, preferred_element_type=jnp.float32
    )
    merged = layer_norm(residual, merge_gain).astype(jnp.bfloat16).reshape(local_rows // 4, 4 * D)
    projected_all = (
        jnp.dot(
            lax.all_gather(merged, "seq", axis=0, tiled=True),
            merge_weight,
            preferred_element_type=jnp.float32,
        )
        + merge_bias.astype(jnp.float32)
    ).astype(jnp.bfloat16)
    images = image_owner.shape[1]
    most = 2 * projected_all.shape[0] // images
    outgoing = route(projected_all, labels[0], image_owner[0], packs, most)
    delivered = lax.all_to_all(outgoing, "pack", split_axis=0, concat_axis=0, tiled=True)
    return delivered[None]


LANES = 128
BLOCK = 512
POSITIONS = 64
FAR_APART = -(2.0**100)
IMAGE_LANE = 96
NORM_ROWS = 16
CHUNKS = (768, 768)


def norm_rows(values, gain_row):
    center = values - jnp.mean(values, axis=-1, keepdims=True)
    spread = jnp.mean(center * center, axis=-1, keepdims=True)
    return center * lax.rsqrt(spread + EPSILON) * gain_row


def stacked(pieces):
    loaded = [piece[...] for piece in pieces]
    return loaded[0] if len(loaded) == 1 else jnp.concatenate(loaded, axis=0)


def in_vmem(value):
    return pltpu.with_memory_space_constraint(value, pltpu.VMEM)


def in_hbm(value):
    return pltpu.with_memory_space_constraint(value, pltpu.HBM)


def label_kernel(segments, rows, columns, mask, out):
    labels = [one[...].astype(jnp.float32) for one in (segments, rows, columns, mask)]
    labels.append(jnp.zeros((4, labels[0].shape[1]), jnp.float32))
    labels = jnp.concatenate(labels, axis=0).astype(jnp.bfloat16)
    shape = (8, LANES)
    row = lax.broadcasted_iota(jnp.int32, shape, 0)
    place = jnp.where(row == lax.broadcasted_iota(jnp.int32, shape, 1), 1.0, 0.0)
    turned = lax.dot_general(
        labels,
        place.astype(jnp.bfloat16),
        (((0,), (0,)), ((), ())),
        preferred_element_type=jnp.float32,
    )
    out[...] = turned.astype(jnp.bfloat16)


def label_call(segments, rows, columns, mask):
    operands = (segments, rows, columns, mask)
    fixed = lambda shape: pl.BlockSpec(shape, lambda i: (0,) * len(shape))
    shape = (segments.shape[1], LANES)
    return pl.pallas_call(
        label_kernel,
        grid=(1,),
        in_specs=[fixed(one.shape) for one in operands],
        out_specs=fixed(shape),
        out_shape=jax.ShapeDtypeStruct(shape, jnp.bfloat16),
        compiler_params=pltpu.CompilerParams(vmem_limit_bytes=4 << 20),
        cost_estimate=pl.CostEstimate(flops=0, bytes_accessed=1024, transcendentals=0),
        name="labels",
    )(*map(in_hbm, operands))


def join_kernel(flip, mine, other, out):
    size = mine.shape[0]
    up = (lax.axis_index("seq") // flip) % 2
    out[pl.ds(pl.multiple_of(up * size, size), size), :] = mine[...]
    out[pl.ds(pl.multiple_of((1 - up) * size, size), size), :] = other[...]


def join_call(flip, mine, other):
    vmem = pl.BlockSpec(memory_space=pltpu.VMEM)
    shape = (2 * mine.shape[0], mine.shape[1])
    return pl.pallas_call(
        functools.partial(join_kernel, flip),
        in_specs=[vmem] * 2,
        out_specs=vmem,
        out_shape=jax.ShapeDtypeStruct(shape, mine.dtype),
        compiler_params=pltpu.CompilerParams(vmem_limit_bytes=4 << 20),
        cost_estimate=pl.CostEstimate(flops=0, bytes_accessed=1024, transcendentals=0),
        name="join",
    )(mine, other)


def qkv_kernel(count, flip, *refs):
    me = lax.axis_index("seq")
    first, second = refs[:count], refs[count : 2 * count]
    all_labels, embed, table, gain, weight = refs[2 * count : 2 * count + 5]
    inputs_out, qkv_out = refs[-2:]
    mine, other = stacked(first), stacked(second)
    leads = me % 2 == 0
    ahead = jnp.where(leads, mine, other)
    behind = jnp.where(leads, other, mine)
    both = jnp.concatenate([ahead, behind], axis=0).astype(jnp.float32)
    rows = both.shape[0]
    at = pl.ds(pl.multiple_of((me // 2 ^ flip) * rows, rows), rows)
    labels = all_labels[at, :].astype(jnp.float32)
    both = jnp.where(labels[:, 3:4] > 0.5, embed[...], both)
    inputs_out[at, :] = both.astype(jnp.bfloat16)
    normed = norm_rows(both, gain[...]).astype(jnp.bfloat16)
    columns = lax.dot_general(
        normed, weight[...], (((1,), (1,)), ((), ())), preferred_element_type=jnp.float32
    )
    lane = lax.broadcasted_iota(jnp.int32, labels.shape, 1)
    numbers = lane.astype(jnp.float32)
    hot = (numbers == labels[:, 1:2]) | (numbers == labels[:, 2:3] + POSITIONS)
    looked = jnp.dot(
        jnp.where(hot, 1.0, 0.0).astype(jnp.bfloat16), table[...], preferred_element_type=jnp.float32
    )
    cosine = looked[:, :LANES] + looked[:, LANES : 2 * LANES]
    sine = looked[:, 2 * LANES : 3 * LANES] + looked[:, 3 * LANES :]
    first_head = lane < HD // 2

    def turn(start):
        a = columns[:, start : start + LANES]
        b = columns[:, start + LANES : start + 2 * LANES]
        return a * cosine - b * sine, b * cosine + a * sine

    factor = HD**-0.5 * float(np.log2(np.e))
    query_a, query_b = (one * factor for one in turn(0))
    key_a, key_b = turn(2 * LANES)
    zero = jnp.zeros_like(key_a)
    image = numbers == labels[:, :1] + IMAGE_LANE
    extra = lane >= IMAGE_LANE
    apart = jnp.where(image, 0.0, FAR_APART)
    parts = [
        jnp.where(image, 1.0, query_a),
        query_b,
        jnp.where(extra, apart, jnp.where(first_head, key_a, zero)),
        jnp.where(first_head, key_b, zero),
        jnp.where(extra, apart, jnp.where(first_head, zero, key_a)),
        jnp.where(first_head, zero, key_b),
    ]
    for head in range(2):
        values = columns[:, (4 + head) * LANES : (5 + head) * LANES]
        parts.append(jnp.where(lane == HD, 1.0, values))
    for number, part in enumerate(parts):
        qkv_out[at, number * LANES : (number + 1) * LANES] = part.astype(jnp.bfloat16)


def qkv_call(flip, first, second, labels, embed, table, gain, weight, earlier, total):
    rows = 2 * sum(piece.shape[0] for piece in first)
    widths = (D, 8 * LANES)
    operands = [*first, *second, labels, embed, table, gain, in_vmem(weight)]
    vmem = pl.BlockSpec(memory_space=pltpu.VMEM)
    held = [in_vmem(one) for one in earlier]
    return pl.pallas_call(
        functools.partial(qkv_kernel, len(first), flip),
        in_specs=[vmem] * (len(operands) + len(earlier)),
        out_specs=[vmem] * len(widths),
        out_shape=[pltpu.VMEM((total, width), jnp.bfloat16) for width in widths],
        input_output_aliases={len(operands) + i: i for i in range(len(earlier))},
        compiler_params=pltpu.CompilerParams(vmem_limit_bytes=14 << 20),
        cost_estimate=pl.CostEstimate(
            flops=6 * rows * D * weight.shape[0],
            bytes_accessed=2 * (rows * 4 * D + weight.size),
            transcendentals=rows,
        ),
        name="norm_qkv",
    )(*operands, *held)


def segment_row(labels):
    pick = jnp.where(lax.broadcasted_iota(jnp.int32, (8, LANES), 1) == 0, 1.0, 0.0)
    return lax.dot_general(
        pick.astype(jnp.bfloat16),
        labels,
        (((1,), (1,)), ((), ())),
        preferred_element_type=jnp.float32,
    )


def attention_kernel(start, images, labels, block, *refs):
    owners, refs = (refs[0], refs[1:]) if images else (None, refs)
    out, *rest = refs
    scores, high = rest[-2:]
    rows = high.shape[1]
    total = block.shape[0]
    segments = segment_row(labels[...])
    one_row = segments[:1]
    lowest = jnp.min(labels[start : start + 16, :1].astype(jnp.float32), axis=0, keepdims=True)
    largest = labels[start + rows - 16 : start + rows, :1].astype(jnp.float32)
    largest = jnp.max(largest, axis=0, keepdims=True)
    begin = jnp.sum(jnp.where(one_row < lowest, 1, 0)) // BLOCK
    end = (jnp.sum(jnp.where(one_row <= largest, 1, 0)) + BLOCK - 1) // BLOCK
    queries = block[start : start + rows, : 2 * LANES]
    high[...] = jnp.full_like(high, 2 * FAR_APART)

    def score(step, carry):
        at = pl.ds(pl.multiple_of(step * BLOCK, BLOCK), BLOCK)
        for head in range(2):
            keys = block[at, (2 + 2 * head) * LANES : (4 + 2 * head) * LANES]
            values = lax.dot_general(
                queries, keys, (((1,), (1,)), ((), ())), preferred_element_type=jnp.float32
            )
            scores[head, step] = values
            tops = [values[:, lane : lane + LANES] for lane in range(0, BLOCK, LANES)]
            high[head] = functools.reduce(jnp.maximum, tops, high[head])
        return carry

    lax.fori_loop(begin, end, score, 0)
    highest = [jnp.max(high[head], axis=-1, keepdims=True) for head in range(2)]

    def weigh(step, carry):
        at = pl.ds(pl.multiple_of(step * BLOCK, BLOCK), BLOCK)
        sums = []
        for head in range(2):
            weights = jnp.exp2(scores[head, step] - highest[head])
            values = block[at, (6 + head) * LANES : (7 + head) * LANES]
            sums.append(
                carry[head]
                + jnp.dot(weights.astype(jnp.bfloat16), values, preferred_element_type=jnp.float32)
            )
        return tuple(sums)

    zero = jnp.zeros((rows, LANES), jnp.float32)
    sums = lax.fori_loop(begin, end, weigh, (zero, zero))
    first, second = (one / one[:, HD : HD + 1] for one in sums)
    lane = lax.broadcasted_iota(jnp.int32, first.shape, 1)
    turned = pltpu.roll(second, HD, 1)
    out[:rows] = jnp.where(lane < HD, first, turned).astype(jnp.bfloat16)
    half = rows // 2
    tail = 2 * HD - LANES
    lane = lane[:half]
    up = pltpu.roll(turned[half:], tail, 1)
    packed = jnp.where(lane < tail, turned[:half], jnp.where(lane < 2 * tail, up, 0.0))
    out[rows:] = packed.astype(jnp.bfloat16)

    if len(rest) > 2:
        note = rest[0]
        row = lax.broadcasted_iota(jnp.int32, note.shape, 0)
        lane = lax.broadcasted_iota(jnp.int32, note.shape, 1)
        found = jnp.zeros(note.shape, jnp.float32)
        for image in range(images):
            below = jnp.sum(jnp.where(one_row < image, 0.25, 0.0), axis=1, keepdims=True)
            inside = jnp.sum(jnp.where(one_row == image, 0.25, 0.0), axis=1, keepdims=True)
            here = row == owners[0, image]
            for place, number in enumerate((below, inside)):
                upper = jnp.floor(number * (1.0 / 16))
                found = jnp.where(here & (lane == 2 * place), upper, found)
                found = jnp.where(here & (lane == 2 * place + 1), number - 16 * upper, found)
        note[...] = found.astype(jnp.bfloat16)


def attention_call(start, rows, labels, block, owners):
    total = block.shape[0]
    vmem = pl.BlockSpec(memory_space=pltpu.VMEM)
    shapes = [jax.ShapeDtypeStruct((rows + rows // 2, LANES), jnp.bfloat16)]
    if owners:
        shapes.append(jax.ShapeDtypeStruct((16, LANES), jnp.bfloat16))
    return pl.pallas_call(
        functools.partial(attention_kernel, start, owners[0].shape[1] if owners else 0),
        in_specs=[vmem, vmem] + [pl.BlockSpec(memory_space=pltpu.SMEM)] * len(owners),
        out_specs=[vmem] * len(shapes),
        out_shape=shapes,
        scratch_shapes=[
            pltpu.VMEM((2, total // BLOCK, rows, BLOCK), jnp.float32),
            pltpu.VMEM((2, rows, LANES), jnp.float32),
        ],
        compiler_params=pltpu.CompilerParams(vmem_limit_bytes=20 << 20),
        cost_estimate=pl.CostEstimate(
            flops=10 * rows * total * 2 * LANES,
            bytes_accessed=2 * block.size,
            transcendentals=rows * total,
        ),
        name="attention",
    )(labels, in_vmem(block), *owners)


def prepare_kernel(shards, ids, out_weight, merge_weight, qkv_weight, spread, *refs):
    *rows, out, merge, qkv, qkv_buffer, spread_buffer, sems = refs
    for row, row_out in zip(rows[: len(rows) // 2], rows[len(rows) // 2 :]):
        row_out[...] = row[...].astype(jnp.float32)[None, :]
    rest = 2 * HD - LANES
    copies = [(qkv_weight, qkv_buffer), (spread, spread_buffer)]
    out[shards * LANES :] = jnp.zeros((shards // 2 * LANES, D), jnp.bfloat16)
    for place in range(shards):
        start = pl.multiple_of(ids[place] * (2 * HD), 16)
        to = (shards + place // 2) * LANES + place % 2 * rest
        copies.append(
            (out_weight.at[pl.ds(start, LANES), :], out.at[pl.ds(place * LANES, LANES), :])
        )
        copies.append((out_weight.at[pl.ds(start + LANES, rest), :], out.at[pl.ds(to, rest), :]))
    copies.append((merge_weight, merge))
    copies = [
        pltpu.make_async_copy(source, target, sems.at[i])
        for i, (source, target) in enumerate(copies)
    ]
    for copy in copies:
        copy.start()
    copies[0].wait()
    copies[1].wait()
    qkv[...] = jnp.dot(
        spread_buffer[...], qkv_buffer[...], preferred_element_type=jnp.float32
    ).astype(jnp.bfloat16)
    for copy in copies[2:]:
        copy.wait()


def prepare_call(shards, ids, out_weight, merge_weight, qkv_weight, spread, rows):
    anywhere = pl.BlockSpec(memory_space=pl.ANY)
    vmem = pl.BlockSpec(memory_space=pltpu.VMEM)
    operands = (out_weight, merge_weight, qkv_weight, spread)
    shapes = [(shards * LANES * 3 // 2, D), merge_weight.shape, (spread.shape[0], D)]
    return pl.pallas_call(
        functools.partial(prepare_kernel, shards),
        in_specs=[pl.BlockSpec(memory_space=pltpu.SMEM)]
        + [anywhere] * len(operands)
        + [vmem] * len(rows),
        out_specs=[vmem] * (len(rows) + len(shapes)),
        out_shape=[pltpu.VMEM((1, row.shape[0]), jnp.float32) for row in rows]
        + [pltpu.VMEM(shape, jnp.bfloat16) for shape in shapes],
        scratch_shapes=[
            pltpu.VMEM(qkv_weight.shape, jnp.bfloat16),
            pltpu.VMEM(spread.shape, jnp.bfloat16),
            pltpu.SemaphoreType.DMA((2 * shards + 3,)),
        ],
        compiler_params=pltpu.CompilerParams(vmem_limit_bytes=10 << 20),
        cost_estimate=pl.CostEstimate(
            flops=2 * spread.size * D,
            bytes_accessed=4 * (out_weight.size + merge_weight.size + qkv_weight.size),
            transcendentals=0,
        ),
        name="prepare",
    )(ids, *map(in_hbm, operands), *rows)


def merge_kernel(start, counts, packs, last, *refs):
    inputs, weight, gain, merge_weight, bias = refs[:5]
    pieces = refs[5 : 5 + sum(counts)]
    *refs, state, tokens = refs[5 + sum(counts) :]
    rows = state.shape[1]
    half = rows // 2
    rest = 2 * HD - LANES
    sources, at = [], 0
    for count in counts:
        sources.append(stacked(pieces[at : at + count]))
        at += count
    shards = len(sources)
    lane = lax.broadcasted_iota(jnp.int32, (half, LANES), 1)
    lined = [source[:rows, :] for source in sources]
    for pair in range(shards // 2):
        mine = sources[2 * pair][rows:, :].astype(jnp.float32)
        other = sources[2 * pair + 1][rows:, :].astype(jnp.float32)
        upper = jnp.where(lane < rest, mine, pltpu.roll(other, rest, 1))
        lower = jnp.where(lane < rest, pltpu.roll(mine, LANES - rest, 1), other)
        lined.append(jnp.concatenate([upper, lower], axis=0).astype(jnp.bfloat16))
    mixed = jnp.dot(
        jnp.concatenate(lined, axis=1), weight[...], preferred_element_type=jnp.float32
    )
    for column in range(D // LANES):
        lanes = slice(column * LANES, (column + 1) * LANES)
        before = inputs[start : start + rows, lanes]
        state[column] = before.astype(jnp.float32) + mixed[:, lanes]
    groups = rows // 4
    for block in range(0, groups, NORM_ROWS):
        for quadrant in range(4):
            at = pl.ds(4 * block + quadrant, NORM_ROWS, stride=4)
            residual = jnp.concatenate(
                [state[column, at, :] for column in range(D // LANES)], axis=1
            )
            tokens[block : block + NORM_ROWS, quadrant * D : (quadrant + 1) * D] = norm_rows(
                residual, gain[...]
            ).astype(jnp.bfloat16)
    total = bias[...] + lax.dot_general(
        tokens[...], merge_weight[...], (((1,), (1,)), ((), ())), preferred_element_type=jnp.float32
    )
    total = total.astype(jnp.bfloat16)
    if not last:
        refs[0][...] = total
        return
    note, *earlier = refs[:-packs]
    me = lax.axis_index("pack")
    outs = refs[-packs:]
    total = jnp.concatenate([*[one[...] for one in earlier], total], axis=0)
    whole = total.shape[1] // LANES
    most = outs[0].shape[0] * LANES // total.shape[1]
    notes = note[...].astype(jnp.float32)
    note_row = lax.broadcasted_iota(jnp.int32, notes.shape, 0)
    slot = lax.broadcasted_iota(jnp.int32, (most, total.shape[0]), 0)
    row = lax.broadcasted_iota(jnp.int32, (most, total.shape[0]), 1)
    for place, out in enumerate(outs):
        found = jnp.where(note_row == (me ^ place), notes, 0.0)
        found = jnp.sum(found, axis=0, keepdims=True)
        first = (16.0 * found[:, :1] + found[:, 1:2]).astype(jnp.int32)
        length = (16.0 * found[:, 2:3] + found[:, 3:4]).astype(jnp.int32)
        chosen = (row == slot + first) & (slot < length)
        chosen = jnp.where(chosen, 1.0, 0.0).astype(jnp.bfloat16)
        block = jnp.dot(chosen, total, preferred_element_type=jnp.float32)
        for column in range(whole):
            out[column * most : (column + 1) * most, :] = block[
                :, column * LANES : (column + 1) * LANES
            ].astype(jnp.bfloat16)
        low = block[: most // 2, whole * LANES :]
        up = block[most // 2 :, whole * LANES :]
        out[whole * most :, :] = jnp.concatenate([low, up], axis=1).astype(jnp.bfloat16)


def merge_call(start, rows, sources, inputs, weight, gain, merge_weight, bias, packs, route):
    groups = rows // 4
    width = merge_weight.shape[0]
    pieces = [piece for source in sources for piece in source]
    vmem = pl.BlockSpec(memory_space=pltpu.VMEM)
    operands = [in_vmem(inputs), in_vmem(weight), gain, in_vmem(merge_weight), bias, *pieces]
    specs = [vmem] * len(operands)
    shapes = [jax.ShapeDtypeStruct((groups, width), jnp.bfloat16)]
    if route:
        most, *others = route
        operands += others
        specs += [vmem] * len(others)
        shapes = [jax.ShapeDtypeStruct((most * width // LANES, LANES), jnp.bfloat16)] * packs
    return pl.pallas_call(
        functools.partial(
            merge_kernel, start, [len(source) for source in sources], packs, bool(route)
        ),
        in_specs=specs,
        out_specs=[vmem] * len(shapes),
        scratch_shapes=[
            pltpu.VMEM((D // LANES, rows, LANES), jnp.float32),
            pltpu.VMEM((groups, 4 * D), jnp.bfloat16),
        ],
        out_shape=shapes,
        compiler_params=pltpu.CompilerParams(vmem_limit_bytes=20 << 20),
        cost_estimate=pl.CostEstimate(
            flops=0,
            bytes_accessed=1024,
            transcendentals=rows,
        ),
        name="out_merge",
    )(*operands)


def place_kernel(place, block, *refs):
    out, rows, sem = refs[-3:]
    most, width = rows.shape
    whole = width // LANES
    half = most // 2
    middle = LANES // 2
    for column in range(whole):
        rows[:, column * LANES : (column + 1) * LANES] = block[
            column * most : (column + 1) * most, :
        ]
    rows[:half, whole * LANES :] = block[whole * most :, :middle]
    rows[half:, whole * LANES :] = block[whole * most :, middle:]
    copy = pltpu.make_async_copy(rows, out.at[lax.axis_index("pack") ^ place], sem)
    copy.start()
    copy.wait()


def place_call(place, block, earlier, shape):
    anywhere = pl.BlockSpec(memory_space=pl.ANY)
    return pl.pallas_call(
        functools.partial(place_kernel, place),
        in_specs=[pl.BlockSpec(memory_space=pltpu.VMEM)] + [anywhere] * len(earlier),
        out_specs=anywhere,
        out_shape=pltpu.HBM(shape, jnp.bfloat16),
        scratch_shapes=[pltpu.VMEM(shape[1:], jnp.bfloat16), pltpu.SemaphoreType.DMA],
        input_output_aliases={1: 0} if earlier else {},
        compiler_params=pltpu.CompilerParams(vmem_limit_bytes=4 << 20),
        cost_estimate=pl.CostEstimate(
            flops=0, bytes_accessed=4 * shape[1] * shape[2], transcendentals=0
        ),
        name="place_rows",
    )(block, *map(in_hbm, earlier))


def send_seq(value, flip):
    size = lax.axis_size("seq")
    return lax.ppermute(value, "seq", [(i, i ^ flip) for i in range(size)])


def after(values, *earlier):
    return lax.optimization_barrier((tuple(values), earlier))[0]


def halves_kernel(across_x, across_y, upper, lower):
    half = upper.shape[0]
    upper[...] = across_x[:half]
    lower[...] = across_y[half:]


def halves_call(across_x, across_y):
    vmem = pl.BlockSpec(memory_space=pltpu.VMEM)
    shape = (across_x.shape[0] // 2, across_x.shape[1])
    return pl.pallas_call(
        halves_kernel,
        in_specs=[vmem] * 2,
        out_specs=[vmem] * 2,
        out_shape=[jax.ShapeDtypeStruct(shape, across_x.dtype)] * 2,
        compiler_params=pltpu.CompilerParams(vmem_limit_bytes=4 << 20),
        cost_estimate=pl.CostEstimate(
            flops=0, bytes_accessed=4 * across_x.size, transcendentals=0
        ),
        name="halves",
    )(across_x, across_y)


def near_shards(value):
    return [send_seq(value, 1), send_seq(value, 2), send_seq(value, 4)]


def far_shards(across_x, across_y):
    upper, lower = halves_call(across_x, across_y)
    return [send_seq(upper, 4), send_seq(lower, 2)]


def weight_order(heads_here):
    quarter = HD // 4
    order = -np.ones((6 * LANES,), np.int32)
    for head in range(heads_here):
        base = head * 3 * HD
        for kind in range(2):
            for half in range(2):
                for letter in range(2):
                    target = (2 * kind + letter) * LANES + head * (HD // 2) + half * quarter
                    source = base + kind * HD + half * (HD // 2) + letter * quarter
                    order[target : target + quarter] = np.arange(source, source + quarter)
        target = (4 + head) * LANES
        order[target : target + HD] = np.arange(base + 2 * HD, base + 3 * HD)
    return order


def angle_table(heads_here):
    quarter = HD // 4
    frequency = (10000.0 ** (-np.arange(quarter) / quarter)).astype(np.float32)
    angles = np.arange(POSITIONS, dtype=np.float32)[:, None] * frequency[None, :]
    pieces = []
    for function in (np.cos, np.sin):
        exact = np.zeros((2 * POSITIONS, LANES), np.float64)
        for head in range(heads_here):
            for half in range(2):
                lane = head * (HD // 2) + half * quarter
                rows = slice(half * POSITIONS, (half + 1) * POSITIONS)
                exact[rows, lane : lane + quarter] = function(angles.astype(np.float64))
        upper = exact.astype(jnp.bfloat16)
        pieces += [upper, (exact - upper.astype(np.float64)).astype(jnp.bfloat16)]
    return np.concatenate(pieces, axis=1)


def fast_local(
    patches,
    patch_mask,
    mask_embed,
    norm_gain,
    qkv_weight,
    segment_ids,
    patch_rows,
    patch_column,
    out_weight,
    merge_gain,
    merge_weight,
    merge_bias,
    image_owner,
):
    local_rows = patches.shape[1]
    shards = lax.axis_size("seq")
    packs = lax.axis_size("pack")
    heads_here = HEADS // shards
    images = image_owner.shape[1]
    total = local_rows * shards
    me = lax.axis_index("seq").astype(jnp.int32)

    value = patches[0]
    own_swap, across_x, across_y = near_shards(value)
    labels = label_call(segment_ids, patch_rows, patch_column, patch_mask)
    for flip in (1, 2, 4):
        labels = join_call(flip, labels, send_seq(labels, flip))

    order = weight_order(heads_here)
    spread = (order[:, None] == np.arange(qkv_weight.shape[1])[None, :]).astype(jnp.bfloat16)
    table = jnp.asarray(angle_table(heads_here))
    ids = jnp.stack([me ^ place for place in range(shards)])
    gain, merge_gain_row, embed, bias, ordered, merge_rows, weight = prepare_call(
        shards,
        ids,
        out_weight,
        merge_weight.T,
        qkv_weight.T,
        jnp.asarray(spread),
        (norm_gain, merge_gain, mask_embed, merge_bias),
    )

    project = lambda place, first, second, earlier: qkv_call(
        place, first, second, labels, embed, table, gain, weight, earlier, total
    )
    buffers = project(0, [value], [own_swap], ())
    across_x, across_y = after([across_x, across_y], buffers[1], ordered)
    far = far_shards(across_x, across_y)
    buffers = project(1, [across_x], [send_seq(across_x, 1)], buffers)
    buffers = project(2, [across_y], [send_seq(across_y, 1)], buffers)
    far = after(far, buffers[1])
    buffers = project(3, far, [send_seq(one, 1) for one in far], buffers)
    inputs, block = buffers

    most = 2 * (total // 4) // images
    first_rows, last_rows = CHUNKS
    (own,) = attention_call(0, first_rows, labels, block, ())
    own_swap, across_x, across_y = near_shards(own)
    labels, block = after([labels, block], own)
    late, note = attention_call(first_rows, last_rows, labels, block, (image_owner,))
    across_x, across_y = after([across_x, across_y], late)
    halves = halves_call(across_x, across_y)
    far = [send_seq(halves[0], 4), send_seq(halves[1], 2)]
    (late,) = after([late], *halves)
    late_shares = [late] + [send_seq(late, flip) for flip in (2, 4, 6)]
    near = [send_seq(one, 1) for one in (across_x, across_y)]
    merge = lambda start, rows, sources, route: merge_call(
        start, rows, sources, inputs, ordered, merge_gain_row, merge_rows, bias, packs, route
    )
    sources = [[own], [own_swap], [across_x], near[:1], [across_y], near[1:], far]
    (projected,) = merge(0, first_rows, sources + [[send_seq(one, 1) for one in far]], ())
    late_shares[1:] = [after([one], projected)[0] for one in late_shares[1:]]
    sources = [[one] for share in late_shares for one in (share, send_seq(share, 1))]
    made = merge(first_rows, last_rows, sources, (most, note, projected))
    sent = {
        flip: lax.ppermute(made[flip], "pack", [(z, z ^ flip) for z in range(packs)])
        for flip in range(packs - 1, 0, -1)
    }
    shape = (packs, most, merge_weight.shape[1])
    routed = place_call(0, made[0], (), shape)
    for flip in (3, 1, 2):
        routed = place_call(flip, sent[flip], (routed,), shape)
    return routed[None]


def local(*arguments):
    patches, weight = arguments[0], arguments[4]
    shards = lax.axis_size("seq")
    fits = shards == 8 and HEADS // shards == 2 and weight.shape[1] == 6 * HD
    fits = fits and patches.shape[1] * shards == sum(CHUNKS) and lax.axis_size("pack") == 4
    return fast_local(*arguments) if fits else general_local(*arguments)


def solution(mesh):
    placed = (
        P("pack", "seq", None),
        P("pack", "seq"),
        P(),
        P(),
        P(None, "seq"),
        P("pack", "seq"),
        P("pack", "seq"),
        P("pack", "seq"),
        P(),
        P(),
        P(None, "seq"),
        P("seq"),
        P("pack", None),
    )
    return jax.shard_map(
        local, mesh=mesh, in_specs=placed, out_specs=P("pack", None, None, "seq"), check_vma=False
    )
```

```python
import functools

import jax
import jax.numpy as jnp
import numpy as np
from jax import lax
from jax.experimental import pallas as pl
from jax.experimental.pallas import tpu as pltpu
from jax.sharding import PartitionSpec as P

D = 1408
HEADS = 16
HD = 88


EPSILON = 1e-06


def layer_norm(values, gain_vector):
    center = values - jnp.mean(values, axis=-1, keepdims=True)
    spread = jnp.mean(center * center, axis=-1, keepdims=True)
    return center * lax.rsqrt(spread + EPSILON) * gain_vector.astype(jnp.float32)


def rotate(vectors, row_index, column_index):
    total_rows, heads_here, head_width = vectors.shape
    quarter = head_width // 4
    frequency = 10000.0 ** (-jnp.arange(quarter, dtype=jnp.float32) / quarter)
    row_angle = row_index.astype(jnp.float32)[:, None] * frequency[None, :]
    column_angle = column_index.astype(jnp.float32)[:, None] * frequency[None, :]
    angles = jnp.stack([row_angle, column_angle], axis=1)[:, None, :, None, :]
    split_up = vectors.reshape(total_rows, heads_here, 2, 2, quarter)
    partner = jnp.stack([-split_up[:, :, :, 1], split_up[:, :, :, 0]], axis=3)
    turned = split_up * jnp.cos(angles) + partner * jnp.sin(angles)
    return turned.reshape(total_rows, heads_here, head_width)


def qkv_block(projected, row_index, column_index):
    turned_queries = rotate(projected[:, :, 0], row_index, column_index)
    turned_keys = rotate(projected[:, :, 1], row_index, column_index)
    return jnp.concatenate([turned_queries, turned_keys, projected[:, :, 2]], axis=-1).astype(
        jnp.bfloat16
    )


def attention(block, segments):
    total_rows, heads_here, triple = block.shape
    head_width = triple // 3
    step_rows = min(512, total_rows)
    query_part = block[:, :, :head_width].reshape(
        total_rows // step_rows, step_rows, heads_here, head_width
    )
    key_part = block[:, :, head_width : 2 * head_width]
    value_part = block[:, :, 2 * head_width :]
    query_segments = segments.reshape(total_rows // step_rows, step_rows)
    scale = head_width ** (-0.5)

    def one_block(inputs_pair):
        queries_here, segments_here = inputs_pair
        scores = (
            jnp.einsum("qhd,khd->hqk", queries_here, key_part, preferred_element_type=jnp.float32)
            * scale
        )
        same_image = (segments_here[:, None] == segments[None, :])[None]
        scores = jnp.where(same_image, scores, -jnp.inf)
        highest = jnp.max(scores, axis=-1, keepdims=True)
        weights = jnp.exp(scores - highest)
        probs = (weights / jnp.sum(weights, axis=-1, keepdims=True)).astype(jnp.bfloat16)
        result = jnp.einsum("hqk,khd->qhd", probs, value_part, preferred_element_type=jnp.float32)
        return result.astype(jnp.bfloat16)

    return lax.map(one_block, (query_part, query_segments)).reshape(
        total_rows, heads_here, head_width
    )


def route(projected, segments, owners_here, packs, most):
    merged_segments = segments[::4]
    images = owners_here.shape[0]
    image_ids = jnp.arange(images, dtype=jnp.int32)
    member = (merged_segments[None, :] == image_ids[:, None]).astype(jnp.int32)
    lengths = jnp.sum(member, axis=1, dtype=jnp.int32)
    starts = jnp.cumsum(lengths, dtype=jnp.int32) - lengths
    owner_ids = jnp.arange(packs, dtype=jnp.int32)
    owned = owners_here[None, :] == owner_ids[:, None]
    first_row = jnp.sum(jnp.where(owned, starts[None, :], 0), axis=1, dtype=jnp.int32)
    owned_length = jnp.sum(jnp.where(owned, lengths[None, :], 0), axis=1, dtype=jnp.int32)
    slots = jnp.arange(most, dtype=jnp.int32)
    source_rows = jnp.clip(first_row[:, None] + slots[None, :], 0, projected.shape[0] - 1)
    picked = jnp.take(projected, source_rows.reshape(-1), axis=0).reshape(
        packs, most, projected.shape[1]
    )
    filled = slots[None, :] < owned_length[:, None]
    return jnp.where(filled[:, :, None], picked, jnp.zeros_like(picked))


def general_local(
    patches,
    patch_mask,
    mask_embed,
    norm_gain,
    qkv_weight,
    segment_ids,
    patch_rows,
    patch_column,
    out_weight,
    merge_gain,
    merge_weight,
    merge_bias,
    image_owner,
):
    local_rows = patches.shape[1]
    shards = lax.axis_size("seq")
    packs = lax.axis_size("pack")
    heads_here = HEADS // shards
    inputs = jnp.where(patch_mask[0][:, None] == 1, mask_embed[None, :], patches[0])
    normed = layer_norm(inputs.astype(jnp.float32), norm_gain).astype(jnp.bfloat16)
    labels = lax.all_gather(
        jnp.stack([segment_ids[0], patch_rows[0], patch_column[0]]), "seq", axis=1, tiled=True
    )
    piece = lax.all_gather(normed, "seq", axis=0, tiled=True)
    span = piece.shape[0]
    projected = jnp.dot(piece, qkv_weight, preferred_element_type=jnp.float32)
    row_part = labels[1]
    column_part = labels[2]
    block = qkv_block(projected.reshape(span, heads_here, 3, HD), row_part, column_part)
    result = attention(block, labels[0])
    mixed_heads = lax.all_to_all(result, "seq", split_axis=0, concat_axis=1, tiled=True)
    attended = mixed_heads.reshape(local_rows, D)
    residual = inputs.astype(jnp.float32) + jnp.dot(
        attended, out_weight, preferred_element_type=jnp.float32
    )
    merged = layer_norm(residual, merge_gain).astype(jnp.bfloat16).reshape(local_rows // 4, 4 * D)
    projected_all = (
        jnp.dot(
            lax.all_gather(merged, "seq", axis=0, tiled=True),
            merge_weight,
            preferred_element_type=jnp.float32,
        )
        + merge_bias.astype(jnp.float32)
    ).astype(jnp.bfloat16)
    images = image_owner.shape[1]
    most = 2 * projected_all.shape[0] // images
    outgoing = route(projected_all, labels[0], image_owner[0], packs, most)
    delivered = lax.all_to_all(outgoing, "pack", split_axis=0, concat_axis=0, tiled=True)
    return delivered[None]


LANES = 128
BLOCK = 512
POSITIONS = 64
FAR_APART = -(2.0**100)
IMAGE_LANE = 96
NORM_ROWS = 16
CHUNKS = (768, 768)


def norm_rows(values, gain_row):
    center = values - jnp.mean(values, axis=-1, keepdims=True)
    spread = jnp.mean(center * center, axis=-1, keepdims=True)
    return center * lax.rsqrt(spread + EPSILON) * gain_row


def stacked(pieces):
    loaded = [piece[...] for piece in pieces]
    return loaded[0] if len(loaded) == 1 else jnp.concatenate(loaded, axis=0)


def in_vmem(value):
    return pltpu.with_memory_space_constraint(value, pltpu.VMEM)


def in_hbm(value):
    return pltpu.with_memory_space_constraint(value, pltpu.HBM)


def payload_kernel(segments, rows, columns, mask, embed, patches, out):
    labels = [one[...].astype(jnp.float32) for one in (segments, rows, columns, mask)]
    labels.append(jnp.zeros((4, labels[0].shape[1]), jnp.float32))
    labels = jnp.concatenate(labels, axis=0).astype(jnp.bfloat16)
    shape = (8, LANES)
    row = lax.broadcasted_iota(jnp.int32, shape, 0)
    place = jnp.where(row == lax.broadcasted_iota(jnp.int32, shape, 1), 1.0, 0.0)
    turned = lax.dot_general(
        labels,
        place.astype(jnp.bfloat16),
        (((0,), (0,)), ((), ())),
        preferred_element_type=jnp.float32,
    )
    masked = turned[:, 3:4] > 0.5
    tokens = jnp.where(
        masked, embed[...].astype(jnp.float32)[None, :], patches[0].astype(jnp.float32)
    )
    out[:, :D] = tokens.astype(jnp.bfloat16)
    out[:, D:] = turned.astype(jnp.bfloat16)


def payload_call(segments, rows, columns, mask, embed, patches):
    count = patches.shape[1]
    operands = (segments, rows, columns, mask, embed, patches)
    fixed = lambda shape: pl.BlockSpec(shape, lambda i: (0,) * len(shape))
    shape = (count, D + LANES)
    return pl.pallas_call(
        payload_kernel,
        grid=(1,),
        in_specs=[fixed(one.shape) for one in operands],
        out_specs=fixed(shape),
        out_shape=jax.ShapeDtypeStruct(shape, jnp.bfloat16),
        compiler_params=pltpu.CompilerParams(vmem_limit_bytes=8 << 20),
        cost_estimate=pl.CostEstimate(
            flops=count * D, bytes_accessed=4 * count * D, transcendentals=0
        ),
        name="payload",
    )(*map(in_hbm, operands))


def qkv_kernel(count, flip, *refs):
    me = lax.axis_index("seq")
    first, second = refs[:count], refs[count : 2 * count]
    table, gain, weight = refs[2 * count : 2 * count + 3]
    inputs_out, qkv_out, label_out = refs[-3:]
    mine, other = stacked(first), stacked(second)
    leads = me % 2 == 0
    ahead = jnp.where(leads, mine, other)
    behind = jnp.where(leads, other, mine)
    both = jnp.concatenate([ahead, behind], axis=0)
    rows = both.shape[0]
    at = pl.ds(pl.multiple_of((me // 2 ^ flip) * rows, rows), rows)
    inputs_out[at, :] = both[:, :D]
    label_out[at, :] = both[:, D:]
    labels = both[:, D:].astype(jnp.float32)
    normed = norm_rows(both[:, :D].astype(jnp.float32), gain[...]).astype(jnp.bfloat16)
    columns = lax.dot_general(
        normed, weight[...], (((1,), (1,)), ((), ())), preferred_element_type=jnp.float32
    )
    lane = lax.broadcasted_iota(jnp.int32, labels.shape, 1)
    numbers = lane.astype(jnp.float32)
    hot = (numbers == labels[:, 1:2]) | (numbers == labels[:, 2:3] + POSITIONS)
    looked = jnp.dot(
        jnp.where(hot, 1.0, 0.0).astype(jnp.bfloat16), table[...], preferred_element_type=jnp.float32
    )
    cosine = looked[:, :LANES] + looked[:, LANES : 2 * LANES]
    sine = looked[:, 2 * LANES : 3 * LANES] + looked[:, 3 * LANES :]
    first_head = lane < HD // 2

    def turn(start):
        a = columns[:, start : start + LANES]
        b = columns[:, start + LANES : start + 2 * LANES]
        return a * cosine - b * sine, b * cosine + a * sine

    query_a, query_b = turn(0)
    key_a, key_b = turn(2 * LANES)
    zero = jnp.zeros_like(key_a)
    image = numbers == labels[:, :1] + IMAGE_LANE
    extra = lane >= IMAGE_LANE
    apart = jnp.where(image, 0.0, FAR_APART)
    parts = [
        jnp.where(image, 1.0, query_a),
        query_b,
        jnp.where(extra, apart, jnp.where(first_head, key_a, zero)),
        jnp.where(first_head, key_b, zero),
        jnp.where(extra, apart, jnp.where(first_head, zero, key_a)),
        jnp.where(first_head, zero, key_b),
    ]
    for head in range(2):
        values = columns[:, (4 + head) * LANES : (5 + head) * LANES]
        parts.append(jnp.where(lane == HD, 1.0, values))
    for number, part in enumerate(parts):
        qkv_out[at, number * LANES : (number + 1) * LANES] = part.astype(jnp.bfloat16)


def qkv_call(flip, first, second, table, gain, weight, earlier, total):
    rows = 2 * sum(piece.shape[0] for piece in first)
    widths = (D, 8 * LANES, LANES)
    operands = [*first, *second, table, gain, in_vmem(weight)]
    vmem = pl.BlockSpec(memory_space=pltpu.VMEM)
    held = [in_vmem(one) for one in earlier]
    return pl.pallas_call(
        functools.partial(qkv_kernel, len(first), flip),
        in_specs=[vmem] * (len(operands) + len(earlier)),
        out_specs=[vmem] * len(widths),
        out_shape=[pltpu.VMEM((total, width), jnp.bfloat16) for width in widths],
        input_output_aliases={len(operands) + i: i for i in range(len(earlier))},
        compiler_params=pltpu.CompilerParams(vmem_limit_bytes=14 << 20),
        cost_estimate=pl.CostEstimate(
            flops=6 * rows * D * weight.shape[0],
            bytes_accessed=2 * (rows * 4 * D + weight.size),
            transcendentals=rows,
        ),
        name="norm_qkv",
    )(*operands, *held)


def segment_row(labels):
    pick = jnp.where(lax.broadcasted_iota(jnp.int32, (8, LANES), 1) == 0, 1.0, 0.0)
    return lax.dot_general(
        pick.astype(jnp.bfloat16),
        labels,
        (((1,), (1,)), ((), ())),
        preferred_element_type=jnp.float32,
    )


def attention_kernel(start, images, labels, block, *refs):
    owners, refs = (refs[0], refs[1:]) if images else (None, refs)
    out, *rest = refs
    scores, high = rest[-2:]
    rows = high.shape[1]
    total = block.shape[0]
    segments = segment_row(labels[...])
    one_row = segments[:1]
    lowest = jnp.min(labels[start : start + 16, :1].astype(jnp.float32), axis=0, keepdims=True)
    largest = labels[start + rows - 16 : start + rows, :1].astype(jnp.float32)
    largest = jnp.max(largest, axis=0, keepdims=True)
    begin = jnp.sum(jnp.where(one_row < lowest, 1, 0)) // BLOCK
    end = (jnp.sum(jnp.where(one_row <= largest, 1, 0)) + BLOCK - 1) // BLOCK
    queries = block[start : start + rows, : 2 * LANES]
    factor = HD**-0.5 * float(np.log2(np.e))
    high[...] = jnp.full_like(high, 2 * FAR_APART)

    def score(step, carry):
        at = pl.ds(pl.multiple_of(step * BLOCK, BLOCK), BLOCK)
        for head in range(2):
            keys = block[at, (2 + 2 * head) * LANES : (4 + 2 * head) * LANES]
            values = lax.dot_general(
                queries, keys, (((1,), (1,)), ((), ())), preferred_element_type=jnp.float32
            )
            scores[head, step] = values
            tops = [values[:, lane : lane + LANES] for lane in range(0, BLOCK, LANES)]
            high[head] = functools.reduce(jnp.maximum, tops, high[head])
        return carry

    lax.fori_loop(begin, end, score, 0)
    highest = [jnp.max(high[head], axis=-1, keepdims=True) for head in range(2)]

    def weigh(step, carry):
        at = pl.ds(pl.multiple_of(step * BLOCK, BLOCK), BLOCK)
        sums = []
        for head in range(2):
            weights = jnp.exp2((scores[head, step] - highest[head]) * factor)
            values = block[at, (6 + head) * LANES : (7 + head) * LANES]
            sums.append(
                carry[head]
                + jnp.dot(weights.astype(jnp.bfloat16), values, preferred_element_type=jnp.float32)
            )
        return tuple(sums)

    zero = jnp.zeros((rows, LANES), jnp.float32)
    sums = lax.fori_loop(begin, end, weigh, (zero, zero))
    first, second = (one / one[:, HD : HD + 1] for one in sums)
    lane = lax.broadcasted_iota(jnp.int32, first.shape, 1)
    turned = pltpu.roll(second, HD, 1)
    out[:rows] = jnp.where(lane < HD, first, turned).astype(jnp.bfloat16)
    half = rows // 2
    tail = 2 * HD - LANES
    lane = lane[:half]
    up = pltpu.roll(turned[half:], tail, 1)
    packed = jnp.where(lane < tail, turned[:half], jnp.where(lane < 2 * tail, up, 0.0))
    out[rows:] = packed.astype(jnp.bfloat16)

    if len(rest) > 2:
        note = rest[0]
        row = lax.broadcasted_iota(jnp.int32, note.shape, 0)
        lane = lax.broadcasted_iota(jnp.int32, note.shape, 1)
        found = jnp.zeros(note.shape, jnp.float32)
        for image in range(images):
            below = jnp.sum(jnp.where(one_row < image, 0.25, 0.0), axis=1, keepdims=True)
            inside = jnp.sum(jnp.where(one_row == image, 0.25, 0.0), axis=1, keepdims=True)
            here = row == owners[0, image]
            for place, number in enumerate((below, inside)):
                upper = jnp.floor(number * (1.0 / 16))
                found = jnp.where(here & (lane == 2 * place), upper, found)
                found = jnp.where(here & (lane == 2 * place + 1), number - 16 * upper, found)
        note[...] = found.astype(jnp.bfloat16)


def attention_call(start, rows, labels, block, owners):
    total = block.shape[0]
    vmem = pl.BlockSpec(memory_space=pltpu.VMEM)
    shapes = [jax.ShapeDtypeStruct((rows + rows // 2, LANES), jnp.bfloat16)]
    if owners:
        shapes.append(jax.ShapeDtypeStruct((16, LANES), jnp.bfloat16))
    return pl.pallas_call(
        functools.partial(attention_kernel, start, owners[0].shape[1] if owners else 0),
        in_specs=[vmem, vmem] + [pl.BlockSpec(memory_space=pltpu.SMEM)] * len(owners),
        out_specs=[vmem] * len(shapes),
        out_shape=shapes,
        scratch_shapes=[
            pltpu.VMEM((2, total // BLOCK, rows, BLOCK), jnp.float32),
            pltpu.VMEM((2, rows, LANES), jnp.float32),
        ],
        compiler_params=pltpu.CompilerParams(vmem_limit_bytes=20 << 20),
        cost_estimate=pl.CostEstimate(
            flops=10 * rows * total * 2 * LANES,
            bytes_accessed=2 * block.size,
            transcendentals=rows * total,
        ),
        name="attention",
    )(in_vmem(labels), in_vmem(block), *owners)


def prepare_kernel(shards, ids, out_weight, merge_weight, qkv_weight, spread, *refs):
    *rows, out, merge, qkv, qkv_buffer, spread_buffer, sems = refs
    for row, row_out in zip(rows[: len(rows) // 2], rows[len(rows) // 2 :]):
        row_out[...] = row[...].astype(jnp.float32)[None, :]
    rest = 2 * HD - LANES
    copies = [(qkv_weight, qkv_buffer), (spread, spread_buffer)]
    out[shards * LANES :] = jnp.zeros((shards // 2 * LANES, D), jnp.bfloat16)
    for place in range(shards):
        start = pl.multiple_of(ids[place] * (2 * HD), 16)
        to = (shards + place // 2) * LANES + place % 2 * rest
        copies.append(
            (out_weight.at[pl.ds(start, LANES), :], out.at[pl.ds(place * LANES, LANES), :])
        )
        copies.append((out_weight.at[pl.ds(start + LANES, rest), :], out.at[pl.ds(to, rest), :]))
    copies.append((merge_weight, merge))
    copies = [
        pltpu.make_async_copy(source, target, sems.at[i])
        for i, (source, target) in enumerate(copies)
    ]
    for copy in copies:
        copy.start()
    copies[0].wait()
    copies[1].wait()
    qkv[...] = jnp.dot(
        spread_buffer[...], qkv_buffer[...], preferred_element_type=jnp.float32
    ).astype(jnp.bfloat16)
    for copy in copies[2:]:
        copy.wait()


def prepare_call(shards, ids, out_weight, merge_weight, qkv_weight, spread, rows):
    anywhere = pl.BlockSpec(memory_space=pl.ANY)
    vmem = pl.BlockSpec(memory_space=pltpu.VMEM)
    operands = (out_weight, merge_weight, qkv_weight, spread)
    shapes = [(shards * LANES * 3 // 2, D), merge_weight.shape, (spread.shape[0], D)]
    return pl.pallas_call(
        functools.partial(prepare_kernel, shards),
        in_specs=[pl.BlockSpec(memory_space=pltpu.SMEM)]
        + [anywhere] * len(operands)
        + [vmem] * len(rows),
        out_specs=[vmem] * (len(rows) + len(shapes)),
        out_shape=[pltpu.VMEM((1, row.shape[0]), jnp.float32) for row in rows]
        + [pltpu.VMEM(shape, jnp.bfloat16) for shape in shapes],
        scratch_shapes=[
            pltpu.VMEM(qkv_weight.shape, jnp.bfloat16),
            pltpu.VMEM(spread.shape, jnp.bfloat16),
            pltpu.SemaphoreType.DMA((2 * shards + 3,)),
        ],
        compiler_params=pltpu.CompilerParams(vmem_limit_bytes=10 << 20),
        cost_estimate=pl.CostEstimate(
            flops=2 * spread.size * D,
            bytes_accessed=4 * (out_weight.size + merge_weight.size + qkv_weight.size),
            transcendentals=0,
        ),
        name="prepare",
    )(ids, *map(in_hbm, operands), *rows)


def merge_kernel(start, counts, packs, last, *refs):
    inputs, weight, gain, merge_weight, bias = refs[:5]
    pieces = refs[5 : 5 + sum(counts)]
    *refs, state, tokens = refs[5 + sum(counts) :]
    rows = state.shape[1]
    half = rows // 2
    rest = 2 * HD - LANES
    sources, at = [], 0
    for count in counts:
        sources.append(stacked(pieces[at : at + count]))
        at += count
    shards = len(sources)
    lane = lax.broadcasted_iota(jnp.int32, (half, LANES), 1)
    lined = [source[:rows, :] for source in sources]
    for pair in range(shards // 2):
        mine = sources[2 * pair][rows:, :].astype(jnp.float32)
        other = sources[2 * pair + 1][rows:, :].astype(jnp.float32)
        upper = jnp.where(lane < rest, mine, pltpu.roll(other, rest, 1))
        lower = jnp.where(lane < rest, pltpu.roll(mine, LANES - rest, 1), other)
        lined.append(jnp.concatenate([upper, lower], axis=0).astype(jnp.bfloat16))
    mixed = jnp.dot(
        jnp.concatenate(lined, axis=1), weight[...], preferred_element_type=jnp.float32
    )
    for column in range(D // LANES):
        lanes = slice(column * LANES, (column + 1) * LANES)
        before = inputs[start : start + rows, lanes]
        state[column] = before.astype(jnp.float32) + mixed[:, lanes]
    groups = rows // 4
    for block in range(0, groups, NORM_ROWS):
        for quadrant in range(4):
            at = pl.ds(4 * block + quadrant, NORM_ROWS, stride=4)
            residual = jnp.concatenate(
                [state[column, at, :] for column in range(D // LANES)], axis=1
            )
            tokens[block : block + NORM_ROWS, quadrant * D : (quadrant + 1) * D] = norm_rows(
                residual, gain[...]
            ).astype(jnp.bfloat16)
    total = bias[...] + lax.dot_general(
        tokens[...], merge_weight[...], (((1,), (1,)), ((), ())), preferred_element_type=jnp.float32
    )
    total = total.astype(jnp.bfloat16)
    if not last:
        refs[0][...] = total
        return
    note, *earlier = refs[:-packs]
    me = lax.axis_index("pack")
    outs = refs[-packs:]
    total = jnp.concatenate([*[one[...] for one in earlier], total], axis=0)
    whole = total.shape[1] // LANES
    most = outs[0].shape[0] * LANES // total.shape[1]
    notes = note[...].astype(jnp.float32)
    note_row = lax.broadcasted_iota(jnp.int32, notes.shape, 0)
    slot = lax.broadcasted_iota(jnp.int32, (most, total.shape[0]), 0)
    row = lax.broadcasted_iota(jnp.int32, (most, total.shape[0]), 1)
    for place, out in enumerate(outs):
        found = jnp.where(note_row == (me ^ place), notes, 0.0)
        found = jnp.sum(found, axis=0, keepdims=True)
        first = (16.0 * found[:, :1] + found[:, 1:2]).astype(jnp.int32)
        length = (16.0 * found[:, 2:3] + found[:, 3:4]).astype(jnp.int32)
        chosen = (row == slot + first) & (slot < length)
        chosen = jnp.where(chosen, 1.0, 0.0).astype(jnp.bfloat16)
        block = jnp.dot(chosen, total, preferred_element_type=jnp.float32)
        for column in range(whole):
            out[column * most : (column + 1) * most, :] = block[
                :, column * LANES : (column + 1) * LANES
            ].astype(jnp.bfloat16)
        low = block[: most // 2, whole * LANES :]
        up = block[most // 2 :, whole * LANES :]
        out[whole * most :, :] = jnp.concatenate([low, up], axis=1).astype(jnp.bfloat16)


def merge_call(start, rows, sources, inputs, weight, gain, merge_weight, bias, packs, route):
    groups = rows // 4
    width = merge_weight.shape[0]
    pieces = [piece for source in sources for piece in source]
    vmem = pl.BlockSpec(memory_space=pltpu.VMEM)
    operands = [in_vmem(inputs), in_vmem(weight), gain, in_vmem(merge_weight), bias, *pieces]
    specs = [vmem] * len(operands)
    shapes = [jax.ShapeDtypeStruct((groups, width), jnp.bfloat16)]
    if route:
        most, *others = route
        operands += others
        specs += [vmem] * len(others)
        shapes = [jax.ShapeDtypeStruct((most * width // LANES, LANES), jnp.bfloat16)] * packs
    return pl.pallas_call(
        functools.partial(
            merge_kernel, start, [len(source) for source in sources], packs, bool(route)
        ),
        in_specs=specs,
        out_specs=[vmem] * len(shapes),
        scratch_shapes=[
            pltpu.VMEM((D // LANES, rows, LANES), jnp.float32),
            pltpu.VMEM((groups, 4 * D), jnp.bfloat16),
        ],
        out_shape=shapes,
        compiler_params=pltpu.CompilerParams(vmem_limit_bytes=20 << 20),
        cost_estimate=pl.CostEstimate(
            flops=0,
            bytes_accessed=1024,
            transcendentals=rows,
        ),
        name="out_merge",
    )(*operands)


def place_kernel(place, block, *refs):
    out, rows, sem = refs[-3:]
    most, width = rows.shape
    whole = width // LANES
    half = most // 2
    middle = LANES // 2
    for column in range(whole):
        rows[:, column * LANES : (column + 1) * LANES] = block[
            column * most : (column + 1) * most, :
        ]
    rows[:half, whole * LANES :] = block[whole * most :, :middle]
    rows[half:, whole * LANES :] = block[whole * most :, middle:]
    copy = pltpu.make_async_copy(rows, out.at[lax.axis_index("pack") ^ place], sem)
    copy.start()
    copy.wait()


def place_call(place, block, earlier, shape):
    anywhere = pl.BlockSpec(memory_space=pl.ANY)
    return pl.pallas_call(
        functools.partial(place_kernel, place),
        in_specs=[pl.BlockSpec(memory_space=pltpu.VMEM)] + [anywhere] * len(earlier),
        out_specs=anywhere,
        out_shape=pltpu.HBM(shape, jnp.bfloat16),
        scratch_shapes=[pltpu.VMEM(shape[1:], jnp.bfloat16), pltpu.SemaphoreType.DMA],
        input_output_aliases={1: 0} if earlier else {},
        compiler_params=pltpu.CompilerParams(vmem_limit_bytes=4 << 20),
        cost_estimate=pl.CostEstimate(
            flops=0, bytes_accessed=4 * shape[1] * shape[2], transcendentals=0
        ),
        name="place_rows",
    )(block, *map(in_hbm, earlier))


def send_seq(value, flip):
    size = lax.axis_size("seq")
    return lax.ppermute(value, "seq", [(i, i ^ flip) for i in range(size)])


def after(values, *earlier):
    return lax.optimization_barrier((tuple(values), earlier))[0]


def halves_kernel(across_x, across_y, upper, lower):
    half = upper.shape[0]
    upper[...] = across_x[:half]
    lower[...] = across_y[half:]


def halves_call(across_x, across_y):
    vmem = pl.BlockSpec(memory_space=pltpu.VMEM)
    shape = (across_x.shape[0] // 2, across_x.shape[1])
    return pl.pallas_call(
        halves_kernel,
        in_specs=[vmem] * 2,
        out_specs=[vmem] * 2,
        out_shape=[jax.ShapeDtypeStruct(shape, across_x.dtype)] * 2,
        compiler_params=pltpu.CompilerParams(vmem_limit_bytes=4 << 20),
        cost_estimate=pl.CostEstimate(
            flops=0, bytes_accessed=4 * across_x.size, transcendentals=0
        ),
        name="halves",
    )(across_x, across_y)


def near_shards(value):
    return [send_seq(value, 1), send_seq(value, 2), send_seq(value, 4)]


def far_shards(across_x, across_y):
    upper, lower = halves_call(across_x, across_y)
    return [send_seq(upper, 4), send_seq(lower, 2)]


def weight_order(heads_here):
    quarter = HD // 4
    order = -np.ones((6 * LANES,), np.int32)
    for head in range(heads_here):
        base = head * 3 * HD
        for kind in range(2):
            for half in range(2):
                for letter in range(2):
                    target = (2 * kind + letter) * LANES + head * (HD // 2) + half * quarter
                    source = base + kind * HD + half * (HD // 2) + letter * quarter
                    order[target : target + quarter] = np.arange(source, source + quarter)
        target = (4 + head) * LANES
        order[target : target + HD] = np.arange(base + 2 * HD, base + 3 * HD)
    return order


def angle_table(heads_here):
    quarter = HD // 4
    frequency = (10000.0 ** (-np.arange(quarter) / quarter)).astype(np.float32)
    angles = np.arange(POSITIONS, dtype=np.float32)[:, None] * frequency[None, :]
    pieces = []
    for function in (np.cos, np.sin):
        exact = np.zeros((2 * POSITIONS, LANES), np.float64)
        for head in range(heads_here):
            for half in range(2):
                lane = head * (HD // 2) + half * quarter
                rows = slice(half * POSITIONS, (half + 1) * POSITIONS)
                exact[rows, lane : lane + quarter] = function(angles.astype(np.float64))
        upper = exact.astype(jnp.bfloat16)
        pieces += [upper, (exact - upper.astype(np.float64)).astype(jnp.bfloat16)]
    return np.concatenate(pieces, axis=1)


def fast_local(
    patches,
    patch_mask,
    mask_embed,
    norm_gain,
    qkv_weight,
    segment_ids,
    patch_rows,
    patch_column,
    out_weight,
    merge_gain,
    merge_weight,
    merge_bias,
    image_owner,
):
    local_rows = patches.shape[1]
    shards = lax.axis_size("seq")
    packs = lax.axis_size("pack")
    heads_here = HEADS // shards
    images = image_owner.shape[1]
    total = local_rows * shards
    me = lax.axis_index("seq").astype(jnp.int32)

    value = payload_call(segment_ids, patch_rows, patch_column, patch_mask, mask_embed, patches)
    own_swap, across_x, across_y = near_shards(value)

    order = weight_order(heads_here)
    spread = (order[:, None] == np.arange(qkv_weight.shape[1])[None, :]).astype(jnp.bfloat16)
    table = jnp.asarray(angle_table(heads_here))
    ids = jnp.stack([me ^ place for place in range(shards)])
    gain, merge_gain_row, bias, ordered, merge_rows, weight = prepare_call(
        shards,
        ids,
        out_weight,
        merge_weight.T,
        qkv_weight.T,
        jnp.asarray(spread),
        (norm_gain, merge_gain, merge_bias),
    )

    project = lambda place, first, second, earlier: qkv_call(
        place, first, second, table, gain, weight, earlier, total
    )
    buffers = project(0, [value], [own_swap], ())
    across_x, across_y = after([across_x, across_y], buffers[2], ordered)
    far = far_shards(across_x, across_y)
    buffers = project(1, [across_x], [send_seq(across_x, 1)], buffers)
    buffers = project(2, [across_y], [send_seq(across_y, 1)], buffers)
    far = after(far, buffers[2])
    buffers = project(3, far, [send_seq(one, 1) for one in far], buffers)
    inputs, block, labels = buffers

    most = 2 * (total // 4) // images
    first_rows, last_rows = CHUNKS
    (own,) = attention_call(0, first_rows, labels, block, ())
    own_swap, across_x, across_y = near_shards(own)
    labels, block = after([labels, block], own)
    late, note = attention_call(first_rows, last_rows, labels, block, (image_owner,))
    across_x, across_y = after([across_x, across_y], late)
    halves = halves_call(across_x, across_y)
    far = [send_seq(halves[0], 4), send_seq(halves[1], 2)]
    (late,) = after([late], *halves)
    late_shares = [late] + [send_seq(late, flip) for flip in (2, 4, 6)]
    near = [send_seq(one, 1) for one in (across_x, across_y)]
    merge = lambda start, rows, sources, route: merge_call(
        start, rows, sources, inputs, ordered, merge_gain_row, merge_rows, bias, packs, route
    )
    sources = [[own], [own_swap], [across_x], near[:1], [across_y], near[1:], far]
    (projected,) = merge(0, first_rows, sources + [[send_seq(one, 1) for one in far]], ())
    late_shares[1:] = [after([one], projected)[0] for one in late_shares[1:]]
    sources = [[one] for share in late_shares for one in (share, send_seq(share, 1))]
    made = merge(first_rows, last_rows, sources, (most, note, projected))
    sent = {
        flip: lax.ppermute(made[flip], "pack", [(z, z ^ flip) for z in range(packs)])
        for flip in range(packs - 1, 0, -1)
    }
    shape = (packs, most, merge_weight.shape[1])
    routed = place_call(0, made[0], (), shape)
    for flip in (3, 1, 2):
        routed = place_call(flip, sent[flip], (routed,), shape)
    return routed[None]


def local(*arguments):
    patches, weight = arguments[0], arguments[4]
    shards = lax.axis_size("seq")
    fits = shards == 8 and HEADS // shards == 2 and weight.shape[1] == 6 * HD
    fits = fits and patches.shape[1] * shards == sum(CHUNKS) and lax.axis_size("pack") == 4
    return fast_local(*arguments) if fits else general_local(*arguments)


def solution(mesh):
    placed = (
        P("pack", "seq", None),
        P("pack", "seq"),
        P(),
        P(),
        P(None, "seq"),
        P("pack", "seq"),
        P("pack", "seq"),
        P("pack", "seq"),
        P(),
        P(),
        P(None, "seq"),
        P("seq"),
        P("pack", None),
    )
    return jax.shard_map(
        local, mesh=mesh, in_specs=placed, out_specs=P("pack", None, None, "seq"), check_vma=False
    )
```
